32 devices in a mesh: rows: 8 (over z, y), frames: 4 (over x, core).
Axes of the slice: x: 2, y: 2, z: 4, core: 2. Of those that a mesh axis runs over, the one named last changes fastest.
Arguments:
- features: bfloat16 [24, 2048, 256], P('rows', 'frames')
- segment_ids: int32 [24, 2048], P('rows'), may hold values from 0 to 7, as said below
- timesteps: int32 [24, 8], P('rows'), may hold values from 0 to 999
- cotangent: bfloat16 [24, 1024, 256], P('rows', 'frames'), may hold values from -6 to 6
- narrow_slab: float32 [4352, 256], P('rows'), may hold values from -0.21875 to 0.21875
- broad_slab: float32 [256, 1536], P('rows')
- model_gains: float32 [12, 256], P(None, 'rows')
- hidden_gains: float32 [3, 1024], P(None, 'rows')
- narrow_first: float32 [4352, 256], P('rows'), may hold values from -128 to 128
- narrow_second: float32 [4352, 256], P('rows'), may hold values from 49.152 to 196.608
- broad_first: float32 [256, 1536], P('rows'), may hold values from -128 to 128
- broad_second: float32 [256, 1536], P('rows'), may hold values from 49.152 to 196.608
- gains_first: float32 [12, 256], P(None, 'rows'), may hold values from -128 to 128
- gains_second: float32 [12, 256], P(None, 'rows'), may hold values from 49.152 to 196.608
- hidden_first: float32 [3, 1024], P(None, 'rows'), may hold values from -128 to 128
- hidden_second: float32 [3, 1024], P(None, 'rows'), may hold values from 49.152 to 196.608
Outputs:
- frames_out: bfloat16 [24, 1024, 256], P('rows', 'frames')
- input_grad: float32 [24, 2048, 256], P('rows', 'frames')
- narrow_moment: float32 [4352, 256], P('rows')
- narrow_square: float32 [4352, 256], P('rows')
- narrow_update: float32 [4352, 256], P('rows')
- broad_moment: float32 [256, 1536], P('rows')
- broad_square: float32 [256, 1536], P('rows')
- broad_update: float32 [256, 1536], P('rows')
- gains_moment: float32 [12, 256], P(None, 'rows')
- gains_square: float32 [12, 256], P(None, 'rows')
- gains_update: float32 [12, 256], P(None, 'rows')
- hidden_moment: float32 [3, 1024], P(None, 'rows')
- hidden_square: float32 [3, 1024], P(None, 'rows')
- hidden_update: float32 [3, 1024], P(None, 'rows')
- narrow_copy: bfloat16 [4352, 256], P('rows')
- broad_copy: bfloat16 [256, 1536], P('rows')
The draws below stay inside these ranges and needn't reach their ends.
Inputs may be any that keep to these rules, and one draw needn't show every extreme that they name: `segment_ids`: along each row the ids never fall, every id from 0 to 7 covers 2 or more frames, and each change of id lies at an even frame within the first or the last 256 frames of the row.
All inputs are finite; a program needn't handle non-finite values.
Results may differ from the reference program's by a relative error of at most 0.013.
Values may be sent and summed in bfloat16 or wider, within the bound.
A program may use at most 128 MiB of HBM per device.

```python
import math
import jax
import jax.numpy as jnp
from jax import lax

C = 256
TE = 1024
H = 2
HD = 64
FF = 1024
G = 8
LEN = 2048
NSEG = 8
STEP = 10
INNER = 128
ROWS = 24
OUT = 1024
HALF_SPAN = 256
KC = 4352
KR = 1536


def draw_features(key, part):
    key = jax.random.fold_in(key, 11)
    ramp = jnp.arange(LEN, dtype=jnp.float32) / LEN
    base = jnp.clip(jax.random.normal(key, (ROWS, LEN, C), jnp.float32), -6.0, 6.0)
    scale_row = 1.0 + 2.0 * ramp
    return (base * scale_row[None, :, None]).astype(jnp.bfloat16)


def draw_segment_ids(key, part):
    key = jax.random.fold_in(key, 5)

    def one_row(row_key):
        key_count, key_low, key_high = jax.random.split(row_key, 3)
        low_count = jax.random.randint(key_count, (), 0, NSEG)
        low_cuts = 2 * (jax.random.permutation(key_low, HALF_SPAN // 2)[:NSEG - 1] + 1)
        high_cuts = LEN - 2 * (jax.random.permutation(key_high, HALF_SPAN // 2)[:NSEG - 1] + 1)
        cuts = jnp.where(jnp.arange(NSEG - 1) < low_count, low_cuts, high_cuts)
        positions = jnp.arange(LEN)
        return jnp.sum((positions[:, None] >= cuts[None, :]).astype(jnp.int32), axis=1).astype(jnp.int32)
    return jax.vmap(one_row)(jax.random.split(key, ROWS))


def draw_broad_slab(key, part):
    key = jax.random.fold_in(key, 7)
    base = jnp.clip(jax.random.normal(key, (C, KR), jnp.float32), -4.0, 4.0)
    column = jnp.arange(KR)
    wide_out = (column >= 3 * INNER) & (column < 4 * INNER)
    scale_col = jnp.where(wide_out, 6.0 / INNER ** 0.5, 1.0 / C ** 0.5)
    return base * scale_col[None, :]


def draw_model_gains(key, part):
    key = jax.random.fold_in(key, 9)
    key_gain, key_shift = jax.random.split(key)
    gain_rows = jnp.exp(jax.random.uniform(key_gain, (12, C), jnp.float32, math.log(0.7), math.log(1.4)))
    shift_rows = 0.3 * jnp.clip(jax.random.normal(key_shift, (12, C), jnp.float32), -4.0, 4.0)
    row_index = jnp.arange(12)
    is_gain = (row_index == 0) | (row_index == 3) | (row_index == 5) | (row_index == 8)
    return jnp.where(is_gain[:, None], gain_rows, shift_rows)


def draw_hidden_gains(key, part):
    key = jax.random.fold_in(key, 13)
    key_bias, key_logs = jax.random.split(key)
    bias_row = 0.3 * jnp.clip(jax.random.normal(key_bias, (1, FF), jnp.float32), -4.0, 4.0)
    log_rows = jax.random.uniform(key_logs, (2, FF), jnp.float32, -0.7, 0.7)
    return jnp.concatenate([bias_row, log_rows], axis=0)


def touch_ends(values, key, least, high):
    longest = values.shape.index(max(values.shape))
    spots = []
    for shift in (0, 1):
        where = [jax.random.randint(jax.random.fold_in(key, axis), (), 0, length) for axis, length in enumerate(values.shape)]
        where[longest] = (where[longest] + shift) % values.shape[longest]
        spots.append(tuple(where))
    return values.at[spots[0]].set(least).at[spots[1]].set(high)


def levels(own_key, dims, cuts, smallest, high):
    level = 1.0
    for dim, blocks in cuts:
        draws = jax.random.uniform(jax.random.fold_in(jax.random.fold_in(own_key, 6), dim), (blocks,), jnp.float32, smallest / len(cuts), high / len(cuts))
        level = level * jnp.repeat(jnp.exp(draws), dims[dim] // blocks).reshape((-1,) + (1,) * (len(dims) - 1 - dim))
    return level


def normal_values(stream_key, shape, deviation, limit, pieces=(), kind=jnp.bfloat16):
    loudness = levels(stream_key, shape, pieces, -0.22, 0.18) if pieces else 1.0
    result = jax.random.normal(stream_key, shape, jnp.float32) * deviation * loudness
    return jnp.minimum(jnp.maximum(result, -limit), limit).astype(kind)


def setup_inputs(seed: int = 0) -> dict:
    streams_of = jax.random.split(jax.random.key(seed), 17)
    features = draw_features(jax.random.fold_in(streams_of[16], 71), 0)
    segment_ids = draw_segment_ids(jax.random.fold_in(streams_of[16], 71), 0)
    timesteps = touch_ends(jax.random.randint(streams_of[2], (ROWS, NSEG), 0, 1000), jax.random.fold_in(streams_of[2], 1), 0, 999).astype(jnp.int32)
    cotangent = normal_values(streams_of[3], (ROWS, OUT, C), 1.0, 6.0, ((0, 8), (1, 4)))
    narrow_slab = normal_values(streams_of[4], (KC, C), (3 * C) ** -0.5, 0.21875, ((0, 8),), jnp.float32)
    broad_slab = draw_broad_slab(jax.random.fold_in(streams_of[16], 71), 0)
    model_gains = draw_model_gains(jax.random.fold_in(streams_of[16], 71), 0)
    hidden_gains = draw_hidden_gains(jax.random.fold_in(streams_of[16], 71), 0)
    narrow_first = normal_values(streams_of[8], (KC, C), (0.11 * (ROWS * LEN) ** 0.5), 128.0, ((0, 8),), jnp.float32)
    narrow_second = jnp.clip(jnp.exp(math.log(196.608) - 1.3862944 * jax.random.uniform(streams_of[9], (KC, C), jnp.float32) ** levels(streams_of[9], (KC, C), ((0, 8),), -0.2, 0.2)), 49.152, 196.608)
    broad_first = normal_values(streams_of[10], (C, KR), (0.11 * (ROWS * LEN) ** 0.5), 128.0, ((0, 8),), jnp.float32)
    broad_second = jnp.clip(jnp.exp(math.log(196.608) - 1.3862944 * jax.random.uniform(streams_of[11], (C, KR), jnp.float32) ** levels(streams_of[11], (C, KR), ((0, 8),), -0.2, 0.2)), 49.152, 196.608)
    gains_first = normal_values(streams_of[12], (12, C), (0.11 * (ROWS * LEN) ** 0.5), 128.0, ((1, 8),), jnp.float32)
    gains_second = jnp.clip(jnp.exp(math.log(196.608) - 1.3862944 * jax.random.uniform(streams_of[13], (12, C), jnp.float32) ** levels(streams_of[13], (12, C), ((1, 8),), -0.2, 0.2)), 49.152, 196.608)
    hidden_first = normal_values(streams_of[14], (3, FF), (0.11 * (ROWS * LEN) ** 0.5), 128.0, ((1, 8),), jnp.float32)
    hidden_second = jnp.clip(jnp.exp(math.log(196.608) - 1.3862944 * jax.random.uniform(streams_of[15], (3, FF), jnp.float32) ** levels(streams_of[15], (3, FF), ((1, 8),), -0.2, 0.2)), 49.152, 196.608)
    return {"features": features, "segment_ids": segment_ids, "timesteps": timesteps, "cotangent": cotangent, "narrow_slab": narrow_slab, "broad_slab": broad_slab, "model_gains": model_gains, "hidden_gains": hidden_gains, "narrow_first": narrow_first, "narrow_second": narrow_second, "broad_first": broad_first, "broad_second": broad_second, "gains_first": gains_first, "gains_second": gains_second, "hidden_first": hidden_first, "hidden_second": hidden_second}


PRECISE = lax.Precision.HIGHEST
EPS_NORM = 1e-05
EPS_ADAM = 1e-08
BETA_ONE = 0.9
BETA_TWO = 0.999
RATE_SLABS = 0.08
RATE_GAINS = 0.4
DECAY_RATE = 0.01
MASK_FILL = -1e+30

@jax.custom_vjp
def low(v):
    return lax.optimization_barrier(v.astype(jnp.bfloat16)).astype(jnp.float32)

@jax.custom_vjp
def low_back(v):
    return v

def low_keep(v):
    return (low(v), None)

def low_pass(kept, grad):
    return (grad,)

def back_keep(v):
    return (v, None)

def back_low(kept, grad):
    return (low(grad),)
low.defvjp(low_keep, low_pass)
low_back.defvjp(back_keep, back_low)

def mish_act(values):
    return values * jnp.tanh(jax.nn.softplus(values))

def snake_beta(values, alpha_log, beta_log):
    return values + jnp.sin(jnp.exp(alpha_log) * values) ** 2 / jnp.exp(beta_log)

def layer_norm(values, gain_row, shift_row):
    centred = values - lax.optimization_barrier(jnp.mean(values, axis=-1, keepdims=True))
    variance = lax.optimization_barrier(jnp.mean(centred * centred, axis=-1, keepdims=True))
    return centred * lax.rsqrt(variance + EPS_NORM) * gain_row + shift_row

def time_embed(steps_in):
    half_width = TE // 2
    frequency = jnp.exp(-math.log(10000.0) * jnp.arange(half_width, dtype=jnp.float32) / half_width)
    angles = steps_in.astype(jnp.float32)[..., None] * frequency
    return jnp.concatenate([jnp.sin(angles), jnp.cos(angles)], axis=-1)

def shifted(values, same_prev, same_next):
    zero_row = jnp.zeros((1, values.shape[1]), values.dtype)
    left_side = jnp.concatenate([zero_row, values[:-1]], axis=0) * same_prev[:, None]
    right_side = jnp.concatenate([values[1:], zero_row], axis=0) * same_next[:, None]
    return jnp.concatenate([left_side, values, right_side], axis=1)

def spread_groups(per_group, onehot):
    return jnp.dot(onehot, jnp.repeat(per_group, C // G, axis=-1), precision=PRECISE)

def group_norm(values, onehot, gain_row, shift_row):
    group_sums = jnp.dot(onehot.T, values, precision=PRECISE).reshape(NSEG, G, C // G).sum(-1)
    squares = jnp.dot(onehot.T, values * values, precision=PRECISE).reshape(NSEG, G, C // G).sum(-1)
    counts = lax.optimization_barrier(jnp.sum(onehot, axis=0))[:, None] * (C // G)
    group_mean = group_sums / counts
    inverse_std = lax.rsqrt(squares / counts - group_mean * group_mean + EPS_NORM)
    normed = (values - spread_groups(group_mean, onehot)) * spread_groups(inverse_std, onehot)
    return normed * gain_row + shift_row

def row_forward(params, features_row, ids_row, embedded_row):
    narrow, broad, gains, hidden = params
    same_prev = jnp.concatenate([jnp.zeros((1,), jnp.float32), (ids_row[1:] == ids_row[:-1]).astype(jnp.float32)])
    same_next = jnp.concatenate([(ids_row[:-1] == ids_row[1:]).astype(jnp.float32), jnp.zeros((1,), jnp.float32)])
    onehot = (ids_row[:, None] == jnp.arange(NSEG)[None, :]).astype(jnp.float32)
    conv_one = narrow[:3 * C]
    conv_two = narrow[3 * C:6 * C]
    conv_down = narrow[6 * C:9 * C]
    time_w = narrow[9 * C:9 * C + TE]
    ff_out = narrow[9 * C + TE:]
    pre_one = low_back(jnp.dot(shifted(features_row, same_prev, same_next), conv_one, precision=PRECISE))
    time_term = jnp.dot(embedded_row, time_w, precision=PRECISE) + gains[2]
    hidden_one = mish_act(group_norm(pre_one, onehot, gains[0], gains[1])) + jnp.dot(onehot, time_term, precision=PRECISE)
    pre_two = low_back(jnp.dot(shifted(low(hidden_one), same_prev, same_next), conv_two, precision=PRECISE))
    resid = mish_act(group_norm(pre_two, onehot, gains[3], gains[4])) + features_row
    normed_one = low(layer_norm(resid, gains[5], gains[6]))
    projected = jnp.dot(normed_one, broad[:, :3 * INNER], precision=PRECISE)
    queries = low_back(low(projected[:, :INNER]))
    key_rows = low_back(low(projected[:, INNER:2 * INNER]))
    value_rows = low_back(low(projected[:, 2 * INNER:]))
    same_utterance = ids_row[:, None] == ids_row[None, :]
    head_outputs = []
    for head_index in range(H):
        column_start = head_index * HD
        column_end = column_start + HD
        scores = low_back(jnp.dot(queries[:, column_start:column_end], key_rows[:, column_start:column_end].T, precision=PRECISE) * HD ** (-0.5))
        probabilities = jax.nn.softmax(jnp.where(same_utterance, scores, MASK_FILL), axis=-1)
        head_outputs.append(jnp.dot(low(probabilities), value_rows[:, column_start:column_end], precision=PRECISE))
    attended = low_back(low(jnp.concatenate(head_outputs, axis=1)))
    mixed = low_back(jnp.dot(attended, broad[:, 3 * INNER:4 * INNER].T, precision=PRECISE) + gains[7])
    resid_two = resid + mixed
    normed_two = low(layer_norm(resid_two, gains[8], gains[9]))
    inner = low_back(jnp.dot(normed_two, broad[:, 4 * INNER:], precision=PRECISE) + hidden[0])
    shaped = low(snake_beta(inner, hidden[1], hidden[2]))
    resid_three = low(resid_two + low_back(jnp.dot(shaped, ff_out, precision=PRECISE) + gains[10]))
    even_part = resid_three[0::2]
    odd_part = resid_three[1::2]
    ids_even = ids_row[0::2]
    ids_odd = ids_row[1::2]
    mask_before = jnp.concatenate([jnp.zeros((1,), jnp.float32), (ids_odd[:-1] == ids_even[1:]).astype(jnp.float32)])
    mask_after = (ids_odd == ids_even).astype(jnp.float32)
    before_odd = jnp.concatenate([jnp.zeros((1, C), jnp.float32), odd_part[:-1]], axis=0)
    stacked = jnp.concatenate([before_odd * mask_before[:, None], even_part, odd_part * mask_after[:, None]], axis=1)
    return jnp.dot(stacked, conv_down, precision=PRECISE) + gains[11]

def adam_update(grad, master, first, second, rate):
    moment = BETA_ONE * first + (1.0 - BETA_ONE) * grad
    square = BETA_TWO * second + (1.0 - BETA_TWO) * grad * grad
    corrected = moment / (1.0 - BETA_ONE ** STEP)
    scaled = jnp.sqrt(square / (1.0 - BETA_TWO ** STEP)) + EPS_ADAM
    return (moment, square, master - rate * (corrected / scaled + DECAY_RATE * master))

def reference(features, segment_ids, timesteps, cotangent, narrow_slab, broad_slab, model_gains, hidden_gains, narrow_first, narrow_second, broad_first, broad_second, gains_first, gains_second, hidden_first, hidden_second):
    embedded = low(mish_act(time_embed(timesteps)))

    def forward(frames_in, narrow, broad, gains, hidden):
        params = (low(narrow), low(broad), low(gains), low(hidden))
        row_step = jax.checkpoint(lambda member: row_forward(params, member[0], member[1], member[2]))
        return lax.map(row_step, (frames_in, segment_ids, embedded))
    frames_out, pull_back = jax.vjp(forward, features.astype(jnp.float32), narrow_slab, broad_slab, model_gains, hidden_gains)
    input_grad, narrow_grad, broad_grad, gains_grad, hidden_grad = pull_back(cotangent.astype(jnp.float32))
    narrow_new = adam_update(narrow_grad, narrow_slab, narrow_first, narrow_second, RATE_SLABS)
    broad_new = adam_update(broad_grad, broad_slab, broad_first, broad_second, RATE_SLABS)
    gains_new = adam_update(gains_grad, model_gains, gains_first, gains_second, RATE_GAINS)
    hidden_new = adam_update(hidden_grad, hidden_gains, hidden_first, hidden_second, RATE_GAINS)
    return (frames_out.astype(jnp.bfloat16), input_grad, narrow_new[0], narrow_new[1], narrow_new[2], broad_new[0], broad_new[1], broad_new[2], gains_new[0], gains_new[1], gains_new[2], hidden_new[0], hidden_new[1], hidden_new[2], narrow_new[2].astype(jnp.bfloat16), broad_new[2].astype(jnp.bfloat16))
```

```python
import functools
import math

import jax
import jax.numpy as jnp
from jax import lax
from jax.experimental import pallas as pl
from jax.experimental.pallas import tpu as pltpu
from jax.sharding import PartitionSpec as P

C = 256
TE = 1024
H = 2
HD = 64
FF = 1024
G = 8
NSEG = 8
STEP = 10
INNER = 128
EPS_NORM = 1e-05
EPS_ADAM = 1e-08
BETA_ONE = 0.9
BETA_TWO = 0.999
RATE_SLABS = 0.08
RATE_GAINS = 0.4
DECAY_RATE = 0.01
MASK_FILL = -1e30

F32 = jnp.float32
BF = jnp.bfloat16
MESH = pl.DeviceIdType.MESH
OFF = 32
GROUP = C // G


def dot(a, b):
    return jnp.dot(a, b, preferred_element_type=F32)


def dot_nt(a, b):
    return lax.dot_general(a, b, (((1,), (1,)), ((), ())), preferred_element_type=F32)


def dot_tn(a, b):
    return lax.dot_general(a, b, (((0,), (0,)), ((), ())), preferred_element_type=F32)


def recip(x):
    r = pltpu.reciprocal(x, approx=True)
    return r * (2.0 - x * r)


def split2(x):
    hi = x.astype(BF)
    lo = (x - hi.astype(F32)).astype(BF)
    return hi, lo


def split3(x):
    hi = x.astype(BF).astype(F32)
    mid = (x - hi).astype(BF).astype(F32)
    lo = (x - hi - mid).astype(BF).astype(F32)
    return hi, mid, lo


def mish_parts(y):
    e = jnp.exp(jnp.minimum(y, 30.0))
    n = e * (e + 2.0)
    rc = recip(n + 2.0)
    t = n * rc
    d = t + y * (2.0 * rc) * (1.0 + t) * (e * recip(1.0 + e))
    return t, d


def reduced_angle(a):
    k = jnp.floor(a * (1.0 / math.pi) + 0.5)
    r = (a - k * 3.140625) - k * 9.67653589793e-4
    r2 = r * r
    s = r * (1.0 + r2 * (-1.0 / 6 + r2 * (1.0 / 120 + r2 * (-1.0 / 5040 + r2 * (1.0 / 362880)))))
    c = 1.0 + r2 * (
        -0.5 + r2 * (1.0 / 24 + r2 * (-1.0 / 720 + r2 * (1.0 / 40320 + r2 * (-1.0 / 3628800))))
    )
    return k, s, c


def iota(shape, dim):
    return lax.broadcasted_iota(jnp.int32, shape, dim)


def group_sum_matrix(shift):
    return jnp.where(iota((C, 128), 0) // GROUP + shift == iota((C, 128), 1), 1.0, 0.0).astype(BF)


def group_spread_matrix():
    return jnp.where(iota((128, C), 0) == iota((128, C), 1) // GROUP, 1.0, 0.0).astype(BF)


def compact(sums, squares):
    a = jnp.concatenate(split3(sums), axis=0).astype(BF)
    b = jnp.concatenate(split3(squares), axis=0).astype(BF)
    both = dot(a, group_sum_matrix(0)) + dot(b, group_sum_matrix(G))
    return both[0:8] + both[8:16] + both[16:24]


def expand(tables):
    stacked = jnp.concatenate([p for t in tables for p in split3(t)], axis=0).astype(BF)
    wide = dot(stacked, group_spread_matrix())
    return [
        wide[24 * i : 24 * i + 8] + wide[24 * i + 8 : 24 * i + 16] + wide[24 * i + 16 : 24 * i + 24]
        for i in range(len(tables))
    ]


def table_of(columns):
    parts = split3(columns)
    zero = jnp.zeros((104, columns.shape[1]), F32)
    return jnp.concatenate(list(parts) + [zero], axis=0).astype(BF)


def segment_sums(onehot_rows, values):
    hi, lo = split2(values)
    return dot(onehot_rows, hi) + dot(onehot_rows, lo)


def layer_norm_parts(v):
    mu = jnp.mean(v, axis=-1, keepdims=True)
    cen = v - mu
    rs = lax.rsqrt(jnp.mean(cen * cen, axis=-1, keepdims=True) + EPS_NORM)
    return cen * rs, rs


def layer_norm_back(d, n, rs, gain):
    dg = d * gain
    return (dg - jnp.mean(dg, axis=-1, keepdims=True) - n * jnp.mean(dg * n, axis=-1, keepdims=True)) * rs


def colsum(x):
    return jnp.sum(x, axis=0, keepdims=True)


def main_kernel(
    feat, ids, steps, cot, narrow, broad, gains, hidden,
    fout, igrad, ngrad, bgrad, ggrad, hgrad,
    uext, gyext, meta, metab, ohrow, keymask, idp, counts, emb, tterm,
    zs, nrm1, der1, u2, nrm2, der2, resid, n3, rs3, ll1, qs, kall, vall,
    statin, statout,
    kt, vt, sbuf, ebuf, otb, invl, dos, dost,
    gr3, gf, nl2, shaped, ginner, r3s, r3b, gm, att, dq,
    part, rbuf, rbuf2, sumbuf, dqkv, g2, tg,
    halo_s, halo_r, cot_s, cot_r, stat_s, stat_r, kv_s, kv_r, dkv_s, dkv_r, gh_s, gh_r, r3_s, r3_r,
):
    R, T = feat.shape[0], feat.shape[1]
    gr2, dn, g3 = igrad, resid, shaped
    TX = T + 2 * OFF
    L = ids.shape[1]
    HT = T // 2
    f = lax.axis_index("frames")
    rw = lax.axis_index("rows")
    sib = f + 1 - 2 * (f % 2)
    cross = (f + 2) % 4
    diag = 3 - f
    peers = (sib, cross, diag)

    barrier = pltpu.get_barrier_semaphore()
    for p in peers:
        pl.semaphore_signal(barrier, inc=1, device_id=(rw, p), device_id_type=MESH)
    pl.semaphore_wait(barrier, 3)

    def remote(src, dst, ssem, rsem, target):
        return pltpu.make_async_remote_copy(
            src_ref=src, dst_ref=dst, send_sem=ssem, recv_sem=rsem,
            device_id=(rw, target), device_id_type=MESH,
        )

    def to_next(src, dst, ssem, rsem):
        return remote(src, dst, ssem, rsem, (f + 1) % 4)

    def to_prev(src, dst, ssem, rsem):
        return remote(src, dst, ssem, rsem, (f + 3) % 4)

    feat_down = to_next(feat.at[:, pl.ds(T - 16, 16)], uext.at[:, pl.ds(OFF - 16, 16)], halo_s.at[0], halo_r.at[0])
    feat_up = to_prev(feat.at[:, pl.ds(0, 16)], uext.at[:, pl.ds(OFF + T, 16)], halo_s.at[1], halo_r.at[1])
    cot_up = to_prev(cot.at[:, pl.ds(0, 16)], gyext.at[:, pl.ds(HT, 16)], cot_s.at[0], cot_r.at[0])

    @pl.when(f < 3)
    def _():
        feat_down.start()

    @pl.when(f > 0)
    def _():
        feat_up.start()
        cot_up.start()

    uext[:, 0 : OFF - 16, :] = jnp.zeros((R, OFF - 16, C), BF)
    uext[:, OFF + T + 16 :, :] = jnp.zeros((R, TX - OFF - T - 16, C), BF)
    g2[:, 0 : OFF - 16, :] = jnp.zeros((R, OFF - 16, C), BF)
    g2[:, OFF + T + 16 :, :] = jnp.zeros((R, TX - OFF - T - 16, C), BF)

    @pl.when(f == 0)
    def _():
        uext[:, OFF - 16 : OFF, :] = jnp.zeros((R, 16, C), BF)

    @pl.when(f == 3)
    def _():
        uext[:, OFF + T : OFF + T + 16, :] = jnp.zeros((R, 16, C), BF)
        gyext[:, HT : HT + 16, :] = jnp.zeros((R, 16, C), BF)

    ggrad[...] = jnp.zeros(ggrad.shape, F32)
    hgrad[...] = jnp.zeros(hgrad.shape, F32)

    idp[...] = jnp.full(idp.shape, -1.0, F32)
    idp[0:R, 128 : 128 + L] = ids[...].astype(F32)
    idv = idp[0:8]
    width = idv.shape[1]
    prev_row = jnp.where(pltpu.roll(idv, 1, 1) == idv, 1.0, 0.0)
    next_row = jnp.where(pltpu.roll(idv, width - 1, 1) == idv, 1.0, 0.0)
    idp[8:16, :] = prev_row
    idp[16:24, :] = next_row
    base = pl.multiple_of(f * T, 128)
    WX = T + 256
    win = idp[:, pl.ds(base, WX)]
    win = pltpu.roll(win, WX - (128 - OFF), 1)[:, : T + 128]
    own = idp[:, pl.ds(pl.multiple_of(base + 128, 128), T)]
    for r in range(R):
        n_lane = T + 128
        row_id = jnp.broadcast_to(win[r : r + 1], (8, n_lane))
        lab = iota((8, n_lane), 0).astype(F32)
        oh = jnp.where(row_id == lab, 1.0, 0.0)
        pn = jnp.where(
            lab == 0.0,
            jnp.broadcast_to(win[8 + r : 9 + r], (8, n_lane)),
            jnp.where(lab == 1.0, jnp.broadcast_to(win[16 + r : 17 + r], (8, n_lane)), 0.0),
        )
        block = jnp.concatenate([oh, oh, oh, pn, jnp.zeros((96, n_lane), F32)], axis=0)
        turned = block.T
        meta[r] = turned[:TX]
        metab[r] = turned[:TX].astype(BF)
        lab_own = iota((8, T), 0).astype(F32)
        ohrow[r] = jnp.where(jnp.broadcast_to(own[r : r + 1], (8, T)) == lab_own, 1.0, 0.0)
        full = jnp.broadcast_to(idv[r : r + 1, 128 : 128 + L], (8, L))
        lab_full = iota((8, L), 0).astype(F32)
        ohf = jnp.where(full == lab_full, 1.0, 0.0)
        counts[r] = jnp.broadcast_to(jnp.sum(ohf, axis=1, keepdims=True) * float(GROUP), (8, 128))
        km = jnp.concatenate([(1.0 - ohf) * MASK_FILL, jnp.zeros((120, L), F32)], axis=0)
        keymask[r] = km.T.astype(BF)

    uext[:, OFF : OFF + T, :] = feat[...]
    gyext[:, 0:HT, :] = cot[...]

    half = TE // 2
    freq = jnp.exp(iota((8, half), 1).astype(F32) * (-math.log(10000.0) / half))
    for r in range(R):
        ang = steps[8 * r : 8 * r + 8, :] * freq
        k, s, c = reduced_angle(ang)
        sign = 1.0 - 2.0 * (k - 2.0 * jnp.floor(k * 0.5))
        both = jnp.concatenate([s * sign, c * sign], axis=1)
        emb[8 * r : 8 * r + 8, :] = both * mish_parts(both)[0]
    embb = emb[...].astype(BF)
    tw = 9 * C
    tterm[...] = dot(embb, narrow[tw : tw + TE, :]) + gains[2:3, :]

    def own_prev(r):
        return meta[r, OFF : OFF + T, 24:25]

    def own_next(r):
        return meta[r, OFF : OFF + T, 25:26]

    def stat_copies(phase, r):
        return [
            remote(statout.at[phase, r], statin.at[phase, r, i], stat_s.at[phase, r, i], stat_r.at[phase, r, i], peers[i])
            for i in range(3)
        ]

    def send_stats(phase, r, sums, squares):
        statout[phase, r] = compact(sums, squares)
        for cp in stat_copies(phase, r):
            cp.start()

    def total_stats(phase, r):
        for cp in stat_copies(phase, r):
            cp.wait()
        return statout[phase, r] + statin[phase, r, 0] + statin[phase, r, 1] + statin[phase, r, 2]

    def norm_tables(phase, r):
        tot = total_stats(phase, r) / jnp.maximum(counts[r], 1.0)
        second = pltpu.roll(tot, 128 - G, 1)
        inv = lax.rsqrt(jnp.maximum(second - tot * tot, 0.0) + EPS_NORM)
        lanes = iota((8, 128), 1) < G
        inv = jnp.where(lanes, inv, 0.0)
        return tot * inv, inv

    def conv_into(r, src, first_row):
        for j in range(3):
            zs[j] = dot(src[r], narrow[first_row + j * C : first_row + (j + 1) * C, :])

    @pl.when(f > 0)
    def _():
        feat_down.wait_recv()

    @pl.when(f < 3)
    def _():
        feat_up.wait_recv()

    def phase_one(r, carry):
        conv_into(r, uext, 0)
        lo, hi = OFF - 16, OFF + T + 16
        n = hi - lo
        v = (
            zs[0, lo - 1 : hi - 1] * meta[r, lo:hi, 24:25]
            + zs[1, lo:hi]
            + zs[2, lo + 1 : hi + 1] * meta[r, lo:hi, 25:26]
        )
        nrm1[r, lo:hi] = v
        nrm1[r, 0:lo] = jnp.zeros((lo, C), F32)
        nrm1[r, hi:] = jnp.zeros((TX - hi, C), F32)
        vo = v[OFF - lo : OFF - lo + T]
        oh = ohrow[r].astype(BF)
        send_stats(0, r, segment_sums(oh, vo), segment_sums(oh, vo * vo))
        return carry

    lax.fori_loop(0, R, phase_one, 0)

    CH = TX // 4

    def phase_two(r, carry):
        mi, iv = expand(norm_tables(0, r))
        tt = tterm[pl.ds(pl.multiple_of(8 * r, 8), 8), :]
        tab = table_of(jnp.concatenate([mi, iv, tt], axis=1))

        def chunk(i, c2):
            rows = pl.ds(pl.multiple_of(i * CH, 16), CH)
            sp = dot(metab[r, rows], tab)
            n = nrm1[r, rows] * sp[:, C : 2 * C] - sp[:, :C]
            y = n * gains[0:1, :] + gains[1:2, :]
            t, d = mish_parts(y)
            nrm1[r, rows] = n
            der1[r, rows] = d
            u2[r, rows] = (y * t + sp[:, 2 * C :]).astype(BF)
            return c2

        lax.fori_loop(0, 4, chunk, 0)
        conv_into(r, u2, 3 * C)
        v = (
            zs[0, OFF - 1 : OFF + T - 1] * own_prev(r)
            + zs[1, OFF : OFF + T]
            + zs[2, OFF + 1 : OFF + T + 1] * own_next(r)
        )
        nrm2[r] = v
        oh = ohrow[r].astype(BF)
        send_stats(1, r, segment_sums(oh, v), segment_sums(oh, v * v))
        return carry

    lax.fori_loop(0, R, phase_two, 0)

    def kv_slot(ref, r, g):
        return ref.at[r, pl.ds(pl.multiple_of(g * T, 128), T)]

    def kv_copies(r):
        out = []
        for i, ref in enumerate((kall, vall)):
            out.append(remote(kv_slot(ref, r, f), kv_slot(ref, r, f), kv_s.at[i, 0, r], kv_r.at[i, 0, r], sib))
            out.append(remote(kv_slot(ref, r, f), kv_slot(ref, r, f), kv_s.at[i, 1, r], kv_r.at[i, 1, r], cross))
            out.append(remote(kv_slot(ref, r, cross), kv_slot(ref, r, cross), kv_s.at[i, 2, r], kv_r.at[i, 2, r], sib))
        return out

    NCH = 4
    CT = T // NCH

    def phase_three(r, carry):
        mi, iv = expand(norm_tables(1, r))
        tab = table_of(jnp.concatenate([mi, iv], axis=1))

        def chunk(i, c2):
            rows = pl.ds(pl.multiple_of(i * CT, 16), CT)
            xrows = pl.ds(pl.multiple_of(OFF + i * CT, 16), CT)
            sp = dot(metab[r, xrows], tab)
            n = nrm2[r, rows] * sp[:, C : 2 * C] - sp[:, :C]
            y = n * gains[3:4, :] + gains[4:5, :]
            t, d = mish_parts(y)
            nrm2[r, rows] = n
            der2[r, rows] = d
            res = y * t + feat[r, rows].astype(F32)
            resid[r, rows] = res
            m, rs = layer_norm_parts(res)
            n3[r, rows] = m
            rs3[r, rows] = jnp.broadcast_to(rs, (CT, 128))
            low = (m * gains[5:6, :] + gains[6:7, :]).astype(BF)
            ll1[r, rows] = low
            qkv = dot(low, broad[:, : 3 * INNER])
            qs[r, rows] = (qkv[:, :INNER].astype(BF).astype(F32) * HD ** (-0.5)).astype(BF)
            krows = pl.ds(pl.multiple_of(f * T + i * CT, 16), CT)
            kall[r, krows] = qkv[:, INNER : 2 * INNER].astype(BF)
            vall[r, krows] = qkv[:, 2 * INNER :].astype(BF)
            return c2

        lax.fori_loop(0, NCH, chunk, 0)
        cps = kv_copies(r)
        for i in (0, 1, 3, 4):
            cps[i].start()
        return carry

    lax.fori_loop(0, R, phase_three, 0)

    @pl.when(f < 3)
    def _():
        cot_up.wait_recv()

    down = 6 * C

    def phase_down_back(r, carry):
        gy = gyext[r, 0:HT]
        even = dot_nt(gy, narrow[down + C : down + 2 * C, :])
        own_gy = dot_nt(gy, narrow[down + 2 * C : down + 3 * C, :])
        nxt = dot_nt(gyext[r], narrow[down : down + C, :])
        zs[0, 0 : HT + 16] = nxt
        for hh in range(2):
            cols = slice(hh * 128, hh * 128 + 128)
            pm = r3s[2, pl.ds(8 + 1, HT, stride=2), :]
            nm = r3s[3, pl.ds(8 + 1, HT, stride=2), :]
            gr3[r, hh, pl.ds(0, HT, stride=2), :] = even[:, cols]
            gr3[r, hh, pl.ds(1, HT, stride=2), :] = own_gy[:, cols] * pm + zs[0, 1 : HT + 1, cols] * nm
        return carry

    def masks_strided(r):
        r3s[2, 8 : 8 + T] = jnp.broadcast_to(own_prev(r), (T, 128))
        r3s[3, 8 : 8 + T] = jnp.broadcast_to(own_next(r), (T, 128))

    def down_back(r, carry):
        masks_strided(r)
        phase_down_back(r, carry)
        ggrad[11:12, :] += colsum(gyext[r, 0:HT].astype(F32))
        for hh in range(2):
            gf[r, :, hh * 128 : hh * 128 + 128] = gr3[r, hh].astype(BF)
        ggrad[10:11, :] += colsum(gf[r].astype(F32))
        return carry

    lax.fori_loop(0, R, down_back, 0)

    def relay(r, carry):
        cps = kv_copies(r)
        for i in (1, 4):
            cps[i].wait_recv()
            cps[i + 1].start()
        return carry

    lax.fori_loop(0, R, relay, 0)

    alpha = jnp.exp(hidden[1:2, :])
    inv_beta = jnp.exp(-hidden[2:3, :])
    alpha_beta = alpha * inv_beta
    NK = L // 256
    lane128 = iota((T, 128), 1)

    def dkv_copies(r):
        out = []
        for i in range(2):
            blk = lambda g: part.at[r, i, pl.ds(pl.multiple_of(g * T, 128), T)]
            out.append(remote(blk(sib), rbuf.at[r, i, 0], dkv_s.at[i, 0, r], dkv_r.at[i, 0, r], sib))
            out.append(remote(blk(diag), rbuf.at[r, i, 1], dkv_s.at[i, 1, r], dkv_r.at[i, 1, r], sib))
            out.append(remote(sumbuf.at[r, i], rbuf2.at[r, i], dkv_s.at[i, 2, r], dkv_r.at[i, 2, r], cross))
        return out

    def phase_four(r, carry):
        cps = kv_copies(r)
        for i in (0, 2, 3, 5):
            cps[i].wait_recv()
        for i in range(6):
            cps[i].wait_send()
        kt[...] = kall[r].T
        vt[...] = vall[r].T
        qv = qs[r]
        ohq = jnp.where(lane128 < 8, meta[r, OFF : OFF + T], 0.0).astype(BF)
        zero_q = jnp.zeros((T, 128), BF)
        q_heads = [jnp.where(lane128 // HD == h, qv, zero_q) for h in range(H)]
        for h in range(H):
            qa = jnp.concatenate([q_heads[h], ohq], axis=1)

            def score(i, m):
                keys = pl.ds(pl.multiple_of(i * 256, 256), 256)
                ka = jnp.concatenate([kall[r, keys], keymask[r, keys]], axis=1)
                s = dot_nt(ka, qa)
                sbuf[keys] = s
                return jnp.maximum(m, jnp.max(s.reshape(32, 8, T), axis=0))

            m8 = lax.fori_loop(0, NK, score, jnp.full((8, T), -3e38, F32))
            m1 = jnp.max(m8, axis=0, keepdims=True)

            def expo(i, l8):
                keys = pl.ds(pl.multiple_of(i * 256, 256), 256)
                e = jnp.exp(sbuf[keys] - m1)
                ebuf[h, keys] = e.astype(BF)
                return l8 + jnp.sum(e.reshape(32, 8, T), axis=0)

            l8 = lax.fori_loop(0, NK, expo, jnp.zeros((8, T), F32))
            inv = 1.0 / jnp.sum(l8, axis=0, keepdims=True)
            invl[h] = jnp.broadcast_to(inv, (8, T))
            otb[h * HD : (h + 1) * HD, :] = dot(vt[h * HD : (h + 1) * HD, :], ebuf[h]) * inv
        att[r] = otb[...].T.astype(BF)

        def ff_chunk(i, c2):
            rows = pl.ds(pl.multiple_of(i * CT, 16), CT)
            res2 = resid[r, rows] + (dot_nt(att[r, rows], broad[:, 3 * INNER : 4 * INNER]) + gains[7:8, :])
            n, rs = layer_norm_parts(res2)
            low = (n * gains[8:9, :] + gains[9:10, :]).astype(BF)
            nl2[r, rows] = low
            gfr = gf[r, rows]
            out = jnp.zeros((CT, C), F32)
            back = jnp.zeros((CT, C), F32)
            for b in range(4):
                cols = slice(b * 256, b * 256 + 256)
                w_in = broad[:, 4 * INNER + b * 256 : 4 * INNER + b * 256 + 256]
                w_out = narrow[tw + TE + b * 256 : tw + TE + b * 256 + 256, :]
                inner = dot(low, w_in) + hidden[0:1, cols]
                gs = dot_nt(gfr, w_out)
                _, s, c = reduced_angle(inner * alpha[:, cols])
                s2 = s * s
                sc2 = (2.0 * s) * c
                sh = (inner + s2 * inv_beta[:, cols]).astype(BF)
                shaped[r, rows, cols] = sh
                gi = (gs * (1.0 + sc2 * alpha_beta[:, cols])).astype(BF)
                ginner[r, rows, cols] = gi
                hgrad[0:1, cols] += colsum(gi.astype(F32))
                hgrad[1:2, cols] += colsum(gs * inner * sc2)
                hgrad[2:3, cols] += colsum(gs * s2)
                out = out + dot(sh, w_out)
                back = back + dot_nt(gi, w_in)
            r3 = (res2 + (out + gains[10:11, :])).astype(BF)
            r3b[r, rows] = r3
            g_in = jnp.concatenate([gr3[r, 0, rows], gr3[r, 1, rows]], axis=1)
            ggrad[8:9, :] += colsum(back * n)
            ggrad[9:10, :] += colsum(back)
            g_res2 = g_in + layer_norm_back(back, n, rs, gains[8:9, :])
            gr2[r, rows] = g_res2
            low_g = g_res2.astype(BF)
            gm[r, rows] = low_g
            ggrad[7:8, :] += colsum(low_g.astype(F32))
            dos[rows] = dot(low_g, broad[:, 3 * INNER : 4 * INNER]).astype(BF).astype(F32)
            return c2

        lax.fori_loop(0, NCH, ff_chunk, 0)

        @pl.when(f < 3)
        def _():
            to_next(r3b.at[r, pl.ds(T - 16, 16)], r3b.at[r, pl.ds(T, 16)], r3_s.at[r], r3_r.at[r]).start()

        dot_t = dos[...].T
        for h in range(H):
            hrows = slice(h * HD, (h + 1) * HD)
            dost[hrows, :] = dot_t[hrows] * invl[h, 0:1, :]
        dscaled = dost[...].T.astype(BF)
        zero_t = jnp.zeros((HD, T), BF)
        d_rows, d_cols = [], []
        for h in range(H):
            hrows = slice(h * HD, (h + 1) * HD)
            d_rows.append(colsum(otb[hrows, :] * dost[hrows, :]))
            dh = dost[hrows, :].astype(BF)
            d_cols.append(jnp.concatenate([dh, zero_t] if h == 0 else [zero_t, dh], axis=0))
        d_heads = [jnp.where(lane128 // HD == h, dscaled, zero_q) for h in range(H)]
        dq[...] = jnp.zeros((INNER, T), F32)

        def key_grad(i, c2):
            keys = pl.ds(pl.multiple_of(i * 256, 256), 256)
            dk = jnp.zeros((256, INNER), F32)
            dv = jnp.zeros((256, INNER), F32)
            for h in range(H):
                hrows = slice(h * HD, (h + 1) * HD)
                eh = ebuf[h, keys]
                dp = dot(vall[r, keys], d_cols[h])
                ds = (eh.astype(F32) * (dp - d_rows[h])).astype(BF)
                dk = dk + dot(ds, q_heads[h])
                dv = dv + dot(eh, d_heads[h])
                dq[hrows, :] += dot(kt[hrows, keys], ds)
            part[r, 0, keys] = dk.astype(BF)
            part[r, 1, keys] = dv.astype(BF)
            return c2

        lax.fori_loop(0, NK, key_grad, 0)
        dqkv[r, :, 0:INNER] = (dq[...].T * HD ** (-0.5)).astype(BF)
        cps = dkv_copies(r)
        for i in (1, 4, 0, 3):
            cps[i].start()
        return carry

    lax.fori_loop(0, R, phase_four, 0)

    def phase_sum(r, carry):
        cps = dkv_copies(r)
        for i in (1, 4):
            cps[i].wait_recv()
        blk = pl.ds(pl.multiple_of(cross * T, 128), T)
        for i in range(2):
            sumbuf[r, i] = (part[r, i, blk].astype(F32) + rbuf[r, i, 1].astype(F32)).astype(BF)
        for i in (2, 5):
            cps[i].start()
        return carry

    lax.fori_loop(0, R, phase_sum, 0)

    flat = lambda ref: ref[...].reshape(R * T, ref.shape[2])
    gf_all = flat(gf)
    for b in range(4):
        cols = slice(b * 256, b * 256 + 256)
        ngrad[tw + TE + b * 256 : tw + TE + b * 256 + 256, :] = dot_tn(
            shaped[:, :, cols].reshape(R * T, 256), gf_all
        ).astype(BF)
        bgrad[:, 4 * INNER + b * 256 : 4 * INNER + b * 256 + 256] = dot_tn(
            flat(nl2), ginner[:, :, cols].reshape(R * T, 256)
        ).astype(BF)
    bgrad[:, 3 * INNER : 4 * INNER] = dot_tn(flat(gm), flat(att)).astype(BF)
    hgrad[1:2, :] = hgrad[1:2, :] * alpha_beta
    hgrad[2:3, :] = hgrad[2:3, :] * (-inv_beta)

    zs[:, 0:C, :] = jnp.zeros((3, C, C), F32)

    def down_forward(r, carry):
        @pl.when(f > 0)
        def _():
            to_next(r3b.at[r, pl.ds(T - 16, 16)], r3b.at[r, pl.ds(T, 16)], r3_s.at[r], r3_r.at[r]).wait_recv()

        @pl.when(f < 3)
        def _():
            to_next(r3b.at[r, pl.ds(T - 16, 16)], r3b.at[r, pl.ds(T, 16)], r3_s.at[r], r3_r.at[r]).wait_send()

        @pl.when(f == 0)
        def _():
            r3b[r, T : T + 16, :] = jnp.zeros((16, C), BF)

        masks_strided(r)
        for hh in range(2):
            cols = slice(hh * 128, hh * 128 + 128)
            r3s[hh, 8 : 8 + T] = r3b[r, 0:T, cols].astype(F32)
            r3s[hh, 0:8] = r3b[r, T : T + 16, cols].astype(F32)[8:16]
        even = jnp.concatenate([r3s[hh, pl.ds(8, HT, stride=2), :] for hh in range(2)], axis=1).astype(BF)
        m_after = r3s[3, pl.ds(8, HT, stride=2), :]
        m_before = r3s[2, pl.ds(8, HT, stride=2), :]
        odd = jnp.concatenate([r3s[hh, pl.ds(9, HT, stride=2), :] * m_after for hh in range(2)], axis=1).astype(BF)
        before = jnp.concatenate([r3s[hh, pl.ds(7, HT, stride=2), :] * m_before for hh in range(2)], axis=1).astype(BF)
        gy = cot[r]
        out = gains[11:12, :]
        for j, blk in enumerate((before, even, odd)):
            w = slice(down + j * C, down + (j + 1) * C)
            out = out + dot(blk, narrow[w, :])
            zs[j, 0:C, :] += dot_tn(blk, gy)
        fout[r] = out.astype(BF)
        return carry

    lax.fori_loop(0, R, down_forward, 0)
    for j in range(3):
        ngrad[down + j * C : down + (j + 1) * C, :] = zs[j, 0:C, :].astype(BF)

    def mean_tables(phase, r, norm_phase):
        tot = total_stats(phase, r) / jnp.maximum(counts[r], 1.0)
        lanes = iota((8, 128), 1) < G
        m1 = jnp.where(lanes, tot, 0.0)
        m2 = jnp.where(lanes, pltpu.roll(tot, 128 - G, 1), 0.0)
        nt = (statout[norm_phase, r] + statin[norm_phase, r, 0] + statin[norm_phase, r, 1] + statin[norm_phase, r, 2]) / jnp.maximum(counts[r], 1.0)
        second = pltpu.roll(nt, 128 - G, 1)
        iv = jnp.where(lanes, lax.rsqrt(jnp.maximum(second - nt * nt, 0.0) + EPS_NORM), 0.0)
        return m1 * iv, m2 * iv, iv

    def norm_back_start(phase, r, d, n, gain_row):
        ggrad[gain_row : gain_row + 1, :] += colsum(d * n)
        ggrad[gain_row + 1 : gain_row + 2, :] += colsum(d)
        scaled = d * gains[gain_row : gain_row + 1, :]
        dn[r] = scaled
        oh = ohrow[r].astype(BF)
        send_stats(phase, r, segment_sums(oh, scaled), segment_sums(oh, scaled * n))

    def phase_five(r, carry):
        cps = dkv_copies(r)
        for i in (0, 3, 2, 5):
            cps[i].wait_recv()
        for i in range(6):
            cps[i].wait_send()
        blk = pl.ds(pl.multiple_of(f * T, 128), T)
        for i in range(2):
            tot = part[r, i, blk].astype(F32) + rbuf[r, i, 0].astype(F32) + rbuf2[r, i].astype(F32)
            dqkv[r, :, (i + 1) * INNER : (i + 2) * INNER] = tot.astype(BF)
        back = dot_nt(dqkv[r], broad[:, : 3 * INNER])
        n = n3[r]
        ggrad[5:6, :] += colsum(back * n)
        ggrad[6:7, :] += colsum(back)
        g_res = gr2[r] + layer_norm_back(back, n, rs3[r][:, 0:1], gains[5:6, :])
        gr2[r] = g_res
        norm_back_start(2, r, g_res * der2[r], nrm2[r], 3)
        return carry

    lax.fori_loop(0, R, phase_five, 0)
    bgrad[:, : 3 * INNER] = dot_tn(flat(ll1), flat(dqkv)).astype(BF)

    def gh_copies(phase, r):
        return (
            to_next(g2.at[r, pl.ds(OFF + T - 16, 16)], g2.at[r, pl.ds(OFF - 16, 16)], gh_s.at[phase, 0, r], gh_r.at[phase, 0, r]),
            to_prev(g2.at[r, pl.ds(OFF, 16)], g2.at[r, pl.ds(OFF + T, 16)], gh_s.at[phase, 1, r], gh_r.at[phase, 1, r]),
        )

    def norm_back_end(phase, r, n, which):
        a, b, iv = expand(mean_tables(phase, r, which))
        tab = table_of(jnp.concatenate([a, b, iv], axis=1))
        sp = dot(metab[r, OFF : OFF + T], tab)
        g = dn[r] * sp[:, 2 * C :] - sp[:, :C] - n * sp[:, C : 2 * C]
        g2[r, OFF : OFF + T] = g.astype(BF)
        down_cp, up_cp = gh_copies(which, r)

        @pl.when(f < 3)
        def _():
            down_cp.start()

        @pl.when(f > 0)
        def _():
            up_cp.start()

    def conv_back(which, r, first_row):
        down_cp, up_cp = gh_copies(which, r)

        @pl.when(f < 3)
        def _():
            down_cp.wait_send()
            up_cp.wait_recv()

        @pl.when(f > 0)
        def _():
            up_cp.wait_send()
            down_cp.wait_recv()

        @pl.when(f == 0)
        def _():
            g2[r, OFF - 16 : OFF, :] = jnp.zeros((16, C), BF)

        @pl.when(f == 3)
        def _():
            g2[r, OFF + T : OFF + T + 16, :] = jnp.zeros((16, C), BF)

        g = g2[r].astype(F32)
        zs[0] = g * meta[r, :, 24:25]
        zs[2] = g * meta[r, :, 25:26]
        g3[r, :, 0:C] = zs[0, OFF + 1 : OFF + T + 1].astype(BF)
        g3[r, :, C : 2 * C] = g2[r, OFF : OFF + T]
        g3[r, :, 2 * C : 3 * C] = zs[2, OFF - 1 : OFF + T - 1].astype(BF)
        out = jnp.zeros((T, C), F32)
        for j in range(3):
            out = out + dot_nt(g3[r, :, j * C : (j + 1) * C], narrow[first_row + j * C : first_row + (j + 1) * C, :])
        return out

    def kernel_grad(src, first_row):
        u = src[:, OFF : OFF + T, :].reshape(R * T, C)
        for j in range(3):
            ngrad[first_row + j * C : first_row + (j + 1) * C, :] = dot_tn(
                u, g3[:, :, j * C : (j + 1) * C].reshape(R * T, C)
            ).astype(BF)

    def phase_six(r, carry):
        norm_back_end(2, r, nrm2[r], 1)
        return carry

    lax.fori_loop(0, R, phase_six, 0)

    def phase_seven(r, carry):
        gh = conv_back(1, r, 3 * C)
        oh = ohrow[r].astype(BF)
        tgr = segment_sums(oh, gh)
        tg[pl.ds(pl.multiple_of(8 * r, 8), 8), :] = tgr
        ggrad[2:3, :] += colsum(tgr)
        norm_back_start(3, r, gh * der1[r, OFF : OFF + T], nrm1[r, OFF : OFF + T], 0)
        return carry

    lax.fori_loop(0, R, phase_seven, 0)
    kernel_grad(u2, 3 * C)
    t_hi, t_lo = split2(tg[...])
    eb = emb[...].astype(BF)
    ngrad[tw : tw + TE, :] = (dot_tn(eb, t_hi) + dot_tn(eb, t_lo)).astype(BF)

    def phase_eight(r, carry):
        norm_back_end(3, r, nrm1[r, OFF : OFF + T], 0)
        return carry

    lax.fori_loop(0, R, phase_eight, 0)

    def phase_nine(r, carry):
        igrad[r] = gr2[r] + conv_back(0, r, 0)
        return carry

    lax.fori_loop(0, R, phase_nine, 0)
    kernel_grad(uext, 0)

    @pl.when(f < 3)
    def _():
        feat_down.wait_send()

    @pl.when(f > 0)
    def _():
        feat_up.wait_send()
        cot_up.wait_send()


def run_main(feat, ids, steps, cot, narrow, broad, gains, hidden):
    R, T, _ = feat.shape
    L = ids.shape[1]
    TX = T + 2 * OFF
    vm = lambda shape, dt=F32: pltpu.VMEM(shape, dt)
    dma = lambda *shape: pltpu.SemaphoreType.DMA(shape)
    scratch = [
        vm((R, TX, C), BF), vm((R, T // 2 + 16, C), BF), vm((R, TX, 128)), vm((R, TX, 128), BF),
        vm((R, 8, T)), vm((R, L, 128), BF), vm((24, L + 256)), vm((R, 8, 128)), vm((8 * R, TE)), vm((8 * R, C)),
        vm((3, TX, C)), vm((R, TX, C)), vm((R, TX, C)), vm((R, TX, C), BF), vm((R, T, C)),
        vm((R, T, C)), vm((R, T, C)), vm((R, T, C)), vm((R, T, 128)), vm((R, T, C), BF), vm((R, T, INNER), BF),
        vm((R, L, INNER), BF), vm((R, L, INNER), BF),
        vm((4, R, 3, 8, 128)), vm((4, R, 8, 128)),
        vm((INNER, L), BF), vm((INNER, L), BF), vm((L, T)), vm((H, L, T), BF), vm((INNER, T)),
        vm((H, 8, T)), vm((T, INNER)), vm((INNER, T)),
        vm((R, 2, T, 128)), vm((R, T, C), BF), vm((R, T, C), BF),
        vm((R, T, FF), BF), vm((R, T, FF), BF), vm((4, T + 8, 128)), vm((R, T + 16, C), BF),
        vm((R, T, C), BF), vm((R, T, INNER), BF), vm((INNER, T)),
        vm((R, 2, L, INNER), BF), vm((R, 2, 2, T, INNER), BF), vm((R, 2, T, INNER), BF), vm((R, 2, T, INNER), BF),
        vm((R, T, 3 * INNER), BF), vm((R, TX, C), BF), vm((8 * R, C)),
        dma(2), dma(2), dma(1), dma(1), dma(4, R, 3), dma(4, R, 3), dma(2, 3, R), dma(2, 3, R),
        dma(2, 3, R), dma(2, 3, R), dma(2, 2, R), dma(2, 2, R), dma(R), dma(R),
    ]
    out_shape = (
        jax.ShapeDtypeStruct((R, T // 2, C), BF),
        jax.ShapeDtypeStruct((R, T, C), F32),
        jax.ShapeDtypeStruct(narrow.shape, BF),
        jax.ShapeDtypeStruct(broad.shape, BF),
        jax.ShapeDtypeStruct((16, C), F32),
        jax.ShapeDtypeStruct((8, FF), F32),
    )
    spec = pl.BlockSpec(memory_space=pltpu.VMEM)
    return pl.pallas_call(
        main_kernel,
        out_shape=out_shape,
        in_specs=[spec] * 8,
        out_specs=tuple([spec] * 6),
        scratch_shapes=scratch,
        compiler_params=pltpu.CompilerParams(collective_id=0, has_side_effects=True, vmem_limit_bytes=63 * 2**20),
        cost_estimate=pl.CostEstimate(flops=2 * 10**10, bytes_accessed=2 * 10**7, transcendentals=10**7),
    )(feat, ids, steps, cot, narrow, broad, gains, hidden)


def adam_update(grad, master, first, second, rate):
    moment = BETA_ONE * first + (1.0 - BETA_ONE) * grad
    square = BETA_TWO * second + (1.0 - BETA_TWO) * grad * grad
    corrected = moment / (1.0 - BETA_ONE**STEP)
    scaled = jnp.sqrt(square / (1.0 - BETA_TWO**STEP)) + EPS_ADAM
    return (moment, square, master - rate * (corrected / scaled + DECAY_RATE * master))


def local(
    features, segment_ids, timesteps, cotangent, narrow_slab, broad_slab, model_gains, hidden_gains,
    narrow_first, narrow_second, broad_first, broad_second, gains_first, gains_second, hidden_first, hidden_second,
):
    narrow_w = lax.all_gather(narrow_slab.astype(BF), "rows", axis=0, tiled=True)
    broad_w = lax.all_gather(broad_slab.astype(BF), "rows", axis=0, tiled=True)
    gains_all = lax.all_gather(model_gains.astype(BF), "rows", axis=1, tiled=True).astype(F32)
    hidden_all = lax.all_gather(hidden_gains.astype(BF), "rows", axis=1, tiled=True).astype(F32)
    steps = timesteps.astype(F32).reshape(-1, 1)
    fout, igrad, ngrad, bgrad, ggrad, hgrad = run_main(
        features, segment_ids, steps, cotangent, narrow_w, broad_w, gains_all, hidden_all
    )
    scat = lambda x, d: lax.psum(
        lax.psum_scatter(x, "rows", scatter_dimension=d, tiled=True), "frames"
    )
    narrow_g = scat(ngrad, 0)
    broad_g = scat(bgrad, 0)
    small = lax.psum((ggrad[:12], hgrad[:3]), ("rows", "frames"))
    i = lax.axis_index("rows")
    gains_g = lax.dynamic_slice_in_dim(small[0], i * model_gains.shape[1], model_gains.shape[1], 1)
    hidden_g = lax.dynamic_slice_in_dim(small[1], i * hidden_gains.shape[1], hidden_gains.shape[1], 1)
    narrow_new = adam_update(narrow_g, narrow_slab, narrow_first, narrow_second, RATE_SLABS)
    broad_new = adam_update(broad_g, broad_slab, broad_first, broad_second, RATE_SLABS)
    gains_new = adam_update(gains_g, model_gains, gains_first, gains_second, RATE_GAINS)
    hidden_new = adam_update(hidden_g, hidden_gains, hidden_first, hidden_second, RATE_GAINS)
    return (
        fout, igrad, *narrow_new, *broad_new, *gains_new, *hidden_new,
        narrow_new[2].astype(BF), broad_new[2].astype(BF),
    )


def solution(mesh):
    rows = P("rows", None)
    cols = P(None, "rows")
    act = P("rows", "frames", None)
    return jax.shard_map(
        local,
        mesh=mesh,
        in_specs=(act, rows, rows, act, rows, rows, cols, cols, rows, rows, rows, rows, cols, cols, cols, cols),
        out_specs=(act, act, rows, rows, rows, rows, rows, rows, cols, cols, cols, cols, cols, cols, rows, rows),
        check_vma=False,
    )
```

```python
import functools
import math

import jax
import jax.numpy as jnp
from jax import lax
from jax.experimental import pallas as pl
from jax.experimental.pallas import tpu as pltpu
from jax.sharding import PartitionSpec as P

C = 256
TE = 1024
H = 2
HD = 64
FF = 1024
G = 8
NSEG = 8
STEP = 10
KC = 4352
KR = 1536
INNER = 128
EPS_NORM = 1e-05
EPS_ADAM = 1e-08
BETA_ONE = 0.9
BETA_TWO = 0.999
RATE_SLABS = 0.08
RATE_GAINS = 0.4
DECAY_RATE = 0.01
MASK_FILL = -1e30

F32 = jnp.float32
BF = jnp.bfloat16
MESH = pl.DeviceIdType.MESH
OFF = 32
GROUP = C // G


def dot(a, b):
    return jnp.dot(a, b, preferred_element_type=F32)


def dot_nt(a, b):
    return lax.dot_general(a, b, (((1,), (1,)), ((), ())), preferred_element_type=F32)


def dot_tn(a, b):
    return lax.dot_general(a, b, (((0,), (0,)), ((), ())), preferred_element_type=F32)


def recip(x):
    r = pltpu.reciprocal(x, approx=True)
    return r * (2.0 - x * r)


def split2(x):
    hi = x.astype(BF)
    lo = (x - hi.astype(F32)).astype(BF)
    return hi, lo


def split3(x):
    hi = x.astype(BF).astype(F32)
    mid = (x - hi).astype(BF).astype(F32)
    lo = (x - hi - mid).astype(BF).astype(F32)
    return hi, mid, lo


def mish_parts(y):
    e = jnp.exp(jnp.minimum(y, 30.0))
    n = e * (e + 2.0)
    rc = recip(n + 2.0)
    t = n * rc
    d = t + y * (2.0 * rc) * (1.0 + t) * (e * recip(1.0 + e))
    return t, d


def reduced_angle(a):
    k = jnp.floor(a * (1.0 / math.pi) + 0.5)
    r = (a - k * 3.140625) - k * 9.67653589793e-4
    r2 = r * r
    s = r * (1.0 + r2 * (-1.0 / 6 + r2 * (1.0 / 120 + r2 * (-1.0 / 5040 + r2 * (1.0 / 362880)))))
    c = 1.0 + r2 * (
        -0.5 + r2 * (1.0 / 24 + r2 * (-1.0 / 720 + r2 * (1.0 / 40320 + r2 * (-1.0 / 3628800))))
    )
    return k, s, c


def iota(shape, dim):
    return lax.broadcasted_iota(jnp.int32, shape, dim)


def group_sum_matrix(shift):
    return jnp.where(iota((C, 128), 0) // GROUP + shift == iota((C, 128), 1), 1.0, 0.0).astype(BF)


def group_spread_matrix():
    return jnp.where(iota((128, C), 0) == iota((128, C), 1) // GROUP, 1.0, 0.0).astype(BF)


def compact(sums, squares):
    a = jnp.concatenate(split3(sums), axis=0).astype(BF)
    b = jnp.concatenate(split3(squares), axis=0).astype(BF)
    both = dot(a, group_sum_matrix(0)) + dot(b, group_sum_matrix(G))
    return both[0:8] + both[8:16] + both[16:24]


def expand(tables):
    stacked = jnp.concatenate([p for t in tables for p in split3(t)], axis=0).astype(BF)
    wide = dot(stacked, group_spread_matrix())
    return [
        wide[24 * i : 24 * i + 8] + wide[24 * i + 8 : 24 * i + 16] + wide[24 * i + 16 : 24 * i + 24]
        for i in range(len(tables))
    ]


def table_of(columns):
    parts = split3(columns)
    zero = jnp.zeros((104, columns.shape[1]), F32)
    return jnp.concatenate(list(parts) + [zero], axis=0).astype(BF)


def segment_sums(onehot_rows, values):
    hi, lo = split2(values)
    return dot(onehot_rows, hi) + dot(onehot_rows, lo)


def layer_norm_parts(v):
    mu = jnp.mean(v, axis=-1, keepdims=True)
    cen = v - mu
    rs = lax.rsqrt(jnp.mean(cen * cen, axis=-1, keepdims=True) + EPS_NORM)
    return cen * rs, rs


def layer_norm_back(d, n, rs, gain):
    dg = d * gain
    return (dg - jnp.mean(dg, axis=-1, keepdims=True) - n * jnp.mean(dg * n, axis=-1, keepdims=True)) * rs


def colsum(x):
    return jnp.sum(x, axis=0, keepdims=True)


def piece_rows(first, count, x):
    return pl.ds(pl.multiple_of(first + x * (count // 2), 16), count // 2)


def main_kernel(
    NR,
    feat, ids, steps, cot, narrow_in, broad_in, gains_in, hidden_in,
    fout, igrad, ngrad, bgrad, small,
    narrow_s, broad_s, gains, hidden, smallw, packf, hgrad,
    uext, gyext, metab, ohrow, keymask, idp, counts, emb, tterm,
    zs, nrm1, der1, u2, nrm2, der2, resid, n3, rs3, ll1, qs, kall, vall,
    statin, statout,
    kt, vt, sbuf, ebuf, otb, invl, dos, dost,
    gr3, gf, nl2, shaped, ginner, r3s, r3b, gm, att, dq,
    part, rbuf, rbuf2, sumbuf, dqkv, g2, tg,
    ga_s, ga_r, gx_s, gx_r, gc_s, gc_r,
    halo_s, halo_r, cot_s, cot_r, stat_s, stat_r, kv_s, kv_r, dkv_s, dkv_r, gh_s, gh_r, r3_s, r3_r,
):
    R, T = feat.shape[0], feat.shape[1]
    gr2, dn, g3 = igrad, resid, shaped
    TX = T + 2 * OFF
    L = ids.shape[1]
    HT = T // 2
    f = lax.axis_index("frames")
    rw = lax.axis_index("rows")
    sib = f + 1 - 2 * (f % 2)
    cross = (f + 2) % 4
    diag = 3 - f
    peers = (sib, cross, diag)

    gather = NR > 0
    barrier = pltpu.get_barrier_semaphore()
    for p in peers:
        pl.semaphore_signal(barrier, inc=1, device_id=(rw, p), device_id_type=MESH)
    for k in range(1, NR):
        pl.semaphore_signal(barrier, inc=1, device_id=((rw + k) % NR, f), device_id_type=MESH)
    narrow, broad = (narrow_s, broad_s) if gather else (narrow_in, broad_in)
    ggrad = small
    if gather:
        SH, SB = narrow_in.shape[0], broad_in.shape[0]
        gx, gc = f // 2, f % 2
        narrow[pl.ds(pl.multiple_of(rw * SH, 16), SH), :] = narrow_in[...].astype(BF)
        broad[pl.ds(pl.multiple_of(rw * SB, 16), SB), :] = broad_in[...].astype(BF)
        packf[...] = jnp.zeros(packf.shape, F32)
        packf[0:12, 0 : C // NR] = gains_in[...]
        packf[12:15, :] = hidden_in[...]
        smallw[rw] = packf[...].astype(BF)
    else:
        gains[0:12, :] = gains_in[...]
        hidden[0:3, :] = hidden_in[...]
    pl.semaphore_wait(barrier, 3 + max(NR - 1, 0))

    def remote(src, dst, ssem, rsem, target):
        return pltpu.make_async_remote_copy(
            src_ref=src, dst_ref=dst, send_sem=ssem, recv_sem=rsem,
            device_id=(rw, target), device_id_type=MESH,
        )

    if gather:
        conv_first = {0: (0, SH), 1: (SH, 3 * C - SH)}
        rest = {s: (s * SH, SH) for s in range(2, NR)}
        rest[1] = (3 * C, 2 * SH - 3 * C)

        def quarter_of(g, kind, s):
            x, c = g // 2, g % 2
            if kind == 3:
                return smallw.at[s]
            if kind == 2:
                return broad.at[pl.ds(s * SB, SB), pl.ds(pl.multiple_of((2 * c + x) * (6 * C // 4), 128), 6 * C // 4)]
            first, count = (conv_first if kind == 0 else rest)[s]
            return narrow.at[piece_rows(first, count, x), pl.ds(pl.multiple_of(c * 128, 128), 128)]

        def spread_copy(kind, s, k):
            ref = quarter_of(f, kind, s)
            return pltpu.make_async_remote_copy(
                src_ref=ref, dst_ref=ref, send_sem=ga_s.at[kind, k], recv_sem=ga_r.at[kind, s],
                device_id=((s + k) % NR, f), device_id_type=MESH,
            )

        def has(kind, s):
            return {0: s in conv_first, 1: s in rest, 2: True, 3: True}[kind]

        def spread_start(kind):
            for s in range(NR):
                if has(kind, s):

                    @pl.when(rw == s)
                    def _():
                        for k in range(1, NR):
                            spread_copy(kind, s, k).start()

        def spread_end(kind):
            for s in range(NR):
                if has(kind, s):

                    @pl.when(rw == s)
                    def _():
                        for k in range(1, NR):
                            spread_copy(kind, s, k).wait_send()

        def cross_copy(kind, s):
            ref = quarter_of(f, kind, s)
            return remote(ref, ref, gx_s.at[kind, s], gx_r.at[kind, s], cross)

        def sib_copies(kind, s):
            a, b = quarter_of(f, kind, s), quarter_of(cross, kind, s)
            return (
                remote(a, a, gc_s.at[kind, 0, s], gc_r.at[kind, 0, s], sib),
                remote(b, b, gc_s.at[kind, 1, s], gc_r.at[kind, 1, s], sib),
            )

        def pass_on(kind, order):
            for s in order:

                @pl.when(rw != s)
                def _():
                    spread_copy(kind, s, 1).wait_recv()
                    cross_copy(kind, s).start()
                    sib_copies(kind, s)[0].start()

        def pass_across(kind, order):
            for s in order:

                @pl.when(rw != s)
                def _():
                    cross_copy(kind, s).wait_recv()
                    sib_copies(kind, s)[1].start()

        def arrive(kind, order):
            for s in order:

                @pl.when(rw != s)
                def _():
                    for cp in sib_copies(kind, s):
                        cp.wait_recv()
                        cp.wait_send()
                    cross_copy(kind, s).wait_send()

        spread_start(3)
        spread_start(0)

    def to_next(src, dst, ssem, rsem):
        return remote(src, dst, ssem, rsem, (f + 1) % 4)

    def to_prev(src, dst, ssem, rsem):
        return remote(src, dst, ssem, rsem, (f + 3) % 4)

    feat_down = to_next(feat.at[:, pl.ds(T - 16, 16)], uext.at[:, pl.ds(OFF - 16, 16)], halo_s.at[0], halo_r.at[0])
    feat_up = to_prev(feat.at[:, pl.ds(0, 16)], uext.at[:, pl.ds(OFF + T, 16)], halo_s.at[1], halo_r.at[1])
    cot_up = to_prev(cot.at[:, pl.ds(0, 16)], gyext.at[:, pl.ds(HT, 16)], cot_s.at[0], cot_r.at[0])

    @pl.when(f < 3)
    def _():
        feat_down.start()

    @pl.when(f > 0)
    def _():
        feat_up.start()
        cot_up.start()

    uext[:, 0 : OFF - 16, :] = jnp.zeros((R, OFF - 16, C), BF)
    uext[:, OFF + T + 16 :, :] = jnp.zeros((R, TX - OFF - T - 16, C), BF)
    g2[:, 0 : OFF - 16, :] = jnp.zeros((R, OFF - 16, C), BF)
    g2[:, OFF + T + 16 :, :] = jnp.zeros((R, TX - OFF - T - 16, C), BF)

    @pl.when(f == 0)
    def _():
        uext[:, OFF - 16 : OFF, :] = jnp.zeros((R, 16, C), BF)

    @pl.when(f == 3)
    def _():
        uext[:, OFF + T : OFF + T + 16, :] = jnp.zeros((R, 16, C), BF)
        gyext[:, HT : HT + 16, :] = jnp.zeros((R, 16, C), BF)

    ggrad[...] = jnp.zeros(ggrad.shape, F32)
    hgrad[...] = jnp.zeros(hgrad.shape, F32)

    idp[...] = jnp.full(idp.shape, -1.0, F32)
    idp[0:R, 128 : 128 + L] = ids[...].astype(F32)
    idv = idp[0:8]
    width = idv.shape[1]
    prev_row = jnp.where(pltpu.roll(idv, 1, 1) == idv, 1.0, 0.0)
    next_row = jnp.where(pltpu.roll(idv, width - 1, 1) == idv, 1.0, 0.0)
    idp[8:16, :] = prev_row
    idp[16:24, :] = next_row
    base = pl.multiple_of(f * T, 128)
    WX = T + 256
    win = idp[:, pl.ds(base, WX)]
    win = pltpu.roll(win, WX - (128 - OFF), 1)[:, : T + 128]
    own = idp[:, pl.ds(pl.multiple_of(base + 128, 128), T)]
    for r in range(R):
        n_lane = T + 128
        row_id = jnp.broadcast_to(win[r : r + 1], (8, n_lane))
        lab = iota((8, n_lane), 0).astype(F32)
        oh = jnp.where(row_id == lab, 1.0, 0.0)
        pn = jnp.where(
            lab == 0.0,
            jnp.broadcast_to(win[8 + r : 9 + r], (8, n_lane)),
            jnp.where(lab == 1.0, jnp.broadcast_to(win[16 + r : 17 + r], (8, n_lane)), 0.0),
        )
        block = jnp.concatenate([oh, oh, oh, pn, jnp.zeros((96, n_lane), F32)], axis=0)
        turned = block.T
        metab[r] = turned[:TX].astype(BF)
        lab_own = iota((8, T), 0).astype(F32)
        ohrow[r] = jnp.where(jnp.broadcast_to(own[r : r + 1], (8, T)) == lab_own, 1.0, 0.0)
        full = jnp.broadcast_to(idv[r : r + 1, 128 : 128 + L], (8, L))
        lab_full = iota((8, L), 0).astype(F32)
        ohf = jnp.where(full == lab_full, 1.0, 0.0)
        counts[r] = jnp.broadcast_to(jnp.sum(ohf, axis=1, keepdims=True) * float(GROUP), (8, 128))
        km = jnp.concatenate([(1.0 - ohf) * MASK_FILL, jnp.zeros((120, L), F32)], axis=0)
        keymask[r] = km.T.astype(BF)

    uext[:, OFF : OFF + T, :] = feat[...]
    gyext[:, 0:HT, :] = cot[...]

    half = TE // 2
    freq = jnp.exp(iota((8, half), 1).astype(F32) * (-math.log(10000.0) / half))
    for r in range(R):
        ang = steps[8 * r : 8 * r + 8, :] * freq
        k, s, c = reduced_angle(ang)
        sign = 1.0 - 2.0 * (k - 2.0 * jnp.floor(k * 0.5))
        both = jnp.concatenate([s * sign, c * sign], axis=1)
        emb[8 * r : 8 * r + 8, :] = both * mish_parts(both)[0]
    tw = 9 * C

    if gather:
        spread_start(1)
        spread_start(2)
        pass_on(0, (0, 1))
        for s in range(NR):

            @pl.when(rw != s)
            def _():
                spread_copy(3, s, 1).wait_recv()

        wide = smallw[...].astype(F32)
        gains[...] = jnp.concatenate([wide[s, :, 0 : C // NR] for s in range(NR)], axis=1)
        hidden[0:3, :] = jnp.concatenate([wide[s, 12:15, :] for s in range(NR)], axis=1)
        pass_across(0, (0, 1))
        arrive(0, (0, 1))

    def own_prev(r):
        return metab[r, OFF : OFF + T, 24:25].astype(F32)

    def own_next(r):
        return metab[r, OFF : OFF + T, 25:26].astype(F32)

    def stat_copies(phase, r):
        return [
            remote(statout.at[phase, r], statin.at[phase, r, i], stat_s.at[phase, r, i], stat_r.at[phase, r, i], peers[i])
            for i in range(3)
        ]

    def send_stats(phase, r, sums, squares):
        statout[phase, r] = compact(sums, squares)
        for cp in stat_copies(phase, r):
            cp.start()

    def total_stats(phase, r):
        for cp in stat_copies(phase, r):
            cp.wait()
        return statout[phase, r] + statin[phase, r, 0] + statin[phase, r, 1] + statin[phase, r, 2]

    def norm_tables(phase, r):
        tot = total_stats(phase, r) / jnp.maximum(counts[r], 1.0)
        second = pltpu.roll(tot, 128 - G, 1)
        inv = lax.rsqrt(jnp.maximum(second - tot * tot, 0.0) + EPS_NORM)
        lanes = iota((8, 128), 1) < G
        inv = jnp.where(lanes, inv, 0.0)
        return tot * inv, inv

    def conv_into(r, src, first_row):
        for j in range(3):
            zs[j] = dot(src[r], narrow[first_row + j * C : first_row + (j + 1) * C, :])

    @pl.when(f > 0)
    def _():
        feat_down.wait_recv()

    @pl.when(f < 3)
    def _():
        feat_up.wait_recv()

    def phase_one(r, carry):
        conv_into(r, uext, 0)
        lo, hi = OFF - 16, OFF + T + 16
        n = hi - lo
        v = (
            zs[0, lo - 1 : hi - 1] * metab[r, lo:hi, 24:25].astype(F32)
            + zs[1, lo:hi]
            + zs[2, lo + 1 : hi + 1] * metab[r, lo:hi, 25:26].astype(F32)
        )
        nrm1[r, lo:hi] = v
        nrm1[r, 0:lo] = jnp.zeros((lo, C), F32)
        nrm1[r, hi:] = jnp.zeros((TX - hi, C), F32)
        vo = v[OFF - lo : OFF - lo + T]
        oh = ohrow[r].astype(BF)
        send_stats(0, r, segment_sums(oh, vo), segment_sums(oh, vo * vo))
        return carry

    lax.fori_loop(0, R, phase_one, 0)

    if gather:
        order = (4, 5, 6, 1, 2, 3, 7)
        every = tuple(range(NR))
        pass_on(1, order)
        pass_on(2, every)
        pass_across(1, order)
        pass_across(2, every)
        arrive(1, order)
        arrive(2, every)
        for kind in range(4):
            spread_end(kind)
    tterm[...] = dot(emb[...].astype(BF), narrow[tw : tw + TE, :]) + gains[2:3, :]

    CH = TX // 4

    def phase_two(r, carry):
        mi, iv = expand(norm_tables(0, r))
        tt = tterm[pl.ds(pl.multiple_of(8 * r, 8), 8), :]
        tab = table_of(jnp.concatenate([mi, iv, tt], axis=1))

        def chunk(i, c2):
            rows = pl.ds(pl.multiple_of(i * CH, 16), CH)
            sp = dot(metab[r, rows], tab)
            n = nrm1[r, rows] * sp[:, C : 2 * C] - sp[:, :C]
            y = n * gains[0:1, :] + gains[1:2, :]
            t, d = mish_parts(y)
            nrm1[r, rows] = n
            der1[r, rows] = d
            u2[r, rows] = (y * t + sp[:, 2 * C :]).astype(BF)
            return c2

        lax.fori_loop(0, 4, chunk, 0)
        conv_into(r, u2, 3 * C)
        v = (
            zs[0, OFF - 1 : OFF + T - 1] * own_prev(r)
            + zs[1, OFF : OFF + T]
            + zs[2, OFF + 1 : OFF + T + 1] * own_next(r)
        )
        nrm2[r] = v
        oh = ohrow[r].astype(BF)
        send_stats(1, r, segment_sums(oh, v), segment_sums(oh, v * v))
        return carry

    lax.fori_loop(0, R, phase_two, 0)

    def kv_slot(ref, r, g):
        return ref.at[r, pl.ds(pl.multiple_of(g * T, 128), T)]

    def kv_copies(r):
        out = []
        for i, ref in enumerate((kall, vall)):
            out.append(remote(kv_slot(ref, r, f), kv_slot(ref, r, f), kv_s.at[i, 0, r], kv_r.at[i, 0, r], sib))
            out.append(remote(kv_slot(ref, r, f), kv_slot(ref, r, f), kv_s.at[i, 1, r], kv_r.at[i, 1, r], cross))
            out.append(remote(kv_slot(ref, r, cross), kv_slot(ref, r, cross), kv_s.at[i, 2, r], kv_r.at[i, 2, r], sib))
        return out

    NCH = 4
    CT = T // NCH

    def phase_three(r, carry):
        mi, iv = expand(norm_tables(1, r))
        tab = table_of(jnp.concatenate([mi, iv], axis=1))

        def chunk(i, c2):
            rows = pl.ds(pl.multiple_of(i * CT, 16), CT)
            xrows = pl.ds(pl.multiple_of(OFF + i * CT, 16), CT)
            sp = dot(metab[r, xrows], tab)
            n = nrm2[r, rows] * sp[:, C : 2 * C] - sp[:, :C]
            y = n * gains[3:4, :] + gains[4:5, :]
            t, d = mish_parts(y)
            nrm2[r, rows] = n
            der2[r, rows] = d
            res = y * t + feat[r, rows].astype(F32)
            resid[r, rows] = res
            m, rs = layer_norm_parts(res)
            n3[r, rows] = m
            rs3[r, rows] = jnp.broadcast_to(rs, (CT, 128))
            low = (m * gains[5:6, :] + gains[6:7, :]).astype(BF)
            ll1[r, rows] = low
            qkv = dot(low, broad[:, : 3 * INNER])
            qs[r, rows] = (qkv[:, :INNER].astype(BF).astype(F32) * HD ** (-0.5)).astype(BF)
            krows = pl.ds(pl.multiple_of(f * T + i * CT, 16), CT)
            kall[r, krows] = qkv[:, INNER : 2 * INNER].astype(BF)
            vall[r, krows] = qkv[:, 2 * INNER :].astype(BF)
            return c2

        lax.fori_loop(0, NCH, chunk, 0)
        cps = kv_copies(r)
        for i in (0, 1, 3, 4):
            cps[i].start()
        return carry

    lax.fori_loop(0, R, phase_three, 0)

    @pl.when(f < 3)
    def _():
        cot_up.wait_recv()

    down = 6 * C

    def phase_down_back(r, carry):
        gy = gyext[r, 0:HT]
        even = dot_nt(gy, narrow[down + C : down + 2 * C, :])
        own_gy = dot_nt(gy, narrow[down + 2 * C : down + 3 * C, :])
        nxt = dot_nt(gyext[r], narrow[down : down + C, :])
        zs[0, 0 : HT + 16] = nxt
        for hh in range(2):
            cols = slice(hh * 128, hh * 128 + 128)
            pm = r3s[2, pl.ds(8 + 1, HT, stride=2), :]
            nm = r3s[3, pl.ds(8 + 1, HT, stride=2), :]
            gr3[r, hh, pl.ds(0, HT, stride=2), :] = even[:, cols]
            gr3[r, hh, pl.ds(1, HT, stride=2), :] = own_gy[:, cols] * pm + zs[0, 1 : HT + 1, cols] * nm
        return carry

    def masks_strided(r):
        r3s[2, 8 : 8 + T] = jnp.broadcast_to(own_prev(r), (T, 128))
        r3s[3, 8 : 8 + T] = jnp.broadcast_to(own_next(r), (T, 128))

    def down_back(r, carry):
        masks_strided(r)
        phase_down_back(r, carry)
        ggrad[11:12, :] += colsum(gyext[r, 0:HT].astype(F32))
        for hh in range(2):
            gf[r, :, hh * 128 : hh * 128 + 128] = gr3[r, hh].astype(BF)
        ggrad[10:11, :] += colsum(gf[r].astype(F32))
        return carry

    lax.fori_loop(0, R, down_back, 0)

    def relay(r, carry):
        cps = kv_copies(r)
        for i in (1, 4):
            cps[i].wait_recv()
            cps[i + 1].start()
        return carry

    lax.fori_loop(0, R, relay, 0)

    alpha = jnp.exp(hidden[1:2, :])
    inv_beta = jnp.exp(-hidden[2:3, :])
    alpha_beta = alpha * inv_beta
    NK = L // 256
    lane128 = iota((T, 128), 1)

    def dkv_copies(r):
        out = []
        for i in range(2):
            blk = lambda g: part.at[r, i, pl.ds(pl.multiple_of(g * T, 128), T)]
            out.append(remote(blk(sib), rbuf.at[r, i, 0], dkv_s.at[i, 0, r], dkv_r.at[i, 0, r], sib))
            out.append(remote(blk(diag), rbuf.at[r, i, 1], dkv_s.at[i, 1, r], dkv_r.at[i, 1, r], sib))
            out.append(remote(sumbuf.at[r, i], rbuf2.at[r, i], dkv_s.at[i, 2, r], dkv_r.at[i, 2, r], cross))
        return out

    def phase_four(r, carry):
        cps = kv_copies(r)
        for i in (0, 2, 3, 5):
            cps[i].wait_recv()
        for i in range(6):
            cps[i].wait_send()
        kt[...] = kall[r].T
        vt[...] = vall[r].T
        qv = qs[r]
        ohq = jnp.where(lane128 < 8, metab[r, OFF : OFF + T], jnp.zeros((T, 128), BF))
        zero_q = jnp.zeros((T, 128), BF)
        q_heads = [jnp.where(lane128 // HD == h, qv, zero_q) for h in range(H)]
        for h in range(H):
            qa = jnp.concatenate([q_heads[h], ohq], axis=1)

            def score(i, m):
                keys = pl.ds(pl.multiple_of(i * 256, 256), 256)
                ka = jnp.concatenate([kall[r, keys], keymask[r, keys]], axis=1)
                s = dot_nt(ka, qa)
                sbuf[keys] = s
                return jnp.maximum(m, jnp.max(s.reshape(32, 8, T), axis=0))

            m8 = lax.fori_loop(0, NK, score, jnp.full((8, T), -3e38, F32))
            m1 = jnp.max(m8, axis=0, keepdims=True)

            def expo(i, l8):
                keys = pl.ds(pl.multiple_of(i * 256, 256), 256)
                e = jnp.exp(sbuf[keys] - m1)
                ebuf[h, keys] = e.astype(BF)
                return l8 + jnp.sum(e.reshape(32, 8, T), axis=0)

            l8 = lax.fori_loop(0, NK, expo, jnp.zeros((8, T), F32))
            inv = 1.0 / jnp.sum(l8, axis=0, keepdims=True)
            invl[h] = jnp.broadcast_to(inv, (8, T))
            otb[h * HD : (h + 1) * HD, :] = dot(vt[h * HD : (h + 1) * HD, :], ebuf[h]) * inv
        att[r] = otb[...].T.astype(BF)

        def ff_chunk(i, c2):
            rows = pl.ds(pl.multiple_of(i * CT, 16), CT)
            res2 = resid[r, rows] + (dot_nt(att[r, rows], broad[:, 3 * INNER : 4 * INNER]) + gains[7:8, :])
            n, rs = layer_norm_parts(res2)
            low = (n * gains[8:9, :] + gains[9:10, :]).astype(BF)
            nl2[r, rows] = low
            gfr = gf[r, rows]
            out = jnp.zeros((CT, C), F32)
            back = jnp.zeros((CT, C), F32)
            for b in range(4):
                cols = slice(b * 256, b * 256 + 256)
                w_in = broad[:, 4 * INNER + b * 256 : 4 * INNER + b * 256 + 256]
                w_out = narrow[tw + TE + b * 256 : tw + TE + b * 256 + 256, :]
                inner = dot(low, w_in) + hidden[0:1, cols]
                gs = dot_nt(gfr, w_out)
                _, s, c = reduced_angle(inner * alpha[:, cols])
                s2 = s * s
                sc2 = (2.0 * s) * c
                sh = (inner + s2 * inv_beta[:, cols]).astype(BF)
                shaped[r, rows, cols] = sh
                gi = (gs * (1.0 + sc2 * alpha_beta[:, cols])).astype(BF)
                ginner[r, rows, cols] = gi
                hgrad[0:1, cols] += colsum(gi.astype(F32))
                hgrad[1:2, cols] += colsum(gs * inner * sc2)
                hgrad[2:3, cols] += colsum(gs * s2)
                out = out + dot(sh, w_out)
                back = back + dot_nt(gi, w_in)
            r3 = (res2 + (out + gains[10:11, :])).astype(BF)
            r3b[r, rows] = r3
            g_in = jnp.concatenate([gr3[r, 0, rows], gr3[r, 1, rows]], axis=1)
            ggrad[8:9, :] += colsum(back * n)
            ggrad[9:10, :] += colsum(back)
            g_res2 = g_in + layer_norm_back(back, n, rs, gains[8:9, :])
            gr2[r, rows] = g_res2
            low_g = g_res2.astype(BF)
            gm[r, rows] = low_g
            ggrad[7:8, :] += colsum(low_g.astype(F32))
            dos[rows] = dot(low_g, broad[:, 3 * INNER : 4 * INNER]).astype(BF).astype(F32)
            return c2

        lax.fori_loop(0, NCH, ff_chunk, 0)

        @pl.when(f < 3)
        def _():
            to_next(r3b.at[r, pl.ds(T - 16, 16)], r3b.at[r, pl.ds(T, 16)], r3_s.at[r], r3_r.at[r]).start()

        dot_t = dos[...].T
        for h in range(H):
            hrows = slice(h * HD, (h + 1) * HD)
            dost[hrows, :] = dot_t[hrows] * invl[h, 0:1, :]
        dscaled = dost[...].T.astype(BF)
        zero_t = jnp.zeros((HD, T), BF)
        d_rows, d_cols = [], []
        for h in range(H):
            hrows = slice(h * HD, (h + 1) * HD)
            d_rows.append(colsum(otb[hrows, :] * dost[hrows, :]))
            dh = dost[hrows, :].astype(BF)
            d_cols.append(jnp.concatenate([dh, zero_t] if h == 0 else [zero_t, dh], axis=0))
        d_heads = [jnp.where(lane128 // HD == h, dscaled, zero_q) for h in range(H)]
        dq[...] = jnp.zeros((INNER, T), F32)

        def key_grad(i, c2):
            keys = pl.ds(pl.multiple_of(i * 256, 256), 256)
            dk = jnp.zeros((256, INNER), F32)
            dv = jnp.zeros((256, INNER), F32)
            for h in range(H):
                hrows = slice(h * HD, (h + 1) * HD)
                eh = ebuf[h, keys]
                dp = dot(vall[r, keys], d_cols[h])
                ds = (eh.astype(F32) * (dp - d_rows[h])).astype(BF)
                dk = dk + dot(ds, q_heads[h])
                dv = dv + dot(eh, d_heads[h])
                dq[hrows, :] += dot(kt[hrows, keys], ds)
            part[r, 0, keys] = dk.astype(BF)
            part[r, 1, keys] = dv.astype(BF)
            return c2

        lax.fori_loop(0, NK, key_grad, 0)
        dqkv[r, :, 0:INNER] = (dq[...].T * HD ** (-0.5)).astype(BF)
        cps = dkv_copies(r)
        for i in (1, 4, 0, 3):
            cps[i].start()
        return carry

    lax.fori_loop(0, R, phase_four, 0)

    def phase_sum(r, carry):
        cps = dkv_copies(r)
        for i in (1, 4):
            cps[i].wait_recv()
        blk = pl.ds(pl.multiple_of(cross * T, 128), T)
        for i in range(2):
            sumbuf[r, i] = (part[r, i, blk].astype(F32) + rbuf[r, i, 1].astype(F32)).astype(BF)
        for i in (2, 5):
            cps[i].start()
        return carry

    lax.fori_loop(0, R, phase_sum, 0)

    flat = lambda ref: ref[...].reshape(R * T, ref.shape[2])
    gf_all = flat(gf)
    for b in range(4):
        cols = slice(b * 256, b * 256 + 256)
        ngrad[tw + TE + b * 256 : tw + TE + b * 256 + 256, :] = dot_tn(
            shaped[:, :, cols].reshape(R * T, 256), gf_all
        ).astype(BF)
        bgrad[:, 4 * INNER + b * 256 : 4 * INNER + b * 256 + 256] = dot_tn(
            flat(nl2), ginner[:, :, cols].reshape(R * T, 256)
        ).astype(BF)
    bgrad[:, 3 * INNER : 4 * INNER] = dot_tn(flat(gm), flat(att)).astype(BF)
    hgrad[1:2, :] = hgrad[1:2, :] * alpha_beta
    hgrad[2:3, :] = hgrad[2:3, :] * (-inv_beta)

    zs[:, 0:C, :] = jnp.zeros((3, C, C), F32)

    def down_forward(r, carry):
        @pl.when(f > 0)
        def _():
            to_next(r3b.at[r, pl.ds(T - 16, 16)], r3b.at[r, pl.ds(T, 16)], r3_s.at[r], r3_r.at[r]).wait_recv()

        @pl.when(f < 3)
        def _():
            to_next(r3b.at[r, pl.ds(T - 16, 16)], r3b.at[r, pl.ds(T, 16)], r3_s.at[r], r3_r.at[r]).wait_send()

        @pl.when(f == 0)
        def _():
            r3b[r, T : T + 16, :] = jnp.zeros((16, C), BF)

        masks_strided(r)
        for hh in range(2):
            cols = slice(hh * 128, hh * 128 + 128)
            r3s[hh, 8 : 8 + T] = r3b[r, 0:T, cols].astype(F32)
            r3s[hh, 0:8] = r3b[r, T : T + 16, cols].astype(F32)[8:16]
        even = jnp.concatenate([r3s[hh, pl.ds(8, HT, stride=2), :] for hh in range(2)], axis=1).astype(BF)
        m_after = r3s[3, pl.ds(8, HT, stride=2), :]
        m_before = r3s[2, pl.ds(8, HT, stride=2), :]
        odd = jnp.concatenate([r3s[hh, pl.ds(9, HT, stride=2), :] * m_after for hh in range(2)], axis=1).astype(BF)
        before = jnp.concatenate([r3s[hh, pl.ds(7, HT, stride=2), :] * m_before for hh in range(2)], axis=1).astype(BF)
        gy = cot[r]
        out = gains[11:12, :]
        for j, blk in enumerate((before, even, odd)):
            w = slice(down + j * C, down + (j + 1) * C)
            out = out + dot(blk, narrow[w, :])
            zs[j, 0:C, :] += dot_tn(blk, gy)
        fout[r] = out.astype(BF)
        return carry

    lax.fori_loop(0, R, down_forward, 0)
    for j in range(3):
        ngrad[down + j * C : down + (j + 1) * C, :] = zs[j, 0:C, :].astype(BF)

    def mean_tables(phase, r, norm_phase):
        tot = total_stats(phase, r) / jnp.maximum(counts[r], 1.0)
        lanes = iota((8, 128), 1) < G
        m1 = jnp.where(lanes, tot, 0.0)
        m2 = jnp.where(lanes, pltpu.roll(tot, 128 - G, 1), 0.0)
        nt = (statout[norm_phase, r] + statin[norm_phase, r, 0] + statin[norm_phase, r, 1] + statin[norm_phase, r, 2]) / jnp.maximum(counts[r], 1.0)
        second = pltpu.roll(nt, 128 - G, 1)
        iv = jnp.where(lanes, lax.rsqrt(jnp.maximum(second - nt * nt, 0.0) + EPS_NORM), 0.0)
        return m1 * iv, m2 * iv, iv

    def norm_back_start(phase, r, d, n, gain_row):
        ggrad[gain_row : gain_row + 1, :] += colsum(d * n)
        ggrad[gain_row + 1 : gain_row + 2, :] += colsum(d)
        scaled = d * gains[gain_row : gain_row + 1, :]
        dn[r] = scaled
        oh = ohrow[r].astype(BF)
        send_stats(phase, r, segment_sums(oh, scaled), segment_sums(oh, scaled * n))

    def phase_five(r, carry):
        cps = dkv_copies(r)
        for i in (0, 3, 2, 5):
            cps[i].wait_recv()
        for i in range(6):
            cps[i].wait_send()
        blk = pl.ds(pl.multiple_of(f * T, 128), T)
        for i in range(2):
            tot = part[r, i, blk].astype(F32) + rbuf[r, i, 0].astype(F32) + rbuf2[r, i].astype(F32)
            dqkv[r, :, (i + 1) * INNER : (i + 2) * INNER] = tot.astype(BF)
        back = dot_nt(dqkv[r], broad[:, : 3 * INNER])
        n = n3[r]
        ggrad[5:6, :] += colsum(back * n)
        ggrad[6:7, :] += colsum(back)
        g_res = gr2[r] + layer_norm_back(back, n, rs3[r][:, 0:1], gains[5:6, :])
        gr2[r] = g_res
        norm_back_start(2, r, g_res * der2[r], nrm2[r], 3)
        return carry

    lax.fori_loop(0, R, phase_five, 0)
    bgrad[:, : 3 * INNER] = dot_tn(flat(ll1), flat(dqkv)).astype(BF)

    def gh_copies(phase, r):
        return (
            to_next(g2.at[r, pl.ds(OFF + T - 16, 16)], g2.at[r, pl.ds(OFF - 16, 16)], gh_s.at[phase, 0, r], gh_r.at[phase, 0, r]),
            to_prev(g2.at[r, pl.ds(OFF, 16)], g2.at[r, pl.ds(OFF + T, 16)], gh_s.at[phase, 1, r], gh_r.at[phase, 1, r]),
        )

    def norm_back_end(phase, r, n, which):
        a, b, iv = expand(mean_tables(phase, r, which))
        tab = table_of(jnp.concatenate([a, b, iv], axis=1))
        sp = dot(metab[r, OFF : OFF + T], tab)
        g = dn[r] * sp[:, 2 * C :] - sp[:, :C] - n * sp[:, C : 2 * C]
        g2[r, OFF : OFF + T] = g.astype(BF)
        down_cp, up_cp = gh_copies(which, r)

        @pl.when(f < 3)
        def _():
            down_cp.start()

        @pl.when(f > 0)
        def _():
            up_cp.start()

    def conv_back(which, r, first_row):
        down_cp, up_cp = gh_copies(which, r)

        @pl.when(f < 3)
        def _():
            down_cp.wait_send()
            up_cp.wait_recv()

        @pl.when(f > 0)
        def _():
            up_cp.wait_send()
            down_cp.wait_recv()

        @pl.when(f == 0)
        def _():
            g2[r, OFF - 16 : OFF, :] = jnp.zeros((16, C), BF)

        @pl.when(f == 3)
        def _():
            g2[r, OFF + T : OFF + T + 16, :] = jnp.zeros((16, C), BF)

        g = g2[r].astype(F32)
        zs[0] = g * metab[r, :, 24:25].astype(F32)
        zs[2] = g * metab[r, :, 25:26].astype(F32)
        g3[r, :, 0:C] = zs[0, OFF + 1 : OFF + T + 1].astype(BF)
        g3[r, :, C : 2 * C] = g2[r, OFF : OFF + T]
        g3[r, :, 2 * C : 3 * C] = zs[2, OFF - 1 : OFF + T - 1].astype(BF)
        out = jnp.zeros((T, C), F32)
        for j in range(3):
            out = out + dot_nt(g3[r, :, j * C : (j + 1) * C], narrow[first_row + j * C : first_row + (j + 1) * C, :])
        return out

    def kernel_grad(src, first_row):
        u = src[:, OFF : OFF + T, :].reshape(R * T, C)
        for j in range(3):
            ngrad[first_row + j * C : first_row + (j + 1) * C, :] = dot_tn(
                u, g3[:, :, j * C : (j + 1) * C].reshape(R * T, C)
            ).astype(BF)

    def phase_six(r, carry):
        norm_back_end(2, r, nrm2[r], 1)
        return carry

    lax.fori_loop(0, R, phase_six, 0)

    def phase_seven(r, carry):
        gh = conv_back(1, r, 3 * C)
        oh = ohrow[r].astype(BF)
        tgr = segment_sums(oh, gh)
        tg[pl.ds(pl.multiple_of(8 * r, 8), 8), :] = tgr
        ggrad[2:3, :] += colsum(tgr)
        norm_back_start(3, r, gh * der1[r, OFF : OFF + T], nrm1[r, OFF : OFF + T], 0)
        return carry

    lax.fori_loop(0, R, phase_seven, 0)
    kernel_grad(u2, 3 * C)
    t_hi, t_lo = split2(tg[...])
    eb = emb[...].astype(BF)
    ngrad[tw : tw + TE, :] = (dot_tn(eb, t_hi) + dot_tn(eb, t_lo)).astype(BF)

    def phase_eight(r, carry):
        norm_back_end(3, r, nrm1[r, OFF : OFF + T], 0)
        return carry

    lax.fori_loop(0, R, phase_eight, 0)

    def phase_nine(r, carry):
        igrad[r] = gr2[r] + conv_back(0, r, 0)
        return carry

    lax.fori_loop(0, R, phase_nine, 0)
    kernel_grad(uext, 0)

    for k in range(3):
        for q in range(FF // C):
            small[16 + 4 * k + q : 17 + 4 * k + q, :] = hgrad[k : k + 1, q * C : (q + 1) * C]

    @pl.when(f < 3)
    def _():
        feat_down.wait_send()

    @pl.when(f > 0)
    def _():
        feat_up.wait_send()
        cot_up.wait_send()


def run_main(fused, feat, ids, steps, cot, narrow, broad, gains, hidden):
    R, T, _ = feat.shape
    L = ids.shape[1]
    TX = T + 2 * OFF
    NR = fused
    vm = lambda shape, dt=F32: pltpu.VMEM(shape, dt)
    dma = lambda *shape: pltpu.SemaphoreType.DMA(shape)
    wide_n, wide_b = ((KC, C), (C, KR)) if NR else ((16, 128), (16, 128))
    slots = max(NR, 1)
    scratch = [
        vm(wide_n, BF), vm(wide_b, BF), vm((16, C)), vm((8, FF)), vm((slots, 16, 128), BF), vm((16, 128)), vm((8, FF)),
        vm((R, TX, C), BF), vm((R, T // 2 + 16, C), BF), vm((R, TX, 128), BF),
        vm((R, 8, T)), vm((R, L, 128), BF), vm((24, L + 256)), vm((R, 8, 128)), vm((8 * R, TE)), vm((8 * R, C)),
        vm((3, TX, C)), vm((R, TX, C)), vm((R, TX, C)), vm((R, TX, C), BF), vm((R, T, C)),
        vm((R, T, C)), vm((R, T, C)), vm((R, T, C)), vm((R, T, 128)), vm((R, T, C), BF), vm((R, T, INNER), BF),
        vm((R, L, INNER), BF), vm((R, L, INNER), BF),
        vm((4, R, 3, 8, 128)), vm((4, R, 8, 128)),
        vm((INNER, L), BF), vm((INNER, L), BF), vm((L, T)), vm((H, L, T), BF), vm((INNER, T)),
        vm((H, 8, T)), vm((T, INNER)), vm((INNER, T)),
        vm((R, 2, T, 128)), vm((R, T, C), BF), vm((R, T, C), BF),
        vm((R, T, FF), BF), vm((R, T, FF), BF), vm((4, T + 8, 128)), vm((R, T + 16, C), BF),
        vm((R, T, C), BF), vm((R, T, INNER), BF), vm((INNER, T)),
        vm((R, 2, L, INNER), BF), vm((R, 2, 2, T, INNER), BF), vm((R, 2, T, INNER), BF), vm((R, 2, T, INNER), BF),
        vm((R, T, 3 * INNER), BF), vm((R, TX, C), BF), vm((8 * R, C)),
        dma(4, slots), dma(4, slots), dma(4, slots), dma(4, slots), dma(4, 2, slots), dma(4, 2, slots),
        dma(2), dma(2), dma(1), dma(1), dma(4, R, 3), dma(4, R, 3), dma(2, 3, R), dma(2, 3, R),
        dma(2, 3, R), dma(2, 3, R), dma(2, 2, R), dma(2, 2, R), dma(R), dma(R),
    ]
    out_shape = (
        jax.ShapeDtypeStruct((R, T // 2, C), BF),
        jax.ShapeDtypeStruct((R, T, C), F32),
        jax.ShapeDtypeStruct((KC, C), BF),
        jax.ShapeDtypeStruct((C, KR), BF),
        jax.ShapeDtypeStruct((32, C), F32),
    )
    spec = pl.BlockSpec(memory_space=pltpu.VMEM)
    return pl.pallas_call(
        functools.partial(main_kernel, NR),
        out_shape=out_shape,
        in_specs=[spec] * 8,
        out_specs=tuple([spec] * 5),
        scratch_shapes=scratch,
        compiler_params=pltpu.CompilerParams(collective_id=0, has_side_effects=True, vmem_limit_bytes=63 * 2**20),
        cost_estimate=pl.CostEstimate(flops=2 * 10**10, bytes_accessed=2 * 10**7, transcendentals=10**7),
    )(feat, ids, steps, cot, narrow, broad, gains, hidden)


def adam_update(grad, master, first, second, rate):
    moment = BETA_ONE * first + (1.0 - BETA_ONE) * grad
    square = BETA_TWO * second + (1.0 - BETA_TWO) * grad * grad
    corrected = moment / (1.0 - BETA_ONE**STEP)
    scaled = jnp.sqrt(square / (1.0 - BETA_TWO**STEP)) + EPS_ADAM
    return (moment, square, master - rate * (corrected / scaled + DECAY_RATE * master))


def reduce_kernel(
    NR,
    ngrad, bgrad, small, nm, nf, ns, bm, bf_, bs, gm, gf, gs, hm, hf, hs,
    nmo, nso, nuo, bmo, bso, buo, gmo, gso, guo, hmo, hso, huo, nco, bco,
    half, bhalf, inh, inb, quart, bquart, inq, inbq, own, bown, got, bgot, full, bfull,
    s_own, s_in, s_rows, s_all,
    c_s, c_r, x_s, x_r, d_s, d_r, f_s, f_r, sa_s, sa_r, sb_s, sb_r, sc_s, sc_r,
):
    f = lax.axis_index("frames")
    rw = lax.axis_index("rows")
    sib = f + 1 - 2 * (f % 2)
    cross = (f + 2) % 4
    diag = 3 - f
    peers = (sib, cross, diag)
    x, c = f // 2, f % 2
    SH, SB = nm.shape[0], bm.shape[0]
    BH, BQ = KR // 2, KR // 4

    def remote(src, dst, ssem, rsem, row, frame):
        return pltpu.make_async_remote_copy(
            src_ref=src, dst_ref=dst, send_sem=ssem, recv_sem=rsem,
            device_id=(row, frame), device_id_type=MESH,
        )

    barrier = pltpu.get_barrier_semaphore()
    for p in peers:
        pl.semaphore_signal(barrier, inc=1, device_id=(rw, p), device_id_type=MESH)
    for k in range(1, NR):
        pl.semaphore_signal(barrier, inc=1, device_id=((rw + k) % NR, f), device_id_type=MESH)
    pl.semaphore_wait(barrier, 3 + NR - 1)

    def cols(core, n):
        return pl.ds(pl.multiple_of(core * n, 128), n)

    core_n = remote(ngrad.at[:, cols(1 - c, 128)], inh, c_s.at[0], c_r.at[0], rw, sib)
    core_b = remote(bgrad.at[:, cols(1 - c, BH)], inb, c_s.at[1], c_r.at[1], rw, sib)
    core_n.start()
    core_b.start()
    small_a = [
        remote(small.at[pl.ds(pl.multiple_of(8 * p, 8), 8)], s_in.at[i], sa_s.at[i], sa_r.at[i], rw, p)
        for i, p in enumerate(peers)
    ]
    for cp in small_a:
        cp.start()
    core_n.wait()
    for s in range(NR):
        rows = slice(s * SH, (s + 1) * SH)
        half[s] = (ngrad[rows, cols(c, 128)].astype(F32) + inh[rows].astype(F32)).astype(BF)
    cross_n = remote(
        half.at[:, pl.ds(pl.multiple_of((1 - x) * (SH // 2), 16), SH // 2)], inq, x_s.at[0], x_r.at[0], rw, cross
    )
    cross_n.start()
    core_b.wait()
    bhalf[...] = (bgrad[:, cols(c, BH)].astype(F32) + inb[...].astype(F32)).astype(BF)
    cross_b = remote(bhalf.at[:, cols(1 - x, BQ)], inbq, x_s.at[1], x_r.at[1], rw, cross)
    cross_b.start()
    for cp in small_a:
        cp.wait()
    s_own[...] = small[pl.ds(pl.multiple_of(8 * f, 8), 8)] + s_in[0] + s_in[1] + s_in[2]
    small_b = [remote(s_own, s_rows.at[k - 1], sb_s.at[k - 1], sb_r.at[k - 1], (rw + k) % NR, f) for k in range(1, NR)]
    for cp in small_b:
        cp.start()
    cross_n.wait()
    own_rows = pl.ds(pl.multiple_of(x * (SH // 2), 16), SH // 2)
    for s in range(NR):
        quart[s] = (half[s, own_rows].astype(F32) + inq[s].astype(F32)).astype(BF)
    direct = []
    for k in range(1, NR):
        to = (rw + k) % NR
        direct.append(remote(quart.at[to], got.at[k - 1], d_s.at[0, k - 1], d_r.at[0, k - 1], to, f))
        direct[-1].start()
    cross_b.wait()
    bquart[...] = (bhalf[:, cols(x, BQ)].astype(F32) + inbq[...].astype(F32)).astype(BF)
    directb = []
    for k in range(1, NR):
        to = (rw + k) % NR
        rows = pl.ds(pl.multiple_of(to * SB, 16), SB)
        directb.append(remote(bquart.at[rows], bgot.at[k - 1], d_s.at[1, k - 1], d_r.at[1, k - 1], to, f))
        directb[-1].start()
    for cp in small_b:
        cp.wait()
    s_all[pl.ds(pl.multiple_of(8 * f, 8), 8)] = (
        s_own[...] + s_rows[0] + s_rows[1] + s_rows[2] + s_rows[3] + s_rows[4] + s_rows[5] + s_rows[6]
    )
    mine = s_all.at[pl.ds(pl.multiple_of(8 * f, 8), 8)]
    small_c = [remote(mine, mine, sc_s.at[i], sc_r.at[i], rw, p) for i, p in enumerate(peers)]
    for cp in small_c:
        cp.start()
    for cp in direct:
        cp.wait()
    total = quart[rw].astype(F32)
    for k in range(NR - 1):
        total = total + got[k].astype(F32)
    blk = full.at[own_rows, cols(c, 128)]
    full[own_rows, cols(c, 128)] = total.astype(BF)
    fin = [remote(blk, blk, f_s.at[0, i], f_r.at[0, i], rw, p) for i, p in enumerate(peers)]
    for cp in fin:
        cp.start()
    for cp in directb:
        cp.wait()
    totalb = bquart[pl.ds(pl.multiple_of(rw * SB, 16), SB), :].astype(F32)
    for k in range(NR - 1):
        totalb = totalb + bgot[k].astype(F32)
    bcols = pl.ds(pl.multiple_of(c * BH + x * BQ, 128), BQ)
    bfull[:, bcols] = totalb.astype(BF)
    finb = [remote(bfull.at[:, bcols], bfull.at[:, bcols], f_s.at[1, i], f_r.at[1, i], rw, p) for i, p in enumerate(peers)]
    for cp in finb:
        cp.start()

    for cp in small_c:
        cp.wait()
    tot = s_all[...]
    gains_g = pltpu.roll(tot[0:16], (NR - rw) * (C // NR), 1)[:12, : C // NR]
    q = rw * (FF // NR) // C
    off = rw * (FF // NR) % C
    pick = iota((4, C), 0) == q
    hid = jnp.concatenate(
        [jnp.sum(jnp.where(pick, tot[16 + 4 * k : 20 + 4 * k], 0.0), axis=0, keepdims=True) for k in range(3)]
        + [jnp.zeros((5, C), F32)],
        axis=0,
    )
    hidden_g = pltpu.roll(hid, C - off, 1)[:3, : FF // NR]
    gmo[...], gso[...], guo[...] = adam_update(gains_g, gm[...], gf[...], gs[...], RATE_GAINS)
    hmo[...], hso[...], huo[...] = adam_update(hidden_g, hm[...], hf[...], hs[...], RATE_GAINS)
    for cp in fin:
        cp.wait()
    for lo in range(0, SH, 136):
        rows = slice(lo, lo + 136)
        m, sq, up = adam_update(full[...][rows].astype(F32), nm[rows], nf[rows], ns[rows], RATE_SLABS)
        nmo[rows], nso[rows], nuo[rows] = m, sq, up
    nco[...] = nuo[...].astype(BF)
    for cp in finb:
        cp.wait()
    m, sq, up = adam_update(bfull[...].astype(F32), bm[...], bf_[...], bs[...], RATE_SLABS)
    bmo[...], bso[...], buo[...] = m, sq, up
    bco[...] = up.astype(BF)


def run_reduce(NR, ngrad, bgrad, small, *state):
    vm = lambda shape, dt=BF: pltpu.VMEM(shape, dt)
    dma = lambda *shape: pltpu.SemaphoreType.DMA(shape)
    SH, SB = KC // NR, C // NR
    shape = lambda a, dt=F32: jax.ShapeDtypeStruct(a.shape, dt)
    nm, bm, gm, hm = state[0], state[3], state[6], state[9]
    out_shape = tuple(shape(a) for a in (nm, bm, gm, hm) for _ in range(3)) + (shape(nm, BF), shape(bm, BF))
    spec = pl.BlockSpec(memory_space=pltpu.VMEM)
    scratch = [
        vm((NR, SH, 128)), vm((C, KR // 2)), vm((KC, 128)), vm((C, KR // 2)),
        vm((NR, SH // 2, 128)), vm((C, KR // 4)), vm((NR, SH // 2, 128)), vm((C, KR // 4)),
        vm((16, 128)), vm((16, 128)), vm((NR - 1, SH // 2, 128)), vm((NR - 1, SB, KR // 4)),
        vm((SH, C)), vm((SB, KR)),
        vm((8, C), F32), vm((3, 8, C), F32), vm((NR - 1, 8, C), F32), vm((32, C), F32),
        dma(2), dma(2), dma(2), dma(2), dma(2, NR - 1), dma(2, NR - 1), dma(2, 3), dma(2, 3),
        dma(3), dma(3), dma(NR - 1), dma(NR - 1), dma(3), dma(3),
    ]
    return pl.pallas_call(
        functools.partial(reduce_kernel, NR),
        out_shape=out_shape,
        in_specs=[spec] * 15,
        out_specs=tuple([spec] * 14),
        scratch_shapes=scratch,
        compiler_params=pltpu.CompilerParams(collective_id=1, has_side_effects=True, vmem_limit_bytes=48 * 2**20),
    )(ngrad, bgrad, small, *state)


def local(
    features, segment_ids, timesteps, cotangent, narrow_slab, broad_slab, model_gains, hidden_gains,
    narrow_first, narrow_second, broad_first, broad_second, gains_first, gains_second, hidden_first, hidden_second,
):
    steps = timesteps.astype(F32).reshape(-1, 1)
    groups = lax.axis_size("rows")
    if groups == 8:
        fout, igrad, ngrad, bgrad, small = run_main(
            groups, features, segment_ids, steps, cotangent, narrow_slab, broad_slab, model_gains, hidden_gains
        )
        new = run_reduce(
            groups, ngrad, bgrad, small,
            narrow_slab, narrow_first, narrow_second, broad_slab, broad_first, broad_second,
            model_gains, gains_first, gains_second, hidden_gains, hidden_first, hidden_second,
        )
        return (fout, igrad, *new)
    narrow_w = lax.all_gather(narrow_slab.astype(BF), "rows", axis=0, tiled=True)
    broad_w = lax.all_gather(broad_slab.astype(BF), "rows", axis=0, tiled=True)
    gains_all = lax.all_gather(model_gains.astype(BF), "rows", axis=1, tiled=True).astype(F32)
    hidden_all = lax.all_gather(hidden_gains.astype(BF), "rows", axis=1, tiled=True).astype(F32)
    fout, igrad, ngrad, bgrad, small = run_main(
        0, features, segment_ids, steps, cotangent, narrow_w, broad_w, gains_all, hidden_all
    )
    scat = lambda v: lax.psum(lax.psum_scatter(v, "rows", scatter_dimension=0, tiled=True), "frames")
    narrow_g = scat(ngrad.astype(F32))
    broad_g = scat(bgrad.astype(F32))
    small = lax.psum(small, ("rows", "frames"))
    i = lax.axis_index("rows")
    own = lambda a, n: lax.dynamic_slice_in_dim(a, i * n, n, 1)
    gains_g = own(small[:12], model_gains.shape[1])
    hidden_g = own(small[16:28].reshape(3, FF), hidden_gains.shape[1])
    narrow_new = adam_update(narrow_g, narrow_slab, narrow_first, narrow_second, RATE_SLABS)
    broad_new = adam_update(broad_g, broad_slab, broad_first, broad_second, RATE_SLABS)
    gains_new = adam_update(gains_g, model_gains, gains_first, gains_second, RATE_GAINS)
    hidden_new = adam_update(hidden_g, hidden_gains, hidden_first, hidden_second, RATE_GAINS)
    return (
        fout, igrad, *narrow_new, *broad_new, *gains_new, *hidden_new,
        narrow_new[2].astype(BF), broad_new[2].astype(BF),
    )


def solution(mesh):
    rows = P("rows", None)
    cols = P(None, "rows")
    act = P("rows", "frames", None)
    return jax.shard_map(
        local,
        mesh=mesh,
        in_specs=(act, rows, rows, act, rows, rows, cols, cols, rows, rows, rows, rows, cols, cols, cols, cols),
        out_specs=(act, act, rows, rows, rows, rows, rows, rows, cols, cols, cols, cols, cols, cols, rows, rows),
        check_vma=False,
    )
```

```python
import functools
import math

import jax
import jax.numpy as jnp
from jax import lax
from jax.experimental import pallas as pl
from jax.experimental.pallas import tpu as pltpu
from jax.sharding import PartitionSpec as P

C = 256
TE = 1024
H = 2
HD = 64
FF = 1024
G = 8
NSEG = 8
STEP = 10
KC = 4352
KR = 1536
INNER = 128
EPS_NORM = 1e-05
EPS_ADAM = 1e-08
BETA_ONE = 0.9
BETA_TWO = 0.999
RATE_SLABS = 0.08
RATE_GAINS = 0.4
DECAY_RATE = 0.01
MASK_FILL = -1e30

F32 = jnp.float32
BF = jnp.bfloat16
MESH = pl.DeviceIdType.MESH
OFF = 32
GROUP = C // G


def dot(a, b):
    return jnp.dot(a, b, preferred_element_type=F32)


def dot_nt(a, b):
    return lax.dot_general(a, b, (((1,), (1,)), ((), ())), preferred_element_type=F32)


def dot_tn(a, b):
    return lax.dot_general(a, b, (((0,), (0,)), ((), ())), preferred_element_type=F32)


def recip(x):
    r = pltpu.reciprocal(x, approx=True)
    return r * (2.0 - x * r)


def split2(x):
    hi = x.astype(BF)
    lo = (x - hi.astype(F32)).astype(BF)
    return hi, lo


def split3(x):
    hi = x.astype(BF).astype(F32)
    mid = (x - hi).astype(BF).astype(F32)
    lo = (x - hi - mid).astype(BF).astype(F32)
    return hi, mid, lo


def mish_parts(y):
    e = jnp.exp(jnp.minimum(y, 30.0))
    n = e * (e + 2.0)
    rc = recip(n + 2.0)
    t = n * rc
    d = t + y * (2.0 * rc) * (1.0 + t) * (e * recip(1.0 + e))
    return t, d


def reduced_angle(a):
    k = jnp.floor(a * (1.0 / math.pi) + 0.5)
    r = (a - k * 3.140625) - k * 9.67653589793e-4
    r2 = r * r
    s = r * (1.0 + r2 * (-1.0 / 6 + r2 * (1.0 / 120 + r2 * (-1.0 / 5040 + r2 * (1.0 / 362880)))))
    c = 1.0 + r2 * (
        -0.5 + r2 * (1.0 / 24 + r2 * (-1.0 / 720 + r2 * (1.0 / 40320 + r2 * (-1.0 / 3628800))))
    )
    return k, s, c


def iota(shape, dim):
    return lax.broadcasted_iota(jnp.int32, shape, dim)


def group_sum_matrix(shift):
    return jnp.where(iota((C, 128), 0) // GROUP + shift == iota((C, 128), 1), 1.0, 0.0).astype(BF)


def group_spread_matrix():
    return jnp.where(iota((128, C), 0) == iota((128, C), 1) // GROUP, 1.0, 0.0).astype(BF)


def compact(sums, squares):
    n = sums.shape[0]
    a = jnp.concatenate(split3(sums), axis=0).astype(BF)
    b = jnp.concatenate(split3(squares), axis=0).astype(BF)
    both = dot(a, group_sum_matrix(0)) + dot(b, group_sum_matrix(G))
    return both[0:n] + both[n : 2 * n] + both[2 * n : 3 * n]


def expand(tables):
    n = tables[0].shape[0]
    stacked = jnp.concatenate([p for t in tables for p in split3(t)], axis=0).astype(BF)
    wide = dot(stacked, group_spread_matrix())
    part = lambda i: wide[n * i : n * i + n]
    return [part(3 * i) + part(3 * i + 1) + part(3 * i + 2) for i in range(len(tables))]


def table_of(columns):
    parts = split3(columns)
    zero = jnp.zeros((104, columns.shape[1]), F32)
    return jnp.concatenate(list(parts) + [zero], axis=0).astype(BF)


def segment_sums(onehot_rows, values):
    hi, lo = split2(values)
    return dot(onehot_rows, hi) + dot(onehot_rows, lo)


def layer_norm_parts(v):
    mu = jnp.mean(v, axis=-1, keepdims=True)
    cen = v - mu
    rs = lax.rsqrt(jnp.mean(cen * cen, axis=-1, keepdims=True) + EPS_NORM)
    return cen * rs, rs


def layer_norm_back(d, n, rs, gain):
    dg = d * gain
    return (dg - jnp.mean(dg, axis=-1, keepdims=True) - n * jnp.mean(dg * n, axis=-1, keepdims=True)) * rs


def colsum(x):
    return jnp.sum(x, axis=0, keepdims=True)


def piece_rows(first, count, x):
    return pl.ds(pl.multiple_of(first + x * (count // 2), 16), count // 2)


def main_kernel(
    NR,
    feat, ids, steps, cot, narrow_in, broad_in, gains_in, hidden_in,
    fout, igrad, small, out_n, out_b,
    narrow_s, broad_s, gains, hidden, smallw, packf, hgrad, ggrad,
    ngrad_s, bgrad_s, inh, inb, inq, inbq, got, bgot, gfull, bfull, s_pack, s_in, s_own, s_rows, s_all,
    uext, gyext, metab, ohrow, keymask, idp, counts, emb, tterm, sums, squares, tabs,
    zs, nrm1, der1, u2, nrm2, der2, resid, ll1, qs, kall, vall,
    statin, statout,
    kt, vt, sbuf, ebuf, otb, invl, dos, dost,
    gf, nl2, shaped, ginner, r3s, r3b, gm, att, dq,
    part, rbuf, rbuf2, sumbuf, dqkv, g2, tg,
    ga_s, ga_r, gx_s, gx_r, gc_s, gc_r,
    rc_s, rc_r, rx_s, rx_r, rd_s, rd_r, rf_s, rf_r, sa_s, sa_r, sb_s, sb_r, sc_s, sc_r,
    halo_s, halo_r, cot_s, cot_r, stat_s, stat_r, kv_s, kv_r, dkv_s, dkv_r, gh_s, gh_r, r3_s, r3_r,
):
    R, T = feat.shape[0], feat.shape[1]
    gr2, dn, g3 = igrad, resid, shaped
    TX = T + 2 * OFF
    L = ids.shape[1]
    HT = T // 2
    f = lax.axis_index("frames")
    rw = lax.axis_index("rows")
    sib = f + 1 - 2 * (f % 2)
    cross = (f + 2) % 4
    diag = 3 - f
    peers = (sib, cross, diag)

    gather = NR > 0
    barrier = pltpu.get_barrier_semaphore()
    for p in peers:
        pl.semaphore_signal(barrier, inc=1, device_id=(rw, p), device_id_type=MESH)
    for k in range(1, NR):
        pl.semaphore_signal(barrier, inc=1, device_id=((rw + k) % NR, f), device_id_type=MESH)
    narrow, broad = (narrow_s, broad_s) if gather else (narrow_in, broad_in)
    ngrad, bgrad = (ngrad_s, bgrad_s) if gather else (out_n, out_b)
    if gather:
        SH, SB = narrow_in.shape[0], broad_in.shape[0]
        narrow[pl.ds(pl.multiple_of(rw * SH, 16), SH), :] = narrow_in[...].astype(BF)
        broad[pl.ds(pl.multiple_of(rw * SB, 16), SB), :] = broad_in[...].astype(BF)
        packf[...] = jnp.zeros(packf.shape, F32)
        packf[0:12, 0 : C // NR] = gains_in[...]
        packf[12:15, :] = hidden_in[...]
        smallw[rw] = packf[...].astype(BF)
    else:
        gains[0:12, :] = gains_in[...]
        hidden[0:3, :] = hidden_in[...]
    pl.semaphore_wait(barrier, 3 + max(NR - 1, 0))

    def remote(src, dst, ssem, rsem, target):
        return pltpu.make_async_remote_copy(
            src_ref=src, dst_ref=dst, send_sem=ssem, recv_sem=rsem,
            device_id=(rw, target), device_id_type=MESH,
        )

    if gather:
        conv_first = {0: (0, SH), 1: (SH, 3 * C - SH)}
        rest = {s: (s * SH, SH) for s in range(2, NR)}
        rest[1] = (3 * C, 2 * SH - 3 * C)

        def quarter_of(g, kind, s):
            x, c = g // 2, g % 2
            if kind == 3:
                return smallw.at[s]
            if kind == 2:
                return broad.at[pl.ds(s * SB, SB), pl.ds(pl.multiple_of((2 * c + x) * (6 * C // 4), 128), 6 * C // 4)]
            first, count = (conv_first if kind == 0 else rest)[s]
            return narrow.at[piece_rows(first, count, x), pl.ds(pl.multiple_of(c * 128, 128), 128)]

        def spread_copy(kind, s, k):
            ref = quarter_of(f, kind, s)
            return pltpu.make_async_remote_copy(
                src_ref=ref, dst_ref=ref, send_sem=ga_s.at[kind, k], recv_sem=ga_r.at[kind, s],
                device_id=((s + k) % NR, f), device_id_type=MESH,
            )

        def has(kind, s):
            return {0: s in conv_first, 1: s in rest, 2: True, 3: True}[kind]

        def spread_start(kind):
            for s in range(NR):
                if has(kind, s):

                    @pl.when(rw == s)
                    def _():
                        for k in range(1, NR):
                            spread_copy(kind, s, k).start()

        def spread_end(kind):
            for s in range(NR):
                if has(kind, s):

                    @pl.when(rw == s)
                    def _():
                        for k in range(1, NR):
                            spread_copy(kind, s, k).wait_send()

        def cross_copy(kind, s):
            ref = quarter_of(f, kind, s)
            return remote(ref, ref, gx_s.at[kind, s], gx_r.at[kind, s], cross)

        def sib_copies(kind, s):
            a, b = quarter_of(f, kind, s), quarter_of(cross, kind, s)
            return (
                remote(a, a, gc_s.at[kind, 0, s], gc_r.at[kind, 0, s], sib),
                remote(b, b, gc_s.at[kind, 1, s], gc_r.at[kind, 1, s], sib),
            )

        def pass_on(kind, order):
            for s in order:

                @pl.when(rw != s)
                def _():
                    spread_copy(kind, s, 1).wait_recv()
                    cross_copy(kind, s).start()
                    sib_copies(kind, s)[0].start()

        def pass_across(kind, order):
            for s in order:

                @pl.when(rw != s)
                def _():
                    cross_copy(kind, s).wait_recv()
                    sib_copies(kind, s)[1].start()

        def arrive(kind, order):
            for s in order:

                @pl.when(rw != s)
                def _():
                    for cp in sib_copies(kind, s):
                        cp.wait_recv()
                        cp.wait_send()
                    cross_copy(kind, s).wait_send()

        every = tuple(range(NR))
        spread_start(3)
        spread_start(0)

    def to_next(src, dst, ssem, rsem):
        return remote(src, dst, ssem, rsem, (f + 1) % 4)

    def to_prev(src, dst, ssem, rsem):
        return remote(src, dst, ssem, rsem, (f + 3) % 4)

    feat_down = to_next(feat.at[:, pl.ds(T - 16, 16)], uext.at[:, pl.ds(OFF - 16, 16)], halo_s.at[0], halo_r.at[0])
    feat_up = to_prev(feat.at[:, pl.ds(0, 16)], uext.at[:, pl.ds(OFF + T, 16)], halo_s.at[1], halo_r.at[1])
    cot_up = to_prev(cot.at[:, pl.ds(0, 16)], gyext.at[:, pl.ds(HT, 16)], cot_s.at[0], cot_r.at[0])

    @pl.when(f < 3)
    def _():
        feat_down.start()

    @pl.when(f > 0)
    def _():
        feat_up.start()
        cot_up.start()

    uext[:, 0 : OFF - 16, :] = jnp.zeros((R, OFF - 16, C), BF)
    uext[:, OFF + T + 16 :, :] = jnp.zeros((R, TX - OFF - T - 16, C), BF)
    g2[:, 0 : OFF - 16, :] = jnp.zeros((R, OFF - 16, C), BF)
    g2[:, OFF + T + 16 :, :] = jnp.zeros((R, TX - OFF - T - 16, C), BF)

    @pl.when(f == 0)
    def _():
        uext[:, OFF - 16 : OFF, :] = jnp.zeros((R, 16, C), BF)

    @pl.when(f == 3)
    def _():
        uext[:, OFF + T : OFF + T + 16, :] = jnp.zeros((R, 16, C), BF)
        gyext[:, HT : HT + 16, :] = jnp.zeros((R, 16, C), BF)

    ggrad[...] = jnp.zeros(ggrad.shape, F32)
    hgrad[...] = jnp.zeros(hgrad.shape, F32)

    idp[...] = jnp.full(idp.shape, -1.0, F32)
    idp[0:R, 128 : 128 + L] = ids[...].astype(F32)
    idv = idp[0:8]
    width = idv.shape[1]
    prev_row = jnp.where(pltpu.roll(idv, 1, 1) == idv, 1.0, 0.0)
    next_row = jnp.where(pltpu.roll(idv, width - 1, 1) == idv, 1.0, 0.0)
    idp[8:16, :] = prev_row
    idp[16:24, :] = next_row
    base = pl.multiple_of(f * T, 128)
    WX = T + 256
    win = idp[:, pl.ds(base, WX)]
    win = pltpu.roll(win, WX - (128 - OFF), 1)[:, : T + 128]
    own = idp[:, pl.ds(pl.multiple_of(base + 128, 128), T)]
    for r in range(R):
        n_lane = T + 128
        row_id = jnp.broadcast_to(win[r : r + 1], (8, n_lane))
        lab = iota((8, n_lane), 0).astype(F32)
        oh = jnp.where(row_id == lab, 1.0, 0.0)
        pn = jnp.where(
            lab == 0.0,
            jnp.broadcast_to(win[8 + r : 9 + r], (8, n_lane)),
            jnp.where(lab == 1.0, jnp.broadcast_to(win[16 + r : 17 + r], (8, n_lane)), 0.0),
        )
        block = jnp.concatenate([oh, oh, oh, pn, jnp.zeros((96, n_lane), F32)], axis=0)
        turned = block.T
        metab[r] = turned[:TX].astype(BF)
        lab_own = iota((8, T), 0).astype(F32)
        ohrow[r] = jnp.where(jnp.broadcast_to(own[r : r + 1], (8, T)) == lab_own, 1.0, 0.0)
        full = jnp.broadcast_to(idv[r : r + 1, 128 : 128 + L], (8, L))
        lab_full = iota((8, L), 0).astype(F32)
        ohf = jnp.where(full == lab_full, 1.0, 0.0)
        counts[8 * r : 8 * r + 8] = jnp.broadcast_to(jnp.sum(ohf, axis=1, keepdims=True) * float(GROUP), (8, 128))
        km = jnp.concatenate([(1.0 - ohf) * MASK_FILL, jnp.zeros((120, L), F32)], axis=0)
        keymask[r] = km.T.astype(BF)

    uext[:, OFF : OFF + T, :] = feat[...]
    gyext[:, 0:HT, :] = cot[...]

    half = TE // 2
    freq = jnp.exp(iota((8, half), 1).astype(F32) * (-math.log(10000.0) / half))
    for r in range(R):
        turn = jnp.broadcast_to(steps[r : r + 1, :].astype(F32), (8, NSEG))
        ang = jnp.sum(jnp.where(iota((8, NSEG), 0) == iota((8, NSEG), 1), turn, 0.0), axis=1, keepdims=True) * freq
        k, s, c = reduced_angle(ang)
        sign = 1.0 - 2.0 * (k - 2.0 * jnp.floor(k * 0.5))
        both = jnp.concatenate([s * sign, c * sign], axis=1)
        emb[8 * r : 8 * r + 8, :] = both * mish_parts(both)[0]
    tw = 9 * C

    if gather:
        spread_start(1)
        spread_start(2)
        pass_on(0, (0, 1))
        for s in range(NR):

            @pl.when(rw != s)
            def _():
                spread_copy(3, s, 1).wait_recv()

        wide = smallw[...].astype(F32)
        gains[...] = jnp.concatenate([wide[s, :, 0 : C // NR] for s in range(NR)], axis=1)
        hidden[0:3, :] = jnp.concatenate([wide[s, 12:15, :] for s in range(NR)], axis=1)
        pass_across(0, (0, 1))
        arrive(0, (0, 1))

    def own_prev(r):
        return metab[r, OFF : OFF + T, 24:25].astype(F32)

    def own_next(r):
        return metab[r, OFF : OFF + T, 25:26].astype(F32)

    def stat_copies(phase):
        return [
            remote(statout.at[phase], statin.at[phase, i], stat_s.at[phase, i], stat_r.at[phase, i], peers[i])
            for i in range(3)
        ]

    def keep_sums(r, first, second):
        oh = ohrow[r].astype(BF)
        at = pl.ds(pl.multiple_of(8 * r, 8), 8)
        sums[at] = segment_sums(oh, first)
        squares[at] = segment_sums(oh, second)

    def send_stats(phase):
        statout[phase] = compact(sums[...], squares[...])
        for cp in stat_copies(phase):
            cp.start()

    def total_stats(phase, wait=True):
        if wait:
            for cp in stat_copies(phase):
                cp.wait()
        return (statout[phase] + statin[phase, 0] + statin[phase, 1] + statin[phase, 2]) / jnp.maximum(counts[...], 1.0)

    group_lanes = iota((8 * R, 128), 1) < G

    def norm_scale(tot):
        second = pltpu.roll(tot, 128 - G, 1)
        return jnp.where(group_lanes, lax.rsqrt(jnp.maximum(second - tot * tot, 0.0) + EPS_NORM), 0.0)

    def norm_tables(phase):
        tot = total_stats(phase)
        inv = norm_scale(tot)
        tabs[:, 0:C], tabs[:, C : 2 * C] = expand([tot * inv, inv])

    def row_table(r, width):
        return table_of(tabs[pl.ds(pl.multiple_of(8 * r, 8), 8), 0:width])

    def conv_into(r, src, first_row):
        for j in range(3):
            zs[j] = dot(src[r], narrow[first_row + j * C : first_row + (j + 1) * C, :])

    @pl.when(f > 0)
    def _():
        feat_down.wait_recv()

    @pl.when(f < 3)
    def _():
        feat_up.wait_recv()

    def phase_one(r):
        conv_into(r, uext, 0)
        lo, hi = OFF - 16, OFF + T + 16
        n = hi - lo
        v = (
            zs[0, lo - 1 : hi - 1] * metab[r, lo:hi, 24:25].astype(F32)
            + zs[1, lo:hi]
            + zs[2, lo + 1 : hi + 1] * metab[r, lo:hi, 25:26].astype(F32)
        )
        nrm1[r, lo:hi] = v
        nrm1[r, 0:lo] = jnp.zeros((lo, C), F32)
        nrm1[r, hi:] = jnp.zeros((TX - hi, C), F32)
        vo = v[OFF - lo : OFF - lo + T]
        keep_sums(r, vo, vo * vo)

    for r in range(R):
        phase_one(r)
        if r == R - 1:
            send_stats(0)
        if gather:
            if r == 0:
                pass_on(1, (1, 2, 4, 5, 6))
            elif r == 1:
                pass_on(2, every)
                pass_across(1, (1, 2, 4, 5, 6))

    if gather:
        pass_on(1, (3, 7))
        arrive(1, (1, 2, 4, 5, 6))
    tterm[...] = dot(emb[...].astype(BF), narrow[tw : tw + TE, :]) + gains[2:3, :]

    CH = TX // 4
    tabs[:, 2 * C : 3 * C] = tterm[...]
    norm_tables(0)

    def phase_two(r, carry):
        tab = row_table(r, 3 * C)

        def chunk(i, c2):
            rows = pl.ds(pl.multiple_of(i * CH, 16), CH)
            sp = dot(metab[r, rows], tab)
            n = nrm1[r, rows] * sp[:, C : 2 * C] - sp[:, :C]
            y = n * gains[0:1, :] + gains[1:2, :]
            t, d = mish_parts(y)
            nrm1[r, rows] = n
            der1[r, rows] = d.astype(BF)
            u2[r, rows] = (y * t + sp[:, 2 * C :]).astype(BF)
            return c2

        lax.fori_loop(0, 4, chunk, 0)
        conv_into(r, u2, 3 * C)
        v = (
            zs[0, OFF - 1 : OFF + T - 1] * own_prev(r)
            + zs[1, OFF : OFF + T]
            + zs[2, OFF + 1 : OFF + T + 1] * own_next(r)
        )
        nrm2[r] = v
        keep_sums(r, v, v * v)
        return carry

    lax.fori_loop(0, R, phase_two, 0)
    send_stats(1)
    if gather:
        pass_across(2, every)
        pass_across(1, (3, 7))
        arrive(2, every)
    norm_tables(1)

    def kv_slot(ref, r, g):
        return ref.at[r, pl.ds(pl.multiple_of(g * T, 128), T)]

    def kv_copies(r):
        out = []
        for i, ref in enumerate((kall, vall)):
            out.append(remote(kv_slot(ref, r, f), kv_slot(ref, r, f), kv_s.at[i, 0, r], kv_r.at[i, 0, r], sib))
            out.append(remote(kv_slot(ref, r, f), kv_slot(ref, r, f), kv_s.at[i, 1, r], kv_r.at[i, 1, r], cross))
            out.append(remote(kv_slot(ref, r, cross), kv_slot(ref, r, cross), kv_s.at[i, 2, r], kv_r.at[i, 2, r], sib))
        return out

    NCH = 4
    CT = T // NCH

    def phase_three(r, carry):
        tab = row_table(r, 2 * C)

        def chunk(i, c2):
            rows = pl.ds(pl.multiple_of(i * CT, 16), CT)
            xrows = pl.ds(pl.multiple_of(OFF + i * CT, 16), CT)
            sp = dot(metab[r, xrows], tab)
            n = nrm2[r, rows] * sp[:, C : 2 * C] - sp[:, :C]
            y = n * gains[3:4, :] + gains[4:5, :]
            t, d = mish_parts(y)
            nrm2[r, rows] = n
            der2[r, rows] = d.astype(BF)
            res = y * t + feat[r, rows].astype(F32)
            resid[r, rows] = res
            m, rs = layer_norm_parts(res)
            low = (m * gains[5:6, :] + gains[6:7, :]).astype(BF)
            ll1[r, rows] = low
            qkv = dot(low, broad[:, : 3 * INNER])
            qs[r, rows] = (qkv[:, :INNER].astype(BF).astype(F32) * HD ** (-0.5)).astype(BF)
            krows = pl.ds(pl.multiple_of(f * T + i * CT, 16), CT)
            kall[r, krows] = qkv[:, INNER : 2 * INNER].astype(BF)
            vall[r, krows] = qkv[:, 2 * INNER :].astype(BF)
            return c2

        lax.fori_loop(0, NCH, chunk, 0)
        cps = kv_copies(r)
        for i in (0, 1, 3, 4):
            cps[i].start()
        return carry

    lax.fori_loop(0, R, phase_three, 0)

    @pl.when(f < 3)
    def _():
        cot_up.wait_recv()

    down = 6 * C

    def phase_down_back(r, carry):
        gy = gyext[r, 0:HT]
        even = dot_nt(gy, narrow[down + C : down + 2 * C, :])
        own_gy = dot_nt(gy, narrow[down + 2 * C : down + 3 * C, :])
        nxt = dot_nt(gyext[r], narrow[down : down + C, :])
        zs[0, 0 : HT + 16] = nxt
        for hh in range(2):
            cols = slice(hh * 128, hh * 128 + 128)
            pm = r3s[2, pl.ds(8 + 1, HT, stride=2), :]
            nm = r3s[3, pl.ds(8 + 1, HT, stride=2), :]
            r3s[hh, pl.ds(8, HT, stride=2), :] = even[:, cols]
            r3s[hh, pl.ds(9, HT, stride=2), :] = own_gy[:, cols] * pm + zs[0, 1 : HT + 1, cols] * nm
        return carry

    def masks_strided(r):
        r3s[2, 8 : 8 + T] = jnp.broadcast_to(own_prev(r), (T, 128))
        r3s[3, 8 : 8 + T] = jnp.broadcast_to(own_next(r), (T, 128))

    def down_back(r, carry):
        masks_strided(r)
        phase_down_back(r, carry)
        ggrad[11:12, :] += colsum(gyext[r, 0:HT].astype(F32))
        for hh in range(2):
            gf[r, :, hh * 128 : hh * 128 + 128] = r3s[hh, 8 : 8 + T].astype(BF)
        ggrad[10:11, :] += colsum(gf[r].astype(F32))
        return carry

    if gather:
        arrive(1, (3, 7))
        for kind in range(4):
            spread_end(kind)
    lax.fori_loop(0, R, down_back, 0)

    def relay(r):
        cps = kv_copies(r)
        for i in (1, 4):
            cps[i].wait_recv()
            cps[i + 1].start()

    relay(0)

    alpha = jnp.exp(hidden[1:2, :])
    inv_beta = jnp.exp(-hidden[2:3, :])
    alpha_beta = alpha * inv_beta
    NK = L // 256
    lane128 = iota((T, 128), 1)

    def dkv_copies(r):
        out = []
        for i in range(2):
            blk = lambda g: part.at[r, i, pl.ds(pl.multiple_of(g * T, 128), T)]
            out.append(remote(blk(sib), rbuf.at[r, i, 0], dkv_s.at[i, 0, r], dkv_r.at[i, 0, r], sib))
            out.append(remote(blk(diag), rbuf.at[r, i, 1], dkv_s.at[i, 1, r], dkv_r.at[i, 1, r], sib))
            out.append(remote(sumbuf.at[r, i], rbuf2.at[r, i], dkv_s.at[i, 2, r], dkv_r.at[i, 2, r], cross))
        return out

    def phase_sum(r):
        cps = dkv_copies(r)
        for i in (1, 4):
            cps[i].wait_recv()
        blk = pl.ds(pl.multiple_of(cross * T, 128), T)
        for i in range(2):
            sumbuf[r, i] = (part[r, i, blk].astype(F32) + rbuf[r, i, 1].astype(F32)).astype(BF)
        for i in (2, 5):
            cps[i].start()

    def phase_four(r, carry):
        cps = kv_copies(r)
        for i in (0, 2, 3, 5):
            cps[i].wait_recv()
        for i in range(6):
            cps[i].wait_send()
        kt[...] = kall[r].T
        vt[...] = vall[r].T
        qv = qs[r]
        ohq = jnp.where(lane128 < 8, metab[r, OFF : OFF + T], jnp.zeros((T, 128), BF))
        zero_q = jnp.zeros((T, 128), BF)
        q_heads = [jnp.where(lane128 // HD == h, qv, zero_q) for h in range(H)]
        for h in range(H):
            qa = jnp.concatenate([q_heads[h], ohq], axis=1)

            def score(i, m):
                keys = pl.ds(pl.multiple_of(i * 256, 256), 256)
                ka = jnp.concatenate([kall[r, keys], keymask[r, keys]], axis=1)
                s = dot_nt(ka, qa)
                sbuf[keys] = s
                return jnp.maximum(m, jnp.max(s.reshape(32, 8, T), axis=0))

            m8 = lax.fori_loop(0, NK, score, jnp.full((8, T), -3e38, F32))
            m1 = jnp.max(m8, axis=0, keepdims=True)

            def expo(i, l8):
                keys = pl.ds(pl.multiple_of(i * 256, 256), 256)
                e = jnp.exp(sbuf[keys] - m1)
                ebuf[h, keys] = e.astype(BF)
                return l8 + jnp.sum(e.reshape(32, 8, T), axis=0)

            l8 = lax.fori_loop(0, NK, expo, jnp.zeros((8, T), F32))
            inv = 1.0 / jnp.sum(l8, axis=0, keepdims=True)
            invl[h] = jnp.broadcast_to(inv, (8, T))
            otb[h * HD : (h + 1) * HD, :] = dot(vt[h * HD : (h + 1) * HD, :], ebuf[h]) * inv
        att[r] = otb[...].T.astype(BF)

        @pl.when(r + 1 < R)
        def _():
            relay(r + 1)

        @pl.when(r > 0)
        def _():
            phase_sum(r - 1)

        def ff_chunk(i, c2):
            rows = pl.ds(pl.multiple_of(i * CT, 16), CT)
            res2 = resid[r, rows] + (dot_nt(att[r, rows], broad[:, 3 * INNER : 4 * INNER]) + gains[7:8, :])
            n, rs = layer_norm_parts(res2)
            low = (n * gains[8:9, :] + gains[9:10, :]).astype(BF)
            nl2[r, rows] = low
            gfr = gf[r, rows]
            out = jnp.zeros((CT, C), F32)
            back = jnp.zeros((CT, C), F32)
            for b in range(4):
                cols = slice(b * 256, b * 256 + 256)
                w_in = broad[:, 4 * INNER + b * 256 : 4 * INNER + b * 256 + 256]
                w_out = narrow[tw + TE + b * 256 : tw + TE + b * 256 + 256, :]
                inner = dot(low, w_in) + hidden[0:1, cols]
                gs = dot_nt(gfr, w_out)
                _, s, c = reduced_angle(inner * alpha[:, cols])
                s2 = s * s
                sc2 = (2.0 * s) * c
                sh = (inner + s2 * inv_beta[:, cols]).astype(BF)
                shaped[r, rows, cols] = sh
                gi = (gs * (1.0 + sc2 * alpha_beta[:, cols])).astype(BF)
                ginner[r, rows, cols] = gi
                hgrad[0:1, cols] += colsum(gi.astype(F32))
                hgrad[1:2, cols] += colsum(gs * inner * sc2)
                hgrad[2:3, cols] += colsum(gs * s2)
                out = out + dot(sh, w_out)
                back = back + dot_nt(gi, w_in)
            r3 = (res2 + (out + gains[10:11, :])).astype(BF)
            r3b[r, rows] = r3
            g_in = gfr.astype(F32)
            ggrad[8:9, :] += colsum(back * n)
            ggrad[9:10, :] += colsum(back)
            g_res2 = g_in + layer_norm_back(back, n, rs, gains[8:9, :])
            gr2[r, rows] = g_res2
            low_g = g_res2.astype(BF)
            gm[r, rows] = low_g
            ggrad[7:8, :] += colsum(low_g.astype(F32))
            dos[rows] = dot(low_g, broad[:, 3 * INNER : 4 * INNER]).astype(BF).astype(F32)
            return c2

        lax.fori_loop(0, NCH, ff_chunk, 0)

        @pl.when(f < 3)
        def _():
            to_next(r3b.at[r, pl.ds(T - 16, 16)], r3b.at[r, pl.ds(T, 16)], r3_s.at[r], r3_r.at[r]).start()

        dot_t = dos[...].T
        for h in range(H):
            hrows = slice(h * HD, (h + 1) * HD)
            dost[hrows, :] = dot_t[hrows] * invl[h, 0:1, :]
        dscaled = dost[...].T.astype(BF)
        zero_t = jnp.zeros((HD, T), BF)
        d_rows, d_cols = [], []
        for h in range(H):
            hrows = slice(h * HD, (h + 1) * HD)
            d_rows.append(colsum(otb[hrows, :] * dost[hrows, :]))
            dh = dost[hrows, :].astype(BF)
            d_cols.append(jnp.concatenate([dh, zero_t] if h == 0 else [zero_t, dh], axis=0))
        d_heads = [jnp.where(lane128 // HD == h, dscaled, zero_q) for h in range(H)]
        dq[...] = jnp.zeros((INNER, T), F32)

        def key_grad(i, c2):
            keys = pl.ds(pl.multiple_of(i * 256, 256), 256)
            dk = jnp.zeros((256, INNER), F32)
            dv = jnp.zeros((256, INNER), F32)
            for h in range(H):
                hrows = slice(h * HD, (h + 1) * HD)
                eh = ebuf[h, keys]
                dp = dot(vall[r, keys], d_cols[h])
                ds = (eh.astype(F32) * (dp - d_rows[h])).astype(BF)
                dk = dk + dot(ds, q_heads[h])
                dv = dv + dot(eh, d_heads[h])
                dq[hrows, :] += dot(kt[hrows, keys], ds)
            part[r, 0, keys] = dk.astype(BF)
            part[r, 1, keys] = dv.astype(BF)
            return c2

        lax.fori_loop(0, NK, key_grad, 0)
        dqkv[r, :, 0:INNER] = (dq[...].T * HD ** (-0.5)).astype(BF)
        cps = dkv_copies(r)
        for i in (1, 4, 0, 3):
            cps[i].start()
        return carry

    lax.fori_loop(0, R, phase_four, 0)

    if gather:
        rx, rc = f // 2, f % 2
        shard_blocks = SH // 32
        n_groups = {1: ((48, 72), (104, 136)), 2: ((24, 48), (72, 104)), 3: ((0, 24),)}
        b_groups = {1: (4 * INNER, 2 * C), 2: (0, C)}
        b_at = {1: C, 2: 0}

        def half_cols(core, first, n):
            return pl.ds(pl.multiple_of(first + core * n, 128), n)

        def core_copies(g):
            out = [
                remote(ngrad.at[lo:hi, :, :, half_cols(1 - rc, 0, 128)], inh.at[lo:hi], rc_s.at[g - 1, i], rc_r.at[g - 1, i], sib)
                for i, (lo, hi) in enumerate(n_groups[g])
            ]
            if g in b_groups:
                first, n = b_groups[g]
                out.append(
                    remote(
                        bgrad.at[:, :, :, half_cols(1 - rc, first, n)], inb.at[:, :, :, b_at[g] : b_at[g] + n],
                        rc_s.at[g - 1, 2], rc_r.at[g - 1, 2], sib,
                    )
                )
            return out

        def cross_copies(g):
            out = [
                remote(ngrad.at[lo:hi, 1 - rx, :, half_cols(rc, 0, 128)], inq.at[lo:hi], rx_s.at[g - 1, i], rx_r.at[g - 1, i], cross)
                for i, (lo, hi) in enumerate(n_groups[g])
            ]
            if g in b_groups:
                first, n = b_groups[g]
                out.append(
                    remote(
                        bgrad.at[:, 1 - rx, :, half_cols(rc, first, n)], inbq.at[:, :, b_at[g] : b_at[g] + n],
                        rx_s.at[g - 1, 2], rx_r.at[g - 1, 2], cross,
                    )
                )
            return out

        def owner_copies(g, s, source):
            out = []
            for i, (lo, hi) in enumerate(n_groups[g]):
                a, b = max(lo, shard_blocks * s), min(hi, shard_blocks * (s + 1))
                if a < b:
                    out.append(
                        pltpu.make_async_remote_copy(
                            src_ref=ngrad.at[a:b, rx, :, half_cols(rc, 0, 128)],
                            dst_ref=got.at[source, a - shard_blocks * s : b - shard_blocks * s],
                            send_sem=rd_s.at[g - 1, i, s], recv_sem=rd_r.at[g - 1, i, source],
                            device_id=(s, f), device_id_type=MESH,
                        )
                    )
            if g in b_groups:
                first, n = b_groups[g]
                out.append(
                    pltpu.make_async_remote_copy(
                        src_ref=bgrad.at[s, rx, :, half_cols(rc, first, n)],
                        dst_ref=bgot.at[source, :, b_at[g] : b_at[g] + n],
                        send_sem=rd_s.at[g - 1, 2, s], recv_sem=rd_r.at[g - 1, 2, source],
                        device_id=(s, f), device_id_type=MESH,
                    )
                )
            return out

        def red_core(g):
            for cp in core_copies(g):
                cp.start()

        def red_cross(g):
            for cp in core_copies(g):
                cp.wait()
            mine = half_cols(rc, 0, 128)
            for lo, hi in n_groups[g]:
                ngrad[lo:hi, :, :, mine] = (ngrad[lo:hi, :, :, mine].astype(F32) + inh[lo:hi].astype(F32)).astype(BF)
            if g in b_groups:
                first, n = b_groups[g]
                cols = half_cols(rc, first, n)
                other = inb[:, :, :, b_at[g] : b_at[g] + n]
                bgrad[:, :, :, cols] = (bgrad[:, :, :, cols].astype(F32) + other.astype(F32)).astype(BF)
            for cp in cross_copies(g):
                cp.start()

        def red_owner(g):
            for cp in cross_copies(g):
                cp.wait()
            mine = half_cols(rc, 0, 128)
            for lo, hi in n_groups[g]:
                ngrad[lo:hi, rx, :, mine] = (ngrad[lo:hi, rx, :, mine].astype(F32) + inq[lo:hi].astype(F32)).astype(BF)
            if g in b_groups:
                first, n = b_groups[g]
                cols = half_cols(rc, first, n)
                other = inbq[:, :, b_at[g] : b_at[g] + n]
                bgrad[:, rx, :, cols] = (bgrad[:, rx, :, cols].astype(F32) + other.astype(F32)).astype(BF)
            for s in range(NR):

                @pl.when(rw != s)
                def _():
                    for cp in owner_copies(g, s, rw):
                        cp.start()

        def red_wait(g):
            for s in range(NR):

                @pl.when(rw != s)
                def _():
                    for cp in owner_copies(g, s, rw):
                        cp.wait_send()

                @pl.when(rw == s)
                def _():
                    for k in range(1, NR):
                        for cp in owner_copies(g, s, (s + k) % NR):
                            cp.wait_recv()

        def red_finish():
            mine = half_cols(rc, 0, 128)
            total = ngrad[pl.ds(shard_blocks * rw, shard_blocks), rx, :, mine].astype(F32)
            totals = [bgrad[rw, rx, :, half_cols(rc, *b_groups[g])].astype(F32) for g in (1, 2)]
            for k in range(1, NR):
                o = (rw + k) % NR
                total = total + got[o].astype(F32)
                for j, g in enumerate((1, 2)):
                    totals[j] = totals[j] + bgot[o, :, b_at[g] : b_at[g] + b_groups[g][1]].astype(F32)
            gfull[:, rx, :, mine] = total.astype(BF)
            fin = []
            blocks = [gfull.at[:, rx, :, mine]]
            for j, g in enumerate((1, 2)):
                cols = half_cols(rc, *b_groups[g])
                bfull[rx, :, cols] = totals[j].astype(BF)
                blocks.append(bfull.at[rx, :, cols])
            for j, blk in enumerate(blocks):
                for i, p in enumerate(peers):
                    fin.append(remote(blk, blk, rf_s.at[j, i], rf_r.at[j, i], p))
                    fin[-1].start()
            return fin

        def small_first():
            s_pack[...] = small_rows()
            out = [
                remote(s_pack.at[pl.ds(pl.multiple_of(8 * p, 8), 8)], s_in.at[i], sa_s.at[i], sa_r.at[i], p)
                for i, p in enumerate(peers)
            ]
            for cp in out:
                cp.start()
            return out

        def small_second(first):
            for cp in first:
                cp.wait()
            s_own[...] = s_pack[pl.ds(pl.multiple_of(8 * f, 8), 8)] + s_in[0] + s_in[1] + s_in[2]
            out = [
                pltpu.make_async_remote_copy(
                    src_ref=s_own, dst_ref=s_rows.at[k - 1], send_sem=sb_s.at[k - 1], recv_sem=sb_r.at[k - 1],
                    device_id=((rw + k) % NR, f), device_id_type=MESH,
                )
                for k in range(1, NR)
            ]
            for cp in out:
                cp.start()
            return out

        def small_third(second):
            for cp in second:
                cp.wait()
            at = pl.ds(pl.multiple_of(8 * f, 8), 8)
            tot = s_own[...]
            for k in range(1, NR):
                tot = tot + s_rows[k - 1]
            s_all[at] = tot
            out = [remote(s_all.at[at], s_all.at[at], sc_s.at[i], sc_r.at[i], p) for i, p in enumerate(peers)]
            for cp in out:
                cp.start()
            return out

    def small_rows():
        hid = [hgrad[k : k + 1, q * C : (q + 1) * C] for k in range(3) for q in range(FF // C)]
        return jnp.concatenate([ggrad[...]] + hid + [jnp.zeros((4, C), F32)], axis=0)

    flat = lambda ref: ref[...].reshape(R * T, ref.shape[2])

    def put_n(first, value):
        n = value.shape[0]
        ngrad[first // 32 : (first + n) // 32] = value.astype(BF).reshape(n // 32, 2, 16, C)

    def put_b(first, value):
        bgrad[:, :, :, first : first + value.shape[1]] = value.astype(BF).reshape(C // 32, 2, 16, value.shape[1])

    zs[:, 0:C, :] = jnp.zeros((3, C, C), F32)

    def down_forward(r, carry):
        @pl.when(f > 0)
        def _():
            to_next(r3b.at[r, pl.ds(T - 16, 16)], r3b.at[r, pl.ds(T, 16)], r3_s.at[r], r3_r.at[r]).wait_recv()

        @pl.when(f < 3)
        def _():
            to_next(r3b.at[r, pl.ds(T - 16, 16)], r3b.at[r, pl.ds(T, 16)], r3_s.at[r], r3_r.at[r]).wait_send()

        @pl.when(f == 0)
        def _():
            r3b[r, T : T + 16, :] = jnp.zeros((16, C), BF)

        masks_strided(r)
        for hh in range(2):
            cols = slice(hh * 128, hh * 128 + 128)
            r3s[hh, 8 : 8 + T] = r3b[r, 0:T, cols].astype(F32)
            r3s[hh, 0:8] = r3b[r, T : T + 16, cols].astype(F32)[8:16]
        even = jnp.concatenate([r3s[hh, pl.ds(8, HT, stride=2), :] for hh in range(2)], axis=1).astype(BF)
        m_after = r3s[3, pl.ds(8, HT, stride=2), :]
        m_before = r3s[2, pl.ds(8, HT, stride=2), :]
        odd = jnp.concatenate([r3s[hh, pl.ds(9, HT, stride=2), :] * m_after for hh in range(2)], axis=1).astype(BF)
        before = jnp.concatenate([r3s[hh, pl.ds(7, HT, stride=2), :] * m_before for hh in range(2)], axis=1).astype(BF)
        gy = cot[r]
        out = gains[11:12, :]
        for j, blk in enumerate((before, even, odd)):
            w = slice(down + j * C, down + (j + 1) * C)
            out = out + dot(blk, narrow[w, :])
            zs[j, 0:C, :] += dot_tn(blk, gy)
        fout[r] = out.astype(BF)
        return carry

    lax.fori_loop(0, R, down_forward, 0)
    for j in range(3):
        put_n(down + j * C, zs[j, 0:C, :])

    gf_all = flat(gf)
    for b in range(4):
        cols = slice(b * 256, b * 256 + 256)
        put_n(tw + TE + b * 256, dot_tn(shaped[:, :, cols].reshape(R * T, 256), gf_all))
        put_b(4 * INNER + b * 256, dot_tn(flat(nl2), ginner[:, :, cols].reshape(R * T, 256)))
    put_b(3 * INNER, dot_tn(flat(gm), flat(att)))
    hgrad[1:2, :] = hgrad[1:2, :] * alpha_beta
    hgrad[2:3, :] = hgrad[2:3, :] * (-inv_beta)
    if gather:
        red_core(1)

    phase_sum(R - 1)

    def mean_tables(phase, norm_phase):
        tot = total_stats(phase)
        iv = norm_scale(total_stats(norm_phase, wait=False))
        m1 = jnp.where(group_lanes, tot, 0.0)
        m2 = jnp.where(group_lanes, pltpu.roll(tot, 128 - G, 1), 0.0)
        tabs[:, 0:C], tabs[:, C : 2 * C], tabs[:, 2 * C : 3 * C] = expand([m1 * iv, m2 * iv, iv])

    def norm_back_start(r, d, n, gain_row):
        ggrad[gain_row : gain_row + 1, :] += colsum(d * n)
        ggrad[gain_row + 1 : gain_row + 2, :] += colsum(d)
        scaled = d * gains[gain_row : gain_row + 1, :]
        dn[r] = scaled
        keep_sums(r, scaled, scaled * n)

    def phase_five(r, carry):
        cps = dkv_copies(r)
        for i in (0, 3, 2, 5):
            cps[i].wait_recv()
        for i in range(6):
            cps[i].wait_send()
        blk = pl.ds(pl.multiple_of(f * T, 128), T)
        for i in range(2):
            tot = part[r, i, blk].astype(F32) + rbuf[r, i, 0].astype(F32) + rbuf2[r, i].astype(F32)
            dqkv[r, :, (i + 1) * INNER : (i + 2) * INNER] = tot.astype(BF)
        back = dot_nt(dqkv[r], broad[:, : 3 * INNER])
        n, rs = layer_norm_parts(resid[r])
        ggrad[5:6, :] += colsum(back * n)
        ggrad[6:7, :] += colsum(back)
        g_res = gr2[r] + layer_norm_back(back, n, rs, gains[5:6, :])
        gr2[r] = g_res
        norm_back_start(r, g_res * der2[r].astype(F32), nrm2[r], 3)
        return carry

    lax.fori_loop(0, R, phase_five, 0)
    send_stats(2)
    if gather:
        red_cross(1)
    put_b(0, dot_tn(flat(ll1), flat(dqkv)))
    mean_tables(2, 1)

    def gh_copies(phase, r):
        return (
            to_next(g2.at[r, pl.ds(OFF + T - 16, 16)], g2.at[r, pl.ds(OFF - 16, 16)], gh_s.at[phase, 0, r], gh_r.at[phase, 0, r]),
            to_prev(g2.at[r, pl.ds(OFF, 16)], g2.at[r, pl.ds(OFF + T, 16)], gh_s.at[phase, 1, r], gh_r.at[phase, 1, r]),
        )

    def norm_back_end(r, n, which):
        sp = dot(metab[r, OFF : OFF + T], row_table(r, 3 * C))
        g = dn[r] * sp[:, 2 * C :] - sp[:, :C] - n * sp[:, C : 2 * C]
        g2[r, OFF : OFF + T] = g.astype(BF)
        down_cp, up_cp = gh_copies(which, r)

        @pl.when(f < 3)
        def _():
            down_cp.start()

        @pl.when(f > 0)
        def _():
            up_cp.start()

    def build_g3(which, r):
        down_cp, up_cp = gh_copies(which, r)

        @pl.when(f < 3)
        def _():
            down_cp.wait_send()
            up_cp.wait_recv()

        @pl.when(f > 0)
        def _():
            up_cp.wait_send()
            down_cp.wait_recv()

        @pl.when(f == 0)
        def _():
            g2[r, OFF - 16 : OFF, :] = jnp.zeros((16, C), BF)

        @pl.when(f == 3)
        def _():
            g2[r, OFF + T : OFF + T + 16, :] = jnp.zeros((16, C), BF)

        g = g2[r].astype(F32)
        zs[0] = g * metab[r, :, 24:25].astype(F32)
        zs[2] = g * metab[r, :, 25:26].astype(F32)
        g3[r, :, 0:C] = zs[0, OFF + 1 : OFF + T + 1].astype(BF)
        g3[r, :, C : 2 * C] = g2[r, OFF : OFF + T]
        g3[r, :, 2 * C : 3 * C] = zs[2, OFF - 1 : OFF + T - 1].astype(BF)

    def conv_back(r, first_row):
        out = jnp.zeros((T, C), F32)
        for j in range(3):
            out = out + dot_nt(g3[r, :, j * C : (j + 1) * C], narrow[first_row + j * C : first_row + (j + 1) * C, :])
        return out

    def kernel_grad(src, first_row):
        u = src[:, OFF : OFF + T, :].reshape(R * T, C)
        for j in range(3):
            put_n(first_row + j * C, dot_tn(u, g3[:, :, j * C : (j + 1) * C].reshape(R * T, C)))

    def phase_six(r, carry):
        norm_back_end(r, nrm2[r], 1)
        return carry

    lax.fori_loop(0, R, phase_six, 0)

    def phase_seven(r, carry):
        build_g3(1, r)
        gh = conv_back(r, 3 * C)
        oh = ohrow[r].astype(BF)
        tgr = segment_sums(oh, gh)
        tg[pl.ds(pl.multiple_of(8 * r, 8), 8), :] = tgr
        ggrad[2:3, :] += colsum(tgr)
        norm_back_start(r, gh * der1[r, OFF : OFF + T].astype(F32), nrm1[r, OFF : OFF + T], 0)
        return carry

    lax.fori_loop(0, R, phase_seven, 0)
    send_stats(3)
    if gather:
        red_owner(1)
    kernel_grad(u2, 3 * C)
    t_hi, t_lo = split2(tg[...])
    eb = emb[...].astype(BF)
    put_n(tw, dot_tn(eb, t_hi) + dot_tn(eb, t_lo))
    if gather:
        red_core(2)
    mean_tables(3, 0)

    def phase_eight(r, carry):
        norm_back_end(r, nrm1[r, OFF : OFF + T], 0)
        return carry

    lax.fori_loop(0, R, phase_eight, 0)

    if gather:
        small_a = small_first()
        red_cross(2)
    else:
        small[...] = small_rows()

    def phase_g3(r, carry):
        build_g3(0, r)
        return carry

    lax.fori_loop(0, R, phase_g3, 0)
    kernel_grad(uext, 0)
    if gather:
        red_core(3)
        small_b = small_second(small_a)
        red_owner(2)
    for r in range(R):
        igrad[r] = gr2[r] + conv_back(r, 0)
        if gather and r == 0:
            red_cross(3)
        if gather and r == R - 1:
            red_owner(3)
    if gather:
        small_c = small_third(small_b)
        for g in (1, 2, 3):
            red_wait(g)
        fin = red_finish()
        for cp in small_c:
            cp.wait()
        small[...] = s_all[...]
        for cp in fin:
            cp.wait()
        out_n[...] = gfull[...]
        out_b[...] = bfull[...]

    @pl.when(f < 3)
    def _():
        feat_down.wait_send()

    @pl.when(f > 0)
    def _():
        feat_up.wait_send()
        cot_up.wait_send()


def run_main(fused, feat, ids, steps, cot, narrow, broad, gains, hidden):
    R, T, _ = feat.shape
    L = ids.shape[1]
    TX = T + 2 * OFF
    NR = fused
    vm = lambda shape, dt=F32: pltpu.VMEM(shape, dt)
    dma = lambda *shape: pltpu.SemaphoreType.DMA(shape)
    slots = max(NR, 1)
    if NR:
        wide = [vm((KC, C), BF), vm((C, KR), BF)]
        red = [
            vm((KC // 32, 2, 16, C), BF), vm((C // 32, 2, 16, KR), BF), vm((KC // 32, 2, 16, 128), BF),
            vm((C // 32, 2, 16, KR // 2), BF), vm((KC // 32, 16, 128), BF), vm((C // 32, 16, KR // 2), BF),
            vm((NR, KC // NR // 32, 16, 128), BF), vm((NR, 16, KR // 2), BF),
            vm((KC // NR // 32, 2, 16, C), BF), vm((2, 16, KR), BF),
        ]
        outs = ((KC // NR // 32, 2, 16, C), (2, 16, KR))
    else:
        wide = [vm((16, 128), BF)] * 2
        red = [vm((16, 128), BF)] * 10
        outs = ((KC // 32, 2, 16, C), (C // 32, 2, 16, KR))
    scratch = wide + [
        vm((16, C)), vm((8, FF)), vm((slots, 16, 128), BF), vm((16, 128)), vm((8, FF)), vm((16, C)),
    ] + red + [
        vm((32, C)), vm((3, 8, C)), vm((8, C)), vm((slots, 8, C)), vm((32, C)),
        vm((R, TX, C), BF), vm((R, T // 2 + 16, C), BF), vm((R, TX, 128), BF),
        vm((R, 8, T)), vm((R, L, 128), BF), vm((24, L + 256)), vm((8 * R, 128)), vm((8 * R, TE)), vm((8 * R, C)),
        vm((8 * R, C)), vm((8 * R, C)), vm((8 * R, 3 * C)),
        vm((3, TX, C)), vm((R, TX, C)), vm((R, TX, C), BF), vm((R, TX, C), BF), vm((R, T, C)),
        vm((R, T, C), BF), vm((R, T, C)), vm((R, T, C), BF), vm((R, T, INNER), BF),
        vm((R, L, INNER), BF), vm((R, L, INNER), BF),
        vm((4, 3, 8 * R, 128)), vm((4, 8 * R, 128)),
        vm((INNER, L), BF), vm((INNER, L), BF), vm((L, T)), vm((H, L, T), BF), vm((INNER, T)),
        vm((H, 8, T)), vm((T, INNER)), vm((INNER, T)),
        vm((R, T, C), BF), vm((R, T, C), BF),
        vm((R, T, FF), BF), vm((R, T, FF), BF), vm((4, T + 8, 128)), vm((R, T + 16, C), BF),
        vm((R, T, C), BF), vm((R, T, INNER), BF), vm((INNER, T)),
        vm((R, 2, L, INNER), BF), vm((R, 2, 2, T, INNER), BF), vm((R, 2, T, INNER), BF), vm((R, 2, T, INNER), BF),
        vm((R, T, 3 * INNER), BF), vm((R, TX, C), BF), vm((8 * R, C)),
        dma(4, slots), dma(4, slots), dma(4, slots), dma(4, slots), dma(4, 2, slots), dma(4, 2, slots),
        dma(3, 3), dma(3, 3), dma(3, 3), dma(3, 3), dma(3, 3, slots), dma(3, 3, slots), dma(3, 3), dma(3, 3),
        dma(3), dma(3), dma(slots), dma(slots), dma(3), dma(3),
        dma(2), dma(2), dma(1), dma(1), dma(4, 3), dma(4, 3), dma(2, 3, R), dma(2, 3, R),
        dma(2, 3, R), dma(2, 3, R), dma(2, 2, R), dma(2, 2, R), dma(R), dma(R),
    ]
    out_shape = (
        jax.ShapeDtypeStruct((R, T // 2, C), BF),
        jax.ShapeDtypeStruct((R, T, C), F32),
        jax.ShapeDtypeStruct((32, C), F32),
        jax.ShapeDtypeStruct(outs[0], BF),
        jax.ShapeDtypeStruct(outs[1], BF),
    )
    spec = pl.BlockSpec(memory_space=pltpu.VMEM)
    return pl.pallas_call(
        functools.partial(main_kernel, NR),
        out_shape=out_shape,
        in_specs=[spec] * 8,
        out_specs=tuple([spec] * 5),
        scratch_shapes=scratch,
        compiler_params=pltpu.CompilerParams(collective_id=0, has_side_effects=True, vmem_limit_bytes=63 * 2**20),
        cost_estimate=pl.CostEstimate(flops=2 * 10**10, bytes_accessed=2 * 10**7, transcendentals=10**7),
    )(feat, ids, steps, cot, narrow, broad, gains, hidden)


def adam_update(grad, master, first, second, rate):
    moment = BETA_ONE * first + (1.0 - BETA_ONE) * grad
    square = BETA_TWO * second + (1.0 - BETA_TWO) * grad * grad
    corrected = moment / (1.0 - BETA_ONE**STEP)
    scaled = jnp.sqrt(square / (1.0 - BETA_TWO**STEP)) + EPS_ADAM
    return (moment, square, master - rate * (corrected / scaled + DECAY_RATE * master))


def adam_kernel(
    NR,
    gfull, bfull, small, nm, nf, ns, bm, bf_, bs, gm, gf, gs, hm, hf, hs, fout_in, igrad_in,
    fout, igrad, nmo, nso, nuo, bmo, bso, buo, gmo, gso, guo, hmo, hso, huo, nco, bco,
):
    igrad[...] = igrad_in[...]
    fout[...] = fout_in[...]
    SH, SB = nm.shape[0], bm.shape[0]
    rw = lax.axis_index("rows")
    for lo in range(0, SH // 32):
        rows = slice(32 * lo, 32 * lo + 32)
        g = gfull[lo].reshape(32, C).astype(F32)
        m, sq, up = adam_update(g, nm[rows], nf[rows], ns[rows], RATE_SLABS)
        nmo[rows], nso[rows], nuo[rows], nco[rows] = m, sq, up, up.astype(BF)
    for q in range(KR // C):
        cols = slice(q * C, q * C + C)
        g = bfull[:, :, cols].reshape(SB, C).astype(F32)
        m, sq, up = adam_update(g, bm[:, cols], bf_[:, cols], bs[:, cols], RATE_SLABS)
        bmo[:, cols], bso[:, cols], buo[:, cols], bco[:, cols] = m, sq, up, up.astype(BF)
    tot = small[...]
    gains_g = pltpu.roll(tot[0:16], (NR - rw) * (C // NR), 1)[:12, : C // NR]
    q = rw * (FF // NR) // C
    off = rw * (FF // NR) % C
    pick = iota((4, C), 0) == q
    hid = jnp.concatenate(
        [jnp.sum(jnp.where(pick, tot[16 + 4 * k : 20 + 4 * k], 0.0), axis=0, keepdims=True) for k in range(3)]
        + [jnp.zeros((5, C), F32)],
        axis=0,
    )
    hidden_g = pltpu.roll(hid, C - off, 1)[:3, : FF // NR]
    gmo[...], gso[...], guo[...] = adam_update(gains_g, gm[...], gf[...], gs[...], RATE_GAINS)
    hmo[...], hso[...], huo[...] = adam_update(hidden_g, hm[...], hf[...], hs[...], RATE_GAINS)


def run_adam(NR, gfull, bfull, small, fout, igrad, *state):
    shape = lambda a, dt=F32: jax.ShapeDtypeStruct(a.shape, dt)
    nm, bm, gm, hm = state[0], state[3], state[6], state[9]
    out_shape = (shape(fout, BF), shape(igrad)) + tuple(shape(a) for a in (nm, bm, gm, hm) for _ in range(3))
    out_shape += (shape(nm, BF), shape(bm, BF))
    spec = pl.BlockSpec(memory_space=pltpu.VMEM)
    return pl.pallas_call(
        functools.partial(adam_kernel, NR),
        out_shape=out_shape,
        in_specs=[spec] * 17,
        out_specs=tuple([spec] * 16),
        compiler_params=pltpu.CompilerParams(vmem_limit_bytes=60 * 2**20),
    )(gfull, bfull, small, *state, fout, igrad)


def local(
    features, segment_ids, timesteps, cotangent, narrow_slab, broad_slab, model_gains, hidden_gains,
    narrow_first, narrow_second, broad_first, broad_second, gains_first, gains_second, hidden_first, hidden_second,
):
    steps = timesteps
    groups = lax.axis_size("rows")
    if groups == 8:
        fout, igrad, small, gfull, bfull = run_main(
            groups, features, segment_ids, steps, cotangent, narrow_slab, broad_slab, model_gains, hidden_gains
        )
        return tuple(
            run_adam(
                groups, gfull, bfull, small, fout, igrad,
                narrow_slab, narrow_first, narrow_second, broad_slab, broad_first, broad_second,
                model_gains, gains_first, gains_second, hidden_gains, hidden_first, hidden_second,
            )
        )
    narrow_w = lax.all_gather(narrow_slab.astype(BF), "rows", axis=0, tiled=True)
    broad_w = lax.all_gather(broad_slab.astype(BF), "rows", axis=0, tiled=True)
    gains_all = lax.all_gather(model_gains.astype(BF), "rows", axis=1, tiled=True).astype(F32)
    hidden_all = lax.all_gather(hidden_gains.astype(BF), "rows", axis=1, tiled=True).astype(F32)
    fout, igrad, small, ngrad, bgrad = run_main(
        0, features, segment_ids, steps, cotangent, narrow_w, broad_w, gains_all, hidden_all
    )
    scat = lambda v: lax.psum(lax.psum_scatter(v, "rows", scatter_dimension=0, tiled=True), "frames")
    narrow_g = scat(ngrad.astype(F32).reshape(KC, C))
    broad_g = scat(bgrad.astype(F32).reshape(C, KR))
    small = lax.psum(small, ("rows", "frames"))
    i = lax.axis_index("rows")
    own = lambda a, n: lax.dynamic_slice_in_dim(a, i * n, n, 1)
    gains_g = own(small[:12], model_gains.shape[1])
    hidden_g = own(small[16:28].reshape(3, FF), hidden_gains.shape[1])
    narrow_new = adam_update(narrow_g, narrow_slab, narrow_first, narrow_second, RATE_SLABS)
    broad_new = adam_update(broad_g, broad_slab, broad_first, broad_second, RATE_SLABS)
    gains_new = adam_update(gains_g, model_gains, gains_first, gains_second, RATE_GAINS)
    hidden_new = adam_update(hidden_g, hidden_gains, hidden_first, hidden_second, RATE_GAINS)
    return (
        fout, igrad, *narrow_new, *broad_new, *gains_new, *hidden_new,
        narrow_new[2].astype(BF), broad_new[2].astype(BF),
    )


def solution(mesh):
    rows = P("rows", None)
    cols = P(None, "rows")
    act = P("rows", "frames", None)
    return jax.shard_map(
        local,
        mesh=mesh,
        in_specs=(act, rows, rows, act, rows, rows, cols, cols, rows, rows, rows, rows, cols, cols, cols, cols),
        out_specs=(act, act, rows, rows, rows, rows, rows, rows, cols, cols, cols, cols, cols, cols, rows, rows),
        check_vma=False,
    )
```

```python
import functools
import math

import jax
import jax.numpy as jnp
from jax import lax
from jax.experimental import pallas as pl
from jax.experimental.pallas import tpu as pltpu
from jax.sharding import PartitionSpec as P

C = 256
TE = 1024
H = 2
HD = 64
FF = 1024
G = 8
NSEG = 8
STEP = 10
KC = 4352
KR = 1536
INNER = 128
EPS_NORM = 1e-05
EPS_ADAM = 1e-08
BETA_ONE = 0.9
BETA_TWO = 0.999
RATE_SLABS = 0.08
RATE_GAINS = 0.4
DECAY_RATE = 0.01
MASK_FILL = -1e30

F32 = jnp.float32
BF = jnp.bfloat16
MESH = pl.DeviceIdType.MESH
OFF = 32
GROUP = C // G


def dot(a, b):
    return jnp.dot(a, b, preferred_element_type=F32)


def dot_nt(a, b):
    return lax.dot_general(a, b, (((1,), (1,)), ((), ())), preferred_element_type=F32)


def dot_tn(a, b):
    return lax.dot_general(a, b, (((0,), (0,)), ((), ())), preferred_element_type=F32)


def recip(x):
    r = pltpu.reciprocal(x, approx=True)
    return r * (2.0 - x * r)


def split2(x):
    hi = x.astype(BF)
    lo = (x - hi.astype(F32)).astype(BF)
    return hi, lo


def split3(x):
    hi = x.astype(BF).astype(F32)
    mid = (x - hi).astype(BF).astype(F32)
    lo = (x - hi - mid).astype(BF).astype(F32)
    return hi, mid, lo


def mish_parts(y):
    e = jnp.exp(jnp.minimum(y, 30.0))
    n = e * (e + 2.0)
    rc = recip(n + 2.0)
    t = n * rc
    d = t + y * (2.0 * rc) * (1.0 + t) * (e * recip(1.0 + e))
    return t, d


def reduced_angle(a):
    k = jnp.floor(a * (1.0 / math.pi) + 0.5)
    r = (a - k * 3.140625) - k * 9.67653589793e-4
    r2 = r * r
    s = r * (1.0 + r2 * (-1.0 / 6 + r2 * (1.0 / 120 + r2 * (-1.0 / 5040 + r2 * (1.0 / 362880)))))
    c = 1.0 + r2 * (
        -0.5 + r2 * (1.0 / 24 + r2 * (-1.0 / 720 + r2 * (1.0 / 40320 + r2 * (-1.0 / 3628800))))
    )
    return k, s, c


def sine_pair(x):
    t = x - jnp.floor(x + 0.5)
    t2 = t * t
    s = t * (3.141582022 + t2 * (-5.167142796 + t2 * (2.541899025 - t2 * 0.5546361918)))
    c = 1.9999999069 + t2 * (-9.869585718 + t2 * (8.116823828 + t2 * (-2.663760321 + t2 * 0.4393935944)))
    return s, c


def iota(shape, dim):
    return lax.broadcasted_iota(jnp.int32, shape, dim)


def group_sum_matrix(shift):
    return jnp.where(iota((C, 128), 0) // GROUP + shift == iota((C, 128), 1), 1.0, 0.0).astype(BF)


def group_spread_matrix():
    return jnp.where(iota((128, C), 0) == iota((128, C), 1) // GROUP, 1.0, 0.0).astype(BF)


def compact(sums, squares):
    n = sums.shape[0]
    a = jnp.concatenate(split3(sums), axis=0).astype(BF)
    b = jnp.concatenate(split3(squares), axis=0).astype(BF)
    both = dot(a, group_sum_matrix(0)) + dot(b, group_sum_matrix(G))
    return both[0:n] + both[n : 2 * n] + both[2 * n : 3 * n]


def expand(tables):
    n = tables[0].shape[0]
    stacked = jnp.concatenate([p for t in tables for p in split3(t)], axis=0).astype(BF)
    wide = dot(stacked, group_spread_matrix())
    part = lambda i: wide[n * i : n * i + n]
    return [part(3 * i) + part(3 * i + 1) + part(3 * i + 2) for i in range(len(tables))]


def table_of(columns):
    parts = split3(columns)
    zero = jnp.zeros((104, columns.shape[1]), F32)
    return jnp.concatenate(list(parts) + [zero], axis=0).astype(BF)


def segment_sums(onehot_rows, values):
    hi, lo = split2(values)
    return dot(onehot_rows, hi) + dot(onehot_rows, lo)


def layer_norm_parts(v):
    mu = jnp.mean(v, axis=-1, keepdims=True)
    cen = v - mu
    rs = lax.rsqrt(jnp.mean(cen * cen, axis=-1, keepdims=True) + EPS_NORM)
    return cen * rs, rs


def layer_norm_back(d, n, rs, gain):
    dg = d * gain
    return (dg - jnp.mean(dg, axis=-1, keepdims=True) - n * jnp.mean(dg * n, axis=-1, keepdims=True)) * rs


def colsum(x):
    return jnp.sum(x, axis=0, keepdims=True)


def main_kernel(
    NR,
    feat, ids, steps, cot, narrow_in, broad_in, gains_in, hidden_in,
    fout, igrad, small, out_n, out_b,
    narrow_s, broad_s, gains, hidden, smallw, packf, hgrad, hacc, ggrad,
    ngrad_s, bgrad_s, inh, inb, inq, inbq, got, bgot, gfull, bfull, s_pack, s_in, s_own, s_rows, s_all,
    uext, gyext, metab, ohrow, keymask, idp, counts, emb, tterm, sums, squares, tabs,
    zs, nrm1, der1, u2, nrm2, der2, resid, ll1, qs, kvall,
    statin, statout,
    kt, vt, qt, ffbuf, sbuf, ebuf, otb, invl, dos, dost,
    gf, nl2, shaped, ginner, r3s, r3b, gm, att, dq,
    part, rbuf, rbuf2, sumbuf, dqkv, g2, tg,
    ga_s, ga_r, gx_s, gx_r, gc_s, gc_r,
    rc_s, rc_r, rx_s, rx_r, rd_s, rd_r, rf_s, rf_r, sa_s, sa_r, sb_s, sb_r, sc_s, sc_r,
    halo_s, halo_r, cot_s, cot_r, stat_s, stat_r, kv_s, kv_r, dkv_s, dkv_r, gh_s, gh_r, r3_s, r3_r,
):
    R, T = feat.shape[0], feat.shape[1]
    gr2, dn, g3 = igrad, resid, shaped
    TX = T + 2 * OFF
    L = ids.shape[1]
    HT = T // 2
    f = lax.axis_index("frames")
    rw = lax.axis_index("rows")
    sib = f + 1 - 2 * (f % 2)
    cross = (f + 2) % 4
    diag = 3 - f
    peers = (sib, cross, diag)

    gather = NR > 0
    ngrad, bgrad = (ngrad_s, bgrad_s) if gather else (out_n, out_b)
    broad = broad_s if gather else broad_in
    if gather:
        SH, SB = narrow_in.shape[0], broad_in.shape[0]
        NB = SH // 32
        narrow_s[pl.ds(rw * NB, NB)] = narrow_in[...].astype(BF).reshape(NB, 2, 16, C)
        broad[pl.ds(pl.multiple_of(rw * SB, 16), SB), :] = broad_in[...].astype(BF)
        packf[...] = jnp.zeros(packf.shape, F32)
        packf[0:12, 0 : C // NR] = gains_in[...]
        packf[12:15, :] = hidden_in[...]
        smallw[rw] = packf[...].astype(BF)
    else:
        gains[0:12, :] = gains_in[...]
        hidden[0:3, :] = hidden_in[...]

    def wn(first, n):
        if gather:
            return narrow_s[first // 32 : (first + n) // 32].reshape(n, C)
        return narrow_in[first : first + n, :]

    barrier = pltpu.get_barrier_semaphore()
    for p in peers:
        pl.semaphore_signal(barrier, inc=1, device_id=(rw, p), device_id_type=MESH)
    for k in range(1, NR):
        pl.semaphore_signal(barrier, inc=1, device_id=((rw + k) % NR, f), device_id_type=MESH)
    pl.semaphore_wait(barrier, 3 + max(NR - 1, 0))

    def remote(src, dst, ssem, rsem, target):
        return pltpu.make_async_remote_copy(
            src_ref=src, dst_ref=dst, send_sem=ssem, recv_sem=rsem,
            device_id=(rw, target), device_id_type=MESH,
        )

    if gather:
        gx, gc = f // 2, f % 2
        conv_blocks = 3 * C // 32
        own_blocks = {
            0: {0: (0, NB), 1: (NB, conv_blocks)},
            1: {s: (max(NB * s, conv_blocks), NB * (s + 1)) for s in (1, 2, 4, 5, 6)},
            4: {s: (NB * s, NB * (s + 1)) for s in (3, 7)},
        }
        ranges = {0: ((0, 24),), 1: ((24, 48), (72, 104)), 4: ((48, 72), (104, 136))}
        kinds = (0, 1, 2, 4)

        def narrow_piece(g, lo, hi):
            return narrow_s.at[lo:hi, g // 2, :, pl.ds(pl.multiple_of(g % 2 * 128, 128), 128)]

        def broad_piece(g, lo, hi):
            width = KR // 4
            return broad.at[lo:hi, pl.ds(pl.multiple_of(g * width, 128), width)]

        def to_row(ref, ssem, rsem, row):
            return pltpu.make_async_remote_copy(
                src_ref=ref, dst_ref=ref, send_sem=ssem, recv_sem=rsem, device_id=(row, f), device_id_type=MESH
            )

        def sized(kind, n):
            if kind == 2:
                return broad.at[0 : n * SB, 0 : KR // 4]
            if kind == 3:
                return smallw.at[0:n]
            return narrow_s.at[0:n, 0, :, 0:128]

        def waits(kind, n, sends, sem):
            ref = sized(kind, n)
            cp = remote(ref, ref, sem, sem, cross)
            (cp.wait_send if sends else cp.wait_recv)()

        def by_row(counts, act):
            for n in sorted(set(counts)):
                if n:
                    rows_of = [s for s in range(NR) if counts[s] == n]
                    cond = functools.reduce(jnp.logical_or, [rw == s for s in rows_of])

                    @pl.when(cond)
                    def _():
                        act(n)

        def spread_start(kind):
            if kind in own_blocks:
                for s, (lo, hi) in own_blocks[kind].items():

                    @pl.when(rw == s)
                    def _():
                        for k in range(1, NR):
                            to_row(narrow_piece(f, lo, hi), ga_s.at[kind], ga_r.at[kind], (s + k) % NR).start()

                return
            for k in range(1, NR):
                if kind == 2:
                    at = pl.ds(pl.multiple_of(rw * SB, 16), SB)
                    ref = broad.at[at, pl.ds(pl.multiple_of(f * (KR // 4), 128), KR // 4)]
                else:
                    ref = smallw.at[rw]
                to_row(ref, ga_s.at[kind], ga_r.at[kind], (rw + k) % NR).start()

        def held(kind):
            sizes = [0] * NR
            for s, (lo, hi) in own_blocks[kind].items():
                sizes[s] = hi - lo
            return sizes

        def spread_arrive(kind):
            if kind in own_blocks:
                sizes = held(kind)
                by_row([sum(sizes) - n for n in sizes], lambda n: waits(kind, n, False, ga_r.at[kind]))
            else:
                waits(kind, NR - 1, False, ga_r.at[kind])

        def spread_end(kind):
            if kind in own_blocks:
                by_row([(NR - 1) * n for n in held(kind)], lambda n: waits(kind, n, True, ga_s.at[kind]))
            else:
                waits(kind, NR - 1, True, ga_s.at[kind])

        def pieces(kind, g):
            if kind == 2:
                return [broad_piece(g, 0, C)]
            return [narrow_piece(g, lo, hi) for lo, hi in ranges[kind]]

        def units(kind):
            return NR if kind == 2 else sum(hi - lo for lo, hi in ranges[kind])

        def pass_on(kind):
            spread_arrive(kind)
            for ref in pieces(kind, f):
                remote(ref, ref, gx_s.at[kind], gx_r.at[kind], cross).start()
            for ref in pieces(kind, f):
                remote(ref, ref, gc_s.at[kind, 0], gc_r.at[kind, 0], sib).start()

        def pass_across(kind):
            waits(kind, units(kind), False, gx_r.at[kind])
            for ref in pieces(kind, cross):
                remote(ref, ref, gc_s.at[kind, 1], gc_r.at[kind, 1], sib).start()

        def arrive(kind):
            for i in range(2):
                waits(kind, units(kind), False, gc_r.at[kind, i])

        def gather_end():
            for kind in kinds:
                spread_end(kind)
                waits(kind, units(kind), True, gx_s.at[kind])
                for i in range(2):
                    waits(kind, units(kind), True, gc_s.at[kind, i])
            spread_end(3)

        spread_start(3)
        spread_start(0)

    def to_next(src, dst, ssem, rsem):
        return remote(src, dst, ssem, rsem, (f + 1) % 4)

    def to_prev(src, dst, ssem, rsem):
        return remote(src, dst, ssem, rsem, (f + 3) % 4)

    feat_down = to_next(feat.at[:, pl.ds(T - 16, 16)], uext.at[:, pl.ds(OFF - 16, 16)], halo_s.at[0], halo_r.at[0])
    feat_up = to_prev(feat.at[:, pl.ds(0, 16)], uext.at[:, pl.ds(OFF + T, 16)], halo_s.at[1], halo_r.at[1])
    cot_up = to_prev(cot.at[:, pl.ds(0, 16)], gyext.at[:, pl.ds(HT, 16)], cot_s.at[0], cot_r.at[0])

    @pl.when(f < 3)
    def _():
        feat_down.start()

    @pl.when(f > 0)
    def _():
        feat_up.start()
        cot_up.start()

    uext[:, 0 : OFF - 16, :] = jnp.zeros((R, OFF - 16, C), BF)
    uext[:, OFF + T + 16 :, :] = jnp.zeros((R, TX - OFF - T - 16, C), BF)
    g2[:, 0 : OFF - 16, :] = jnp.zeros((R, OFF - 16, C), BF)
    g2[:, OFF + T + 16 :, :] = jnp.zeros((R, TX - OFF - T - 16, C), BF)

    @pl.when(f == 0)
    def _():
        uext[:, OFF - 16 : OFF, :] = jnp.zeros((R, 16, C), BF)

    @pl.when(f == 3)
    def _():
        uext[:, OFF + T : OFF + T + 16, :] = jnp.zeros((R, 16, C), BF)
        gyext[:, HT : HT + 16, :] = jnp.zeros((R, 16, C), BF)

    ggrad[...] = jnp.zeros(ggrad.shape, F32)
    hgrad[...] = jnp.zeros(hgrad.shape, F32)

    idp[...] = jnp.full(idp.shape, -1.0, F32)
    idp[0:R, 128 : 128 + L] = ids[...].astype(F32)
    idv = idp[0:8]
    width = idv.shape[1]
    prev_row = jnp.where(pltpu.roll(idv, 1, 1) == idv, 1.0, 0.0)
    next_row = jnp.where(pltpu.roll(idv, width - 1, 1) == idv, 1.0, 0.0)
    idp[8:16, :] = prev_row
    idp[16:24, :] = next_row
    base = pl.multiple_of(f * T, 128)
    WX = T + 256
    win = idp[:, pl.ds(base, WX)]
    win = pltpu.roll(win, WX - (128 - OFF), 1)[:, : T + 128]
    own = idp[:, pl.ds(pl.multiple_of(base + 128, 128), T)]
    for r in range(R):
        n_lane = T + 128
        row_id = jnp.broadcast_to(win[r : r + 1], (8, n_lane))
        lab = iota((8, n_lane), 0).astype(F32)
        oh = jnp.where(row_id == lab, 1.0, 0.0)
        pn = jnp.where(
            lab == 0.0,
            jnp.broadcast_to(win[8 + r : 9 + r], (8, n_lane)),
            jnp.where(lab == 1.0, jnp.broadcast_to(win[16 + r : 17 + r], (8, n_lane)), 0.0),
        )
        block = jnp.concatenate([oh, oh, oh, pn, jnp.zeros((96, n_lane), F32)], axis=0)
        turned = block.T
        metab[r] = turned[:TX].astype(BF)
        lab_own = iota((8, T), 0).astype(F32)
        ohrow[r] = jnp.where(jnp.broadcast_to(own[r : r + 1], (8, T)) == lab_own, 1.0, 0.0)
        full = jnp.broadcast_to(idv[r : r + 1, 128 : 128 + L], (8, L))
        lab_full = iota((8, L), 0).astype(F32)
        ohf = jnp.where(full == lab_full, 1.0, 0.0)
        counts[8 * r : 8 * r + 8] = jnp.broadcast_to(jnp.sum(ohf, axis=1, keepdims=True) * float(GROUP), (8, 128))
        km = jnp.concatenate([(1.0 - ohf) * MASK_FILL, jnp.zeros((120, L), F32)], axis=0)
        keymask[r] = km.T.astype(BF)

    uext[:, OFF : OFF + T, :] = feat[...]
    gyext[:, 0:HT, :] = cot[...]

    half = TE // 2
    freq = jnp.exp(iota((8, half), 1).astype(F32) * (-math.log(10000.0) / half))
    for r in range(R):
        turn = jnp.broadcast_to(steps[r : r + 1, :].astype(F32), (8, NSEG))
        ang = jnp.sum(jnp.where(iota((8, NSEG), 0) == iota((8, NSEG), 1), turn, 0.0), axis=1, keepdims=True) * freq
        k, s, c = reduced_angle(ang)
        sign = 1.0 - 2.0 * (k - 2.0 * jnp.floor(k * 0.5))
        both = jnp.concatenate([s * sign, c * sign], axis=1)
        emb[8 * r : 8 * r + 8, :] = both * mish_parts(both)[0]
    tw = 9 * C

    if gather:
        spread_start(1)
        spread_start(2)
        pass_on(0)
        spread_start(4)
        spread_arrive(3)
        wide = smallw[...].astype(F32)
        gains[...] = jnp.concatenate([wide[s, :, 0 : C // NR] for s in range(NR)], axis=1)
        hidden[0:3, :] = jnp.concatenate([wide[s, 12:15, :] for s in range(NR)], axis=1)
        pass_across(0)
        arrive(0)

    def own_prev(r):
        return metab[r, OFF : OFF + T, 24:25].astype(F32)

    def own_next(r):
        return metab[r, OFF : OFF + T, 25:26].astype(F32)

    def stat_copies(phase):
        return [
            remote(statout.at[phase], statin.at[phase, i], stat_s.at[phase], stat_r.at[phase, i], peers[i])
            for i in range(3)
        ]

    def keep_sums(r, first, second):
        oh = ohrow[r].astype(BF)
        at = pl.ds(pl.multiple_of(8 * r, 8), 8)
        sums[at] = segment_sums(oh, first)
        squares[at] = segment_sums(oh, second)

    def send_stats(phase):
        statout[phase] = compact(sums[...], squares[...])
        for cp in stat_copies(phase):
            cp.start()

    def total_stats(phase, wait=True):
        if wait:
            for cp in stat_copies(phase):
                cp.wait_recv()
            remote(statin.at[phase], statin.at[phase], stat_s.at[phase], stat_s.at[phase], sib).wait_send()
        return (statout[phase] + statin[phase, 0] + statin[phase, 1] + statin[phase, 2]) / jnp.maximum(counts[...], 1.0)

    group_lanes = iota((8 * R, 128), 1) < G

    def norm_scale(tot):
        second = pltpu.roll(tot, 128 - G, 1)
        return jnp.where(group_lanes, lax.rsqrt(jnp.maximum(second - tot * tot, 0.0) + EPS_NORM), 0.0)

    def norm_tables(phase):
        tot = total_stats(phase)
        inv = norm_scale(tot)
        tabs[:, 0:C], tabs[:, C : 2 * C] = expand([tot * inv, inv])

    def row_table(r, width):
        return table_of(tabs[pl.ds(pl.multiple_of(8 * r, 8), 8), 0:width])

    def conv_into(r, src, first_row):
        for j in range(3):
            zs[j] = dot(src[r], wn(first_row + j * C, C))

    @pl.when(f > 0)
    def _():
        feat_down.wait_recv()

    @pl.when(f < 3)
    def _():
        feat_up.wait_recv()

    def phase_one(r):
        conv_into(r, uext, 0)
        lo, hi = OFF - 16, OFF + T + 16
        n = hi - lo
        v = (
            zs[0, lo - 1 : hi - 1] * metab[r, lo:hi, 24:25].astype(F32)
            + zs[1, lo:hi]
            + zs[2, lo + 1 : hi + 1] * metab[r, lo:hi, 25:26].astype(F32)
        )
        nrm1[r, lo:hi] = v
        nrm1[r, 0:lo] = jnp.zeros((lo, C), F32)
        nrm1[r, hi:] = jnp.zeros((TX - hi, C), F32)
        vo = v[OFF - lo : OFF - lo + T]
        keep_sums(r, vo, vo * vo)

    for r in range(R):
        phase_one(r)
        if r == R - 1:
            send_stats(0)
        if gather:
            if r == 0:
                pass_on(1)
            elif r == 1:
                pass_on(2)
                pass_across(1)

    if gather:
        arrive(1)
    tterm[...] = dot(emb[...].astype(BF), wn(tw, TE)) + gains[2:3, :]

    CH = TX // 4
    tabs[:, 2 * C : 3 * C] = tterm[...]
    norm_tables(0)

    def phase_two(r, carry):
        tab = row_table(r, 3 * C)

        def chunk(i, c2):
            rows = pl.ds(pl.multiple_of(i * CH, 16), CH)
            sp = dot(metab[r, rows], tab)
            n = nrm1[r, rows] * sp[:, C : 2 * C] - sp[:, :C]
            y = n * gains[0:1, :] + gains[1:2, :]
            t, d = mish_parts(y)
            nrm1[r, rows] = n
            der1[r, rows] = d.astype(BF)
            u2[r, rows] = (y * t + sp[:, 2 * C :]).astype(BF)
            return c2

        lax.fori_loop(0, 4, chunk, 0)
        conv_into(r, u2, 3 * C)
        v = (
            zs[0, OFF - 1 : OFF + T - 1] * own_prev(r)
            + zs[1, OFF : OFF + T]
            + zs[2, OFF + 1 : OFF + T + 1] * own_next(r)
        )
        nrm2[r] = v
        keep_sums(r, v, v * v)
        return carry

    lax.fori_loop(0, R, phase_two, 0)
    send_stats(1)
    if gather:
        pass_across(2)
        pass_on(4)
        arrive(2)
    norm_tables(1)

    def kv_copies(r):
        slot = lambda g: kvall.at[r, :, pl.ds(pl.multiple_of(g * T, 128), T)]
        mine, other = slot(f), slot(cross)
        return (
            remote(mine, mine, kv_s.at[0, r], kv_r.at[0, r], sib),
            remote(mine, mine, kv_s.at[1, r], kv_r.at[1, r], cross),
            remote(other, other, kv_s.at[2, r], kv_r.at[2, r], sib),
        )

    NCH = 4
    CT = T // NCH

    def phase_three(r, carry):
        tab = row_table(r, 2 * C)

        def chunk(i, c2):
            rows = pl.ds(pl.multiple_of(i * CT, 16), CT)
            xrows = pl.ds(pl.multiple_of(OFF + i * CT, 16), CT)
            sp = dot(metab[r, xrows], tab)
            n = nrm2[r, rows] * sp[:, C : 2 * C] - sp[:, :C]
            y = n * gains[3:4, :] + gains[4:5, :]
            t, d = mish_parts(y)
            nrm2[r, rows] = n
            der2[r, rows] = d.astype(BF)
            res = y * t + feat[r, rows].astype(F32)
            resid[r, rows] = res
            m, rs = layer_norm_parts(res)
            low = (m * gains[5:6, :] + gains[6:7, :]).astype(BF)
            ll1[r, rows] = low
            qkv = dot(low, broad[:, : 3 * INNER])
            qs[r, rows] = (qkv[:, :INNER].astype(BF).astype(F32) * HD ** (-0.5)).astype(BF)
            krows = pl.ds(pl.multiple_of(f * T + i * CT, 16), CT)
            kvall[r, 0, krows] = qkv[:, INNER : 2 * INNER].astype(BF)
            kvall[r, 1, krows] = qkv[:, 2 * INNER :].astype(BF)
            return c2

        lax.fori_loop(0, NCH, chunk, 0)
        if gather:

            @pl.when(r == 0)
            def _():
                pass_across(4)

        cps = kv_copies(r)
        cps[1].start()
        cps[0].start()
        return carry

    lax.fori_loop(0, R, phase_three, 0)

    @pl.when(f < 3)
    def _():
        cot_up.wait_recv()

    down = 6 * C

    def phase_down_back(r, carry):
        gy = gyext[r, 0:HT]
        even = dot_nt(gy, wn(down + C, C))
        own_gy = dot_nt(gy, wn(down + 2 * C, C))
        nxt = dot_nt(gyext[r], wn(down, C))
        zs[0, 0 : HT + 16] = nxt
        for hh in range(2):
            cols = slice(hh * 128, hh * 128 + 128)
            pm = r3s[2, pl.ds(8 + 1, HT, stride=2), :]
            nm = r3s[3, pl.ds(8 + 1, HT, stride=2), :]
            r3s[hh, pl.ds(8, HT, stride=2), :] = even[:, cols]
            r3s[hh, pl.ds(9, HT, stride=2), :] = own_gy[:, cols] * pm + zs[0, 1 : HT + 1, cols] * nm
        return carry

    def masks_strided(r):
        r3s[2, 8 : 8 + T] = jnp.broadcast_to(own_prev(r), (T, 128))
        r3s[3, 8 : 8 + T] = jnp.broadcast_to(own_next(r), (T, 128))

    def down_back(r, carry):
        masks_strided(r)
        phase_down_back(r, carry)
        ggrad[11:12, :] += colsum(gyext[r, 0:HT].astype(F32))
        for hh in range(2):
            gf[r, :, hh * 128 : hh * 128 + 128] = r3s[hh, 8 : 8 + T].astype(BF)
        ggrad[10:11, :] += colsum(gf[r].astype(F32))
        return carry

    if gather:
        arrive(4)
    lax.fori_loop(0, R, down_back, 0)

    def relay(r):
        cps = kv_copies(r)
        cps[1].wait_recv()
        cps[2].start()

    relay(0)
    if gather:
        gather_end()

    alpha = jnp.exp(hidden[1:2, :])
    inv_beta = jnp.exp(-hidden[2:3, :])
    alpha_beta = alpha * inv_beta
    alpha_pi = alpha * (1.0 / math.pi)
    NK = L // 256
    CF = T // 2
    hacc[...] = jnp.zeros(hacc.shape, F32)
    lane128 = iota((T, 128), 1)

    def dkv_copies(r):
        return (
            remote(part.at[r, sib], rbuf.at[r, 0], dkv_s.at[0, r], dkv_r.at[0, r], sib),
            remote(part.at[r, diag], rbuf.at[r, 1], dkv_s.at[1, r], dkv_r.at[1, r], sib),
            remote(sumbuf.at[r], rbuf2.at[r], dkv_s.at[2, r], dkv_r.at[2, r], cross),
        )

    def phase_sum(r):
        cps = dkv_copies(r)
        cps[1].wait_recv()
        sumbuf[r] = (part[r, cross].astype(F32) + rbuf[r, 1].astype(F32)).astype(BF)
        cps[2].start()

    def phase_four(r, carry):
        cps = kv_copies(r)
        cps[0].wait_recv()
        cps[2].wait_recv()
        for cp in cps:
            cp.wait_send()
        kt[...] = kvall[r, 0].T
        vt[...] = kvall[r, 1].T
        qv = qs[r]
        ohq = jnp.where(lane128 < 8, metab[r, OFF : OFF + T], jnp.zeros((T, 128), BF))
        zero_q = jnp.zeros((T, 128), BF)
        q_heads = [jnp.where(lane128 // HD == h, qv, zero_q) for h in range(H)]
        TQ = T // 2
        units = [(h, q) for h in range(H) for q in range(2)]

        def scores(n):
            h, q = units[n]
            qrows = slice(q * TQ, q * TQ + TQ)
            qa = jnp.concatenate([q_heads[h][qrows], ohq[qrows]], axis=1)
            m8 = jnp.full((8, TQ), -3e38, F32)
            for i in range(NK):
                keys = slice(i * 256, i * 256 + 256)
                ka = jnp.concatenate([kvall[r, 0, keys], keymask[r, keys]], axis=1)
                sc = dot_nt(ka, qa)
                sbuf[n % 2, keys] = sc
                m8 = jnp.maximum(m8, jnp.max(sc.reshape(32, 8, TQ), axis=0))
            return jnp.max(m8, axis=0, keepdims=True)

        top = scores(0)
        for n, (h, q) in enumerate(units):
            later = scores(n + 1) if n + 1 < len(units) else None
            qcols = slice(q * TQ, q * TQ + TQ)
            l8 = jnp.zeros((8, TQ), F32)
            for i in range(NK):
                keys = slice(i * 256, i * 256 + 256)
                e = jnp.exp(sbuf[n % 2, keys] - top)
                ebuf[h, keys, qcols] = e.astype(BF)
                l8 = l8 + jnp.sum(e.reshape(32, 8, TQ), axis=0)
            inv = 1.0 / jnp.sum(l8, axis=0, keepdims=True)
            invl[h, :, qcols] = jnp.broadcast_to(inv, (8, TQ))
            hrows = slice(h * HD, (h + 1) * HD)
            otb[hrows, qcols] = dot(vt[hrows, :], ebuf[h, :, qcols]) * inv
            top = later
        att[r] = otb[...].T.astype(BF)

        @pl.when(r + 1 < R)
        def _():
            relay(r + 1)

        @pl.when(r > 0)
        def _():
            phase_sum(r - 1)

        def ff_chunk(i, c2):
            rows = pl.ds(pl.multiple_of(i * CF, 16), CF)
            res2 = resid[r, rows] + (dot_nt(att[r, rows], broad[:, 3 * INNER : 4 * INNER]) + gains[7:8, :])
            n, rs = layer_norm_parts(res2)
            low = (n * gains[8:9, :] + gains[9:10, :]).astype(BF)
            nl2[r, rows] = low
            gfr = gf[r, rows]
            def products(b):
                w_in = broad[:, 4 * INNER + b * 256 : 4 * INNER + b * 256 + 256]
                w_out = wn(tw + TE + b * 256, 256)
                ffbuf[b % 2, 0] = dot(low, w_in)
                ffbuf[b % 2, 1] = dot_nt(gfr, w_out)
                return w_in, w_out

            out, back = None, None
            weights = products(0)
            for b in range(4):
                following = products(b + 1) if b < 3 else None
                cols = slice(b * 256, b * 256 + 256)
                acc = [hacc[k, :, cols] for k in range(3)]
                shs, gis = [], []
                for u in range(0, CF, 32):
                    inner = ffbuf[b % 2, 0, u : u + 32] + hidden[0:1, cols]
                    gs = ffbuf[b % 2, 1, u : u + 32]
                    s, c = sine_pair(inner * alpha_pi[:, cols])
                    s2 = s * s
                    part_g = gs * (s * c)
                    shs.append((inner + s2 * inv_beta[:, cols]).astype(BF))
                    gi = gs + part_g * alpha_beta[:, cols]
                    gis.append(gi.astype(BF))
                    for k, v in enumerate((gi, part_g * inner, gs * s2)):
                        acc[k] = acc[k] + jnp.sum(v.reshape(4, 8, 256), axis=0)
                for k in range(3):
                    hacc[k, :, cols] = acc[k]
                sh_all, gi_all = jnp.concatenate(shs, axis=0), jnp.concatenate(gis, axis=0)
                shaped[r, rows, cols] = sh_all
                ginner[r, rows, cols] = gi_all
                more, more_back = dot(sh_all, weights[1]), dot_nt(gi_all, weights[0])
                out = more if out is None else out + more
                back = more_back if back is None else back + more_back
                weights = following
            r3 = (res2 + (out + gains[10:11, :])).astype(BF)
            r3b[r, rows] = r3
            g_in = gfr.astype(F32)
            ggrad[8:9, :] += colsum(back * n)
            ggrad[9:10, :] += colsum(back)
            g_res2 = g_in + layer_norm_back(back, n, rs, gains[8:9, :])
            gr2[r, rows] = g_res2
            low_g = g_res2.astype(BF)
            gm[r, rows] = low_g
            ggrad[7:8, :] += colsum(low_g.astype(F32))
            dos[rows] = dot(low_g, broad[:, 3 * INNER : 4 * INNER]).astype(BF).astype(F32)
            return c2

        lax.fori_loop(0, T // CF, ff_chunk, 0)

        @pl.when(f < 3)
        def _():
            to_next(r3b.at[r, pl.ds(T - 16, 16)], r3b.at[r, pl.ds(T, 16)], r3_s.at[r], r3_r.at[r]).start()

        dot_t = dos[...].T
        for h in range(H):
            hrows = slice(h * HD, (h + 1) * HD)
            dost[hrows, :] = dot_t[hrows] * invl[h, 0:1, :]
        zero_t = jnp.zeros((HD, T), BF)
        d_rows, d_cols, d_half = [], [], []
        per_block = T // 256
        for h in range(H):
            hrows = slice(h * HD, (h + 1) * HD)
            d_rows.append(colsum(otb[hrows, :] * dost[hrows, :]))
            dh = dost[hrows, :].astype(BF)
            d_half.append(dh)
            d_cols.append(jnp.concatenate([dh, zero_t] if h == 0 else [zero_t, dh], axis=0))
        qt[...] = qs[r].T
        for i in range(NK):
            keys = slice(i * 256, i * 256 + 256)
            for h in range(H):
                hrows = slice(h * HD, (h + 1) * HD)
                eh = ebuf[h, keys]
                dp = dot(kvall[r, 1, keys], d_cols[h])
                ds = (eh.astype(F32) * (dp - d_rows[h])).astype(BF)
                part[r, i // per_block, 0, hrows, i % per_block * 256 : i % per_block * 256 + 256] = dot_nt(qt[hrows, :], ds).astype(BF)
                part[r, i // per_block, 1, hrows, i % per_block * 256 : i % per_block * 256 + 256] = dot_nt(d_half[h], eh).astype(BF)
                if i == 0:
                    dq[hrows, :] = dot(kt[hrows, keys], ds)
                else:
                    dq[hrows, :] += dot(kt[hrows, keys], ds)
        dqkv[r, :, 0:INNER] = (dq[...].T * HD ** (-0.5)).astype(BF)
        cps = dkv_copies(r)
        cps[1].start()
        cps[0].start()
        return carry

    lax.fori_loop(0, R, phase_four, 0)

    if gather:
        rx, rc = f // 2, f % 2
        shard_blocks = NB
        n_groups = {1: ((48, 72), (104, 136)), 2: ((24, 48), (72, 104)), 3: ((0, 24),)}
        b_groups = {1: (4 * INNER, 2 * C), 2: (0, C)}
        b_at = {1: C, 2: 0}

        def half_cols(core, first, n):
            return pl.ds(pl.multiple_of(first + core * n, 128), n)

        def core_copies(g):
            out = [
                remote(ngrad.at[lo:hi, :, :, half_cols(1 - rc, 0, 128)], inh.at[lo:hi], rc_s.at[g - 1, i], rc_r.at[g - 1, i], sib)
                for i, (lo, hi) in enumerate(n_groups[g])
            ]
            if g in b_groups:
                first, n = b_groups[g]
                out.append(
                    remote(
                        bgrad.at[:, :, :, half_cols(1 - rc, first, n)], inb.at[:, :, :, b_at[g] : b_at[g] + n],
                        rc_s.at[g - 1, 2], rc_r.at[g - 1, 2], sib,
                    )
                )
            return out

        def cross_copies(g):
            out = [
                remote(ngrad.at[lo:hi, 1 - rx, :, half_cols(rc, 0, 128)], inq.at[lo:hi], rx_s.at[g - 1, i], rx_r.at[g - 1, i], cross)
                for i, (lo, hi) in enumerate(n_groups[g])
            ]
            if g in b_groups:
                first, n = b_groups[g]
                out.append(
                    remote(
                        bgrad.at[:, 1 - rx, :, half_cols(rc, first, n)], inbq.at[:, :, b_at[g] : b_at[g] + n],
                        rx_s.at[g - 1, 2], rx_r.at[g - 1, 2], cross,
                    )
                )
            return out

        def owner_copies(g, s, source):
            out = []
            for i, (lo, hi) in enumerate(n_groups[g]):
                a, b = max(lo, shard_blocks * s), min(hi, shard_blocks * (s + 1))
                if a < b:
                    out.append(
                        pltpu.make_async_remote_copy(
                            src_ref=ngrad.at[a:b, rx, :, half_cols(rc, 0, 128)],
                            dst_ref=got.at[source, a - shard_blocks * s : b - shard_blocks * s],
                            send_sem=rd_s.at[g - 1, 0], recv_sem=rd_r.at[g - 1, 0],
                            device_id=(s, f), device_id_type=MESH,
                        )
                    )
            if g in b_groups:
                first, n = b_groups[g]
                out.append(
                    pltpu.make_async_remote_copy(
                        src_ref=bgrad.at[s, rx, :, half_cols(rc, first, n)],
                        dst_ref=bgot.at[source, :, b_at[g] : b_at[g] + n],
                        send_sem=rd_s.at[g - 1, 1], recv_sem=rd_r.at[g - 1, 1],
                        device_id=(s, f), device_id_type=MESH,
                    )
                )
            return out

        def red_core(g):
            for cp in core_copies(g):
                cp.start()

        def red_cross(g):
            for cp in core_copies(g):
                cp.wait()
            mine = half_cols(rc, 0, 128)
            for lo, hi in n_groups[g]:
                ngrad[lo:hi, :, :, mine] = (ngrad[lo:hi, :, :, mine].astype(F32) + inh[lo:hi].astype(F32)).astype(BF)
            if g in b_groups:
                first, n = b_groups[g]
                cols = half_cols(rc, first, n)
                other = inb[:, :, :, b_at[g] : b_at[g] + n]
                bgrad[:, :, :, cols] = (bgrad[:, :, :, cols].astype(F32) + other.astype(F32)).astype(BF)
            for cp in cross_copies(g):
                cp.start()

        def red_owner(g):
            for cp in cross_copies(g):
                cp.wait()
            mine = half_cols(rc, 0, 128)
            for lo, hi in n_groups[g]:
                ngrad[lo:hi, rx, :, mine] = (ngrad[lo:hi, rx, :, mine].astype(F32) + inq[lo:hi].astype(F32)).astype(BF)
            if g in b_groups:
                first, n = b_groups[g]
                cols = half_cols(rc, first, n)
                other = inbq[:, :, b_at[g] : b_at[g] + n]
                bgrad[:, rx, :, cols] = (bgrad[:, rx, :, cols].astype(F32) + other.astype(F32)).astype(BF)
            for s in range(NR):

                @pl.when(rw != s)
                def _():
                    for cp in owner_copies(g, s, rw):
                        cp.start()

        def red_wait(g):
            overlap = [
                sum(max(0, min(hi, NB * (s + 1)) - max(lo, NB * s)) for lo, hi in n_groups[g]) for s in range(NR)
            ]

            def take(n, sends, sem):
                cp = remote(inq.at[0:n], inq.at[0:n], sem, sem, cross)
                (cp.wait_send if sends else cp.wait_recv)()

            by_row([sum(overlap) - n for n in overlap], lambda n: take(n, True, rd_s.at[g - 1, 0]))
            by_row([(NR - 1) * n for n in overlap], lambda n: take(n, False, rd_r.at[g - 1, 0]))
            if g in b_groups:
                ref = bgot.at[0 : NR - 1, :, b_at[g] : b_at[g] + b_groups[g][1]]
                cp = remote(ref, ref, rd_s.at[g - 1, 1], rd_r.at[g - 1, 1], cross)
                cp.wait_send()
                cp.wait_recv()

        def red_finish():
            mine = half_cols(rc, 0, 128)
            total = ngrad[pl.ds(shard_blocks * rw, shard_blocks), rx, :, mine].astype(F32)
            totals = [bgrad[rw, rx, :, half_cols(rc, *b_groups[g])].astype(F32) for g in (1, 2)]
            for k in range(1, NR):
                o = (rw + k) % NR
                total = total + got[o].astype(F32)
                for j, g in enumerate((1, 2)):
                    totals[j] = totals[j] + bgot[o, :, b_at[g] : b_at[g] + b_groups[g][1]].astype(F32)
            gfull[:, rx, :, mine] = total.astype(BF)
            fin = []
            blocks = [gfull.at[:, rx, :, mine]]
            for j, g in enumerate((1, 2)):
                cols = half_cols(rc, *b_groups[g])
                bfull[rx, :, cols] = totals[j].astype(BF)
                blocks.append(bfull.at[rx, :, cols])
            for j, blk in enumerate(blocks):
                for p in peers:
                    remote(blk, blk, rf_s.at[j], rf_r.at[j], p).start()
                fin.append((rf_s.at[j], rf_r.at[j]))
            sizes = [inq.at[0 : 3 * NB]] + [bgot.at[0:3, :, b_at[g] : b_at[g] + b_groups[g][1]] for g in (1, 2)]
            return [remote(ref, ref, ss, rs, cross) for ref, (ss, rs) in zip(sizes, fin)]

        def small_first():
            s_pack[...] = small_rows()
            for i, p in enumerate(peers):
                remote(s_pack.at[pl.ds(pl.multiple_of(8 * p, 8), 8)], s_in.at[i], sa_s.at[0], sa_r.at[0], p).start()

        def small_second():
            remote(s_in, s_in, sa_s.at[0], sa_r.at[0], sib).wait()
            s_own[...] = s_pack[pl.ds(pl.multiple_of(8 * f, 8), 8)] + s_in[0] + s_in[1] + s_in[2]
            for k in range(1, NR):
                pltpu.make_async_remote_copy(
                    src_ref=s_own, dst_ref=s_rows.at[k - 1], send_sem=sb_s.at[0], recv_sem=sb_r.at[0],
                    device_id=((rw + k) % NR, f), device_id_type=MESH,
                ).start()

        def small_third():
            ref = s_rows.at[0 : NR - 1]
            remote(ref, ref, sb_s.at[0], sb_r.at[0], sib).wait()
            at = pl.ds(pl.multiple_of(8 * f, 8), 8)
            tot = s_own[...]
            for k in range(1, NR):
                tot = tot + s_rows[k - 1]
            s_all[at] = tot
            for p in peers:
                remote(s_all.at[at], s_all.at[at], sc_s.at[0], sc_r.at[0], p).start()

        def small_last():
            remote(s_in, s_in, sc_s.at[0], sc_r.at[0], sib).wait()

    def small_rows():
        hid = [hgrad[k : k + 1, q * C : (q + 1) * C] for k in range(3) for q in range(FF // C)]
        return jnp.concatenate([ggrad[...]] + hid + [jnp.zeros((4, C), F32)], axis=0)

    flat = lambda ref: ref[...].reshape(R * T, ref.shape[2])

    def put_n(first, value):
        n = value.shape[0]
        ngrad[first // 32 : (first + n) // 32] = value.astype(BF).reshape(n // 32, 2, 16, C)

    def put_b(first, value):
        bgrad[:, :, :, first : first + value.shape[1]] = value.astype(BF).reshape(C // 32, 2, 16, value.shape[1])

    zs[:, 0:C, :] = jnp.zeros((3, C, C), F32)

    def down_forward(r, carry):
        @pl.when(f > 0)
        def _():
            to_next(r3b.at[r, pl.ds(T - 16, 16)], r3b.at[r, pl.ds(T, 16)], r3_s.at[r], r3_r.at[r]).wait_recv()

        @pl.when(f < 3)
        def _():
            to_next(r3b.at[r, pl.ds(T - 16, 16)], r3b.at[r, pl.ds(T, 16)], r3_s.at[r], r3_r.at[r]).wait_send()

        @pl.when(f == 0)
        def _():
            r3b[r, T : T + 16, :] = jnp.zeros((16, C), BF)

        masks_strided(r)
        for hh in range(2):
            cols = slice(hh * 128, hh * 128 + 128)
            r3s[hh, 8 : 8 + T] = r3b[r, 0:T, cols].astype(F32)
            r3s[hh, 0:8] = r3b[r, T : T + 16, cols].astype(F32)[8:16]
        even = jnp.concatenate([r3s[hh, pl.ds(8, HT, stride=2), :] for hh in range(2)], axis=1).astype(BF)
        m_after = r3s[3, pl.ds(8, HT, stride=2), :]
        m_before = r3s[2, pl.ds(8, HT, stride=2), :]
        odd = jnp.concatenate([r3s[hh, pl.ds(9, HT, stride=2), :] * m_after for hh in range(2)], axis=1).astype(BF)
        before = jnp.concatenate([r3s[hh, pl.ds(7, HT, stride=2), :] * m_before for hh in range(2)], axis=1).astype(BF)
        gy = cot[r]
        out = gains[11:12, :]
        for j, blk in enumerate((before, even, odd)):
            out = out + dot(blk, wn(down + j * C, C))
            zs[j, 0:C, :] += dot_tn(blk, gy)
        fout[r] = out.astype(BF)
        return carry

    lax.fori_loop(0, R, down_forward, 0)
    for j in range(3):
        put_n(down + j * C, zs[j, 0:C, :])

    gf_all = flat(gf)
    for b in range(4):
        cols = slice(b * 256, b * 256 + 256)
        put_n(tw + TE + b * 256, dot_tn(shaped[:, :, cols].reshape(R * T, 256), gf_all))
        put_b(4 * INNER + b * 256, dot_tn(flat(nl2), ginner[:, :, cols].reshape(R * T, 256)))
    put_b(3 * INNER, dot_tn(flat(gm), flat(att)))
    hgrad[0:1, :] = colsum(hacc[0])
    hgrad[1:2, :] = colsum(hacc[1]) * alpha_beta
    hgrad[2:3, :] = colsum(hacc[2]) * (-inv_beta)
    if gather:
        red_core(1)

    phase_sum(R - 1)

    def mean_tables(phase, norm_phase):
        tot = total_stats(phase)
        iv = norm_scale(total_stats(norm_phase, wait=False))
        m1 = jnp.where(group_lanes, tot, 0.0)
        m2 = jnp.where(group_lanes, pltpu.roll(tot, 128 - G, 1), 0.0)
        tabs[:, 0:C], tabs[:, C : 2 * C], tabs[:, 2 * C : 3 * C] = expand([m1 * iv, m2 * iv, iv])

    def norm_back_start(r, d, n, gain_row):
        ggrad[gain_row : gain_row + 1, :] += colsum(d * n)
        ggrad[gain_row + 1 : gain_row + 2, :] += colsum(d)
        scaled = d * gains[gain_row : gain_row + 1, :]
        dn[r] = scaled
        keep_sums(r, scaled, scaled * n)

    def phase_five(r, carry):
        cps = dkv_copies(r)
        cps[0].wait_recv()
        cps[2].wait_recv()
        for cp in cps:
            cp.wait_send()
        for i in range(2):
            tot = part[r, f, i].astype(F32) + rbuf[r, 0, i].astype(F32) + rbuf2[r, i].astype(F32)
            dqkv[r, :, (i + 1) * INNER : (i + 2) * INNER] = tot.T.astype(BF)
        back = dot_nt(dqkv[r], broad[:, : 3 * INNER])
        n, rs = layer_norm_parts(resid[r])
        ggrad[5:6, :] += colsum(back * n)
        ggrad[6:7, :] += colsum(back)
        g_res = gr2[r] + layer_norm_back(back, n, rs, gains[5:6, :])
        gr2[r] = g_res
        norm_back_start(r, g_res * der2[r].astype(F32), nrm2[r], 3)
        return carry

    lax.fori_loop(0, R, phase_five, 0)
    send_stats(2)
    if gather:
        red_cross(1)
    put_b(0, dot_tn(flat(ll1), flat(dqkv)))
    mean_tables(2, 1)

    def gh_copies(phase, r):
        return (
            to_next(g2.at[r, pl.ds(OFF + T - 16, 16)], g2.at[r, pl.ds(OFF - 16, 16)], gh_s.at[phase, 0, r], gh_r.at[phase, 0, r]),
            to_prev(g2.at[r, pl.ds(OFF, 16)], g2.at[r, pl.ds(OFF + T, 16)], gh_s.at[phase, 1, r], gh_r.at[phase, 1, r]),
        )

    def norm_back_end(r, n, which):
        sp = dot(metab[r, OFF : OFF + T], row_table(r, 3 * C))
        g = dn[r] * sp[:, 2 * C :] - sp[:, :C] - n * sp[:, C : 2 * C]
        g2[r, OFF : OFF + T] = g.astype(BF)
        down_cp, up_cp = gh_copies(which, r)

        @pl.when(f < 3)
        def _():
            down_cp.start()

        @pl.when(f > 0)
        def _():
            up_cp.start()

    def build_g3(which, r):
        down_cp, up_cp = gh_copies(which, r)

        @pl.when(f < 3)
        def _():
            down_cp.wait_send()
            up_cp.wait_recv()

        @pl.when(f > 0)
        def _():
            up_cp.wait_send()
            down_cp.wait_recv()

        @pl.when(f == 0)
        def _():
            g2[r, OFF - 16 : OFF, :] = jnp.zeros((16, C), BF)

        @pl.when(f == 3)
        def _():
            g2[r, OFF + T : OFF + T + 16, :] = jnp.zeros((16, C), BF)

        g = g2[r].astype(F32)
        zs[0] = g * metab[r, :, 24:25].astype(F32)
        zs[2] = g * metab[r, :, 25:26].astype(F32)
        g3[r, :, 0:C] = zs[0, OFF + 1 : OFF + T + 1].astype(BF)
        g3[r, :, C : 2 * C] = g2[r, OFF : OFF + T]
        g3[r, :, 2 * C : 3 * C] = zs[2, OFF - 1 : OFF + T - 1].astype(BF)

    def conv_back(r, first_row):
        out = jnp.zeros((T, C), F32)
        for j in range(3):
            out = out + dot_nt(g3[r, :, j * C : (j + 1) * C], wn(first_row + j * C, C))
        return out

    def kernel_grad(src, first_row):
        u = src[:, OFF : OFF + T, :].reshape(R * T, C)
        for j in range(3):
            put_n(first_row + j * C, dot_tn(u, g3[:, :, j * C : (j + 1) * C].reshape(R * T, C)))

    def phase_six(r, carry):
        norm_back_end(r, nrm2[r], 1)
        return carry

    lax.fori_loop(0, R, phase_six, 0)

    def phase_seven(r, carry):
        build_g3(1, r)
        gh = conv_back(r, 3 * C)
        oh = ohrow[r].astype(BF)
        tgr = segment_sums(oh, gh)
        tg[pl.ds(pl.multiple_of(8 * r, 8), 8), :] = tgr
        ggrad[2:3, :] += colsum(tgr)
        norm_back_start(r, gh * der1[r, OFF : OFF + T].astype(F32), nrm1[r, OFF : OFF + T], 0)
        return carry

    lax.fori_loop(0, R, phase_seven, 0)
    send_stats(3)
    if gather:
        red_owner(1)
    kernel_grad(u2, 3 * C)
    t_hi, t_lo = split2(tg[...])
    eb = emb[...].astype(BF)
    put_n(tw, dot_tn(eb, t_hi) + dot_tn(eb, t_lo))
    if gather:
        red_core(2)
    mean_tables(3, 0)

    def phase_eight(r, carry):
        norm_back_end(r, nrm1[r, OFF : OFF + T], 0)
        return carry

    lax.fori_loop(0, R, phase_eight, 0)

    if gather:
        small_first()
        red_cross(2)
    else:
        small[...] = small_rows()

    def phase_g3(r, carry):
        build_g3(0, r)
        return carry

    lax.fori_loop(0, R, phase_g3, 0)
    kernel_grad(uext, 0)
    if gather:
        red_core(3)
        small_second()
        red_owner(2)
    for r in range(R):
        igrad[r] = gr2[r] + conv_back(r, 0)
        if gather and r == 0:
            red_cross(3)
        if gather and r == R - 1:
            red_owner(3)
    if gather:
        small_third()
        for g in (1, 2, 3):
            red_wait(g)
        fin = red_finish()
        small_last()
        small[...] = s_all[...]
        for cp in fin:
            cp.wait()
        out_n[...] = gfull[...]
        out_b[...] = bfull[...]

    @pl.when(f < 3)
    def _():
        feat_down.wait_send()

    @pl.when(f > 0)
    def _():
        feat_up.wait_send()
        cot_up.wait_send()


def run_main(fused, feat, ids, steps, cot, narrow, broad, gains, hidden):
    R, T, _ = feat.shape
    L = ids.shape[1]
    TX = T + 2 * OFF
    NR = fused
    vm = lambda shape, dt=F32: pltpu.VMEM(shape, dt)
    dma = lambda *shape: pltpu.SemaphoreType.DMA(shape)
    slots = max(NR, 1)
    if NR:
        wide = [vm((KC // 32, 2, 16, C), BF), vm((C, KR), BF)]
        red = [
            vm((KC // 32, 2, 16, C), BF), vm((C // 32, 2, 16, KR), BF), vm((KC // 32, 2, 16, 128), BF),
            vm((C // 32, 2, 16, KR // 2), BF), vm((KC // 32, 16, 128), BF), vm((C // 32, 16, KR // 2), BF),
            vm((NR, KC // NR // 32, 16, 128), BF), vm((NR, 16, KR // 2), BF),
            vm((KC // NR // 32, 2, 16, C), BF), vm((2, 16, KR), BF),
        ]
        outs = ((KC // NR // 32, 2, 16, C), (2, 16, KR))
    else:
        wide = [vm((16, 128), BF)] * 2
        red = [vm((16, 128), BF)] * 10
        outs = ((KC // 32, 2, 16, C), (C // 32, 2, 16, KR))
    scratch = wide + [
        vm((16, C)), vm((8, FF)), vm((slots, 16, 128), BF), vm((16, 128)), vm((8, FF)), vm((3, 8, FF)), vm((16, C)),
    ] + red + [
        vm((32, C)), vm((3, 8, C)), vm((8, C)), vm((slots, 8, C)), vm((32, C)),
        vm((R, TX, C), BF), vm((R, T // 2 + 16, C), BF), vm((R, TX, 128), BF),
        vm((R, 8, T)), vm((R, L, 128), BF), vm((24, L + 256)), vm((8 * R, 128)), vm((8 * R, TE)), vm((8 * R, C)),
        vm((8 * R, C)), vm((8 * R, C)), vm((8 * R, 3 * C)),
        vm((3, TX, C)), vm((R, TX, C)), vm((R, TX, C), BF), vm((R, TX, C), BF), vm((R, T, C)),
        vm((R, T, C), BF), vm((R, T, C)), vm((R, T, C), BF), vm((R, T, INNER), BF),
        vm((R, 2, L, INNER), BF),
        vm((4, 3, 8 * R, 128)), vm((4, 8 * R, 128)),
        vm((INNER, L), BF), vm((INNER, L), BF), vm((INNER, T), BF), vm((2, 2, T // 2, C)), vm((2, L, T // 2)), vm((H, L, T), BF), vm((INNER, T)),
        vm((H, 8, T)), vm((T, INNER)), vm((INNER, T)),
        vm((R, T, C), BF), vm((R, T, C), BF),
        vm((R, T, FF), BF), vm((R, T, FF), BF), vm((4, T + 8, 128)), vm((R, T + 16, C), BF),
        vm((R, T, C), BF), vm((R, T, INNER), BF), vm((INNER, T)),
        vm((R, 4, 2, INNER, T), BF), vm((R, 2, 2, INNER, T), BF), vm((R, 2, INNER, T), BF), vm((R, 2, INNER, T), BF),
        vm((R, T, 3 * INNER), BF), vm((R, TX, C), BF), vm((8 * R, C)),
        dma(5), dma(5), dma(5), dma(5), dma(5, 2), dma(5, 2),
        dma(3, 3), dma(3, 3), dma(3, 3), dma(3, 3), dma(3, 2), dma(3, 2), dma(3), dma(3),
        dma(1), dma(1), dma(1), dma(1), dma(1), dma(1),
        dma(2), dma(2), dma(1), dma(1), dma(4), dma(4, 3), dma(3, R), dma(3, R),
        dma(3, R), dma(3, R), dma(2, 2, R), dma(2, 2, R), dma(R), dma(R),
    ]
    out_shape = (
        jax.ShapeDtypeStruct((R, T // 2, C), BF),
        jax.ShapeDtypeStruct((R, T, C), F32),
        jax.ShapeDtypeStruct((32, C), F32),
        jax.ShapeDtypeStruct(outs[0], BF),
        jax.ShapeDtypeStruct(outs[1], BF),
    )
    spec = pl.BlockSpec(memory_space=pltpu.VMEM)
    return pl.pallas_call(
        functools.partial(main_kernel, NR),
        out_shape=out_shape,
        in_specs=[spec] * 8,
        out_specs=tuple([spec] * 5),
        scratch_shapes=scratch,
        compiler_params=pltpu.CompilerParams(collective_id=0, has_side_effects=True, vmem_limit_bytes=63 * 2**20),
        cost_estimate=pl.CostEstimate(flops=2 * 10**10, bytes_accessed=2 * 10**7, transcendentals=10**7),
    )(feat, ids, steps, cot, narrow, broad, gains, hidden)


def adam_update(grad, master, first, second, rate):
    moment = BETA_ONE * first + (1.0 - BETA_ONE) * grad
    square = BETA_TWO * second + (1.0 - BETA_TWO) * grad * grad
    corrected = moment / (1.0 - BETA_ONE**STEP)
    scaled = jnp.sqrt(square / (1.0 - BETA_TWO**STEP)) + EPS_ADAM
    return (moment, square, master - rate * (corrected / scaled + DECAY_RATE * master))


def adam_kernel(
    NR,
    gfull, bfull, small, nm, nf, ns, bm, bf_, bs, gm, gf, gs, hm, hf, hs, fout_in, igrad_in,
    fout, igrad, nmo, nso, nuo, bmo, bso, buo, gmo, gso, guo, hmo, hso, huo, nco, bco,
):
    igrad[...] = igrad_in[...]
    fout[...] = fout_in[...]
    SH, SB = nm.shape[0], bm.shape[0]
    rw = lax.axis_index("rows")
    for lo in range(0, SH // 32):
        rows = slice(32 * lo, 32 * lo + 32)
        g = gfull[lo].reshape(32, C).astype(F32)
        m, sq, up = adam_update(g, nm[rows], nf[rows], ns[rows], RATE_SLABS)
        nmo[rows], nso[rows], nuo[rows], nco[rows] = m, sq, up, up.astype(BF)
    for q in range(KR // C):
        cols = slice(q * C, q * C + C)
        g = bfull[:, :, cols].reshape(SB, C).astype(F32)
        m, sq, up = adam_update(g, bm[:, cols], bf_[:, cols], bs[:, cols], RATE_SLABS)
        bmo[:, cols], bso[:, cols], buo[:, cols], bco[:, cols] = m, sq, up, up.astype(BF)
    tot = small[...]
    gains_g = pltpu.roll(tot[0:16], (NR - rw) * (C // NR), 1)[:12, : C // NR]
    q = rw * (FF // NR) // C
    off = rw * (FF // NR) % C
    pick = iota((4, C), 0) == q
    hid = jnp.concatenate(
        [jnp.sum(jnp.where(pick, tot[16 + 4 * k : 20 + 4 * k], 0.0), axis=0, keepdims=True) for k in range(3)]
        + [jnp.zeros((5, C), F32)],
        axis=0,
    )
    hidden_g = pltpu.roll(hid, C - off, 1)[:3, : FF // NR]
    gmo[...], gso[...], guo[...] = adam_update(gains_g, gm[...], gf[...], gs[...], RATE_GAINS)
    hmo[...], hso[...], huo[...] = adam_update(hidden_g, hm[...], hf[...], hs[...], RATE_GAINS)


def run_adam(NR, gfull, bfull, small, fout, igrad, *state):
    shape = lambda a, dt=F32: jax.ShapeDtypeStruct(a.shape, dt)
    nm, bm, gm, hm = state[0], state[3], state[6], state[9]
    out_shape = (shape(fout, BF), shape(igrad)) + tuple(shape(a) for a in (nm, bm, gm, hm) for _ in range(3))
    out_shape += (shape(nm, BF), shape(bm, BF))
    spec = pl.BlockSpec(memory_space=pltpu.VMEM)
    return pl.pallas_call(
        functools.partial(adam_kernel, NR),
        out_shape=out_shape,
        in_specs=[spec] * 17,
        out_specs=tuple([spec] * 16),
        compiler_params=pltpu.CompilerParams(vmem_limit_bytes=60 * 2**20),
    )(gfull, bfull, small, *state, fout, igrad)


def local(
    features, segment_ids, timesteps, cotangent, narrow_slab, broad_slab, model_gains, hidden_gains,
    narrow_first, narrow_second, broad_first, broad_second, gains_first, gains_second, hidden_first, hidden_second,
):
    steps = timesteps
    groups = lax.axis_size("rows")
    if groups == 8:
        fout, igrad, small, gfull, bfull = run_main(
            groups, features, segment_ids, steps, cotangent, narrow_slab, broad_slab, model_gains, hidden_gains
        )
        return tuple(
            run_adam(
                groups, gfull, bfull, small, fout, igrad,
                narrow_slab, narrow_first, narrow_second, broad_slab, broad_first, broad_second,
                model_gains, gains_first, gains_second, hidden_gains, hidden_first, hidden_second,
            )
        )
    narrow_w = lax.all_gather(narrow_slab.astype(BF), "rows", axis=0, tiled=True)
    broad_w = lax.all_gather(broad_slab.astype(BF), "rows", axis=0, tiled=True)
    gains_all = lax.all_gather(model_gains.astype(BF), "rows", axis=1, tiled=True).astype(F32)
    hidden_all = lax.all_gather(hidden_gains.astype(BF), "rows", axis=1, tiled=True).astype(F32)
    fout, igrad, small, ngrad, bgrad = run_main(
        0, features, segment_ids, steps, cotangent, narrow_w, broad_w, gains_all, hidden_all
    )
    scat = lambda v: lax.psum(lax.psum_scatter(v, "rows", scatter_dimension=0, tiled=True), "frames")
    narrow_g = scat(ngrad.astype(F32).reshape(KC, C))
    broad_g = scat(bgrad.astype(F32).reshape(C, KR))
    small = lax.psum(small, ("rows", "frames"))
    i = lax.axis_index("rows")
    own = lambda a, n: lax.dynamic_slice_in_dim(a, i * n, n, 1)
    gains_g = own(small[:12], model_gains.shape[1])
    hidden_g = own(small[16:28].reshape(3, FF), hidden_gains.shape[1])
    narrow_new = adam_update(narrow_g, narrow_slab, narrow_first, narrow_second, RATE_SLABS)
    broad_new = adam_update(broad_g, broad_slab, broad_first, broad_second, RATE_SLABS)
    gains_new = adam_update(gains_g, model_gains, gains_first, gains_second, RATE_GAINS)
    hidden_new = adam_update(hidden_g, hidden_gains, hidden_first, hidden_second, RATE_GAINS)
    return (
        fout, igrad, *narrow_new, *broad_new, *gains_new, *hidden_new,
        narrow_new[2].astype(BF), broad_new[2].astype(BF),
    )


def solution(mesh):
    rows = P("rows", None)
    cols = P(None, "rows")
    act = P("rows", "frames", None)
    return jax.shard_map(
        local,
        mesh=mesh,
        in_specs=(act, rows, rows, act, rows, rows, cols, cols, rows, rows, rows, rows, cols, cols, cols, cols),
        out_specs=(act, act, rows, rows, rows, rows, rows, rows, cols, cols, cols, cols, cols, cols, rows, rows),
        check_vma=False,
    )
```

```python
import functools
import math

import jax
import jax.numpy as jnp
from jax import lax
from jax.experimental import pallas as pl
from jax.experimental.pallas import tpu as pltpu
from jax.sharding import PartitionSpec as P

C = 256
TE = 1024
H = 2
HD = 64
FF = 1024
G = 8
NSEG = 8
STEP = 10
KC = 4352
KR = 1536
INNER = 128
EPS_NORM = 1e-05
EPS_ADAM = 1e-08
BETA_ONE = 0.9
BETA_TWO = 0.999
RATE_SLABS = 0.08
RATE_GAINS = 0.4
DECAY_RATE = 0.01
MASK_FILL = -1e30

F32 = jnp.float32
BF = jnp.bfloat16
MESH = pl.DeviceIdType.MESH
OFF = 32
GROUP = C // G


def dot(a, b):
    return jnp.dot(a, b, preferred_element_type=F32)


def dot_nt(a, b):
    return lax.dot_general(a, b, (((1,), (1,)), ((), ())), preferred_element_type=F32)


def dot_tn(a, b):
    return lax.dot_general(a, b, (((0,), (0,)), ((), ())), preferred_element_type=F32)


def recip(x):
    r = pltpu.reciprocal(x, approx=True)
    return r * (2.0 - x * r)


def split2(x):
    hi = x.astype(BF)
    lo = (x - hi.astype(F32)).astype(BF)
    return hi, lo


def split3(x):
    hi = x.astype(BF).astype(F32)
    mid = (x - hi).astype(BF).astype(F32)
    lo = (x - hi - mid).astype(BF).astype(F32)
    return hi, mid, lo


def mish_parts(y):
    e = jnp.exp(jnp.minimum(y, 30.0))
    n = e * (e + 2.0)
    rc = recip(n + 2.0)
    t = n * rc
    d = t + y * (2.0 * rc) * (1.0 + t) * (e * pltpu.reciprocal(1.0 + e, approx=True))
    return t, d


def reduced_angle(a):
    k = jnp.floor(a * (1.0 / math.pi) + 0.5)
    r = (a - k * 3.140625) - k * 9.67653589793e-4
    r2 = r * r
    s = r * (1.0 + r2 * (-1.0 / 6 + r2 * (1.0 / 120 + r2 * (-1.0 / 5040 + r2 * (1.0 / 362880)))))
    c = 1.0 + r2 * (
        -0.5 + r2 * (1.0 / 24 + r2 * (-1.0 / 720 + r2 * (1.0 / 40320 + r2 * (-1.0 / 3628800))))
    )
    return k, s, c


def sine_pair(x):
    t = x - jnp.floor(x + 0.5)
    t2 = t * t
    s = t * (3.141582022 + t2 * (-5.167142796 + t2 * (2.541899025 - t2 * 0.5546361918)))
    c = 1.9999999069 + t2 * (-9.869585718 + t2 * (8.116823828 + t2 * (-2.663760321 + t2 * 0.4393935944)))
    return s, c


def iota(shape, dim):
    return lax.broadcasted_iota(jnp.int32, shape, dim)


def group_sum_matrix(shift):
    return jnp.where(iota((C, 128), 0) // GROUP + shift == iota((C, 128), 1), 1.0, 0.0).astype(BF)


def group_spread_matrix():
    return jnp.where(iota((128, C), 0) == iota((128, C), 1) // GROUP, 1.0, 0.0).astype(BF)


def compact(sums, squares):
    n = sums.shape[0]
    a = jnp.concatenate(split3(sums), axis=0).astype(BF)
    b = jnp.concatenate(split3(squares), axis=0).astype(BF)
    both = dot(a, group_sum_matrix(0)) + dot(b, group_sum_matrix(G))
    return both[0:n] + both[n : 2 * n] + both[2 * n : 3 * n]


def expand(tables):
    n = tables[0].shape[0]
    stacked = jnp.concatenate([p for t in tables for p in split3(t)], axis=0).astype(BF)
    wide = dot(stacked, group_spread_matrix())
    part = lambda i: wide[n * i : n * i + n]
    return [part(3 * i) + part(3 * i + 1) + part(3 * i + 2) for i in range(len(tables))]


def table_of(columns):
    parts = split3(columns)
    zero = jnp.zeros((104, columns.shape[1]), F32)
    return jnp.concatenate(list(parts) + [zero], axis=0).astype(BF)


def segment_sums(onehot_rows, values):
    hi, lo = split2(values)
    return dot(onehot_rows, hi) + dot(onehot_rows, lo)


def layer_norm_parts(v):
    mu = jnp.mean(v, axis=-1, keepdims=True)
    cen = v - mu
    rs = lax.rsqrt(jnp.mean(cen * cen, axis=-1, keepdims=True) + EPS_NORM)
    return cen * rs, rs


def layer_norm_back(d, n, rs, gain):
    dg = d * gain
    return (dg - jnp.mean(dg, axis=-1, keepdims=True) - n * jnp.mean(dg * n, axis=-1, keepdims=True)) * rs


def colsum(x):
    return jnp.sum(x, axis=0, keepdims=True)


def main_kernel(
    NR,
    feat, ids, steps, cot, narrow_in, broad_in, gains_in, hidden_in,
    fout, igrad, small, out_n, out_b,
    narrow_s, broad_s, gains, hidden, smallw, packf, hgrad, hacc, ggrad,
    ngrad_s, bgrad_s, inh, inb, inq, inbq, got, bgot, gfull, bfull, s_pack, s_in, s_own, s_rows, s_all,
    uext, gyext, metab, ohrow, keymask, idp, counts, emb, tterm, sums, squares, tabs,
    zs, nrm1, der1, u2, nrm2, der2, resid, ll1, qs, kvall,
    statin, statout,
    kt, vt, qt, ffbuf, sbuf, ebuf, otb, invl, dos, dost,
    gf, nl2, shaped, ginner, r3s, r3b, gm, att, dq,
    part, rbuf, rbuf2, sumbuf, dqkv, g2, tg, edge,
    ga_s, ga_r, gx_s, gx_r, gc_s, gc_r,
    rc_s, rc_r, rx_s, rx_r, rd_s, rd_r, rf_s, rf_r, sa_s, sa_r, sb_s, sb_r, sc_s, sc_r,
    halo_s, halo_r, cot_s, cot_r, stat_s, stat_r, kv_s, kv_r, dkv_s, dkv_r, eg_s, eg_r, r3_s, r3_r,
):
    R, T = feat.shape[0], feat.shape[1]
    gr2, dn, g3 = igrad, resid, shaped
    TX = T + 2 * OFF
    L = ids.shape[1]
    HT = T // 2
    f = lax.axis_index("frames")
    rw = lax.axis_index("rows")
    sib = f + 1 - 2 * (f % 2)
    cross = (f + 2) % 4
    diag = 3 - f
    peers = (sib, cross, diag)

    gather = NR > 0
    ngrad, bgrad = (ngrad_s, bgrad_s) if gather else (out_n, out_b)
    broad = broad_s if gather else broad_in
    if gather:
        SH, SB = narrow_in.shape[0], broad_in.shape[0]
        NB = SH // 32
        narrow_s[pl.ds(rw * NB, NB)] = narrow_in[...].astype(BF).reshape(NB, 2, 16, C)
        broad[pl.ds(pl.multiple_of(rw * SB, 16), SB), :] = broad_in[...].astype(BF)
        packf[...] = jnp.zeros(packf.shape, F32)
        packf[0:12, 0 : C // NR] = gains_in[...]
        packf[12:15, :] = hidden_in[...]
        smallw[rw] = packf[...].astype(BF)
    else:
        gains[0:12, :] = gains_in[...]
        hidden[0:3, :] = hidden_in[...]

    def wn(first, n):
        if gather:
            return narrow_s[first // 32 : (first + n) // 32].reshape(n, C)
        return narrow_in[first : first + n, :]

    barrier = pltpu.get_barrier_semaphore()
    for p in peers:
        pl.semaphore_signal(barrier, inc=1, device_id=(rw, p), device_id_type=MESH)
    for k in range(1, NR):
        pl.semaphore_signal(barrier, inc=1, device_id=((rw + k) % NR, f), device_id_type=MESH)
    pl.semaphore_wait(barrier, 3 + max(NR - 1, 0))

    def remote(src, dst, ssem, rsem, target):
        return pltpu.make_async_remote_copy(
            src_ref=src, dst_ref=dst, send_sem=ssem, recv_sem=rsem,
            device_id=(rw, target), device_id_type=MESH,
        )

    if gather:
        gx, gc = f // 2, f % 2
        conv_blocks = 3 * C // 32
        own_blocks = {
            0: {0: (0, NB), 1: (NB, conv_blocks)},
            1: {s: (max(NB * s, conv_blocks), NB * (s + 1)) for s in (1, 2, 4, 5, 6)},
            4: {s: (NB * s, NB * (s + 1)) for s in (3, 7)},
        }
        ranges = {0: ((0, 24),), 1: ((24, 48), (72, 104)), 4: ((48, 72), (104, 136))}
        kinds = (0, 1, 2, 4)

        def narrow_piece(g, lo, hi):
            return narrow_s.at[lo:hi, g // 2, :, pl.ds(pl.multiple_of(g % 2 * 128, 128), 128)]

        def broad_piece(g, lo, hi):
            width = KR // 4
            return broad.at[lo:hi, pl.ds(pl.multiple_of(g * width, 128), width)]

        def to_row(ref, ssem, rsem, row):
            return pltpu.make_async_remote_copy(
                src_ref=ref, dst_ref=ref, send_sem=ssem, recv_sem=rsem, device_id=(row, f), device_id_type=MESH
            )

        def sized(kind, n):
            if kind == 2:
                return broad.at[0 : n * SB, 0 : KR // 4]
            if kind == 3:
                return smallw.at[0:n]
            return narrow_s.at[0:n, 0, :, 0:128]

        def waits(kind, n, sends, sem):
            ref = sized(kind, n)
            cp = remote(ref, ref, sem, sem, cross)
            (cp.wait_send if sends else cp.wait_recv)()

        def by_row(counts, act):
            for n in sorted(set(counts)):
                if n:
                    rows_of = [s for s in range(NR) if counts[s] == n]
                    cond = functools.reduce(jnp.logical_or, [rw == s for s in rows_of])

                    @pl.when(cond)
                    def _():
                        act(n)

        def spread_start(kind):
            if kind in own_blocks:
                for s, (lo, hi) in own_blocks[kind].items():

                    @pl.when(rw == s)
                    def _():
                        for k in range(1, NR):
                            to_row(narrow_piece(f, lo, hi), ga_s.at[kind], ga_r.at[kind], (s + k) % NR).start()

                return
            for k in range(1, NR):
                if kind == 2:
                    at = pl.ds(pl.multiple_of(rw * SB, 16), SB)
                    ref = broad.at[at, pl.ds(pl.multiple_of(f * (KR // 4), 128), KR // 4)]
                else:
                    ref = smallw.at[rw]
                to_row(ref, ga_s.at[kind], ga_r.at[kind], (rw + k) % NR).start()

        def held(kind):
            sizes = [0] * NR
            for s, (lo, hi) in own_blocks[kind].items():
                sizes[s] = hi - lo
            return sizes

        def spread_arrive(kind):
            if kind in own_blocks:
                sizes = held(kind)
                by_row([sum(sizes) - n for n in sizes], lambda n: waits(kind, n, False, ga_r.at[kind]))
            else:
                waits(kind, NR - 1, False, ga_r.at[kind])

        def spread_end(kind):
            if kind in own_blocks:
                by_row([(NR - 1) * n for n in held(kind)], lambda n: waits(kind, n, True, ga_s.at[kind]))
            else:
                waits(kind, NR - 1, True, ga_s.at[kind])

        def pieces(kind, g):
            if kind == 2:
                return [broad_piece(g, 0, C)]
            return [narrow_piece(g, lo, hi) for lo, hi in ranges[kind]]

        def units(kind):
            return NR if kind == 2 else sum(hi - lo for lo, hi in ranges[kind])

        def pass_on(kind):
            spread_arrive(kind)
            for ref in pieces(kind, f):
                remote(ref, ref, gx_s.at[kind], gx_r.at[kind], cross).start()
            for ref in pieces(kind, f):
                remote(ref, ref, gc_s.at[kind, 0], gc_r.at[kind, 0], sib).start()

        def pass_across(kind):
            waits(kind, units(kind), False, gx_r.at[kind])
            for ref in pieces(kind, cross):
                remote(ref, ref, gc_s.at[kind, 1], gc_r.at[kind, 1], sib).start()

        def arrive(kind):
            for i in range(2):
                waits(kind, units(kind), False, gc_r.at[kind, i])

        def gather_end():
            for kind in kinds:
                spread_end(kind)
                waits(kind, units(kind), True, gx_s.at[kind])
                for i in range(2):
                    waits(kind, units(kind), True, gc_s.at[kind, i])
            spread_end(3)

        spread_start(3)
        spread_start(0)

    def to_next(src, dst, ssem, rsem):
        return remote(src, dst, ssem, rsem, (f + 1) % 4)

    def to_prev(src, dst, ssem, rsem):
        return remote(src, dst, ssem, rsem, (f + 3) % 4)

    feat_down = to_next(feat.at[:, pl.ds(T - 16, 16)], uext.at[:, pl.ds(OFF - 16, 16)], halo_s.at[0], halo_r.at[0])
    feat_up = to_prev(feat.at[:, pl.ds(0, 16)], uext.at[:, pl.ds(OFF + T, 16)], halo_s.at[1], halo_r.at[1])
    cot_up = to_prev(cot.at[:, pl.ds(0, 16)], gyext.at[:, pl.ds(HT, 16)], cot_s.at[0], cot_r.at[0])

    @pl.when(f < 3)
    def _():
        feat_down.start()

    @pl.when(f > 0)
    def _():
        feat_up.start()
        cot_up.start()

    uext[:, 0 : OFF - 16, :] = jnp.zeros((R, OFF - 16, C), BF)
    uext[:, OFF + T + 16 :, :] = jnp.zeros((R, TX - OFF - T - 16, C), BF)
    g2[:, 0 : OFF - 16, :] = jnp.zeros((R, OFF - 16, C), BF)
    g2[:, OFF + T + 16 :, :] = jnp.zeros((R, TX - OFF - T - 16, C), BF)

    @pl.when(f == 0)
    def _():
        edge[:, 0] = jnp.zeros((3, R, 8, C), F32)
        uext[:, OFF - 16 : OFF, :] = jnp.zeros((R, 16, C), BF)

    @pl.when(f == 3)
    def _():
        edge[:, 1] = jnp.zeros((3, R, 8, C), F32)
        uext[:, OFF + T : OFF + T + 16, :] = jnp.zeros((R, 16, C), BF)
        gyext[:, HT : HT + 16, :] = jnp.zeros((R, 16, C), BF)

    ggrad[...] = jnp.zeros(ggrad.shape, F32)
    hgrad[...] = jnp.zeros(hgrad.shape, F32)

    idp[...] = jnp.full(idp.shape, -1.0, F32)
    idp[0:R, 128 : 128 + L] = ids[...].astype(F32)
    idv = idp[0:8]
    width = idv.shape[1]
    prev_row = jnp.where(pltpu.roll(idv, 1, 1) == idv, 1.0, 0.0)
    next_row = jnp.where(pltpu.roll(idv, width - 1, 1) == idv, 1.0, 0.0)
    idp[8:16, :] = prev_row
    idp[16:24, :] = next_row
    base = pl.multiple_of(f * T, 128)
    WX = T + 256
    win = idp[:, pl.ds(base, WX)]
    win = pltpu.roll(win, WX - (128 - OFF), 1)[:, : T + 128]
    own = idp[:, pl.ds(pl.multiple_of(base + 128, 128), T)]
    for r in range(R):
        n_lane = T + 128
        row_id = jnp.broadcast_to(win[r : r + 1], (8, n_lane))
        lab = iota((8, n_lane), 0).astype(F32)
        oh = jnp.where(row_id == lab, 1.0, 0.0)
        pn = jnp.where(
            lab == 0.0,
            jnp.broadcast_to(win[8 + r : 9 + r], (8, n_lane)),
            jnp.where(lab == 1.0, jnp.broadcast_to(win[16 + r : 17 + r], (8, n_lane)), 0.0),
        )
        block = jnp.concatenate([oh, oh, oh, pn, jnp.zeros((96, n_lane), F32)], axis=0)
        turned = block.T
        metab[r] = turned[:TX].astype(BF)
        lab_own = iota((8, T), 0).astype(F32)
        ohrow[r] = jnp.where(jnp.broadcast_to(own[r : r + 1], (8, T)) == lab_own, 1.0, 0.0)
        full = jnp.broadcast_to(idv[r : r + 1, 128 : 128 + L], (8, L))
        lab_full = iota((8, L), 0).astype(F32)
        ohf = jnp.where(full == lab_full, 1.0, 0.0)
        counts[8 * r : 8 * r + 8] = jnp.broadcast_to(jnp.sum(ohf, axis=1, keepdims=True) * float(GROUP), (8, 128))
        km = jnp.concatenate([(1.0 - ohf) * MASK_FILL, jnp.zeros((120, L), F32)], axis=0)
        keymask[r] = km.T.astype(BF)

    uext[:, OFF : OFF + T, :] = feat[...]
    gyext[:, 0:HT, :] = cot[...]

    half = TE // 2
    freq = jnp.exp(iota((8, half), 1).astype(F32) * (-math.log(10000.0) / half))
    for r in range(R):
        turn = jnp.broadcast_to(steps[r : r + 1, :].astype(F32), (8, NSEG))
        ang = jnp.sum(jnp.where(iota((8, NSEG), 0) == iota((8, NSEG), 1), turn, 0.0), axis=1, keepdims=True) * freq
        k, s, c = reduced_angle(ang)
        sign = 1.0 - 2.0 * (k - 2.0 * jnp.floor(k * 0.5))
        both = jnp.concatenate([s * sign, c * sign], axis=1)
        emb[8 * r : 8 * r + 8, :] = both * mish_parts(both)[0]
    tw = 9 * C

    if gather:
        spread_start(1)
        spread_start(2)
        pass_on(0)
        spread_start(4)
        spread_arrive(3)
        wide = smallw[...].astype(F32)
        gains[...] = jnp.concatenate([wide[s, :, 0 : C // NR] for s in range(NR)], axis=1)
        hidden[0:3, :] = jnp.concatenate([wide[s, 12:15, :] for s in range(NR)], axis=1)
        pass_across(0)
        arrive(0)

    def own_prev(r):
        return metab[r, OFF : OFF + T, 24:25].astype(F32)

    def own_next(r):
        return metab[r, OFF : OFF + T, 25:26].astype(F32)

    def edge_copies(which, src):
        return (
            to_next(src.at[:, pl.ds(T - 8, 8)], edge.at[which, 0], eg_s.at[which, 0], eg_r.at[which, 0]),
            to_prev(src.at[:, pl.ds(0, 8)], edge.at[which, 1], eg_s.at[which, 1], eg_r.at[which, 1]),
        )

    def send_edges(which, src):
        down_cp, up_cp = edge_copies(which, src)

        @pl.when(f < 3)
        def _():
            down_cp.start()

        @pl.when(f > 0)
        def _():
            up_cp.start()

    def await_edges(which, src):
        down_cp, up_cp = edge_copies(which, src)

        @pl.when(f < 3)
        def _():
            down_cp.wait_send()
            up_cp.wait_recv()

        @pl.when(f > 0)
        def _():
            up_cp.wait_send()
            down_cp.wait_recv()

    def stat_copies(phase):
        return [
            remote(statout.at[phase], statin.at[phase, i], stat_s.at[phase], stat_r.at[phase, i], peers[i])
            for i in range(3)
        ]

    def keep_sums(r, first, second):
        oh = ohrow[r].astype(BF)
        at = pl.ds(pl.multiple_of(8 * r, 8), 8)
        sums[at] = segment_sums(oh, first)
        squares[at] = segment_sums(oh, second)

    def send_stats(phase):
        statout[phase] = compact(sums[...], squares[...])
        for cp in stat_copies(phase):
            cp.start()

    def total_stats(phase, wait=True):
        if wait:
            for cp in stat_copies(phase):
                cp.wait_recv()
            remote(statin.at[phase], statin.at[phase], stat_s.at[phase], stat_s.at[phase], sib).wait_send()
        return (statout[phase] + statin[phase, 0] + statin[phase, 1] + statin[phase, 2]) / jnp.maximum(counts[...], 1.0)

    group_lanes = iota((8 * R, 128), 1) < G

    def norm_scale(tot):
        second = pltpu.roll(tot, 128 - G, 1)
        return jnp.where(group_lanes, lax.rsqrt(jnp.maximum(second - tot * tot, 0.0) + EPS_NORM), 0.0)

    def norm_tables(phase):
        tot = total_stats(phase)
        inv = norm_scale(tot)
        tabs[:, 0:C], tabs[:, C : 2 * C] = expand([tot * inv, inv])

    def row_table(r, width):
        return table_of(tabs[pl.ds(pl.multiple_of(8 * r, 8), 8), 0:width])

    def conv_into(r, src, first_row):
        for j in range(3):
            zs[j] = dot(src[r], wn(first_row + j * C, C))

    @pl.when(f > 0)
    def _():
        feat_down.wait_recv()

    @pl.when(f < 3)
    def _():
        feat_up.wait_recv()

    def phase_one(r):
        conv_into(r, uext, 0)
        lo, hi = OFF - 16, OFF + T + 16
        n = hi - lo
        v = (
            zs[0, lo - 1 : hi - 1] * metab[r, lo:hi, 24:25].astype(F32)
            + zs[1, lo:hi]
            + zs[2, lo + 1 : hi + 1] * metab[r, lo:hi, 25:26].astype(F32)
        )
        nrm1[r, lo:hi] = v
        nrm1[r, 0:lo] = jnp.zeros((lo, C), F32)
        nrm1[r, hi:] = jnp.zeros((TX - hi, C), F32)
        vo = v[OFF - lo : OFF - lo + T]
        keep_sums(r, vo, vo * vo)

    for r in range(R):
        phase_one(r)
        if r == R - 1:
            send_stats(0)
        if gather:
            if r == 0:
                pass_on(1)
            elif r == 1:
                pass_on(2)
                pass_across(1)

    if gather:
        arrive(1)
    tterm[...] = dot(emb[...].astype(BF), wn(tw, TE)) + gains[2:3, :]

    CH = TX // 4
    tabs[:, 2 * C : 3 * C] = tterm[...]
    norm_tables(0)

    def phase_two(r, carry):
        tab = row_table(r, 3 * C)

        def chunk(i, c2):
            rows = pl.ds(pl.multiple_of(i * CH, 16), CH)
            sp = dot(metab[r, rows], tab)
            n = nrm1[r, rows] * sp[:, C : 2 * C] - sp[:, :C]
            y = n * gains[0:1, :] + gains[1:2, :]
            t, d = mish_parts(y)
            nrm1[r, rows] = n
            der1[r, rows] = d.astype(BF)
            u2[r, rows] = (y * t + sp[:, 2 * C :]).astype(BF)
            return c2

        lax.fori_loop(0, 4, chunk, 0)
        conv_into(r, u2, 3 * C)
        v = (
            zs[0, OFF - 1 : OFF + T - 1] * own_prev(r)
            + zs[1, OFF : OFF + T]
            + zs[2, OFF + 1 : OFF + T + 1] * own_next(r)
        )
        nrm2[r] = v
        keep_sums(r, v, v * v)
        return carry

    lax.fori_loop(0, R, phase_two, 0)
    send_stats(1)
    if gather:
        pass_across(2)
        pass_on(4)
        arrive(2)
    norm_tables(1)

    def kv_copies(r):
        slot = lambda g: kvall.at[r, :, pl.ds(pl.multiple_of(g * T, 128), T)]
        mine, other = slot(f), slot(cross)
        return (
            remote(mine, mine, kv_s.at[0, r], kv_r.at[0, r], sib),
            remote(mine, mine, kv_s.at[1, r], kv_r.at[1, r], cross),
            remote(other, other, kv_s.at[2, r], kv_r.at[2, r], sib),
        )

    NCH = 4
    CT = T // NCH

    def phase_three(r, carry):
        tab = row_table(r, 2 * C)

        def chunk(i, c2):
            rows = pl.ds(pl.multiple_of(i * CT, 16), CT)
            xrows = pl.ds(pl.multiple_of(OFF + i * CT, 16), CT)
            sp = dot(metab[r, xrows], tab)
            n = nrm2[r, rows] * sp[:, C : 2 * C] - sp[:, :C]
            y = n * gains[3:4, :] + gains[4:5, :]
            t, d = mish_parts(y)
            nrm2[r, rows] = n
            der2[r, rows] = d.astype(BF)
            res = y * t + feat[r, rows].astype(F32)
            resid[r, rows] = res
            m, rs = layer_norm_parts(res)
            low = (m * gains[5:6, :] + gains[6:7, :]).astype(BF)
            ll1[r, rows] = low
            qkv = dot(low, broad[:, : 3 * INNER])
            qs[r, rows] = (qkv[:, :INNER].astype(BF).astype(F32) * HD ** (-0.5)).astype(BF)
            krows = pl.ds(pl.multiple_of(f * T + i * CT, 16), CT)
            kvall[r, 0, krows] = qkv[:, INNER : 2 * INNER].astype(BF)
            kvall[r, 1, krows] = qkv[:, 2 * INNER :].astype(BF)
            return c2

        lax.fori_loop(0, NCH, chunk, 0)
        if gather:

            @pl.when(r == 0)
            def _():
                pass_across(4)

        cps = kv_copies(r)
        cps[1].start()
        cps[0].start()
        return carry

    lax.fori_loop(0, R, phase_three, 0)
    send_edges(2, nrm2)

    @pl.when(f < 3)
    def _():
        cot_up.wait_recv()

    down = 6 * C

    def phase_down_back(r, carry):
        gy = gyext[r, 0:HT]
        even = dot_nt(gy, wn(down + C, C))
        own_gy = dot_nt(gy, wn(down + 2 * C, C))
        nxt = dot_nt(gyext[r], wn(down, C))
        zs[0, 0 : HT + 16] = nxt
        for hh in range(2):
            cols = slice(hh * 128, hh * 128 + 128)
            pm = r3s[2, pl.ds(8 + 1, HT, stride=2), :]
            nm = r3s[3, pl.ds(8 + 1, HT, stride=2), :]
            r3s[hh, pl.ds(8, HT, stride=2), :] = even[:, cols]
            r3s[hh, pl.ds(9, HT, stride=2), :] = own_gy[:, cols] * pm + zs[0, 1 : HT + 1, cols] * nm
        return carry

    def masks_strided(r):
        r3s[2, 8 : 8 + T] = jnp.broadcast_to(own_prev(r), (T, 128))
        r3s[3, 8 : 8 + T] = jnp.broadcast_to(own_next(r), (T, 128))

    def down_back(r, carry):
        masks_strided(r)
        phase_down_back(r, carry)
        ggrad[11:12, :] += colsum(gyext[r, 0:HT].astype(F32))
        for hh in range(2):
            gf[r, :, hh * 128 : hh * 128 + 128] = r3s[hh, 8 : 8 + T].astype(BF)
        ggrad[10:11, :] += colsum(gf[r].astype(F32))
        return carry

    if gather:
        arrive(4)
    lax.fori_loop(0, R, down_back, 0)

    def relay(r):
        cps = kv_copies(r)
        cps[1].wait_recv()
        cps[2].start()

    relay(0)
    if gather:
        gather_end()

    alpha = jnp.exp(hidden[1:2, :])
    inv_beta = jnp.exp(-hidden[2:3, :])
    alpha_beta = alpha * inv_beta
    alpha_pi = alpha * (1.0 / math.pi)
    NK = L // 256
    CF = T // 2
    hacc[...] = jnp.zeros(hacc.shape, F32)
    lane128 = iota((T, 128), 1)

    def dkv_copies(r):
        return (
            remote(part.at[r, sib], rbuf.at[r, 0], dkv_s.at[0, r], dkv_r.at[0, r], sib),
            remote(part.at[r, diag], rbuf.at[r, 1], dkv_s.at[1, r], dkv_r.at[1, r], sib),
            remote(sumbuf.at[r], rbuf2.at[r], dkv_s.at[2, r], dkv_r.at[2, r], cross),
        )

    def phase_sum(r):
        cps = dkv_copies(r)
        cps[1].wait_recv()
        sumbuf[r] = (part[r, cross].astype(F32) + rbuf[r, 1].astype(F32)).astype(BF)
        cps[2].start()

    def phase_four(r, carry):
        cps = kv_copies(r)
        cps[0].wait_recv()
        cps[2].wait_recv()
        for cp in cps:
            cp.wait_send()
        kt[...] = kvall[r, 0].T
        vt[...] = kvall[r, 1].T
        qv = qs[r]
        ohq = jnp.where(lane128 < 8, metab[r, OFF : OFF + T], jnp.zeros((T, 128), BF))
        zero_q = jnp.zeros((T, 128), BF)
        q_heads = [jnp.where(lane128 // HD == h, qv, zero_q) for h in range(H)]
        TQ = T // 2
        units = [(h, q) for h in range(H) for q in range(2)]

        def scores(n):
            h, q = units[n]
            qrows = slice(q * TQ, q * TQ + TQ)
            qa = jnp.concatenate([q_heads[h][qrows], ohq[qrows]], axis=1)
            m8 = jnp.full((8, TQ), -3e38, F32)
            for i in range(NK):
                keys = slice(i * 256, i * 256 + 256)
                ka = jnp.concatenate([kvall[r, 0, keys], keymask[r, keys]], axis=1)
                sc = dot_nt(ka, qa)
                sbuf[n % 2, keys] = sc
                m8 = jnp.maximum(m8, jnp.max(sc.reshape(32, 8, TQ), axis=0))
            return jnp.max(m8, axis=0, keepdims=True)

        top = scores(0)
        for n, (h, q) in enumerate(units):
            later = scores(n + 1) if n + 1 < len(units) else None
            qcols = slice(q * TQ, q * TQ + TQ)
            l8 = jnp.zeros((8, TQ), F32)
            for i in range(NK):
                keys = slice(i * 256, i * 256 + 256)
                e = jnp.exp(sbuf[n % 2, keys] - top)
                ebuf[h, keys, qcols] = e.astype(BF)
                l8 = l8 + jnp.sum(e.reshape(32, 8, TQ), axis=0)
            inv = 1.0 / jnp.sum(l8, axis=0, keepdims=True)
            invl[h, :, qcols] = jnp.broadcast_to(inv, (8, TQ))
            hrows = slice(h * HD, (h + 1) * HD)
            otb[hrows, qcols] = dot(vt[hrows, :], ebuf[h, :, qcols]) * inv
            top = later
        att[r] = otb[...].T.astype(BF)

        @pl.when(r + 1 < R)
        def _():
            relay(r + 1)

        def ff_chunk(i, c2):
            rows = pl.ds(pl.multiple_of(i * CF, 16), CF)
            res2 = resid[r, rows] + (dot_nt(att[r, rows], broad[:, 3 * INNER : 4 * INNER]) + gains[7:8, :])
            n, rs = layer_norm_parts(res2)
            low = (n * gains[8:9, :] + gains[9:10, :]).astype(BF)
            nl2[r, rows] = low
            gfr = gf[r, rows]
            def products(b):
                w_in = broad[:, 4 * INNER + b * 256 : 4 * INNER + b * 256 + 256]
                w_out = wn(tw + TE + b * 256, 256)
                ffbuf[b % 2, 0] = dot(low, w_in)
                ffbuf[b % 2, 1] = dot_nt(gfr, w_out)
                return w_in, w_out

            out, back = None, None
            weights = products(0)
            for b in range(4):
                following = products(b + 1) if b < 3 else None
                cols = slice(b * 256, b * 256 + 256)
                acc = [hacc[k, :, cols] for k in range(3)]
                shs, gis = [], []
                for u in range(0, CF, 32):
                    inner = ffbuf[b % 2, 0, u : u + 32] + hidden[0:1, cols]
                    gs = ffbuf[b % 2, 1, u : u + 32]
                    s, c = sine_pair(inner * alpha_pi[:, cols])
                    s2 = s * s
                    part_g = gs * (s * c)
                    shs.append((inner + s2 * inv_beta[:, cols]).astype(BF))
                    gi = gs + part_g * alpha_beta[:, cols]
                    gis.append(gi.astype(BF))
                    for k, v in enumerate((gi, part_g * inner, gs * s2)):
                        acc[k] = acc[k] + jnp.sum(v.reshape(4, 8, 256), axis=0)
                for k in range(3):
                    hacc[k, :, cols] = acc[k]
                sh_all, gi_all = jnp.concatenate(shs, axis=0), jnp.concatenate(gis, axis=0)
                shaped[r, rows, cols] = sh_all
                ginner[r, rows, cols] = gi_all
                more, more_back = dot(sh_all, weights[1]), dot_nt(gi_all, weights[0])
                out = more if out is None else out + more
                back = more_back if back is None else back + more_back
                weights = following
            r3 = (res2 + (out + gains[10:11, :])).astype(BF)
            r3b[r, rows] = r3
            g_in = gfr.astype(F32)
            ggrad[8:9, :] += colsum(back * n)
            ggrad[9:10, :] += colsum(back)
            g_res2 = g_in + layer_norm_back(back, n, rs, gains[8:9, :])
            gr2[r, rows] = g_res2
            low_g = g_res2.astype(BF)
            gm[r, rows] = low_g
            ggrad[7:8, :] += colsum(low_g.astype(F32))
            dos[rows] = dot(low_g, broad[:, 3 * INNER : 4 * INNER]).astype(BF).astype(F32)
            return c2

        lax.fori_loop(0, T // CF, ff_chunk, 0)

        @pl.when(f < 3)
        def _():
            to_next(r3b.at[r, pl.ds(T - 16, 16)], r3b.at[r, pl.ds(T, 16)], r3_s.at[r], r3_r.at[r]).start()

        dot_t = dos[...].T
        for h in range(H):
            hrows = slice(h * HD, (h + 1) * HD)
            dost[hrows, :] = dot_t[hrows] * invl[h, 0:1, :]
        zero_t = jnp.zeros((HD, T), BF)
        d_rows, d_cols, d_half = [], [], []
        per_block = T // 256
        for h in range(H):
            hrows = slice(h * HD, (h + 1) * HD)
            d_rows.append(colsum(otb[hrows, :] * dost[hrows, :]))
            dh = dost[hrows, :].astype(BF)
            d_half.append(dh)
            d_cols.append(jnp.concatenate([dh, zero_t] if h == 0 else [zero_t, dh], axis=0))
        qt[...] = qs[r].T
        cps = dkv_copies(r)
        for n, block in enumerate((diag, sib, cross, f)):
            for i in range(per_block):
                keys = pl.ds(pl.multiple_of(block * T + i * 256, 256), 256)
                within = slice(i * 256, i * 256 + 256)
                for h in range(H):
                    hrows = slice(h * HD, (h + 1) * HD)
                    eh = ebuf[h, keys]
                    dp = dot(kvall[r, 1, keys], d_cols[h])
                    ds = (eh.astype(F32) * (dp - d_rows[h])).astype(BF)
                    part[r, block, 0, hrows, within] = dot_nt(qt[hrows, :], ds).astype(BF)
                    part[r, block, 1, hrows, within] = dot_nt(d_half[h], eh).astype(BF)
                    if n == 0 and i == 0:
                        dq[hrows, :] = dot(kt[hrows, keys], ds)
                    else:
                        dq[hrows, :] += dot(kt[hrows, keys], ds)
            if n == 0:
                cps[1].start()
            elif n == 1:
                cps[0].start()
            elif n == 2:
                phase_sum(r)
        dqkv[r, :, 0:INNER] = (dq[...].T * HD ** (-0.5)).astype(BF)
        return carry

    lax.fori_loop(0, R, phase_four, 0)

    if gather:
        rx, rc = f // 2, f % 2
        shard_blocks = NB
        n_groups = {1: ((48, 72), (104, 136)), 2: ((24, 48), (72, 104)), 3: ((0, 24),)}
        b_groups = {1: (4 * INNER, 2 * C), 2: (0, C)}
        b_at = {1: C, 2: 0}

        def half_cols(core, first, n):
            return pl.ds(pl.multiple_of(first + core * n, 128), n)

        def core_copies(g):
            out = [
                remote(ngrad.at[lo:hi, :, :, half_cols(1 - rc, 0, 128)], inh.at[lo:hi], rc_s.at[g - 1, i], rc_r.at[g - 1, i], sib)
                for i, (lo, hi) in enumerate(n_groups[g])
            ]
            if g in b_groups:
                first, n = b_groups[g]
                out.append(
                    remote(
                        bgrad.at[:, :, :, half_cols(1 - rc, first, n)], inb.at[:, :, :, b_at[g] : b_at[g] + n],
                        rc_s.at[g - 1, 2], rc_r.at[g - 1, 2], sib,
                    )
                )
            return out

        def cross_copies(g):
            out = [
                remote(ngrad.at[lo:hi, 1 - rx, :, half_cols(rc, 0, 128)], inq.at[lo:hi], rx_s.at[g - 1, i], rx_r.at[g - 1, i], cross)
                for i, (lo, hi) in enumerate(n_groups[g])
            ]
            if g in b_groups:
                first, n = b_groups[g]
                out.append(
                    remote(
                        bgrad.at[:, 1 - rx, :, half_cols(rc, first, n)], inbq.at[:, :, b_at[g] : b_at[g] + n],
                        rx_s.at[g - 1, 2], rx_r.at[g - 1, 2], cross,
                    )
                )
            return out

        def owner_copies(g, s, source):
            out = []
            for i, (lo, hi) in enumerate(n_groups[g]):
                a, b = max(lo, shard_blocks * s), min(hi, shard_blocks * (s + 1))
                if a < b:
                    out.append(
                        pltpu.make_async_remote_copy(
                            src_ref=ngrad.at[a:b, rx, :, half_cols(rc, 0, 128)],
                            dst_ref=got.at[source, a - shard_blocks * s : b - shard_blocks * s],
                            send_sem=rd_s.at[g - 1, 0], recv_sem=rd_r.at[g - 1, 0],
                            device_id=(s, f), device_id_type=MESH,
                        )
                    )
            if g in b_groups:
                first, n = b_groups[g]
                out.append(
                    pltpu.make_async_remote_copy(
                        src_ref=bgrad.at[s, rx, :, half_cols(rc, first, n)],
                        dst_ref=bgot.at[source, :, b_at[g] : b_at[g] + n],
                        send_sem=rd_s.at[g - 1, 1], recv_sem=rd_r.at[g - 1, 1],
                        device_id=(s, f), device_id_type=MESH,
                    )
                )
            return out

        def red_core(g):
            for cp in core_copies(g):
                cp.start()

        def red_cross(g):
            for cp in core_copies(g):
                cp.wait()
            mine = half_cols(rc, 0, 128)
            for lo, hi in n_groups[g]:
                ngrad[lo:hi, :, :, mine] = (ngrad[lo:hi, :, :, mine].astype(F32) + inh[lo:hi].astype(F32)).astype(BF)
            if g in b_groups:
                first, n = b_groups[g]
                cols = half_cols(rc, first, n)
                other = inb[:, :, :, b_at[g] : b_at[g] + n]
                bgrad[:, :, :, cols] = (bgrad[:, :, :, cols].astype(F32) + other.astype(F32)).astype(BF)
            for cp in cross_copies(g):
                cp.start()

        def red_owner(g):
            for cp in cross_copies(g):
                cp.wait()
            mine = half_cols(rc, 0, 128)
            for lo, hi in n_groups[g]:
                ngrad[lo:hi, rx, :, mine] = (ngrad[lo:hi, rx, :, mine].astype(F32) + inq[lo:hi].astype(F32)).astype(BF)
            if g in b_groups:
                first, n = b_groups[g]
                cols = half_cols(rc, first, n)
                other = inbq[:, :, b_at[g] : b_at[g] + n]
                bgrad[:, rx, :, cols] = (bgrad[:, rx, :, cols].astype(F32) + other.astype(F32)).astype(BF)
            for s in range(NR):

                @pl.when(rw != s)
                def _():
                    for cp in owner_copies(g, s, rw):
                        cp.start()

        def red_wait(g):
            overlap = [
                sum(max(0, min(hi, NB * (s + 1)) - max(lo, NB * s)) for lo, hi in n_groups[g]) for s in range(NR)
            ]

            def take(n, sends, sem):
                cp = remote(inq.at[0:n], inq.at[0:n], sem, sem, cross)
                (cp.wait_send if sends else cp.wait_recv)()

            by_row([sum(overlap) - n for n in overlap], lambda n: take(n, True, rd_s.at[g - 1, 0]))
            by_row([(NR - 1) * n for n in overlap], lambda n: take(n, False, rd_r.at[g - 1, 0]))
            if g in b_groups:
                ref = bgot.at[0 : NR - 1, :, b_at[g] : b_at[g] + b_groups[g][1]]
                cp = remote(ref, ref, rd_s.at[g - 1, 1], rd_r.at[g - 1, 1], cross)
                cp.wait_send()
                cp.wait_recv()

        def red_finish():
            mine = half_cols(rc, 0, 128)
            total = ngrad[pl.ds(shard_blocks * rw, shard_blocks), rx, :, mine].astype(F32)
            totals = [bgrad[rw, rx, :, half_cols(rc, *b_groups[g])].astype(F32) for g in (1, 2)]
            for k in range(1, NR):
                o = (rw + k) % NR
                total = total + got[o].astype(F32)
                for j, g in enumerate((1, 2)):
                    totals[j] = totals[j] + bgot[o, :, b_at[g] : b_at[g] + b_groups[g][1]].astype(F32)
            gfull[:, rx, :, mine] = total.astype(BF)
            fin = []
            blocks = [gfull.at[:, rx, :, mine]]
            for j, g in enumerate((1, 2)):
                cols = half_cols(rc, *b_groups[g])
                bfull[rx, :, cols] = totals[j].astype(BF)
                blocks.append(bfull.at[rx, :, cols])
            for j, blk in enumerate(blocks):
                for p in peers:
                    remote(blk, blk, rf_s.at[j], rf_r.at[j], p).start()
                fin.append((rf_s.at[j], rf_r.at[j]))
            sizes = [inq.at[0 : 3 * NB]] + [bgot.at[0:3, :, b_at[g] : b_at[g] + b_groups[g][1]] for g in (1, 2)]
            return [remote(ref, ref, ss, rs, cross) for ref, (ss, rs) in zip(sizes, fin)]

        def small_first():
            s_pack[...] = small_rows()
            for i, p in enumerate(peers):
                remote(s_pack.at[pl.ds(pl.multiple_of(8 * p, 8), 8)], s_in.at[i], sa_s.at[0], sa_r.at[0], p).start()

        def small_second():
            remote(s_in, s_in, sa_s.at[0], sa_r.at[0], sib).wait()
            s_own[...] = s_pack[pl.ds(pl.multiple_of(8 * f, 8), 8)] + s_in[0] + s_in[1] + s_in[2]
            for k in range(1, NR):
                pltpu.make_async_remote_copy(
                    src_ref=s_own, dst_ref=s_rows.at[k - 1], send_sem=sb_s.at[0], recv_sem=sb_r.at[0],
                    device_id=((rw + k) % NR, f), device_id_type=MESH,
                ).start()

        def small_third():
            ref = s_rows.at[0 : NR - 1]
            remote(ref, ref, sb_s.at[0], sb_r.at[0], sib).wait()
            at = pl.ds(pl.multiple_of(8 * f, 8), 8)
            tot = s_own[...]
            for k in range(1, NR):
                tot = tot + s_rows[k - 1]
            s_all[at] = tot
            for p in peers:
                remote(s_all.at[at], s_all.at[at], sc_s.at[0], sc_r.at[0], p).start()

        def small_last():
            remote(s_in, s_in, sc_s.at[0], sc_r.at[0], sib).wait()

    def small_rows():
        hid = [hgrad[k : k + 1, q * C : (q + 1) * C] for k in range(3) for q in range(FF // C)]
        return jnp.concatenate([ggrad[...]] + hid + [jnp.zeros((4, C), F32)], axis=0)

    flat = lambda ref: ref[...].reshape(R * T, ref.shape[2])

    def put_n(first, value):
        n = value.shape[0]
        ngrad[first // 32 : (first + n) // 32] = value.astype(BF).reshape(n // 32, 2, 16, C)

    def put_b(first, value):
        bgrad[:, :, :, first : first + value.shape[1]] = value.astype(BF).reshape(C // 32, 2, 16, value.shape[1])

    zs[:, 0:C, :] = jnp.zeros((3, C, C), F32)

    def down_forward(r, carry):
        @pl.when(f > 0)
        def _():
            to_next(r3b.at[r, pl.ds(T - 16, 16)], r3b.at[r, pl.ds(T, 16)], r3_s.at[r], r3_r.at[r]).wait_recv()

        @pl.when(f < 3)
        def _():
            to_next(r3b.at[r, pl.ds(T - 16, 16)], r3b.at[r, pl.ds(T, 16)], r3_s.at[r], r3_r.at[r]).wait_send()

        @pl.when(f == 0)
        def _():
            r3b[r, T : T + 16, :] = jnp.zeros((16, C), BF)

        masks_strided(r)
        for hh in range(2):
            cols = slice(hh * 128, hh * 128 + 128)
            r3s[hh, 8 : 8 + T] = r3b[r, 0:T, cols].astype(F32)
            r3s[hh, 0:8] = r3b[r, T : T + 16, cols].astype(F32)[8:16]
        even = jnp.concatenate([r3s[hh, pl.ds(8, HT, stride=2), :] for hh in range(2)], axis=1).astype(BF)
        m_after = r3s[3, pl.ds(8, HT, stride=2), :]
        m_before = r3s[2, pl.ds(8, HT, stride=2), :]
        odd = jnp.concatenate([r3s[hh, pl.ds(9, HT, stride=2), :] * m_after for hh in range(2)], axis=1).astype(BF)
        before = jnp.concatenate([r3s[hh, pl.ds(7, HT, stride=2), :] * m_before for hh in range(2)], axis=1).astype(BF)
        gy = cot[r]
        out = gains[11:12, :]
        for j, blk in enumerate((before, even, odd)):
            out = out + dot(blk, wn(down + j * C, C))
            zs[j, 0:C, :] += dot_tn(blk, gy)
        fout[r] = out.astype(BF)
        return carry

    lax.fori_loop(0, R, down_forward, 0)
    for j in range(3):
        put_n(down + j * C, zs[j, 0:C, :])

    gf_all = flat(gf)
    for b in range(4):
        cols = slice(b * 256, b * 256 + 256)
        put_n(tw + TE + b * 256, dot_tn(shaped[:, :, cols].reshape(R * T, 256), gf_all))
        put_b(4 * INNER + b * 256, dot_tn(flat(nl2), ginner[:, :, cols].reshape(R * T, 256)))
    put_b(3 * INNER, dot_tn(flat(gm), flat(att)))
    hgrad[0:1, :] = colsum(hacc[0])
    hgrad[1:2, :] = colsum(hacc[1]) * alpha_beta
    hgrad[2:3, :] = colsum(hacc[2]) * (-inv_beta)
    if gather:
        red_core(1)

    def mean_tables(phase, norm_phase):
        tot = total_stats(phase)
        iv = norm_scale(total_stats(norm_phase, wait=False))
        m1 = jnp.where(group_lanes, tot, 0.0)
        m2 = jnp.where(group_lanes, pltpu.roll(tot, 128 - G, 1), 0.0)
        tabs[:, 0:C], tabs[:, C : 2 * C], tabs[:, 2 * C : 3 * C] = expand([m1 * iv, m2 * iv, iv])

    def norm_back_start(r, d, n, gain_row):
        ggrad[gain_row : gain_row + 1, :] += colsum(d * n)
        ggrad[gain_row + 1 : gain_row + 2, :] += colsum(d)
        scaled = d * gains[gain_row : gain_row + 1, :]
        dn[r] = scaled
        keep_sums(r, scaled, scaled * n)

    def phase_five(r, carry):
        cps = dkv_copies(r)
        cps[0].wait_recv()
        cps[2].wait_recv()
        for cp in cps:
            cp.wait_send()
        for i in range(2):
            tot = part[r, f, i].astype(F32) + rbuf[r, 0, i].astype(F32) + rbuf2[r, i].astype(F32)
            dqkv[r, :, (i + 1) * INNER : (i + 2) * INNER] = tot.T.astype(BF)
        back = dot_nt(dqkv[r], broad[:, : 3 * INNER])
        n, rs = layer_norm_parts(resid[r])
        ggrad[5:6, :] += colsum(back * n)
        ggrad[6:7, :] += colsum(back)
        g_res = gr2[r] + layer_norm_back(back, n, rs, gains[5:6, :])
        gr2[r] = g_res
        norm_back_start(r, g_res * der2[r].astype(F32), nrm2[r], 3)
        return carry

    lax.fori_loop(0, R, phase_five, 0)
    send_stats(2)
    send_edges(1, dn)
    if gather:
        red_cross(1)
    put_b(0, dot_tn(flat(ll1), flat(dqkv)))
    mean_tables(2, 1)
    await_edges(2, nrm2)
    await_edges(1, dn)

    def norm_back_end(r, n, which, n_above, n_below):
        tab = row_table(r, 3 * C)

        def back(rows, d, norm):
            sp = dot(metab[r, rows], tab)[-d.shape[0] :] if rows.stop == OFF else dot(metab[r, rows], tab)[: d.shape[0]]
            return d * sp[:, 2 * C :] - sp[:, :C] - norm * sp[:, C : 2 * C]

        zero = jnp.zeros((8, C), F32)
        above = back(slice(OFF - 16, OFF), edge[which, 0, r], n_above)
        below = back(slice(OFF + T, OFF + T + 16), edge[which, 1, r], n_below)
        g2[r, OFF - 16 : OFF] = jnp.concatenate([zero, above], axis=0).astype(BF)
        g2[r, OFF + T : OFF + T + 16] = jnp.concatenate([below, zero], axis=0).astype(BF)
        g2[r, OFF : OFF + T] = back(slice(OFF, OFF + T), dn[r], n).astype(BF)

    def build_g3(r):
        g = g2[r].astype(F32)
        zs[0] = g * metab[r, :, 24:25].astype(F32)
        zs[2] = g * metab[r, :, 25:26].astype(F32)
        g3[r, :, 0:C] = zs[0, OFF + 1 : OFF + T + 1].astype(BF)
        g3[r, :, C : 2 * C] = g2[r, OFF : OFF + T]
        g3[r, :, 2 * C : 3 * C] = zs[2, OFF - 1 : OFF + T - 1].astype(BF)

    def conv_back(r, first_row):
        out = jnp.zeros((T, C), F32)
        for j in range(3):
            out = out + dot_nt(g3[r, :, j * C : (j + 1) * C], wn(first_row + j * C, C))
        return out

    def kernel_grad(src, first_row):
        u = src[:, OFF : OFF + T, :].reshape(R * T, C)
        for j in range(3):
            put_n(first_row + j * C, dot_tn(u, g3[:, :, j * C : (j + 1) * C].reshape(R * T, C)))

    def phase_seven(r, carry):
        norm_back_end(r, nrm2[r], 1, edge[2, 0, r], edge[2, 1, r])
        build_g3(r)
        gh = conv_back(r, 3 * C)
        oh = ohrow[r].astype(BF)
        tgr = segment_sums(oh, gh)
        tg[pl.ds(pl.multiple_of(8 * r, 8), 8), :] = tgr
        ggrad[2:3, :] += colsum(tgr)
        norm_back_start(r, gh * der1[r, OFF : OFF + T].astype(F32), nrm1[r, OFF : OFF + T], 0)
        return carry

    lax.fori_loop(0, R, phase_seven, 0)
    send_stats(3)
    send_edges(0, dn)
    if gather:
        red_owner(1)
    kernel_grad(u2, 3 * C)
    t_hi, t_lo = split2(tg[...])
    eb = emb[...].astype(BF)
    put_n(tw, dot_tn(eb, t_hi) + dot_tn(eb, t_lo))
    if gather:
        red_core(2)
    mean_tables(3, 0)
    await_edges(0, dn)

    if gather:
        small_first()
        red_cross(2)
    else:
        small[...] = small_rows()

    def phase_g3(r, carry):
        norm_back_end(
            r, nrm1[r, OFF : OFF + T], 0, nrm1[r, OFF - 8 : OFF], nrm1[r, OFF + T : OFF + T + 8]
        )
        build_g3(r)
        return carry

    lax.fori_loop(0, R, phase_g3, 0)
    kernel_grad(uext, 0)
    if gather:
        red_core(3)
        small_second()
        red_owner(2)
    for r in range(R):
        igrad[r] = gr2[r] + conv_back(r, 0)
        if gather and r == 0:
            red_cross(3)
        if gather and r == R - 1:
            red_owner(3)
    if gather:
        small_third()
        for g in (1, 2, 3):
            red_wait(g)
        fin = red_finish()
        small_last()
        small[...] = s_all[...]
        for cp in fin:
            cp.wait()
        out_n[...] = gfull[...]
        out_b[...] = bfull[...]

    @pl.when(f < 3)
    def _():
        feat_down.wait_send()

    @pl.when(f > 0)
    def _():
        feat_up.wait_send()
        cot_up.wait_send()


def run_main(fused, feat, ids, steps, cot, narrow, broad, gains, hidden):
    R, T, _ = feat.shape
    L = ids.shape[1]
    TX = T + 2 * OFF
    NR = fused
    vm = lambda shape, dt=F32: pltpu.VMEM(shape, dt)
    dma = lambda *shape: pltpu.SemaphoreType.DMA(shape)
    slots = max(NR, 1)
    if NR:
        wide = [vm((KC // 32, 2, 16, C), BF), vm((C, KR), BF)]
        red = [
            vm((KC // 32, 2, 16, C), BF), vm((C // 32, 2, 16, KR), BF), vm((KC // 32, 2, 16, 128), BF),
            vm((C // 32, 2, 16, KR // 2), BF), vm((KC // 32, 16, 128), BF), vm((C // 32, 16, KR // 2), BF),
            vm((NR, KC // NR // 32, 16, 128), BF), vm((NR, 16, KR // 2), BF),
            vm((KC // NR // 32, 2, 16, C), BF), vm((2, 16, KR), BF),
        ]
        outs = ((KC // NR // 32, 2, 16, C), (2, 16, KR))
    else:
        wide = [vm((16, 128), BF)] * 2
        red = [vm((16, 128), BF)] * 10
        outs = ((KC // 32, 2, 16, C), (C // 32, 2, 16, KR))
    scratch = wide + [
        vm((16, C)), vm((8, FF)), vm((slots, 16, 128), BF), vm((16, 128)), vm((8, FF)), vm((3, 8, FF)), vm((16, C)),
    ] + red + [
        vm((32, C)), vm((3, 8, C)), vm((8, C)), vm((slots, 8, C)), vm((32, C)),
        vm((R, TX, C), BF), vm((R, T // 2 + 16, C), BF), vm((R, TX, 128), BF),
        vm((R, 8, T)), vm((R, L, 128), BF), vm((24, L + 256)), vm((8 * R, 128)), vm((8 * R, TE)), vm((8 * R, C)),
        vm((8 * R, C)), vm((8 * R, C)), vm((8 * R, 3 * C)),
        vm((3, TX, C)), vm((R, TX, C)), vm((R, TX, C), BF), vm((R, TX, C), BF), vm((R, T, C)),
        vm((R, T, C), BF), vm((R, T, C)), vm((R, T, C), BF), vm((R, T, INNER), BF),
        vm((R, 2, L, INNER), BF),
        vm((4, 3, 8 * R, 128)), vm((4, 8 * R, 128)),
        vm((INNER, L), BF), vm((INNER, L), BF), vm((INNER, T), BF), vm((2, 2, T // 2, C)), vm((2, L, T // 2)), vm((H, L, T), BF), vm((INNER, T)),
        vm((H, 8, T)), vm((T, INNER)), vm((INNER, T)),
        vm((R, T, C), BF), vm((R, T, C), BF),
        vm((R, T, FF), BF), vm((R, T, FF), BF), vm((4, T + 8, 128)), vm((R, T + 16, C), BF),
        vm((R, T, C), BF), vm((R, T, INNER), BF), vm((INNER, T)),
        vm((R, 4, 2, INNER, T), BF), vm((R, 2, 2, INNER, T), BF), vm((R, 2, INNER, T), BF), vm((R, 2, INNER, T), BF),
        vm((R, T, 3 * INNER), BF), vm((R, TX, C), BF), vm((8 * R, C)), vm((3, 2, R, 8, C)),
        dma(5), dma(5), dma(5), dma(5), dma(5, 2), dma(5, 2),
        dma(3, 3), dma(3, 3), dma(3, 3), dma(3, 3), dma(3, 2), dma(3, 2), dma(3), dma(3),
        dma(1), dma(1), dma(1), dma(1), dma(1), dma(1),
        dma(2), dma(2), dma(1), dma(1), dma(4), dma(4, 3), dma(3, R), dma(3, R),
        dma(3, R), dma(3, R), dma(3, 2), dma(3, 2), dma(R), dma(R),
    ]
    out_shape = (
        jax.ShapeDtypeStruct((R, T // 2, C), BF),
        jax.ShapeDtypeStruct((R, T, C), F32),
        jax.ShapeDtypeStruct((32, C), F32),
        jax.ShapeDtypeStruct(outs[0], BF),
        jax.ShapeDtypeStruct(outs[1], BF),
    )
    spec = pl.BlockSpec(memory_space=pltpu.VMEM)
    return pl.pallas_call(
        functools.partial(main_kernel, NR),
        out_shape=out_shape,
        in_specs=[spec] * 8,
        out_specs=tuple([spec] * 5),
        scratch_shapes=scratch,
        compiler_params=pltpu.CompilerParams(collective_id=0, has_side_effects=True, vmem_limit_bytes=63 * 2**20),
        cost_estimate=pl.CostEstimate(flops=2 * 10**10, bytes_accessed=2 * 10**7, transcendentals=10**7),
    )(feat, ids, steps, cot, narrow, broad, gains, hidden)


def adam_update(grad, master, first, second, rate):
    moment = BETA_ONE * first + (1.0 - BETA_ONE) * grad
    square = BETA_TWO * second + (1.0 - BETA_TWO) * grad * grad
    corrected = moment / (1.0 - BETA_ONE**STEP)
    scaled = jnp.sqrt(square / (1.0 - BETA_TWO**STEP)) + EPS_ADAM
    return (moment, square, master - rate * (corrected / scaled + DECAY_RATE * master))


def adam_kernel(
    NR,
    gfull, bfull, small, nm, nf, ns, bm, bf_, bs, gm, gf, gs, hm, hf, hs, fout_in, igrad_in,
    fout, igrad, nmo, nso, nuo, bmo, bso, buo, gmo, gso, guo, hmo, hso, huo, nco, bco,
):
    igrad[...] = igrad_in[...]
    fout[...] = fout_in[...]
    SH, SB = nm.shape[0], bm.shape[0]
    rw = lax.axis_index("rows")
    for lo in range(0, SH // 32):
        rows = slice(32 * lo, 32 * lo + 32)
        g = gfull[lo].reshape(32, C).astype(F32)
        m, sq, up = adam_update(g, nm[rows], nf[rows], ns[rows], RATE_SLABS)
        nmo[rows], nso[rows], nuo[rows], nco[rows] = m, sq, up, up.astype(BF)
    for q in range(KR // C):
        cols = slice(q * C, q * C + C)
        g = bfull[:, :, cols].reshape(SB, C).astype(F32)
        m, sq, up = adam_update(g, bm[:, cols], bf_[:, cols], bs[:, cols], RATE_SLABS)
        bmo[:, cols], bso[:, cols], buo[:, cols], bco[:, cols] = m, sq, up, up.astype(BF)
    tot = small[...]
    gains_g = pltpu.roll(tot[0:16], (NR - rw) * (C // NR), 1)[:12, : C // NR]
    q = rw * (FF // NR) // C
    off = rw * (FF // NR) % C
    pick = iota((4, C), 0) == q
    hid = jnp.concatenate(
        [jnp.sum(jnp.where(pick, tot[16 + 4 * k : 20 + 4 * k], 0.0), axis=0, keepdims=True) for k in range(3)]
        + [jnp.zeros((5, C), F32)],
        axis=0,
    )
    hidden_g = pltpu.roll(hid, C - off, 1)[:3, : FF // NR]
    gmo[...], gso[...], guo[...] = adam_update(gains_g, gm[...], gf[...], gs[...], RATE_GAINS)
    hmo[...], hso[...], huo[...] = adam_update(hidden_g, hm[...], hf[...], hs[...], RATE_GAINS)


def run_adam(NR, gfull, bfull, small, fout, igrad, *state):
    shape = lambda a, dt=F32: jax.ShapeDtypeStruct(a.shape, dt)
    nm, bm, gm, hm = state[0], state[3], state[6], state[9]
    out_shape = (shape(fout, BF), shape(igrad)) + tuple(shape(a) for a in (nm, bm, gm, hm) for _ in range(3))
    out_shape += (shape(nm, BF), shape(bm, BF))
    spec = pl.BlockSpec(memory_space=pltpu.VMEM)
    return pl.pallas_call(
        functools.partial(adam_kernel, NR),
        out_shape=out_shape,
        in_specs=[spec] * 17,
        out_specs=tuple([spec] * 16),
        compiler_params=pltpu.CompilerParams(vmem_limit_bytes=60 * 2**20),
    )(gfull, bfull, small, *state, fout, igrad)


def local(
    features, segment_ids, timesteps, cotangent, narrow_slab, broad_slab, model_gains, hidden_gains,
    narrow_first, narrow_second, broad_first, broad_second, gains_first, gains_second, hidden_first, hidden_second,
):
    steps = timesteps
    groups = lax.axis_size("rows")
    if groups == 8:
        fout, igrad, small, gfull, bfull = run_main(
            groups, features, segment_ids, steps, cotangent, narrow_slab, broad_slab, model_gains, hidden_gains
        )
        return tuple(
            run_adam(
                groups, gfull, bfull, small, fout, igrad,
                narrow_slab, narrow_first, narrow_second, broad_slab, broad_first, broad_second,
                model_gains, gains_first, gains_second, hidden_gains, hidden_first, hidden_second,
            )
        )
    narrow_w = lax.all_gather(narrow_slab.astype(BF), "rows", axis=0, tiled=True)
    broad_w = lax.all_gather(broad_slab.astype(BF), "rows", axis=0, tiled=True)
    gains_all = lax.all_gather(model_gains.astype(BF), "rows", axis=1, tiled=True).astype(F32)
    hidden_all = lax.all_gather(hidden_gains.astype(BF), "rows", axis=1, tiled=True).astype(F32)
    fout, igrad, small, ngrad, bgrad = run_main(
        0, features, segment_ids, steps, cotangent, narrow_w, broad_w, gains_all, hidden_all
    )
    scat = lambda v: lax.psum(lax.psum_scatter(v, "rows", scatter_dimension=0, tiled=True), "frames")
    narrow_g = scat(ngrad.astype(F32).reshape(KC, C))
    broad_g = scat(bgrad.astype(F32).reshape(C, KR))
    small = lax.psum(small, ("rows", "frames"))
    i = lax.axis_index("rows")
    own = lambda a, n: lax.dynamic_slice_in_dim(a, i * n, n, 1)
    gains_g = own(small[:12], model_gains.shape[1])
    hidden_g = own(small[16:28].reshape(3, FF), hidden_gains.shape[1])
    narrow_new = adam_update(narrow_g, narrow_slab, narrow_first, narrow_second, RATE_SLABS)
    broad_new = adam_update(broad_g, broad_slab, broad_first, broad_second, RATE_SLABS)
    gains_new = adam_update(gains_g, model_gains, gains_first, gains_second, RATE_GAINS)
    hidden_new = adam_update(hidden_g, hidden_gains, hidden_first, hidden_second, RATE_GAINS)
    return (
        fout, igrad, *narrow_new, *broad_new, *gains_new, *hidden_new,
        narrow_new[2].astype(BF), broad_new[2].astype(BF),
    )


def solution(mesh):
    rows = P("rows", None)
    cols = P(None, "rows")
    act = P("rows", "frames", None)
    return jax.shard_map(
        local,
        mesh=mesh,
        in_specs=(act, rows, rows, act, rows, rows, cols, cols, rows, rows, rows, rows, cols, cols, cols, cols),
        out_specs=(act, act, rows, rows, rows, rows, rows, rows, cols, cols, cols, cols, cols, cols, rows, rows),
        check_vma=False,
    )
```

```python
import functools
import math

import jax
import jax.numpy as jnp
from jax import lax
from jax.experimental import pallas as pl
from jax.experimental.pallas import tpu as pltpu
from jax.sharding import PartitionSpec as P

C = 256
TE = 1024
H = 2
HD = 64
FF = 1024
G = 8
NSEG = 8
STEP = 10
KC = 4352
KR = 1536
INNER = 128
EPS_NORM = 1e-05
EPS_ADAM = 1e-08
BETA_ONE = 0.9
BETA_TWO = 0.999
RATE_SLABS = 0.08
RATE_GAINS = 0.4
DECAY_RATE = 0.01
MASK_FILL = -1e30

F32 = jnp.float32
BF = jnp.bfloat16
MESH = pl.DeviceIdType.MESH
OFF = 32
GROUP = C // G


def dot(a, b):
    return jnp.dot(a, b, preferred_element_type=F32)


def dot_nt(a, b):
    return lax.dot_general(a, b, (((1,), (1,)), ((), ())), preferred_element_type=F32)


def dot_tn(a, b):
    return lax.dot_general(a, b, (((0,), (0,)), ((), ())), preferred_element_type=F32)


def recip(x):
    r = pltpu.reciprocal(x, approx=True)
    return r * (2.0 - x * r)


def split2(x):
    hi = x.astype(BF)
    lo = (x - hi.astype(F32)).astype(BF)
    return hi, lo


def split3(x):
    hi = x.astype(BF).astype(F32)
    mid = (x - hi).astype(BF).astype(F32)
    lo = (x - hi - mid).astype(BF).astype(F32)
    return hi, mid, lo


def mish_parts(y):
    e = jnp.exp(jnp.minimum(y, 30.0))
    n = e * (e + 2.0)
    rc = recip(n + 2.0)
    t = n * rc
    d = t + y * (2.0 * rc) * (1.0 + t) * (e * pltpu.reciprocal(1.0 + e, approx=True))
    return t, d


def reduced_angle(a):
    k = jnp.floor(a * (1.0 / math.pi) + 0.5)
    r = (a - k * 3.140625) - k * 9.67653589793e-4
    r2 = r * r
    s = r * (1.0 + r2 * (-1.0 / 6 + r2 * (1.0 / 120 + r2 * (-1.0 / 5040 + r2 * (1.0 / 362880)))))
    c = 1.0 + r2 * (
        -0.5 + r2 * (1.0 / 24 + r2 * (-1.0 / 720 + r2 * (1.0 / 40320 + r2 * (-1.0 / 3628800))))
    )
    return k, s, c


def sine_pair(x):
    t = x - jnp.floor(x + 0.5)
    t2 = t * t
    s = t * (3.141582022 + t2 * (-5.167142796 + t2 * (2.541899025 - t2 * 0.5546361918)))
    c = 1.9999999069 + t2 * (-9.869585718 + t2 * (8.116823828 + t2 * (-2.663760321 + t2 * 0.4393935944)))
    return s, c


def iota(shape, dim):
    return lax.broadcasted_iota(jnp.int32, shape, dim)


def group_sum_matrix(shift):
    return jnp.where(iota((C, 128), 0) // GROUP + shift == iota((C, 128), 1), 1.0, 0.0).astype(BF)


def group_spread_matrix():
    return jnp.where(iota((128, C), 0) == iota((128, C), 1) // GROUP, 1.0, 0.0).astype(BF)


def compact(sums, squares):
    n = sums.shape[0]
    a = jnp.concatenate(split3(sums), axis=0).astype(BF)
    b = jnp.concatenate(split3(squares), axis=0).astype(BF)
    both = dot(a, group_sum_matrix(0)) + dot(b, group_sum_matrix(G))
    return both[0:n] + both[n : 2 * n] + both[2 * n : 3 * n]


def expand(tables):
    n = tables[0].shape[0]
    stacked = jnp.concatenate([p for t in tables for p in split3(t)], axis=0).astype(BF)
    wide = dot(stacked, group_spread_matrix())
    part = lambda i: wide[n * i : n * i + n]
    return [part(3 * i) + part(3 * i + 1) + part(3 * i + 2) for i in range(len(tables))]


def table_of(columns):
    parts = split3(columns)
    zero = jnp.zeros((104, columns.shape[1]), F32)
    return jnp.concatenate(list(parts) + [zero], axis=0).astype(BF)


def segment_sums(onehot_rows, values):
    hi, lo = split2(values)
    return dot(onehot_rows, hi) + dot(onehot_rows, lo)


def layer_norm_parts(v):
    mu = jnp.mean(v, axis=-1, keepdims=True)
    cen = v - mu
    rs = lax.rsqrt(jnp.mean(cen * cen, axis=-1, keepdims=True) + EPS_NORM)
    return cen * rs, rs


def layer_norm_back(d, n, rs, gain):
    dg = d * gain
    return (dg - jnp.mean(dg, axis=-1, keepdims=True) - n * jnp.mean(dg * n, axis=-1, keepdims=True)) * rs


def colsum(x):
    return jnp.sum(x, axis=0, keepdims=True)


def main_kernel(
    NR,
    feat, ids, steps, cot, narrow_in, broad_in, gains_in, hidden_in,
    fout, igrad, small, out_n, out_b,
    narrow_s, broad_s, gains, hidden, smallw, packf, hgrad, hacc, ggrad,
    ngrad_s, bgrad_s, inh, inb, inq, inbq, got, bgot, gfull, bfull, s_pack, s_in, s_own, s_rows, s_all, embp, ttout, ttin, tgbuf, tgall,
    uext, gyext, metab, ohrow, keymask, idp, counts, emb, tterm, sums, squares, tabs,
    zs, nrm1, der1, u2, nrm2, der2, resid, ll1, qs, kvall,
    statin, statout,
    kt, vt, qt, ffbuf, sbuf, ebuf, otb, invl, dos, dost,
    gf, nl2, shaped, ginner, r3s, r3b, gm, att, dq,
    part, rbuf, rbuf2, sumbuf, dqkv, g2, tg, edge,
    ga_s, ga_r, gx_s, gx_r, gc_s, gc_r,
    rc_s, rc_r, rx_s, rx_r, rd_s, rd_r, rf_s, rf_r, sa_s, sa_r, sb_s, sb_r, sc_s, sc_r, tt_s, tt_r, tf_s, tf_r, to_s, to_r,
    halo_s, halo_r, cot_s, cot_r, stat_s, stat_r, kv_s, kv_r, dkv_s, dkv_r, eg_s, eg_r, r3_s, r3_r,
):
    R, T = feat.shape[0], feat.shape[1]
    gr2, dn, g3 = igrad, resid, shaped
    TX = T + 2 * OFF
    L = ids.shape[1]
    HT = T // 2
    f = lax.axis_index("frames")
    rw = lax.axis_index("rows")
    sib = f + 1 - 2 * (f % 2)
    cross = (f + 2) % 4
    diag = 3 - f
    peers = (sib, cross, diag)

    gather = NR > 0
    ngrad, bgrad = (ngrad_s, bgrad_s) if gather else (out_n, out_b)
    broad = broad_s if gather else broad_in
    if gather:
        SH, SB = narrow_in.shape[0], broad_in.shape[0]
        NB = SH // 32
        narrow_s[pl.ds(rw * NB, NB)] = narrow_in[...].astype(BF).reshape(NB, 2, 16, C)
        broad[pl.ds(pl.multiple_of(rw * SB, 16), SB), :] = broad_in[...].astype(BF)
        packf[...] = jnp.zeros(packf.shape, F32)
        packf[0:12, 0 : C // NR] = gains_in[...]
        packf[12:15, :] = hidden_in[...]
        step_f = steps[...].astype(F32)
        step_hi = jnp.floor(step_f * (1.0 / 32.0))
        for r in range(R):
            packf[15:16, NSEG * r : NSEG * r + NSEG] = step_hi[r : r + 1]
            packf[15:16, 64 + NSEG * r : 64 + NSEG * r + NSEG] = step_f[r : r + 1] - 32.0 * step_hi[r : r + 1]
        smallw[rw] = packf[...].astype(BF)
    else:
        gains[0:12, :] = gains_in[...]
        hidden[0:3, :] = hidden_in[...]

    def wn(first, n):
        if gather:
            return narrow_s[first // 32 : (first + n) // 32].reshape(n, C)
        return narrow_in[first : first + n, :]

    barrier = pltpu.get_barrier_semaphore()
    for p in peers:
        pl.semaphore_signal(barrier, inc=1, device_id=(rw, p), device_id_type=MESH)
    for k in range(1, NR):
        pl.semaphore_signal(barrier, inc=1, device_id=((rw + k) % NR, f), device_id_type=MESH)
    pl.semaphore_wait(barrier, 3 + max(NR - 1, 0))

    def remote(src, dst, ssem, rsem, target):
        return pltpu.make_async_remote_copy(
            src_ref=src, dst_ref=dst, send_sem=ssem, recv_sem=rsem,
            device_id=(rw, target), device_id_type=MESH,
        )

    if gather:
        gx, gc = f // 2, f % 2
        conv_blocks = 3 * C // 32
        own_blocks = {
            0: {0: (0, NB), 1: (NB, conv_blocks)},
            1: {1: (24, 34), 2: (34, 48)},
            4: {2: (48, 51), 3: (51, 68), 4: (68, 72), 6: (104, 119), 7: (119, 136)},
        }
        ranges = {0: ((0, 24),), 1: ((24, 48),), 4: ((48, 72), (104, 136))}
        t_lo, t_hi = 9 * C // 32, (9 * C + TE) // 32
        owners = [s for s in range(NR) if max(NB * s, t_lo) < min(NB * (s + 1), t_hi)]
        is_owner = functools.reduce(jnp.logical_or, [rw == o for o in owners])
        kinds = (0, 1, 2, 4)

        def narrow_piece(g, lo, hi):
            return narrow_s.at[lo:hi, g // 2, :, pl.ds(pl.multiple_of(g % 2 * 128, 128), 128)]

        def broad_piece(g, lo, hi):
            width = KR // 4
            return broad.at[lo:hi, pl.ds(pl.multiple_of(g * width, 128), width)]

        def to_row(ref, ssem, rsem, row):
            return pltpu.make_async_remote_copy(
                src_ref=ref, dst_ref=ref, send_sem=ssem, recv_sem=rsem, device_id=(row, f), device_id_type=MESH
            )

        def sized(kind, n):
            if kind == 2:
                return broad.at[0 : n * SB, 0 : KR // 4]
            if kind == 3:
                return smallw.at[0:n]
            return narrow_s.at[0:n, 0, :, 0:128]

        def waits(kind, n, sends, sem):
            ref = sized(kind, n)
            cp = remote(ref, ref, sem, sem, cross)
            (cp.wait_send if sends else cp.wait_recv)()

        def by_row(counts, act):
            for n in sorted(set(counts)):
                if n:
                    rows_of = [s for s in range(NR) if counts[s] == n]
                    cond = functools.reduce(jnp.logical_or, [rw == s for s in rows_of])

                    @pl.when(cond)
                    def _():
                        act(n)

        def spread_start(kind):
            if kind in own_blocks:
                for s, (lo, hi) in own_blocks[kind].items():

                    @pl.when(rw == s)
                    def _():
                        for k in range(1, NR):
                            to_row(narrow_piece(f, lo, hi), ga_s.at[kind], ga_r.at[kind], (s + k) % NR).start()

                return
            for k in range(1, NR):
                if kind == 2:
                    at = pl.ds(pl.multiple_of(rw * SB, 16), SB)
                    ref = broad.at[at, pl.ds(pl.multiple_of(f * (KR // 4), 128), KR // 4)]
                else:
                    ref = smallw.at[rw]
                to_row(ref, ga_s.at[kind], ga_r.at[kind], (rw + k) % NR).start()

        def held(kind):
            sizes = [0] * NR
            for s, (lo, hi) in own_blocks[kind].items():
                sizes[s] = hi - lo
            return sizes

        def spread_arrive(kind):
            if kind in own_blocks:
                sizes = held(kind)
                by_row([sum(sizes) - n for n in sizes], lambda n: waits(kind, n, False, ga_r.at[kind]))
            else:
                waits(kind, NR - 1, False, ga_r.at[kind])

        def spread_end(kind):
            if kind in own_blocks:
                by_row([(NR - 1) * n for n in held(kind)], lambda n: waits(kind, n, True, ga_s.at[kind]))
            else:
                waits(kind, NR - 1, True, ga_s.at[kind])

        def pieces(kind, g):
            if kind == 2:
                return [broad_piece(g, 0, C)]
            return [narrow_piece(g, lo, hi) for lo, hi in ranges[kind]]

        def units(kind):
            return NR if kind == 2 else sum(hi - lo for lo, hi in ranges[kind])

        def pass_on(kind):
            spread_arrive(kind)
            for ref in pieces(kind, f):
                remote(ref, ref, gx_s.at[kind], gx_r.at[kind], cross).start()
            for ref in pieces(kind, f):
                remote(ref, ref, gc_s.at[kind, 0], gc_r.at[kind, 0], sib).start()

        def pass_across(kind):
            waits(kind, units(kind), False, gx_r.at[kind])
            for ref in pieces(kind, cross):
                remote(ref, ref, gc_s.at[kind, 1], gc_r.at[kind, 1], sib).start()

        def arrive(kind):
            for i in range(2):
                waits(kind, units(kind), False, gc_r.at[kind, i])

        def gather_end():
            for kind in kinds:
                spread_end(kind)
                waits(kind, units(kind), True, gx_s.at[kind])
                for i in range(2):
                    waits(kind, units(kind), True, gc_s.at[kind, i])
            spread_end(3)

            @pl.when(is_owner)
            def _():
                ref = ttout.at[0 : (NR - 1) * 8 * R]
                remote(ref, ref, tt_s.at[0], tt_s.at[0], cross).wait_send()

        spread_start(3)
        spread_start(0)

    def to_next(src, dst, ssem, rsem):
        return remote(src, dst, ssem, rsem, (f + 1) % 4)

    def to_prev(src, dst, ssem, rsem):
        return remote(src, dst, ssem, rsem, (f + 3) % 4)

    feat_down = to_next(feat.at[:, pl.ds(T - 16, 16)], uext.at[:, pl.ds(OFF - 16, 16)], halo_s.at[0], halo_r.at[0])
    feat_up = to_prev(feat.at[:, pl.ds(0, 16)], uext.at[:, pl.ds(OFF + T, 16)], halo_s.at[1], halo_r.at[1])
    cot_up = to_prev(cot.at[:, pl.ds(0, 16)], gyext.at[:, pl.ds(HT, 16)], cot_s.at[0], cot_r.at[0])

    @pl.when(f < 3)
    def _():
        feat_down.start()

    @pl.when(f > 0)
    def _():
        feat_up.start()
        cot_up.start()

    uext[:, 0 : OFF - 16, :] = jnp.zeros((R, OFF - 16, C), BF)
    uext[:, OFF + T + 16 :, :] = jnp.zeros((R, TX - OFF - T - 16, C), BF)
    g2[:, 0 : OFF - 16, :] = jnp.zeros((R, OFF - 16, C), BF)
    g2[:, OFF + T + 16 :, :] = jnp.zeros((R, TX - OFF - T - 16, C), BF)

    @pl.when(f == 0)
    def _():
        edge[:, 0] = jnp.zeros((3, R, 8, C), F32)
        uext[:, OFF - 16 : OFF, :] = jnp.zeros((R, 16, C), BF)

    @pl.when(f == 3)
    def _():
        edge[:, 1] = jnp.zeros((3, R, 8, C), F32)
        uext[:, OFF + T : OFF + T + 16, :] = jnp.zeros((R, 16, C), BF)
        gyext[:, HT : HT + 16, :] = jnp.zeros((R, 16, C), BF)

    ggrad[...] = jnp.zeros(ggrad.shape, F32)
    hgrad[...] = jnp.zeros(hgrad.shape, F32)

    idp[...] = jnp.full(idp.shape, -1.0, F32)
    idp[0:R, 128 : 128 + L] = ids[...].astype(F32)
    idv = idp[0:8]
    width = idv.shape[1]
    prev_row = jnp.where(pltpu.roll(idv, 1, 1) == idv, 1.0, 0.0)
    next_row = jnp.where(pltpu.roll(idv, width - 1, 1) == idv, 1.0, 0.0)
    idp[8:16, :] = prev_row
    idp[16:24, :] = next_row
    base = pl.multiple_of(f * T, 128)
    WX = T + 256
    win = idp[:, pl.ds(base, WX)]
    win = pltpu.roll(win, WX - (128 - OFF), 1)[:, : T + 128]
    own = idp[:, pl.ds(pl.multiple_of(base + 128, 128), T)]
    for r in range(R):
        n_lane = T + 128
        row_id = jnp.broadcast_to(win[r : r + 1], (8, n_lane))
        lab = iota((8, n_lane), 0).astype(F32)
        oh = jnp.where(row_id == lab, 1.0, 0.0)
        pn = jnp.where(
            lab == 0.0,
            jnp.broadcast_to(win[8 + r : 9 + r], (8, n_lane)),
            jnp.where(lab == 1.0, jnp.broadcast_to(win[16 + r : 17 + r], (8, n_lane)), 0.0),
        )
        block = jnp.concatenate([oh, oh, oh, pn, jnp.zeros((96, n_lane), F32)], axis=0)
        turned = block.T
        metab[r] = turned[:TX].astype(BF)
        lab_own = iota((8, T), 0).astype(F32)
        ohrow[r] = jnp.where(jnp.broadcast_to(own[r : r + 1], (8, T)) == lab_own, 1.0, 0.0)
        full = jnp.broadcast_to(idv[r : r + 1, 128 : 128 + L], (8, L))
        lab_full = iota((8, L), 0).astype(F32)
        ohf = jnp.where(full == lab_full, 1.0, 0.0)
        counts[8 * r : 8 * r + 8] = jnp.broadcast_to(jnp.sum(ohf, axis=1, keepdims=True) * float(GROUP), (8, 128))
        km = jnp.concatenate([(1.0 - ohf) * MASK_FILL, jnp.zeros((120, L), F32)], axis=0)
        keymask[r] = km.T.astype(BF)

    uext[:, OFF : OFF + T, :] = feat[...]
    gyext[:, 0:HT, :] = cot[...]

    half = TE // 2
    if not gather:
        freq = jnp.exp(iota((8, half), 1).astype(F32) * (-math.log(10000.0) / half))
        for r in range(R):
            turn = jnp.broadcast_to(steps[r : r + 1, :].astype(F32), (8, NSEG))
            ang = jnp.sum(jnp.where(iota((8, NSEG), 0) == iota((8, NSEG), 1), turn, 0.0), axis=1, keepdims=True) * freq
            k, s, c = reduced_angle(ang)
            sign = 1.0 - 2.0 * (k - 2.0 * jnp.floor(k * 0.5))
            both = jnp.concatenate([s * sign, c * sign], axis=1)
            emb[8 * r : 8 * r + 8, :] = both * mish_parts(both)[0]
    tw = 9 * C

    if gather:
        spread_start(1)
        spread_start(2)
        pass_on(0)
        spread_start(4)
        spread_arrive(3)
        wide = smallw[...].astype(F32)
        gains[...] = jnp.concatenate([wide[s, :, 0 : C // NR] for s in range(NR)], axis=1)
        hidden[0:3, :] = jnp.concatenate([wide[s, 12:15, :] for s in range(NR)], axis=1)
        @pl.when(is_owner)
        def _():
            same = iota((8 * R, 8 * R), 0) == iota((8 * R, 8 * R), 1)
            column = []
            for g in range(NR):
                row = wide[g, 15:16, 0 : 8 * R] * 32.0 + wide[g, 15:16, 64 : 64 + 8 * R]
                spread = jnp.broadcast_to(row, (8 * R, 8 * R))
                column.append(jnp.sum(jnp.where(same, spread, 0.0), axis=1, keepdims=True))
            at = iota((1, SH), 1) + (NB * rw - t_lo) * 32
            low = at < half
            freq = jnp.exp(jnp.where(low, at, at - half).astype(F32) * (-math.log(10000.0) / half))
            k, si, co = reduced_angle(jnp.concatenate(column, axis=0) * freq)
            v = jnp.where(low, si, co) * (1.0 - 2.0 * (k - 2.0 * jnp.floor(k * 0.5)))
            v = jnp.where((at >= 0) & (at < TE), v * mish_parts(v)[0], 0.0)
            embp[...] = v.astype(BF)
            ttout[...] = dot(embp[...], narrow_s[pl.ds(rw * NB, NB)].reshape(SH, C))
            for k2 in range(1, NR):
                to = (rw + k2) % NR
                pltpu.make_async_remote_copy(
                    src_ref=ttout.at[pl.ds(pl.multiple_of(to * 8 * R, 8), 8 * R)], dst_ref=ttin.at[rw],
                    send_sem=tt_s.at[0], recv_sem=tt_r.at[0], device_id=(to, f), device_id_type=MESH,
                ).start()
            ttin[rw] = ttout[pl.ds(pl.multiple_of(rw * 8 * R, 8), 8 * R)]

        pass_across(0)
        arrive(0)

    def own_prev(r):
        return metab[r, OFF : OFF + T, 24:25].astype(F32)

    def own_next(r):
        return metab[r, OFF : OFF + T, 25:26].astype(F32)

    def edge_copies(which, src):
        return (
            to_next(src.at[:, pl.ds(T - 8, 8)], edge.at[which, 0], eg_s.at[which, 0], eg_r.at[which, 0]),
            to_prev(src.at[:, pl.ds(0, 8)], edge.at[which, 1], eg_s.at[which, 1], eg_r.at[which, 1]),
        )

    def send_edges(which, src):
        down_cp, up_cp = edge_copies(which, src)

        @pl.when(f < 3)
        def _():
            down_cp.start()

        @pl.when(f > 0)
        def _():
            up_cp.start()

    def await_edges(which, src):
        down_cp, up_cp = edge_copies(which, src)

        @pl.when(f < 3)
        def _():
            down_cp.wait_send()
            up_cp.wait_recv()

        @pl.when(f > 0)
        def _():
            up_cp.wait_send()
            down_cp.wait_recv()

    def stat_copies(phase):
        return [
            remote(statout.at[phase], statin.at[phase, i], stat_s.at[phase], stat_r.at[phase, i], peers[i])
            for i in range(3)
        ]

    def keep_sums(r, first, second):
        oh = ohrow[r].astype(BF)
        at = pl.ds(pl.multiple_of(8 * r, 8), 8)
        sums[at] = segment_sums(oh, first)
        squares[at] = segment_sums(oh, second)

    def send_stats(phase):
        statout[phase] = compact(sums[...], squares[...])
        for cp in stat_copies(phase):
            cp.start()

    def total_stats(phase, wait=True):
        if wait:
            for cp in stat_copies(phase):
                cp.wait_recv()
            remote(statin.at[phase], statin.at[phase], stat_s.at[phase], stat_s.at[phase], sib).wait_send()
        return (statout[phase] + statin[phase, 0] + statin[phase, 1] + statin[phase, 2]) / jnp.maximum(counts[...], 1.0)

    group_lanes = iota((8 * R, 128), 1) < G

    def norm_scale(tot):
        second = pltpu.roll(tot, 128 - G, 1)
        return jnp.where(group_lanes, lax.rsqrt(jnp.maximum(second - tot * tot, 0.0) + EPS_NORM), 0.0)

    def norm_tables(phase):
        tot = total_stats(phase)
        inv = norm_scale(tot)
        tabs[:, 0:C], tabs[:, C : 2 * C] = expand([tot * inv, inv])

    def row_table(r, width):
        return table_of(tabs[pl.ds(pl.multiple_of(8 * r, 8), 8), 0:width])

    def conv_into(r, src, first_row):
        for j in range(3):
            zs[j] = dot(src[r], wn(first_row + j * C, C))

    @pl.when(f > 0)
    def _():
        feat_down.wait_recv()

    @pl.when(f < 3)
    def _():
        feat_up.wait_recv()

    def phase_one(r):
        conv_into(r, uext, 0)
        lo, hi = OFF - 16, OFF + T + 16
        n = hi - lo
        v = (
            zs[0, lo - 1 : hi - 1] * metab[r, lo:hi, 24:25].astype(F32)
            + zs[1, lo:hi]
            + zs[2, lo + 1 : hi + 1] * metab[r, lo:hi, 25:26].astype(F32)
        )
        nrm1[r, lo:hi] = v
        nrm1[r, 0:lo] = jnp.zeros((lo, C), F32)
        nrm1[r, hi:] = jnp.zeros((TX - hi, C), F32)
        vo = v[OFF - lo : OFF - lo + T]
        keep_sums(r, vo, vo * vo)

    for r in range(R):
        phase_one(r)
        if r == R - 1:
            send_stats(0)
        if gather:
            if r == 0:
                pass_on(1)
            elif r == 1:
                pass_on(2)
                pass_across(1)

    if gather:
        arrive(1)
    if gather:

        def take_terms(n):
            remote(ttin.at[0:n], ttin.at[0:n], tt_r.at[0], tt_r.at[0], cross).wait_recv()

        by_row([len(owners) - (s in owners) for s in range(NR)], take_terms)
        total = gains[2:3, :]
        for o in owners:
            total = total + ttin[o]
        tterm[...] = total
    else:
        tterm[...] = dot(emb[...].astype(BF), wn(tw, TE)) + gains[2:3, :]

    CH = TX // 4
    tabs[:, 2 * C : 3 * C] = tterm[...]
    norm_tables(0)

    def phase_two(r, carry):
        tab = row_table(r, 3 * C)

        def chunk(i, c2):
            rows = pl.ds(pl.multiple_of(i * CH, 16), CH)
            sp = dot(metab[r, rows], tab)
            n = nrm1[r, rows] * sp[:, C : 2 * C] - sp[:, :C]
            y = n * gains[0:1, :] + gains[1:2, :]
            t, d = mish_parts(y)
            nrm1[r, rows] = n
            der1[r, rows] = d.astype(BF)
            u2[r, rows] = (y * t + sp[:, 2 * C :]).astype(BF)
            return c2

        lax.fori_loop(0, 4, chunk, 0)
        conv_into(r, u2, 3 * C)
        v = (
            zs[0, OFF - 1 : OFF + T - 1] * own_prev(r)
            + zs[1, OFF : OFF + T]
            + zs[2, OFF + 1 : OFF + T + 1] * own_next(r)
        )
        nrm2[r] = v
        keep_sums(r, v, v * v)
        return carry

    lax.fori_loop(0, R, phase_two, 0)
    send_stats(1)
    if gather:
        pass_across(2)
        pass_on(4)
        arrive(2)
    norm_tables(1)

    def kv_copies(r):
        slot = lambda g: kvall.at[r, :, pl.ds(pl.multiple_of(g * T, 128), T)]
        mine, other = slot(f), slot(cross)
        return (
            remote(mine, mine, kv_s.at[0, r], kv_r.at[0, r], sib),
            remote(mine, mine, kv_s.at[1, r], kv_r.at[1, r], cross),
            remote(other, other, kv_s.at[2, r], kv_r.at[2, r], sib),
        )

    NCH = 4
    CT = T // NCH

    def phase_three(r, carry):
        tab = row_table(r, 2 * C)

        def chunk(i, c2):
            rows = pl.ds(pl.multiple_of(i * CT, 16), CT)
            xrows = pl.ds(pl.multiple_of(OFF + i * CT, 16), CT)
            sp = dot(metab[r, xrows], tab)
            n = nrm2[r, rows] * sp[:, C : 2 * C] - sp[:, :C]
            y = n * gains[3:4, :] + gains[4:5, :]
            t, d = mish_parts(y)
            nrm2[r, rows] = n
            der2[r, rows] = d.astype(BF)
            res = y * t + feat[r, rows].astype(F32)
            resid[r, rows] = res
            m, rs = layer_norm_parts(res)
            low = (m * gains[5:6, :] + gains[6:7, :]).astype(BF)
            ll1[r, rows] = low
            qkv = dot(low, broad[:, : 3 * INNER])
            qs[r, rows] = (qkv[:, :INNER].astype(BF).astype(F32) * HD ** (-0.5)).astype(BF)
            krows = pl.ds(pl.multiple_of(f * T + i * CT, 16), CT)
            kvall[r, 0, krows] = qkv[:, INNER : 2 * INNER].astype(BF)
            kvall[r, 1, krows] = qkv[:, 2 * INNER :].astype(BF)
            return c2

        lax.fori_loop(0, NCH, chunk, 0)
        if gather:

            @pl.when(r == 0)
            def _():
                pass_across(4)

        cps = kv_copies(r)
        cps[1].start()
        cps[0].start()
        return carry

    lax.fori_loop(0, R, phase_three, 0)
    send_edges(2, nrm2)

    @pl.when(f < 3)
    def _():
        cot_up.wait_recv()

    down = 6 * C

    def phase_down_back(r, carry):
        gy = gyext[r, 0:HT]
        even = dot_nt(gy, wn(down + C, C))
        own_gy = dot_nt(gy, wn(down + 2 * C, C))
        nxt = dot_nt(gyext[r], wn(down, C))
        zs[0, 0 : HT + 16] = nxt
        for hh in range(2):
            cols = slice(hh * 128, hh * 128 + 128)
            pm = r3s[2, pl.ds(8 + 1, HT, stride=2), :]
            nm = r3s[3, pl.ds(8 + 1, HT, stride=2), :]
            r3s[hh, pl.ds(8, HT, stride=2), :] = even[:, cols]
            r3s[hh, pl.ds(9, HT, stride=2), :] = own_gy[:, cols] * pm + zs[0, 1 : HT + 1, cols] * nm
        return carry

    def masks_strided(r):
        r3s[2, 8 : 8 + T] = jnp.broadcast_to(own_prev(r), (T, 128))
        r3s[3, 8 : 8 + T] = jnp.broadcast_to(own_next(r), (T, 128))

    def down_back(r, carry):
        masks_strided(r)
        phase_down_back(r, carry)
        ggrad[11:12, :] += colsum(gyext[r, 0:HT].astype(F32))
        for hh in range(2):
            gf[r, :, hh * 128 : hh * 128 + 128] = r3s[hh, 8 : 8 + T].astype(BF)
        ggrad[10:11, :] += colsum(gf[r].astype(F32))
        return carry

    if gather:
        arrive(4)
    lax.fori_loop(0, R, down_back, 0)

    def relay(r):
        cps = kv_copies(r)
        cps[1].wait_recv()
        cps[2].start()

    relay(0)
    if gather:
        gather_end()

    alpha = jnp.exp(hidden[1:2, :])
    inv_beta = jnp.exp(-hidden[2:3, :])
    alpha_beta = alpha * inv_beta
    alpha_pi = alpha * (1.0 / math.pi)
    NK = L // 256
    CF = T // 2
    hacc[...] = jnp.zeros(hacc.shape, F32)
    lane128 = iota((T, 128), 1)

    def dkv_copies(r):
        return (
            remote(part.at[r, sib], rbuf.at[r, 0], dkv_s.at[0, r], dkv_r.at[0, r], sib),
            remote(part.at[r, diag], rbuf.at[r, 1], dkv_s.at[1, r], dkv_r.at[1, r], sib),
            remote(sumbuf.at[r], rbuf2.at[r], dkv_s.at[2, r], dkv_r.at[2, r], cross),
        )

    def phase_sum(r):
        cps = dkv_copies(r)
        cps[1].wait_recv()
        sumbuf[r] = (part[r, cross].astype(F32) + rbuf[r, 1].astype(F32)).astype(BF)
        cps[2].start()

    def phase_four(r, carry):
        cps = kv_copies(r)
        cps[0].wait_recv()
        cps[2].wait_recv()
        for cp in cps:
            cp.wait_send()
        kt[...] = kvall[r, 0].T
        vt[...] = kvall[r, 1].T
        qv = qs[r]
        ohq = jnp.where(lane128 < 8, metab[r, OFF : OFF + T], jnp.zeros((T, 128), BF))
        zero_q = jnp.zeros((T, 128), BF)
        q_heads = [jnp.where(lane128 // HD == h, qv, zero_q) for h in range(H)]
        TQ = T // 2
        units = [(h, q) for h in range(H) for q in range(2)]

        def scores(n):
            h, q = units[n]
            qrows = slice(q * TQ, q * TQ + TQ)
            qa = jnp.concatenate([q_heads[h][qrows], ohq[qrows]], axis=1)
            m8 = jnp.full((8, TQ), -3e38, F32)
            for i in range(NK):
                keys = slice(i * 256, i * 256 + 256)
                ka = jnp.concatenate([kvall[r, 0, keys], keymask[r, keys]], axis=1)
                sc = dot_nt(ka, qa)
                sbuf[n % 2, keys] = sc
                m8 = jnp.maximum(m8, jnp.max(sc.reshape(32, 8, TQ), axis=0))
            return jnp.max(m8, axis=0, keepdims=True)

        top = scores(0)
        for n, (h, q) in enumerate(units):
            later = scores(n + 1) if n + 1 < len(units) else None
            qcols = slice(q * TQ, q * TQ + TQ)
            l8 = jnp.zeros((8, TQ), F32)
            for i in range(NK):
                keys = slice(i * 256, i * 256 + 256)
                e = jnp.exp(sbuf[n % 2, keys] - top)
                ebuf[h, keys, qcols] = e.astype(BF)
                l8 = l8 + jnp.sum(e.reshape(32, 8, TQ), axis=0)
            inv = 1.0 / jnp.sum(l8, axis=0, keepdims=True)
            invl[h, :, qcols] = jnp.broadcast_to(inv, (8, TQ))
            hrows = slice(h * HD, (h + 1) * HD)
            otb[hrows, qcols] = dot(vt[hrows, :], ebuf[h, :, qcols]) * inv
            top = later
        att[r] = otb[...].T.astype(BF)

        @pl.when(r + 1 < R)
        def _():
            relay(r + 1)

        def ff_chunk(i, c2):
            rows = pl.ds(pl.multiple_of(i * CF, 16), CF)
            res2 = resid[r, rows] + (dot_nt(att[r, rows], broad[:, 3 * INNER : 4 * INNER]) + gains[7:8, :])
            n, rs = layer_norm_parts(res2)
            low = (n * gains[8:9, :] + gains[9:10, :]).astype(BF)
            nl2[r, rows] = low
            gfr = gf[r, rows]
            def products(b):
                w_in = broad[:, 4 * INNER + b * 256 : 4 * INNER + b * 256 + 256]
                w_out = wn(tw + TE + b * 256, 256)
                ffbuf[b % 2, 0] = dot(low, w_in)
                ffbuf[b % 2, 1] = dot_nt(gfr, w_out)
                return w_in, w_out

            out, back = None, None
            weights = products(0)
            for b in range(4):
                following = products(b + 1) if b < 3 else None
                cols = slice(b * 256, b * 256 + 256)
                acc = [hacc[k, :, cols] for k in range(3)]
                shs, gis = [], []
                for u in range(0, CF, 32):
                    inner = ffbuf[b % 2, 0, u : u + 32] + hidden[0:1, cols]
                    gs = ffbuf[b % 2, 1, u : u + 32]
                    s, c = sine_pair(inner * alpha_pi[:, cols])
                    s2 = s * s
                    part_g = gs * (s * c)
                    shs.append((inner + s2 * inv_beta[:, cols]).astype(BF))
                    gi = gs + part_g * alpha_beta[:, cols]
                    gis.append(gi.astype(BF))
                    for k, v in enumerate((gi, part_g * inner, gs * s2)):
                        acc[k] = acc[k] + jnp.sum(v.reshape(4, 8, 256), axis=0)
                for k in range(3):
                    hacc[k, :, cols] = acc[k]
                sh_all, gi_all = jnp.concatenate(shs, axis=0), jnp.concatenate(gis, axis=0)
                shaped[r, rows, cols] = sh_all
                ginner[r, rows, cols] = gi_all
                more, more_back = dot(sh_all, weights[1]), dot_nt(gi_all, weights[0])
                out = more if out is None else out + more
                back = more_back if back is None else back + more_back
                weights = following
            r3 = (res2 + (out + gains[10:11, :])).astype(BF)
            r3b[r, rows] = r3
            g_in = gfr.astype(F32)
            ggrad[8:9, :] += colsum(back * n)
            ggrad[9:10, :] += colsum(back)
            g_res2 = g_in + layer_norm_back(back, n, rs, gains[8:9, :])
            gr2[r, rows] = g_res2
            low_g = g_res2.astype(BF)
            gm[r, rows] = low_g
            ggrad[7:8, :] += colsum(low_g.astype(F32))
            dos[rows] = dot(low_g, broad[:, 3 * INNER : 4 * INNER]).astype(BF).astype(F32)
            return c2

        lax.fori_loop(0, T // CF, ff_chunk, 0)

        @pl.when(f < 3)
        def _():
            to_next(r3b.at[r, pl.ds(T - 16, 16)], r3b.at[r, pl.ds(T, 16)], r3_s.at[r], r3_r.at[r]).start()

        dot_t = dos[...].T
        for h in range(H):
            hrows = slice(h * HD, (h + 1) * HD)
            dost[hrows, :] = dot_t[hrows] * invl[h, 0:1, :]
        zero_t = jnp.zeros((HD, T), BF)
        d_rows, d_cols, d_half = [], [], []
        per_block = T // 256
        for h in range(H):
            hrows = slice(h * HD, (h + 1) * HD)
            d_rows.append(colsum(otb[hrows, :] * dost[hrows, :]))
            dh = dost[hrows, :].astype(BF)
            d_half.append(dh)
            d_cols.append(jnp.concatenate([dh, zero_t] if h == 0 else [zero_t, dh], axis=0))
        qt[...] = qs[r].T
        cps = dkv_copies(r)
        for n, block in enumerate((diag, sib, cross, f)):
            for i in range(per_block):
                keys = pl.ds(pl.multiple_of(block * T + i * 256, 256), 256)
                within = slice(i * 256, i * 256 + 256)
                for h in range(H):
                    hrows = slice(h * HD, (h + 1) * HD)
                    eh = ebuf[h, keys]
                    dp = dot(kvall[r, 1, keys], d_cols[h])
                    ds = (eh.astype(F32) * (dp - d_rows[h])).astype(BF)
                    part[r, block, 0, hrows, within] = dot_nt(qt[hrows, :], ds).astype(BF)
                    part[r, block, 1, hrows, within] = dot_nt(d_half[h], eh).astype(BF)
                    if n == 0 and i == 0:
                        dq[hrows, :] = dot(kt[hrows, keys], ds)
                    else:
                        dq[hrows, :] += dot(kt[hrows, keys], ds)
            if n == 0:
                cps[1].start()
            elif n == 1:
                cps[0].start()
            elif n == 2:
                phase_sum(r)
        dqkv[r, :, 0:INNER] = (dq[...].T * HD ** (-0.5)).astype(BF)
        return carry

    lax.fori_loop(0, R, phase_four, 0)

    if gather:
        rx, rc = f // 2, f % 2
        shard_blocks = NB
        n_groups = {1: ((48, 72), (104, 136)), 2: ((24, 48),), 3: ((0, 24),)}
        b_groups = {1: (4 * INNER, 2 * C), 2: (0, C)}
        b_at = {1: C, 2: 0}

        def half_cols(core, first, n):
            return pl.ds(pl.multiple_of(first + core * n, 128), n)

        def core_copies(g):
            out = [
                remote(ngrad.at[lo:hi, :, :, half_cols(1 - rc, 0, 128)], inh.at[lo:hi], rc_s.at[g - 1, i], rc_r.at[g - 1, i], sib)
                for i, (lo, hi) in enumerate(n_groups[g])
            ]
            if g in b_groups:
                first, n = b_groups[g]
                out.append(
                    remote(
                        bgrad.at[:, :, :, half_cols(1 - rc, first, n)], inb.at[:, :, :, b_at[g] : b_at[g] + n],
                        rc_s.at[g - 1, 2], rc_r.at[g - 1, 2], sib,
                    )
                )
            return out

        def cross_copies(g):
            out = [
                remote(ngrad.at[lo:hi, 1 - rx, :, half_cols(rc, 0, 128)], inq.at[lo:hi], rx_s.at[g - 1, i], rx_r.at[g - 1, i], cross)
                for i, (lo, hi) in enumerate(n_groups[g])
            ]
            if g in b_groups:
                first, n = b_groups[g]
                out.append(
                    remote(
                        bgrad.at[:, 1 - rx, :, half_cols(rc, first, n)], inbq.at[:, :, b_at[g] : b_at[g] + n],
                        rx_s.at[g - 1, 2], rx_r.at[g - 1, 2], cross,
                    )
                )
            return out

        def owner_copies(g, s, source):
            out = []
            for i, (lo, hi) in enumerate(n_groups[g]):
                a, b = max(lo, shard_blocks * s), min(hi, shard_blocks * (s + 1))
                if a < b:
                    out.append(
                        pltpu.make_async_remote_copy(
                            src_ref=ngrad.at[a:b, rx, :, half_cols(rc, 0, 128)],
                            dst_ref=got.at[source, a - shard_blocks * s : b - shard_blocks * s],
                            send_sem=rd_s.at[g - 1, 0], recv_sem=rd_r.at[g - 1, 0],
                            device_id=(s, f), device_id_type=MESH,
                        )
                    )
            if g in b_groups:
                first, n = b_groups[g]
                out.append(
                    pltpu.make_async_remote_copy(
                        src_ref=bgrad.at[s, rx, :, half_cols(rc, first, n)],
                        dst_ref=bgot.at[source, :, b_at[g] : b_at[g] + n],
                        send_sem=rd_s.at[g - 1, 1], recv_sem=rd_r.at[g - 1, 1],
                        device_id=(s, f), device_id_type=MESH,
                    )
                )
            return out

        def red_core(g):
            for cp in core_copies(g):
                cp.start()

        def red_cross(g):
            for cp in core_copies(g):
                cp.wait()
            mine = half_cols(rc, 0, 128)
            for lo, hi in n_groups[g]:
                ngrad[lo:hi, :, :, mine] = (ngrad[lo:hi, :, :, mine].astype(F32) + inh[lo:hi].astype(F32)).astype(BF)
            if g in b_groups:
                first, n = b_groups[g]
                cols = half_cols(rc, first, n)
                other = inb[:, :, :, b_at[g] : b_at[g] + n]
                bgrad[:, :, :, cols] = (bgrad[:, :, :, cols].astype(F32) + other.astype(F32)).astype(BF)
            for cp in cross_copies(g):
                cp.start()

        def red_owner(g):
            for cp in cross_copies(g):
                cp.wait()
            mine = half_cols(rc, 0, 128)
            for lo, hi in n_groups[g]:
                ngrad[lo:hi, rx, :, mine] = (ngrad[lo:hi, rx, :, mine].astype(F32) + inq[lo:hi].astype(F32)).astype(BF)
            if g in b_groups:
                first, n = b_groups[g]
                cols = half_cols(rc, first, n)
                other = inbq[:, :, b_at[g] : b_at[g] + n]
                bgrad[:, rx, :, cols] = (bgrad[:, rx, :, cols].astype(F32) + other.astype(F32)).astype(BF)
            for s in range(NR):

                @pl.when(rw != s)
                def _():
                    for cp in owner_copies(g, s, rw):
                        cp.start()

        def red_wait(g):
            overlap = [
                sum(max(0, min(hi, NB * (s + 1)) - max(lo, NB * s)) for lo, hi in n_groups[g]) for s in range(NR)
            ]

            def take(n, sends, sem):
                cp = remote(inq.at[0:n], inq.at[0:n], sem, sem, cross)
                (cp.wait_send if sends else cp.wait_recv)()

            by_row([sum(overlap) - n for n in overlap], lambda n: take(n, True, rd_s.at[g - 1, 0]))
            by_row([(NR - 1) * n for n in overlap], lambda n: take(n, False, rd_r.at[g - 1, 0]))
            if g in b_groups:
                ref = bgot.at[0 : NR - 1, :, b_at[g] : b_at[g] + b_groups[g][1]]
                cp = remote(ref, ref, rd_s.at[g - 1, 1], rd_r.at[g - 1, 1], cross)
                cp.wait_send()
                cp.wait_recv()

        def send_final(j, blk, size):
            for p in peers:
                remote(blk, blk, rf_s.at[j], rf_r.at[j], p).start()
            return remote(size, size, rf_s.at[j], rf_r.at[j], cross)

        def red_finish_broad():
            out = []
            for j, g in enumerate((1, 2)):
                cols = half_cols(rc, *b_groups[g])
                here = slice(b_at[g], b_at[g] + b_groups[g][1])
                total = bgrad[rw, rx, :, cols].astype(F32)
                for k in range(1, NR):
                    total = total + bgot[(rw + k) % NR, :, here].astype(F32)
                bfull[rx, :, cols] = total.astype(BF)
                out.append(send_final(j, bfull.at[rx, :, cols], bgot.at[0:3, :, here]))
            return out

        def red_finish_narrow():
            mine = half_cols(rc, 0, 128)
            total = ngrad[pl.ds(shard_blocks * rw, shard_blocks), rx, :, mine].astype(F32)
            for k in range(1, NR):
                total = total + got[(rw + k) % NR].astype(F32)
            gfull[:, rx, :, mine] = total.astype(BF)
            return [send_final(2, gfull.at[:, rx, :, mine], inq.at[0 : 3 * NB])]

        def terms_first():
            tgbuf[f] = tg[...]
            for p in peers:
                remote(tgbuf.at[f], tgbuf.at[f], tf_s.at[0], tf_r.at[0], p).start()

        def terms_second():
            remote(tgbuf.at[0:3], tgbuf.at[0:3], tf_s.at[0], tf_r.at[0], cross).wait()
            tgall[rw] = tgbuf[0] + tgbuf[1] + tgbuf[2] + tgbuf[3]
            for o in owners:

                @pl.when(rw != o)
                def _():
                    pltpu.make_async_remote_copy(
                        src_ref=tgall.at[rw], dst_ref=tgall.at[rw], send_sem=to_s.at[0], recv_sem=to_r.at[0],
                        device_id=(o, f), device_id_type=MESH,
                    ).start()

        def terms_third():
            def sent(n):
                remote(tgall.at[0:n], tgall.at[0:n], to_s.at[0], to_s.at[0], cross).wait_send()

            by_row([len(owners) - (s in owners) for s in range(NR)], sent)

            @pl.when(is_owner)
            def _():
                ref = tgall.at[0 : NR - 1]
                remote(ref, ref, to_r.at[0], to_r.at[0], cross).wait_recv()
                hi, lo = split2(tgall[...].reshape(NR * 8 * R, C))
                grad = (dot_tn(embp[...], hi) + dot_tn(embp[...], lo)).astype(BF).reshape(NB, 2, 16, C)
                for o in owners:
                    a, b = max(NB * o, t_lo) - NB * o, min(NB * (o + 1), t_hi) - NB * o

                    @pl.when(rw == o)
                    def _():
                        out_n[a:b] = grad[a:b]

        def small_first():
            s_pack[...] = small_rows()
            for i, p in enumerate(peers):
                remote(s_pack.at[pl.ds(pl.multiple_of(8 * p, 8), 8)], s_in.at[i], sa_s.at[0], sa_r.at[0], p).start()

        def small_second():
            remote(s_in, s_in, sa_s.at[0], sa_r.at[0], sib).wait()
            s_own[...] = s_pack[pl.ds(pl.multiple_of(8 * f, 8), 8)] + s_in[0] + s_in[1] + s_in[2]
            for k in range(1, NR):
                pltpu.make_async_remote_copy(
                    src_ref=s_own, dst_ref=s_rows.at[k - 1], send_sem=sb_s.at[0], recv_sem=sb_r.at[0],
                    device_id=((rw + k) % NR, f), device_id_type=MESH,
                ).start()

        def small_third():
            ref = s_rows.at[0 : NR - 1]
            remote(ref, ref, sb_s.at[0], sb_r.at[0], sib).wait()
            at = pl.ds(pl.multiple_of(8 * f, 8), 8)
            tot = s_own[...]
            for k in range(1, NR):
                tot = tot + s_rows[k - 1]
            s_all[at] = tot
            for p in peers:
                remote(s_all.at[at], s_all.at[at], sc_s.at[0], sc_r.at[0], p).start()

        def small_last():
            remote(s_in, s_in, sc_s.at[0], sc_r.at[0], sib).wait()

    def small_rows():
        hid = [hgrad[k : k + 1, q * C : (q + 1) * C] for k in range(3) for q in range(FF // C)]
        return jnp.concatenate([ggrad[...]] + hid + [jnp.zeros((4, C), F32)], axis=0)

    flat = lambda ref: ref[...].reshape(R * T, ref.shape[2])

    def put_n(first, value):
        n = value.shape[0]
        ngrad[first // 32 : (first + n) // 32] = value.astype(BF).reshape(n // 32, 2, 16, C)

    def put_b(first, value):
        bgrad[:, :, :, first : first + value.shape[1]] = value.astype(BF).reshape(C // 32, 2, 16, value.shape[1])

    zs[:, 0:C, :] = jnp.zeros((3, C, C), F32)

    def down_forward(r, carry):
        @pl.when(f > 0)
        def _():
            to_next(r3b.at[r, pl.ds(T - 16, 16)], r3b.at[r, pl.ds(T, 16)], r3_s.at[r], r3_r.at[r]).wait_recv()

        @pl.when(f < 3)
        def _():
            to_next(r3b.at[r, pl.ds(T - 16, 16)], r3b.at[r, pl.ds(T, 16)], r3_s.at[r], r3_r.at[r]).wait_send()

        @pl.when(f == 0)
        def _():
            r3b[r, T : T + 16, :] = jnp.zeros((16, C), BF)

        masks_strided(r)
        for hh in range(2):
            cols = slice(hh * 128, hh * 128 + 128)
            r3s[hh, 8 : 8 + T] = r3b[r, 0:T, cols].astype(F32)
            r3s[hh, 0:8] = r3b[r, T : T + 16, cols].astype(F32)[8:16]
        even = jnp.concatenate([r3s[hh, pl.ds(8, HT, stride=2), :] for hh in range(2)], axis=1).astype(BF)
        m_after = r3s[3, pl.ds(8, HT, stride=2), :]
        m_before = r3s[2, pl.ds(8, HT, stride=2), :]
        odd = jnp.concatenate([r3s[hh, pl.ds(9, HT, stride=2), :] * m_after for hh in range(2)], axis=1).astype(BF)
        before = jnp.concatenate([r3s[hh, pl.ds(7, HT, stride=2), :] * m_before for hh in range(2)], axis=1).astype(BF)
        gy = cot[r]
        out = gains[11:12, :]
        for j, blk in enumerate((before, even, odd)):
            out = out + dot(blk, wn(down + j * C, C))
            zs[j, 0:C, :] += dot_tn(blk, gy)
        fout[r] = out.astype(BF)
        return carry

    lax.fori_loop(0, R, down_forward, 0)
    for j in range(3):
        put_n(down + j * C, zs[j, 0:C, :])

    gf_all = flat(gf)
    for b in range(4):
        cols = slice(b * 256, b * 256 + 256)
        put_n(tw + TE + b * 256, dot_tn(shaped[:, :, cols].reshape(R * T, 256), gf_all))
        put_b(4 * INNER + b * 256, dot_tn(flat(nl2), ginner[:, :, cols].reshape(R * T, 256)))
    put_b(3 * INNER, dot_tn(flat(gm), flat(att)))
    hgrad[0:1, :] = colsum(hacc[0])
    hgrad[1:2, :] = colsum(hacc[1]) * alpha_beta
    hgrad[2:3, :] = colsum(hacc[2]) * (-inv_beta)
    if gather:
        red_core(1)

    def mean_tables(phase, norm_phase):
        tot = total_stats(phase)
        iv = norm_scale(total_stats(norm_phase, wait=False))
        m1 = jnp.where(group_lanes, tot, 0.0)
        m2 = jnp.where(group_lanes, pltpu.roll(tot, 128 - G, 1), 0.0)
        tabs[:, 0:C], tabs[:, C : 2 * C], tabs[:, 2 * C : 3 * C] = expand([m1 * iv, m2 * iv, iv])

    def norm_back_start(r, d, n, gain_row):
        ggrad[gain_row : gain_row + 1, :] += colsum(d * n)
        ggrad[gain_row + 1 : gain_row + 2, :] += colsum(d)
        scaled = d * gains[gain_row : gain_row + 1, :]
        dn[r] = scaled
        keep_sums(r, scaled, scaled * n)

    def phase_five(r, carry):
        cps = dkv_copies(r)
        cps[0].wait_recv()
        cps[2].wait_recv()
        for cp in cps:
            cp.wait_send()
        for i in range(2):
            tot = part[r, f, i].astype(F32) + rbuf[r, 0, i].astype(F32) + rbuf2[r, i].astype(F32)
            dqkv[r, :, (i + 1) * INNER : (i + 2) * INNER] = tot.T.astype(BF)
        back = dot_nt(dqkv[r], broad[:, : 3 * INNER])
        n, rs = layer_norm_parts(resid[r])
        ggrad[5:6, :] += colsum(back * n)
        ggrad[6:7, :] += colsum(back)
        g_res = gr2[r] + layer_norm_back(back, n, rs, gains[5:6, :])
        gr2[r] = g_res
        norm_back_start(r, g_res * der2[r].astype(F32), nrm2[r], 3)
        return carry

    lax.fori_loop(0, R, phase_five, 0)
    send_stats(2)
    send_edges(1, dn)
    if gather:
        red_cross(1)
    put_b(0, dot_tn(flat(ll1), flat(dqkv)))
    mean_tables(2, 1)
    await_edges(2, nrm2)
    await_edges(1, dn)

    def norm_back_end(r, n, which, n_above, n_below):
        tab = row_table(r, 3 * C)

        def back(rows, d, norm):
            sp = dot(metab[r, rows], tab)[-d.shape[0] :] if rows.stop == OFF else dot(metab[r, rows], tab)[: d.shape[0]]
            return d * sp[:, 2 * C :] - sp[:, :C] - norm * sp[:, C : 2 * C]

        zero = jnp.zeros((8, C), F32)
        above = back(slice(OFF - 16, OFF), edge[which, 0, r], n_above)
        below = back(slice(OFF + T, OFF + T + 16), edge[which, 1, r], n_below)
        g2[r, OFF - 16 : OFF] = jnp.concatenate([zero, above], axis=0).astype(BF)
        g2[r, OFF + T : OFF + T + 16] = jnp.concatenate([below, zero], axis=0).astype(BF)
        g2[r, OFF : OFF + T] = back(slice(OFF, OFF + T), dn[r], n).astype(BF)

    def build_g3(r):
        g = g2[r].astype(F32)
        zs[0] = g * metab[r, :, 24:25].astype(F32)
        zs[2] = g * metab[r, :, 25:26].astype(F32)
        g3[r, :, 0:C] = zs[0, OFF + 1 : OFF + T + 1].astype(BF)
        g3[r, :, C : 2 * C] = g2[r, OFF : OFF + T]
        g3[r, :, 2 * C : 3 * C] = zs[2, OFF - 1 : OFF + T - 1].astype(BF)

    def conv_back(r, first_row):
        out = jnp.zeros((T, C), F32)
        for j in range(3):
            out = out + dot_nt(g3[r, :, j * C : (j + 1) * C], wn(first_row + j * C, C))
        return out

    def kernel_grad(src, first_row):
        u = src[:, OFF : OFF + T, :].reshape(R * T, C)
        for j in range(3):
            put_n(first_row + j * C, dot_tn(u, g3[:, :, j * C : (j + 1) * C].reshape(R * T, C)))

    def phase_seven(r, carry):
        norm_back_end(r, nrm2[r], 1, edge[2, 0, r], edge[2, 1, r])
        build_g3(r)
        gh = conv_back(r, 3 * C)
        oh = ohrow[r].astype(BF)
        tgr = segment_sums(oh, gh)
        tg[pl.ds(pl.multiple_of(8 * r, 8), 8), :] = tgr
        ggrad[2:3, :] += colsum(tgr)
        norm_back_start(r, gh * der1[r, OFF : OFF + T].astype(F32), nrm1[r, OFF : OFF + T], 0)
        return carry

    lax.fori_loop(0, R, phase_seven, 0)
    send_stats(3)
    send_edges(0, dn)
    if gather:
        terms_first()
        red_owner(1)
    kernel_grad(u2, 3 * C)
    if gather:
        red_core(2)
        terms_second()
    else:
        part_hi, part_lo = split2(tg[...])
        eb = emb[...].astype(BF)
        put_n(tw, dot_tn(eb, part_hi) + dot_tn(eb, part_lo))
    mean_tables(3, 0)
    await_edges(0, dn)

    if gather:
        small_first()
        red_cross(2)
    else:
        small[...] = small_rows()

    def phase_g3(r, carry):
        norm_back_end(
            r, nrm1[r, OFF : OFF + T], 0, nrm1[r, OFF - 8 : OFF], nrm1[r, OFF + T : OFF + T + 8]
        )
        build_g3(r)
        return carry

    lax.fori_loop(0, R, phase_g3, 0)
    kernel_grad(uext, 0)
    if gather:
        red_core(3)
        small_second()
        red_owner(2)
        red_cross(3)
    for r in range(R):
        igrad[r] = gr2[r] + conv_back(r, 0)
        if gather and r == 1:
            red_owner(3)
    if gather:
        small_third()
        red_wait(1)
        red_wait(2)
        fin = red_finish_broad()
        red_wait(3)
        fin += red_finish_narrow()
        small_last()
        small[...] = s_all[...]
        for cp in fin:
            cp.wait()
        out_n[...] = gfull[...]
        out_b[...] = bfull[...]
        terms_third()

    @pl.when(f < 3)
    def _():
        feat_down.wait_send()

    @pl.when(f > 0)
    def _():
        feat_up.wait_send()
        cot_up.wait_send()


def run_main(fused, feat, ids, steps, cot, narrow, broad, gains, hidden):
    R, T, _ = feat.shape
    L = ids.shape[1]
    TX = T + 2 * OFF
    NR = fused
    vm = lambda shape, dt=F32: pltpu.VMEM(shape, dt)
    dma = lambda *shape: pltpu.SemaphoreType.DMA(shape)
    slots = max(NR, 1)
    if NR:
        wide = [vm((KC // 32, 2, 16, C), BF), vm((C, KR), BF)]
        red = [
            vm((KC // 32, 2, 16, C), BF), vm((C // 32, 2, 16, KR), BF), vm((KC // 32, 2, 16, 128), BF),
            vm((C // 32, 2, 16, KR // 2), BF), vm((KC // 32, 16, 128), BF), vm((C // 32, 16, KR // 2), BF),
            vm((NR, KC // NR // 32, 16, 128), BF), vm((NR, 16, KR // 2), BF),
            vm((KC // NR // 32, 2, 16, C), BF), vm((2, 16, KR), BF),
        ]
        outs = ((KC // NR // 32, 2, 16, C), (2, 16, KR))
    else:
        wide = [vm((16, 128), BF)] * 2
        red = [vm((16, 128), BF)] * 10
        outs = ((KC // 32, 2, 16, C), (C // 32, 2, 16, KR))
    scratch = wide + [
        vm((16, C)), vm((8, FF)), vm((slots, 16, 128), BF), vm((16, 128)), vm((8, FF)), vm((3, 8, FF)), vm((16, C)),
    ] + red + [
        vm((32, C)), vm((3, 8, C)), vm((8, C)), vm((slots, 8, C)), vm((32, C)),
        vm((slots * 8 * R, KC // slots if NR else 128), BF), vm((slots * 8 * R, C)), vm((slots, 8 * R, C)), vm((4, 8 * R, C)), vm((slots, 8 * R, C)),
        vm((R, TX, C), BF), vm((R, T // 2 + 16, C), BF), vm((R, TX, 128), BF),
        vm((R, 8, T)), vm((R, L, 128), BF), vm((24, L + 256)), vm((8 * R, 128)), vm((8 * R, TE)), vm((8 * R, C)),
        vm((8 * R, C)), vm((8 * R, C)), vm((8 * R, 3 * C)),
        vm((3, TX, C)), vm((R, TX, C)), vm((R, TX, C), BF), vm((R, TX, C), BF), vm((R, T, C)),
        vm((R, T, C), BF), vm((R, T, C)), vm((R, T, C), BF), vm((R, T, INNER), BF),
        vm((R, 2, L, INNER), BF),
        vm((4, 3, 8 * R, 128)), vm((4, 8 * R, 128)),
        vm((INNER, L), BF), vm((INNER, L), BF), vm((INNER, T), BF), vm((2, 2, T // 2, C)), vm((2, L, T // 2)), vm((H, L, T), BF), vm((INNER, T)),
        vm((H, 8, T)), vm((T, INNER)), vm((INNER, T)),
        vm((R, T, C), BF), vm((R, T, C), BF),
        vm((R, T, FF), BF), vm((R, T, FF), BF), vm((4, T + 8, 128)), vm((R, T + 16, C), BF),
        vm((R, T, C), BF), vm((R, T, INNER), BF), vm((INNER, T)),
        vm((R, 4, 2, INNER, T), BF), vm((R, 2, 2, INNER, T), BF), vm((R, 2, INNER, T), BF), vm((R, 2, INNER, T), BF),
        vm((R, T, 3 * INNER), BF), vm((R, TX, C), BF), vm((8 * R, C)), vm((3, 2, R, 8, C)),
        dma(5), dma(5), dma(5), dma(5), dma(5, 2), dma(5, 2),
        dma(3, 3), dma(3, 3), dma(3, 3), dma(3, 3), dma(3, 2), dma(3, 2), dma(3), dma(3),
        dma(1), dma(1), dma(1), dma(1), dma(1), dma(1), dma(1), dma(1), dma(1), dma(1), dma(1), dma(1),
        dma(2), dma(2), dma(1), dma(1), dma(4), dma(4, 3), dma(3, R), dma(3, R),
        dma(3, R), dma(3, R), dma(3, 2), dma(3, 2), dma(R), dma(R),
    ]
    out_shape = (
        jax.ShapeDtypeStruct((R, T // 2, C), BF),
        jax.ShapeDtypeStruct((R, T, C), F32),
        jax.ShapeDtypeStruct((32, C), F32),
        jax.ShapeDtypeStruct(outs[0], BF),
        jax.ShapeDtypeStruct(outs[1], BF),
    )
    spec = pl.BlockSpec(memory_space=pltpu.VMEM)
    return pl.pallas_call(
        functools.partial(main_kernel, NR),
        out_shape=out_shape,
        in_specs=[spec] * 8,
        out_specs=tuple([spec] * 5),
        scratch_shapes=scratch,
        compiler_params=pltpu.CompilerParams(collective_id=0, has_side_effects=True, vmem_limit_bytes=63 * 2**20),
        cost_estimate=pl.CostEstimate(flops=2 * 10**10, bytes_accessed=2 * 10**7, transcendentals=10**7),
    )(feat, ids, steps, cot, narrow, broad, gains, hidden)


def adam_update(grad, master, first, second, rate):
    moment = BETA_ONE * first + (1.0 - BETA_ONE) * grad
    square = BETA_TWO * second + (1.0 - BETA_TWO) * grad * grad
    corrected = moment / (1.0 - BETA_ONE**STEP)
    scaled = jnp.sqrt(square / (1.0 - BETA_TWO**STEP)) + EPS_ADAM
    return (moment, square, master - rate * (corrected / scaled + DECAY_RATE * master))


def adam_kernel(
    NR,
    gfull, bfull, small, nm, nf, ns, bm, bf_, bs, gm, gf, gs, hm, hf, hs, fout_in, igrad_in,
    fout, igrad, nmo, nso, nuo, bmo, bso, buo, gmo, gso, guo, hmo, hso, huo, nco, bco,
):
    igrad[...] = igrad_in[...]
    fout[...] = fout_in[...]
    SH, SB = nm.shape[0], bm.shape[0]
    rw = lax.axis_index("rows")
    for lo in range(0, SH // 32):
        rows = slice(32 * lo, 32 * lo + 32)
        g = gfull[lo].reshape(32, C).astype(F32)
        m, sq, up = adam_update(g, nm[rows], nf[rows], ns[rows], RATE_SLABS)
        nmo[rows], nso[rows], nuo[rows], nco[rows] = m, sq, up, up.astype(BF)
    for q in range(KR // C):
        cols = slice(q * C, q * C + C)
        g = bfull[:, :, cols].reshape(SB, C).astype(F32)
        m, sq, up = adam_update(g, bm[:, cols], bf_[:, cols], bs[:, cols], RATE_SLABS)
        bmo[:, cols], bso[:, cols], buo[:, cols], bco[:, cols] = m, sq, up, up.astype(BF)
    tot = small[...]
    gains_g = pltpu.roll(tot[0:16], (NR - rw) * (C // NR), 1)[:12, : C // NR]
    q = rw * (FF // NR) // C
    off = rw * (FF // NR) % C
    pick = iota((4, C), 0) == q
    hid = jnp.concatenate(
        [jnp.sum(jnp.where(pick, tot[16 + 4 * k : 20 + 4 * k], 0.0), axis=0, keepdims=True) for k in range(3)]
        + [jnp.zeros((5, C), F32)],
        axis=0,
    )
    hidden_g = pltpu.roll(hid, C - off, 1)[:3, : FF // NR]
    gmo[...], gso[...], guo[...] = adam_update(gains_g, gm[...], gf[...], gs[...], RATE_GAINS)
    hmo[...], hso[...], huo[...] = adam_update(hidden_g, hm[...], hf[...], hs[...], RATE_GAINS)


def run_adam(NR, gfull, bfull, small, fout, igrad, *state):
    shape = lambda a, dt=F32: jax.ShapeDtypeStruct(a.shape, dt)
    nm, bm, gm, hm = state[0], state[3], state[6], state[9]
    out_shape = (shape(fout, BF), shape(igrad)) + tuple(shape(a) for a in (nm, bm, gm, hm) for _ in range(3))
    out_shape += (shape(nm, BF), shape(bm, BF))
    spec = pl.BlockSpec(memory_space=pltpu.VMEM)
    return pl.pallas_call(
        functools.partial(adam_kernel, NR),
        out_shape=out_shape,
        in_specs=[spec] * 17,
        out_specs=tuple([spec] * 16),
        compiler_params=pltpu.CompilerParams(vmem_limit_bytes=60 * 2**20),
    )(gfull, bfull, small, *state, fout, igrad)


def local(
    features, segment_ids, timesteps, cotangent, narrow_slab, broad_slab, model_gains, hidden_gains,
    narrow_first, narrow_second, broad_first, broad_second, gains_first, gains_second, hidden_first, hidden_second,
):
    steps = timesteps
    groups = lax.axis_size("rows")
    if groups == 8:
        fout, igrad, small, gfull, bfull = run_main(
            groups, features, segment_ids, steps, cotangent, narrow_slab, broad_slab, model_gains, hidden_gains
        )
        return tuple(
            run_adam(
                groups, gfull, bfull, small, fout, igrad,
                narrow_slab, narrow_first, narrow_second, broad_slab, broad_first, broad_second,
                model_gains, gains_first, gains_second, hidden_gains, hidden_first, hidden_second,
            )
        )
    narrow_w = lax.all_gather(narrow_slab.astype(BF), "rows", axis=0, tiled=True)
    broad_w = lax.all_gather(broad_slab.astype(BF), "rows", axis=0, tiled=True)
    gains_all = lax.all_gather(model_gains.astype(BF), "rows", axis=1, tiled=True).astype(F32)
    hidden_all = lax.all_gather(hidden_gains.astype(BF), "rows", axis=1, tiled=True).astype(F32)
    fout, igrad, small, ngrad, bgrad = run_main(
        0, features, segment_ids, steps, cotangent, narrow_w, broad_w, gains_all, hidden_all
    )
    scat = lambda v: lax.psum(lax.psum_scatter(v, "rows", scatter_dimension=0, tiled=True), "frames")
    narrow_g = scat(ngrad.astype(F32).reshape(KC, C))
    broad_g = scat(bgrad.astype(F32).reshape(C, KR))
    small = lax.psum(small, ("rows", "frames"))
    i = lax.axis_index("rows")
    own = lambda a, n: lax.dynamic_slice_in_dim(a, i * n, n, 1)
    gains_g = own(small[:12], model_gains.shape[1])
    hidden_g = own(small[16:28].reshape(3, FF), hidden_gains.shape[1])
    narrow_new = adam_update(narrow_g, narrow_slab, narrow_first, narrow_second, RATE_SLABS)
    broad_new = adam_update(broad_g, broad_slab, broad_first, broad_second, RATE_SLABS)
    gains_new = adam_update(gains_g, model_gains, gains_first, gains_second, RATE_GAINS)
    hidden_new = adam_update(hidden_g, hidden_gains, hidden_first, hidden_second, RATE_GAINS)
    return (
        fout, igrad, *narrow_new, *broad_new, *gains_new, *hidden_new,
        narrow_new[2].astype(BF), broad_new[2].astype(BF),
    )


def solution(mesh):
    rows = P("rows", None)
    cols = P(None, "rows")
    act = P("rows", "frames", None)
    return jax.shard_map(
        local,
        mesh=mesh,
        in_specs=(act, rows, rows, act, rows, rows, cols, cols, rows, rows, rows, rows, cols, cols, cols, cols),
        out_specs=(act, act, rows, rows, rows, rows, rows, rows, cols, cols, cols, cols, cols, cols, rows, rows),
        check_vma=False,
    )
```

```python
import functools
import math

import jax
import jax.numpy as jnp
from jax import lax
from jax.experimental import pallas as pl
from jax.experimental.pallas import tpu as pltpu
from jax.sharding import PartitionSpec as P

C = 256
TE = 1024
H = 2
HD = 64
FF = 1024
G = 8
NSEG = 8
STEP = 10
KC = 4352
KR = 1536
INNER = 128
EPS_NORM = 1e-05
EPS_ADAM = 1e-08
BETA_ONE = 0.9
BETA_TWO = 0.999
RATE_SLABS = 0.08
RATE_GAINS = 0.4
DECAY_RATE = 0.01
MASK_FILL = -1e30

F32 = jnp.float32
BF = jnp.bfloat16
MESH = pl.DeviceIdType.MESH
OFF = 32
GROUP = C // G


def dot(a, b):
    return jnp.dot(a, b, preferred_element_type=F32)


def dot_nt(a, b):
    return lax.dot_general(a, b, (((1,), (1,)), ((), ())), preferred_element_type=F32)


def dot_tn(a, b):
    return lax.dot_general(a, b, (((0,), (0,)), ((), ())), preferred_element_type=F32)


def recip(x):
    r = pltpu.reciprocal(x, approx=True)
    return r * (2.0 - x * r)


def split2(x):
    hi = x.astype(BF)
    lo = (x - hi.astype(F32)).astype(BF)
    return hi, lo


def split3(x):
    hi = x.astype(BF).astype(F32)
    mid = (x - hi).astype(BF).astype(F32)
    lo = (x - hi - mid).astype(BF).astype(F32)
    return hi, mid, lo


def mish_parts(y):
    e = jnp.exp(jnp.minimum(y, 30.0))
    n = e * (e + 2.0)
    rc = recip(n + 2.0)
    t = n * rc
    d = t + y * (2.0 * rc) * (1.0 + t) * (e * pltpu.reciprocal(1.0 + e, approx=True))
    return t, d


def reduced_angle(a):
    k = jnp.floor(a * (1.0 / math.pi) + 0.5)
    r = (a - k * 3.140625) - k * 9.67653589793e-4
    r2 = r * r
    s = r * (1.0 + r2 * (-1.0 / 6 + r2 * (1.0 / 120 + r2 * (-1.0 / 5040 + r2 * (1.0 / 362880)))))
    c = 1.0 + r2 * (
        -0.5 + r2 * (1.0 / 24 + r2 * (-1.0 / 720 + r2 * (1.0 / 40320 + r2 * (-1.0 / 3628800))))
    )
    return k, s, c


def sine_pair(x):
    t = x - jnp.floor(x + 0.5)
    t2 = t * t
    s = t * (3.141582022 + t2 * (-5.167142796 + t2 * (2.541899025 - t2 * 0.5546361918)))
    c = 1.9999999069 + t2 * (-9.869585718 + t2 * (8.116823828 + t2 * (-2.663760321 + t2 * 0.4393935944)))
    return s, c


def iota(shape, dim):
    return lax.broadcasted_iota(jnp.int32, shape, dim)


def group_sum_matrix(shift):
    return jnp.where(iota((C, 128), 0) // GROUP + shift == iota((C, 128), 1), 1.0, 0.0).astype(BF)


def group_spread_matrix():
    return jnp.where(iota((128, C), 0) == iota((128, C), 1) // GROUP, 1.0, 0.0).astype(BF)


def compact(sums, squares):
    n = sums.shape[0]
    a = jnp.concatenate(split3(sums), axis=0).astype(BF)
    b = jnp.concatenate(split3(squares), axis=0).astype(BF)
    both = dot(a, group_sum_matrix(0)) + dot(b, group_sum_matrix(G))
    return both[0:n] + both[n : 2 * n] + both[2 * n : 3 * n]


def expand(tables):
    n = tables[0].shape[0]
    stacked = jnp.concatenate([p for t in tables for p in split3(t)], axis=0).astype(BF)
    wide = dot(stacked, group_spread_matrix())
    part = lambda i: wide[n * i : n * i + n]
    return [part(3 * i) + part(3 * i + 1) + part(3 * i + 2) for i in range(len(tables))]


def table_of(columns):
    parts = split3(columns)
    zero = jnp.zeros((104, columns.shape[1]), F32)
    return jnp.concatenate(list(parts) + [zero], axis=0).astype(BF)


def segment_sums(onehot_rows, values):
    hi, lo = split2(values)
    return dot(onehot_rows, hi) + dot(onehot_rows, lo)


def layer_norm_parts(v):
    mu = jnp.mean(v, axis=-1, keepdims=True)
    cen = v - mu
    rs = lax.rsqrt(jnp.mean(cen * cen, axis=-1, keepdims=True) + EPS_NORM)
    return cen * rs, rs


def layer_norm_back(d, n, rs, gain):
    dg = d * gain
    return (dg - jnp.mean(dg, axis=-1, keepdims=True) - n * jnp.mean(dg * n, axis=-1, keepdims=True)) * rs


def colsum(x):
    return jnp.sum(x, axis=0, keepdims=True)


def main_kernel(
    NR,
    feat, ids, steps, cot, narrow_in, broad_in, gains_in, hidden_in,
    fout, igrad, small, out_n, out_b,
    narrow_s, broad_s, gains, hidden, smallw, packf, hgrad, hacc, ggrad,
    ngrad_s, bgrad_s, inh, inb, inq, inbq, got, bgot, gfull, bfull, s_pack, s_in, s_own, s_rows, s_all, embp, ttout, ttin, tgbuf, tgall,
    uext, gyext, metab, ohrow, keymask, idp, counts, emb, tterm, sums, squares, tabs,
    zs, nrm1, der1, u2, nrm2, der2, resid, ll1, qs, kvall,
    statin, statout,
    kt, vt, qt, ffbuf, sbuf, ebuf, otb, invl, dos, dost,
    gf, nl2, shaped, ginner, r3s, r3b, gm, att, dq,
    part, rbuf, rbuf2, sumbuf, dqkv, g2, tg, edge,
    ga_s, ga_r, gx_s, gx_r, gc_s, gc_r,
    rc_s, rc_r, rx_s, rx_r, rd_s, rd_r, rf_s, rf_r, sa_s, sa_r, sb_s, sb_r, sc_s, sc_r, tt_s, tt_r, tf_s, tf_r, to_s, to_r,
    halo_s, halo_r, cot_s, cot_r, stat_s, stat_r, kv_s, kv_r, dkv_s, dkv_r, eg_s, eg_r, r3_s, r3_r,
):
    R, T = feat.shape[0], feat.shape[1]
    gr2, dn, g3 = igrad, resid, shaped
    TX = T + 2 * OFF
    L = ids.shape[1]
    HT = T // 2
    f = lax.axis_index("frames")
    rw = lax.axis_index("rows")
    sib = f + 1 - 2 * (f % 2)
    cross = (f + 2) % 4
    diag = 3 - f
    peers = (sib, cross, diag)

    gather = NR > 0
    ngrad, bgrad = (ngrad_s, bgrad_s) if gather else (out_n, out_b)
    broad = broad_s if gather else broad_in
    if gather:
        SH, SB = narrow_in.shape[0], broad_in.shape[0]
        NB = SH // 32
        narrow_s[pl.ds(rw * NB, NB)] = narrow_in[...].astype(BF).reshape(NB, 2, 16, C)
        broad[pl.ds(pl.multiple_of(rw * SB, 16), SB), :] = broad_in[...].astype(BF)
        packf[...] = jnp.zeros(packf.shape, F32)
        packf[0:12, 0 : C // NR] = gains_in[...]
        packf[12:15, :] = hidden_in[...]
        step_f = steps[...].astype(F32)
        step_hi = jnp.floor(step_f * (1.0 / 32.0))
        for r in range(R):
            packf[15:16, NSEG * r : NSEG * r + NSEG] = step_hi[r : r + 1]
            packf[15:16, 64 + NSEG * r : 64 + NSEG * r + NSEG] = step_f[r : r + 1] - 32.0 * step_hi[r : r + 1]
        smallw[rw] = packf[...].astype(BF)
    else:
        gains[0:12, :] = gains_in[...]
        hidden[0:3, :] = hidden_in[...]

    def wn(first, n):
        if gather:
            return narrow_s[first // 32 : (first + n) // 32].reshape(n, C)
        return narrow_in[first : first + n, :]

    barrier = pltpu.get_barrier_semaphore()
    for p in peers:
        pl.semaphore_signal(barrier, inc=1, device_id=(rw, p), device_id_type=MESH)
    for k in range(1, NR):
        pl.semaphore_signal(barrier, inc=1, device_id=((rw + k) % NR, f), device_id_type=MESH)
    pl.semaphore_wait(barrier, 3 + max(NR - 1, 0))

    def remote(src, dst, ssem, rsem, target):
        return pltpu.make_async_remote_copy(
            src_ref=src, dst_ref=dst, send_sem=ssem, recv_sem=rsem,
            device_id=(rw, target), device_id_type=MESH,
        )

    if gather:
        gx, gc = f // 2, f % 2
        conv_blocks = 3 * C // 32
        own_blocks = {
            0: {0: (0, NB), 1: (NB, conv_blocks)},
            1: {1: (24, 34), 2: (34, 48)},
            4: {2: (48, 51), 3: (51, 68), 4: (68, 72), 6: (104, 119), 7: (119, 136)},
        }
        ranges = {0: ((0, 24),), 1: ((24, 48),), 4: ((48, 72), (104, 136))}
        t_lo, t_hi = 9 * C // 32, (9 * C + TE) // 32
        owners = [s for s in range(NR) if max(NB * s, t_lo) < min(NB * (s + 1), t_hi)]
        is_owner = functools.reduce(jnp.logical_or, [rw == o for o in owners])
        kinds = (0, 1, 2, 4)

        def narrow_piece(g, lo, hi):
            return narrow_s.at[lo:hi, g // 2, :, pl.ds(pl.multiple_of(g % 2 * 128, 128), 128)]

        def broad_piece(g, lo, hi):
            width = KR // 4
            return broad.at[lo:hi, pl.ds(pl.multiple_of(g * width, 128), width)]

        def to_row(ref, ssem, rsem, row):
            return pltpu.make_async_remote_copy(
                src_ref=ref, dst_ref=ref, send_sem=ssem, recv_sem=rsem, device_id=(row, f), device_id_type=MESH
            )

        def sized(kind, n):
            if kind == 2:
                return broad.at[0 : n * SB, 0 : KR // 4]
            if kind == 3:
                return smallw.at[0:n]
            return narrow_s.at[0:n, 0, :, 0:128]

        def waits(kind, n, sends, sem):
            ref = sized(kind, n)
            cp = remote(ref, ref, sem, sem, cross)
            (cp.wait_send if sends else cp.wait_recv)()

        def by_row(counts, act):
            for n in sorted(set(counts)):
                if n:
                    rows_of = [s for s in range(NR) if counts[s] == n]
                    cond = functools.reduce(jnp.logical_or, [rw == s for s in rows_of])

                    @pl.when(cond)
                    def _():
                        act(n)

        def spread_start(kind):
            if kind in own_blocks:
                for s, (lo, hi) in own_blocks[kind].items():

                    @pl.when(rw == s)
                    def _():
                        for k in range(1, NR):
                            to_row(narrow_piece(f, lo, hi), ga_s.at[kind], ga_r.at[kind], (s + k) % NR).start()

                return
            for k in range(1, NR):
                if kind == 2:
                    at = pl.ds(pl.multiple_of(rw * SB, 16), SB)
                    ref = broad.at[at, pl.ds(pl.multiple_of(f * (KR // 4), 128), KR // 4)]
                else:
                    ref = smallw.at[rw]
                to_row(ref, ga_s.at[kind], ga_r.at[kind], (rw + k) % NR).start()

        def held(kind):
            sizes = [0] * NR
            for s, (lo, hi) in own_blocks[kind].items():
                sizes[s] = hi - lo
            return sizes

        def spread_arrive(kind):
            if kind in own_blocks:
                sizes = held(kind)
                by_row([sum(sizes) - n for n in sizes], lambda n: waits(kind, n, False, ga_r.at[kind]))
            else:
                waits(kind, NR - 1, False, ga_r.at[kind])

        def spread_end(kind):
            if kind in own_blocks:
                by_row([(NR - 1) * n for n in held(kind)], lambda n: waits(kind, n, True, ga_s.at[kind]))
            else:
                waits(kind, NR - 1, True, ga_s.at[kind])

        def pieces(kind, g):
            if kind == 2:
                return [broad_piece(g, 0, C)]
            return [narrow_piece(g, lo, hi) for lo, hi in ranges[kind]]

        def units(kind):
            return NR if kind == 2 else sum(hi - lo for lo, hi in ranges[kind])

        def pass_on(kind):
            spread_arrive(kind)
            for ref in pieces(kind, f):
                remote(ref, ref, gx_s.at[kind], gx_r.at[kind], cross).start()
            for ref in pieces(kind, f):
                remote(ref, ref, gc_s.at[kind, 0], gc_r.at[kind, 0], sib).start()

        def pass_across(kind):
            waits(kind, units(kind), False, gx_r.at[kind])
            for ref in pieces(kind, cross):
                remote(ref, ref, gc_s.at[kind, 1], gc_r.at[kind, 1], sib).start()

        def arrive(kind):
            for i in range(2):
                waits(kind, units(kind), False, gc_r.at[kind, i])

        def gather_end():
            for kind in kinds:
                spread_end(kind)
                waits(kind, units(kind), True, gx_s.at[kind])
                for i in range(2):
                    waits(kind, units(kind), True, gc_s.at[kind, i])
            spread_end(3)

            @pl.when(is_owner)
            def _():
                ref = ttout.at[0 : (NR - 1) * 8 * R]
                remote(ref, ref, tt_s.at[0], tt_s.at[0], cross).wait_send()

        spread_start(3)
        spread_start(0)

    def to_next(src, dst, ssem, rsem):
        return remote(src, dst, ssem, rsem, (f + 1) % 4)

    def to_prev(src, dst, ssem, rsem):
        return remote(src, dst, ssem, rsem, (f + 3) % 4)

    feat_down = to_next(feat.at[:, pl.ds(T - 16, 16)], uext.at[:, pl.ds(OFF - 16, 16)], halo_s.at[0], halo_r.at[0])
    feat_up = to_prev(feat.at[:, pl.ds(0, 16)], uext.at[:, pl.ds(OFF + T, 16)], halo_s.at[1], halo_r.at[1])
    cot_up = to_prev(cot.at[:, pl.ds(0, 16)], gyext.at[:, pl.ds(HT, 16)], cot_s.at[0], cot_r.at[0])

    @pl.when(f < 3)
    def _():
        feat_down.start()

    @pl.when(f > 0)
    def _():
        feat_up.start()
        cot_up.start()

    uext[:, 0 : OFF - 16, :] = jnp.zeros((R, OFF - 16, C), BF)
    uext[:, OFF + T + 16 :, :] = jnp.zeros((R, TX - OFF - T - 16, C), BF)
    g2[:, 0 : OFF - 16, :] = jnp.zeros((R, OFF - 16, C), BF)
    g2[:, OFF + T + 16 :, :] = jnp.zeros((R, TX - OFF - T - 16, C), BF)

    @pl.when(f == 0)
    def _():
        edge[:, 0] = jnp.zeros((3, R, 8, C), F32)
        uext[:, OFF - 16 : OFF, :] = jnp.zeros((R, 16, C), BF)

    @pl.when(f == 3)
    def _():
        edge[:, 1] = jnp.zeros((3, R, 8, C), F32)
        uext[:, OFF + T : OFF + T + 16, :] = jnp.zeros((R, 16, C), BF)
        gyext[:, HT : HT + 16, :] = jnp.zeros((R, 16, C), BF)

    ggrad[...] = jnp.zeros(ggrad.shape, F32)
    hgrad[...] = jnp.zeros(hgrad.shape, F32)

    idp[...] = jnp.full(idp.shape, -1.0, F32)
    idp[0:R, 128 : 128 + L] = ids[...].astype(F32)
    idv = idp[0:8]
    width = idv.shape[1]
    prev_row = jnp.where(pltpu.roll(idv, 1, 1) == idv, 1.0, 0.0)
    next_row = jnp.where(pltpu.roll(idv, width - 1, 1) == idv, 1.0, 0.0)
    idp[8:16, :] = prev_row
    idp[16:24, :] = next_row
    base = pl.multiple_of(f * T, 128)
    WX = T + 256
    win = idp[:, pl.ds(base, WX)]
    win = pltpu.roll(win, WX - (128 - OFF), 1)[:, : T + 128]
    own = idp[:, pl.ds(pl.multiple_of(base + 128, 128), T)]
    for r in range(R):
        n_lane = T + 128
        row_id = jnp.broadcast_to(win[r : r + 1], (8, n_lane))
        lab = iota((8, n_lane), 0).astype(F32)
        oh = jnp.where(row_id == lab, 1.0, 0.0)
        pn = jnp.where(
            lab == 0.0,
            jnp.broadcast_to(win[8 + r : 9 + r], (8, n_lane)),
            jnp.where(lab == 1.0, jnp.broadcast_to(win[16 + r : 17 + r], (8, n_lane)), 0.0),
        )
        block = jnp.concatenate([oh, oh, oh, pn, jnp.zeros((96, n_lane), F32)], axis=0)
        turned = block.T
        metab[r] = turned[:TX].astype(BF)
        lab_own = iota((8, T), 0).astype(F32)
        ohrow[r] = jnp.where(jnp.broadcast_to(own[r : r + 1], (8, T)) == lab_own, 1.0, 0.0)
        full = jnp.broadcast_to(idv[r : r + 1, 128 : 128 + L], (8, L))
        lab_full = iota((8, L), 0).astype(F32)
        ohf = jnp.where(full == lab_full, 1.0, 0.0)
        counts[8 * r : 8 * r + 8] = jnp.broadcast_to(jnp.sum(ohf, axis=1, keepdims=True) * float(GROUP), (8, 128))
        km = jnp.concatenate([(1.0 - ohf) * MASK_FILL, jnp.zeros((120, L), F32)], axis=0)
        keymask[r] = km.T.astype(BF)

    uext[:, OFF : OFF + T, :] = feat[...]
    gyext[:, 0:HT, :] = cot[...]

    half = TE // 2
    if not gather:
        freq = jnp.exp(iota((8, half), 1).astype(F32) * (-math.log(10000.0) / half))
        for r in range(R):
            turn = jnp.broadcast_to(steps[r : r + 1, :].astype(F32), (8, NSEG))
            ang = jnp.sum(jnp.where(iota((8, NSEG), 0) == iota((8, NSEG), 1), turn, 0.0), axis=1, keepdims=True) * freq
            k, s, c = reduced_angle(ang)
            sign = 1.0 - 2.0 * (k - 2.0 * jnp.floor(k * 0.5))
            both = jnp.concatenate([s * sign, c * sign], axis=1)
            emb[8 * r : 8 * r + 8, :] = both * mish_parts(both)[0]
    tw = 9 * C

    if gather:
        spread_start(1)
        spread_start(2)
        pass_on(0)
        spread_start(4)
        spread_arrive(3)
        wide = smallw[...].astype(F32)
        gains[...] = jnp.concatenate([wide[s, :, 0 : C // NR] for s in range(NR)], axis=1)
        hidden[0:3, :] = jnp.concatenate([wide[s, 12:15, :] for s in range(NR)], axis=1)
        @pl.when(is_owner)
        def _():
            same = iota((8 * R, 8 * R), 0) == iota((8 * R, 8 * R), 1)
            column = []
            for g in range(NR):
                row = wide[g, 15:16, 0 : 8 * R] * 32.0 + wide[g, 15:16, 64 : 64 + 8 * R]
                spread = jnp.broadcast_to(row, (8 * R, 8 * R))
                column.append(jnp.sum(jnp.where(same, spread, 0.0), axis=1, keepdims=True))
            at = iota((1, SH), 1) + (NB * rw - t_lo) * 32
            low = at < half
            freq = jnp.exp(jnp.where(low, at, at - half).astype(F32) * (-math.log(10000.0) / half))
            k, si, co = reduced_angle(jnp.concatenate(column, axis=0) * freq)
            v = jnp.where(low, si, co) * (1.0 - 2.0 * (k - 2.0 * jnp.floor(k * 0.5)))
            v = jnp.where((at >= 0) & (at < TE), v * mish_parts(v)[0], 0.0)
            embp[...] = v.astype(BF)
            ttout[...] = dot(embp[...], narrow_s[pl.ds(rw * NB, NB)].reshape(SH, C))
            for k2 in range(1, NR):
                to = (rw + k2) % NR
                pltpu.make_async_remote_copy(
                    src_ref=ttout.at[pl.ds(pl.multiple_of(to * 8 * R, 8), 8 * R)], dst_ref=ttin.at[rw],
                    send_sem=tt_s.at[0], recv_sem=tt_r.at[0], device_id=(to, f), device_id_type=MESH,
                ).start()
            ttin[rw] = ttout[pl.ds(pl.multiple_of(rw * 8 * R, 8), 8 * R)]

        pass_across(0)
        arrive(0)

    def own_prev(r):
        return metab[r, OFF : OFF + T, 24:25].astype(F32)

    def own_next(r):
        return metab[r, OFF : OFF + T, 25:26].astype(F32)

    def edge_copies(which, src):
        return (
            to_next(src.at[:, pl.ds(T - 8, 8)], edge.at[which, 0], eg_s.at[which, 0], eg_r.at[which, 0]),
            to_prev(src.at[:, pl.ds(0, 8)], edge.at[which, 1], eg_s.at[which, 1], eg_r.at[which, 1]),
        )

    def send_edges(which, src):
        down_cp, up_cp = edge_copies(which, src)

        @pl.when(f < 3)
        def _():
            down_cp.start()

        @pl.when(f > 0)
        def _():
            up_cp.start()

    def await_edges(which, src):
        down_cp, up_cp = edge_copies(which, src)

        @pl.when(f < 3)
        def _():
            down_cp.wait_send()
            up_cp.wait_recv()

        @pl.when(f > 0)
        def _():
            up_cp.wait_send()
            down_cp.wait_recv()

    def stat_copies(phase):
        return [
            remote(statout.at[phase], statin.at[phase, i], stat_s.at[phase], stat_r.at[phase, i], peers[i])
            for i in range(3)
        ]

    def keep_sums(r, first, second):
        oh = ohrow[r].astype(BF)
        at = pl.ds(pl.multiple_of(8 * r, 8), 8)
        sums[at] = segment_sums(oh, first)
        squares[at] = segment_sums(oh, second)

    def send_stats(phase):
        statout[phase] = compact(sums[...], squares[...])
        for cp in stat_copies(phase):
            cp.start()

    def total_stats(phase, wait=True):
        if wait:
            for cp in stat_copies(phase):
                cp.wait_recv()
            remote(statin.at[phase], statin.at[phase], stat_s.at[phase], stat_s.at[phase], sib).wait_send()
        return (statout[phase] + statin[phase, 0] + statin[phase, 1] + statin[phase, 2]) / jnp.maximum(counts[...], 1.0)

    group_lanes = iota((8 * R, 128), 1) < G

    def norm_scale(tot):
        second = pltpu.roll(tot, 128 - G, 1)
        return jnp.where(group_lanes, lax.rsqrt(jnp.maximum(second - tot * tot, 0.0) + EPS_NORM), 0.0)

    def norm_tables(phase):
        tot = total_stats(phase)
        inv = norm_scale(tot)
        tabs[:, 0:C], tabs[:, C : 2 * C] = expand([tot * inv, inv])

    def row_table(r, width):
        return table_of(tabs[pl.ds(pl.multiple_of(8 * r, 8), 8), 0:width])

    def conv_into(r, src, first_row):
        for j in range(3):
            zs[j] = dot(src[r], wn(first_row + j * C, C))

    @pl.when(f > 0)
    def _():
        feat_down.wait_recv()

    @pl.when(f < 3)
    def _():
        feat_up.wait_recv()

    def phase_one(r):
        conv_into(r, uext, 0)
        lo, hi = OFF - 16, OFF + T + 16
        n = hi - lo
        v = (
            zs[0, lo - 1 : hi - 1] * metab[r, lo:hi, 24:25].astype(F32)
            + zs[1, lo:hi]
            + zs[2, lo + 1 : hi + 1] * metab[r, lo:hi, 25:26].astype(F32)
        )
        nrm1[r, lo:hi] = v
        nrm1[r, 0:lo] = jnp.zeros((lo, C), F32)
        nrm1[r, hi:] = jnp.zeros((TX - hi, C), F32)
        vo = v[OFF - lo : OFF - lo + T]
        keep_sums(r, vo, vo * vo)

    for r in range(R):
        phase_one(r)
        if r == R - 1:
            send_stats(0)
        if gather:
            if r == 0:
                pass_on(1)
            elif r == 1:
                pass_on(2)
                pass_across(1)

    if gather:
        arrive(1)
    if gather:

        def take_terms(n):
            remote(ttin.at[0:n], ttin.at[0:n], tt_r.at[0], tt_r.at[0], cross).wait_recv()

        by_row([len(owners) - (s in owners) for s in range(NR)], take_terms)
        total = gains[2:3, :]
        for o in owners:
            total = total + ttin[o]
        tterm[...] = total
    else:
        tterm[...] = dot(emb[...].astype(BF), wn(tw, TE)) + gains[2:3, :]

    CH = TX // 4
    tabs[:, 2 * C : 3 * C] = tterm[...]
    norm_tables(0)

    def phase_two(r, carry):
        tab = row_table(r, 3 * C)

        def chunk(i, c2):
            rows = pl.ds(pl.multiple_of(i * CH, 16), CH)
            sp = dot(metab[r, rows], tab)
            n = nrm1[r, rows] * sp[:, C : 2 * C] - sp[:, :C]
            y = n * gains[0:1, :] + gains[1:2, :]
            t, d = mish_parts(y)
            nrm1[r, rows] = n
            der1[r, rows] = d.astype(BF)
            u2[r, rows] = (y * t + sp[:, 2 * C :]).astype(BF)
            return c2

        lax.fori_loop(0, 4, chunk, 0, unroll=True)
        conv_into(r, u2, 3 * C)
        v = (
            zs[0, OFF - 1 : OFF + T - 1] * own_prev(r)
            + zs[1, OFF : OFF + T]
            + zs[2, OFF + 1 : OFF + T + 1] * own_next(r)
        )
        nrm2[r] = v
        keep_sums(r, v, v * v)
        return carry

    lax.fori_loop(0, R, phase_two, 0)
    send_stats(1)
    if gather:
        pass_across(2)
        pass_on(4)
        arrive(2)
    norm_tables(1)

    def kv_copies(r):
        slot = lambda g: kvall.at[r, :, pl.ds(pl.multiple_of(g * T, 128), T)]
        mine, other = slot(f), slot(cross)
        return (
            remote(mine, mine, kv_s.at[0, r], kv_r.at[0, r], sib),
            remote(mine, mine, kv_s.at[1, r], kv_r.at[1, r], cross),
            remote(other, other, kv_s.at[2, r], kv_r.at[2, r], sib),
        )

    NCH = 4
    CT = T // NCH

    def phase_three(r, carry):
        tab = row_table(r, 2 * C)

        def chunk(i, c2):
            rows = pl.ds(pl.multiple_of(i * CT, 16), CT)
            xrows = pl.ds(pl.multiple_of(OFF + i * CT, 16), CT)
            sp = dot(metab[r, xrows], tab)
            n = nrm2[r, rows] * sp[:, C : 2 * C] - sp[:, :C]
            y = n * gains[3:4, :] + gains[4:5, :]
            t, d = mish_parts(y)
            nrm2[r, rows] = n
            der2[r, rows] = d.astype(BF)
            res = y * t + feat[r, rows].astype(F32)
            resid[r, rows] = res
            m, rs = layer_norm_parts(res)
            low = (m * gains[5:6, :] + gains[6:7, :]).astype(BF)
            ll1[r, rows] = low
            qkv = dot(low, broad[:, : 3 * INNER])
            qs[r, rows] = (qkv[:, :INNER].astype(BF).astype(F32) * HD ** (-0.5)).astype(BF)
            krows = pl.ds(pl.multiple_of(f * T + i * CT, 16), CT)
            kvall[r, 0, krows] = qkv[:, INNER : 2 * INNER].astype(BF)
            kvall[r, 1, krows] = qkv[:, 2 * INNER :].astype(BF)
            return c2

        lax.fori_loop(0, NCH, chunk, 0, unroll=True)
        if gather:

            @pl.when(r == 0)
            def _():
                pass_across(4)

        cps = kv_copies(r)
        cps[1].start()
        cps[0].start()
        return carry

    lax.fori_loop(0, R, phase_three, 0)
    send_edges(2, nrm2)

    @pl.when(f < 3)
    def _():
        cot_up.wait_recv()

    down = 6 * C

    def phase_down_back(r, carry):
        gy = gyext[r, 0:HT]
        even = dot_nt(gy, wn(down + C, C))
        own_gy = dot_nt(gy, wn(down + 2 * C, C))
        nxt = dot_nt(gyext[r], wn(down, C))
        zs[0, 0 : HT + 16] = nxt
        for hh in range(2):
            cols = slice(hh * 128, hh * 128 + 128)
            pm = r3s[2, pl.ds(8 + 1, HT, stride=2), :]
            nm = r3s[3, pl.ds(8 + 1, HT, stride=2), :]
            r3s[hh, pl.ds(8, HT, stride=2), :] = even[:, cols]
            r3s[hh, pl.ds(9, HT, stride=2), :] = own_gy[:, cols] * pm + zs[0, 1 : HT + 1, cols] * nm
        return carry

    def masks_strided(r):
        r3s[2, 8 : 8 + T] = jnp.broadcast_to(own_prev(r), (T, 128))
        r3s[3, 8 : 8 + T] = jnp.broadcast_to(own_next(r), (T, 128))

    def down_back(r, carry):
        masks_strided(r)
        phase_down_back(r, carry)
        ggrad[11:12, :] += colsum(gyext[r, 0:HT].astype(F32))
        for hh in range(2):
            gf[r, :, hh * 128 : hh * 128 + 128] = r3s[hh, 8 : 8 + T].astype(BF)
        ggrad[10:11, :] += colsum(gf[r].astype(F32))
        return carry

    if gather:
        arrive(4)
    lax.fori_loop(0, R, down_back, 0)

    def relay(r):
        cps = kv_copies(r)
        cps[1].wait_recv()
        cps[2].start()

    relay(0)
    if gather:
        gather_end()

    alpha = jnp.exp(hidden[1:2, :])
    inv_beta = jnp.exp(-hidden[2:3, :])
    alpha_beta = alpha * inv_beta
    alpha_pi = alpha * (1.0 / math.pi)
    NK = L // 256
    CF = T
    hacc[...] = jnp.zeros(hacc.shape, F32)
    lane128 = iota((T, 128), 1)

    def dkv_copies(r):
        return (
            remote(part.at[r, sib], rbuf.at[r, 0], dkv_s.at[0, r], dkv_r.at[0, r], sib),
            remote(part.at[r, diag], rbuf.at[r, 1], dkv_s.at[1, r], dkv_r.at[1, r], sib),
            remote(sumbuf.at[r], rbuf2.at[r], dkv_s.at[2, r], dkv_r.at[2, r], cross),
        )

    def phase_sum(r):
        cps = dkv_copies(r)
        cps[1].wait_recv()
        sumbuf[r] = (part[r, cross].astype(F32) + rbuf[r, 1].astype(F32)).astype(BF)
        cps[2].start()

    def phase_four(r, carry):
        cps = kv_copies(r)
        cps[0].wait_recv()
        cps[2].wait_recv()
        for cp in cps:
            cp.wait_send()
        kt[...] = kvall[r, 0].T
        vt[...] = kvall[r, 1].T
        qv = qs[r]
        ohq = jnp.where(lane128 < 8, metab[r, OFF : OFF + T], jnp.zeros((T, 128), BF))
        zero_q = jnp.zeros((T, 128), BF)
        q_heads = [jnp.where(lane128 // HD == h, qv, zero_q) for h in range(H)]
        TQ = T // 2
        units = [(h, q) for h in range(H) for q in range(2)]

        def scores(n):
            h, q = units[n]
            qrows = slice(q * TQ, q * TQ + TQ)
            qa = jnp.concatenate([q_heads[h][qrows], ohq[qrows]], axis=1)
            m8 = jnp.full((8, TQ), -3e38, F32)
            for i in range(NK):
                keys = slice(i * 256, i * 256 + 256)
                ka = jnp.concatenate([kvall[r, 0, keys], keymask[r, keys]], axis=1)
                sc = dot_nt(ka, qa)
                sbuf[n % 2, keys] = sc
                m8 = jnp.maximum(m8, jnp.max(sc.reshape(32, 8, TQ), axis=0))
            return jnp.max(m8, axis=0, keepdims=True)

        top = scores(0)
        for n, (h, q) in enumerate(units):
            later = scores(n + 1) if n + 1 < len(units) else None
            qcols = slice(q * TQ, q * TQ + TQ)
            l8 = jnp.zeros((8, TQ), F32)
            for i in range(NK):
                keys = slice(i * 256, i * 256 + 256)
                e = jnp.exp(sbuf[n % 2, keys] - top)
                ebuf[h, keys, qcols] = e.astype(BF)
                l8 = l8 + jnp.sum(e.reshape(32, 8, TQ), axis=0)
            inv = 1.0 / jnp.sum(l8, axis=0, keepdims=True)
            invl[h, :, qcols] = jnp.broadcast_to(inv, (8, TQ))
            hrows = slice(h * HD, (h + 1) * HD)
            otb[hrows, qcols] = dot(vt[hrows, :], ebuf[h, :, qcols]) * inv
            top = later
        att[r] = otb[...].T.astype(BF)

        @pl.when(r + 1 < R)
        def _():
            relay(r + 1)

        def ff_chunk(i, c2):
            rows = pl.ds(pl.multiple_of(i * CF, 16), CF)
            res2 = resid[r, rows] + (dot_nt(att[r, rows], broad[:, 3 * INNER : 4 * INNER]) + gains[7:8, :])
            n, rs = layer_norm_parts(res2)
            low = (n * gains[8:9, :] + gains[9:10, :]).astype(BF)
            nl2[r, rows] = low
            gfr = gf[r, rows]
            def products(b):
                w_in = broad[:, 4 * INNER + b * 256 : 4 * INNER + b * 256 + 256]
                w_out = wn(tw + TE + b * 256, 256)
                ffbuf[b % 2, 0] = dot(low, w_in)
                ffbuf[b % 2, 1] = dot_nt(gfr, w_out)
                return w_in, w_out

            out, back = None, None
            weights = products(0)
            for b in range(4):
                following = products(b + 1) if b < 3 else None
                cols = slice(b * 256, b * 256 + 256)
                acc = [hacc[k, :, cols] for k in range(3)]
                shs, gis = [], []
                for u in range(0, CF, 32):
                    inner = ffbuf[b % 2, 0, u : u + 32] + hidden[0:1, cols]
                    gs = ffbuf[b % 2, 1, u : u + 32]
                    s, c = sine_pair(inner * alpha_pi[:, cols])
                    s2 = s * s
                    part_g = gs * (s * c)
                    shs.append((inner + s2 * inv_beta[:, cols]).astype(BF))
                    gi = gs + part_g * alpha_beta[:, cols]
                    gis.append(gi.astype(BF))
                    for k, v in enumerate((gi, part_g * inner, gs * s2)):
                        acc[k] = acc[k] + jnp.sum(v.reshape(4, 8, 256), axis=0)
                for k in range(3):
                    hacc[k, :, cols] = acc[k]
                sh_all, gi_all = jnp.concatenate(shs, axis=0), jnp.concatenate(gis, axis=0)
                shaped[r, rows, cols] = sh_all
                ginner[r, rows, cols] = gi_all
                more, more_back = dot(sh_all, weights[1]), dot_nt(gi_all, weights[0])
                out = more if out is None else out + more
                back = more_back if back is None else back + more_back
                weights = following
            r3 = (res2 + (out + gains[10:11, :])).astype(BF)
            r3b[r, rows] = r3
            g_in = gfr.astype(F32)
            ggrad[8:9, :] += colsum(back * n)
            ggrad[9:10, :] += colsum(back)
            g_res2 = g_in + layer_norm_back(back, n, rs, gains[8:9, :])
            gr2[r, rows] = g_res2
            low_g = g_res2.astype(BF)
            gm[r, rows] = low_g
            ggrad[7:8, :] += colsum(low_g.astype(F32))
            dos[rows] = dot(low_g, broad[:, 3 * INNER : 4 * INNER]).astype(BF).astype(F32)
            return c2

        lax.fori_loop(0, T // CF, ff_chunk, 0)

        @pl.when(f < 3)
        def _():
            to_next(r3b.at[r, pl.ds(T - 16, 16)], r3b.at[r, pl.ds(T, 16)], r3_s.at[r], r3_r.at[r]).start()

        dot_t = dos[...].T
        for h in range(H):
            hrows = slice(h * HD, (h + 1) * HD)
            dost[hrows, :] = dot_t[hrows] * invl[h, 0:1, :]
        zero_t = jnp.zeros((HD, T), BF)
        d_rows, d_cols, d_half = [], [], []
        per_block = T // 256
        for h in range(H):
            hrows = slice(h * HD, (h + 1) * HD)
            d_rows.append(colsum(otb[hrows, :] * dost[hrows, :]))
            dh = dost[hrows, :].astype(BF)
            d_half.append(dh)
            d_cols.append(jnp.concatenate([dh, zero_t] if h == 0 else [zero_t, dh], axis=0))
        qt[...] = qs[r].T
        cps = dkv_copies(r)
        for n, block in enumerate((diag, sib, cross, f)):
            for i in range(per_block):
                keys = pl.ds(pl.multiple_of(block * T + i * 256, 256), 256)
                within = slice(i * 256, i * 256 + 256)
                for h in range(H):
                    hrows = slice(h * HD, (h + 1) * HD)
                    eh = ebuf[h, keys]
                    dp = dot(kvall[r, 1, keys], d_cols[h])
                    ds = (eh.astype(F32) * (dp - d_rows[h])).astype(BF)
                    part[r, block, 0, hrows, within] = dot_nt(qt[hrows, :], ds).astype(BF)
                    part[r, block, 1, hrows, within] = dot_nt(d_half[h], eh).astype(BF)
                    if n == 0 and i == 0:
                        dq[hrows, :] = dot(kt[hrows, keys], ds)
                    else:
                        dq[hrows, :] += dot(kt[hrows, keys], ds)
            if n == 0:
                cps[1].start()
            elif n == 1:
                cps[0].start()
            elif n == 2:
                phase_sum(r)
        dqkv[r, :, 0:INNER] = (dq[...].T * HD ** (-0.5)).astype(BF)
        return carry

    lax.fori_loop(0, R, phase_four, 0)

    if gather:
        rx, rc = f // 2, f % 2
        shard_blocks = NB
        n_groups = {1: ((48, 72), (104, 136)), 2: ((24, 48),), 3: ((0, 24),)}
        b_groups = {1: (4 * INNER, 2 * C), 2: (0, C)}
        b_at = {1: C, 2: 0}

        def half_cols(core, first, n):
            return pl.ds(pl.multiple_of(first + core * n, 128), n)

        def core_copies(g):
            out = [
                remote(ngrad.at[lo:hi, :, :, half_cols(1 - rc, 0, 128)], inh.at[lo:hi], rc_s.at[g - 1, i], rc_r.at[g - 1, i], sib)
                for i, (lo, hi) in enumerate(n_groups[g])
            ]
            if g in b_groups:
                first, n = b_groups[g]
                out.append(
                    remote(
                        bgrad.at[:, :, :, half_cols(1 - rc, first, n)], inb.at[:, :, :, b_at[g] : b_at[g] + n],
                        rc_s.at[g - 1, 2], rc_r.at[g - 1, 2], sib,
                    )
                )
            return out

        def cross_copies(g):
            out = [
                remote(ngrad.at[lo:hi, 1 - rx, :, half_cols(rc, 0, 128)], inq.at[lo:hi], rx_s.at[g - 1, i], rx_r.at[g - 1, i], cross)
                for i, (lo, hi) in enumerate(n_groups[g])
            ]
            if g in b_groups:
                first, n = b_groups[g]
                out.append(
                    remote(
                        bgrad.at[:, 1 - rx, :, half_cols(rc, first, n)], inbq.at[:, :, b_at[g] : b_at[g] + n],
                        rx_s.at[g - 1, 2], rx_r.at[g - 1, 2], cross,
                    )
                )
            return out

        def owner_copies(g, s, source):
            out = []
            for i, (lo, hi) in enumerate(n_groups[g]):
                a, b = max(lo, shard_blocks * s), min(hi, shard_blocks * (s + 1))
                if a < b:
                    out.append(
                        pltpu.make_async_remote_copy(
                            src_ref=ngrad.at[a:b, rx, :, half_cols(rc, 0, 128)],
                            dst_ref=got.at[source, a - shard_blocks * s : b - shard_blocks * s],
                            send_sem=rd_s.at[g - 1, 0], recv_sem=rd_r.at[g - 1, 0],
                            device_id=(s, f), device_id_type=MESH,
                        )
                    )
            if g in b_groups:
                first, n = b_groups[g]
                out.append(
                    pltpu.make_async_remote_copy(
                        src_ref=bgrad.at[s, rx, :, half_cols(rc, first, n)],
                        dst_ref=bgot.at[source, :, b_at[g] : b_at[g] + n],
                        send_sem=rd_s.at[g - 1, 1], recv_sem=rd_r.at[g - 1, 1],
                        device_id=(s, f), device_id_type=MESH,
                    )
                )
            return out

        def red_core(g):
            for cp in core_copies(g):
                cp.start()

        def red_cross(g):
            for cp in core_copies(g):
                cp.wait()
            mine = half_cols(rc, 0, 128)
            for lo, hi in n_groups[g]:
                ngrad[lo:hi, :, :, mine] = (ngrad[lo:hi, :, :, mine].astype(F32) + inh[lo:hi].astype(F32)).astype(BF)
            if g in b_groups:
                first, n = b_groups[g]
                cols = half_cols(rc, first, n)
                other = inb[:, :, :, b_at[g] : b_at[g] + n]
                bgrad[:, :, :, cols] = (bgrad[:, :, :, cols].astype(F32) + other.astype(F32)).astype(BF)
            for cp in cross_copies(g):
                cp.start()

        def red_owner(g):
            for cp in cross_copies(g):
                cp.wait()
            mine = half_cols(rc, 0, 128)
            for lo, hi in n_groups[g]:
                ngrad[lo:hi, rx, :, mine] = (ngrad[lo:hi, rx, :, mine].astype(F32) + inq[lo:hi].astype(F32)).astype(BF)
            if g in b_groups:
                first, n = b_groups[g]
                cols = half_cols(rc, first, n)
                other = inbq[:, :, b_at[g] : b_at[g] + n]
                bgrad[:, rx, :, cols] = (bgrad[:, rx, :, cols].astype(F32) + other.astype(F32)).astype(BF)
            for s in range(NR):

                @pl.when(rw != s)
                def _():
                    for cp in owner_copies(g, s, rw):
                        cp.start()

        def red_wait(g):
            overlap = [
                sum(max(0, min(hi, NB * (s + 1)) - max(lo, NB * s)) for lo, hi in n_groups[g]) for s in range(NR)
            ]

            def take(n, sends, sem):
                cp = remote(inq.at[0:n], inq.at[0:n], sem, sem, cross)
                (cp.wait_send if sends else cp.wait_recv)()

            by_row([sum(overlap) - n for n in overlap], lambda n: take(n, True, rd_s.at[g - 1, 0]))
            by_row([(NR - 1) * n for n in overlap], lambda n: take(n, False, rd_r.at[g - 1, 0]))
            if g in b_groups:
                ref = bgot.at[0 : NR - 1, :, b_at[g] : b_at[g] + b_groups[g][1]]
                cp = remote(ref, ref, rd_s.at[g - 1, 1], rd_r.at[g - 1, 1], cross)
                cp.wait_send()
                cp.wait_recv()

        def send_final(j, blk, size):
            for p in peers:
                remote(blk, blk, rf_s.at[j], rf_r.at[j], p).start()
            return remote(size, size, rf_s.at[j], rf_r.at[j], cross)

        def red_finish_broad():
            out = []
            for j, g in enumerate((1, 2)):
                cols = half_cols(rc, *b_groups[g])
                here = slice(b_at[g], b_at[g] + b_groups[g][1])
                total = bgrad[rw, rx, :, cols].astype(F32)
                for k in range(1, NR):
                    total = total + bgot[(rw + k) % NR, :, here].astype(F32)
                bfull[rx, :, cols] = total.astype(BF)
                out.append(send_final(j, bfull.at[rx, :, cols], bgot.at[0:3, :, here]))
            return out

        def red_finish_narrow():
            mine = half_cols(rc, 0, 128)
            total = ngrad[pl.ds(shard_blocks * rw, shard_blocks), rx, :, mine].astype(F32)
            for k in range(1, NR):
                total = total + got[(rw + k) % NR].astype(F32)
            gfull[:, rx, :, mine] = total.astype(BF)
            return [send_final(2, gfull.at[:, rx, :, mine], inq.at[0 : 3 * NB])]

        def terms_first():
            tgbuf[f] = tg[...]
            for p in peers:
                remote(tgbuf.at[f], tgbuf.at[f], tf_s.at[0], tf_r.at[0], p).start()

        def terms_second():
            remote(tgbuf.at[0:3], tgbuf.at[0:3], tf_s.at[0], tf_r.at[0], cross).wait()
            tgall[rw] = tgbuf[0] + tgbuf[1] + tgbuf[2] + tgbuf[3]
            for o in owners:

                @pl.when(rw != o)
                def _():
                    pltpu.make_async_remote_copy(
                        src_ref=tgall.at[rw], dst_ref=tgall.at[rw], send_sem=to_s.at[0], recv_sem=to_r.at[0],
                        device_id=(o, f), device_id_type=MESH,
                    ).start()

        def terms_third():
            def sent(n):
                remote(tgall.at[0:n], tgall.at[0:n], to_s.at[0], to_s.at[0], cross).wait_send()

            by_row([len(owners) - (s in owners) for s in range(NR)], sent)

            @pl.when(is_owner)
            def _():
                ref = tgall.at[0 : NR - 1]
                remote(ref, ref, to_r.at[0], to_r.at[0], cross).wait_recv()
                hi, lo = split2(tgall[...].reshape(NR * 8 * R, C))
                grad = (dot_tn(embp[...], hi) + dot_tn(embp[...], lo)).astype(BF).reshape(NB, 2, 16, C)
                for o in owners:
                    a, b = max(NB * o, t_lo) - NB * o, min(NB * (o + 1), t_hi) - NB * o

                    @pl.when(rw == o)
                    def _():
                        out_n[a:b] = grad[a:b]

        def small_first():
            s_pack[...] = small_rows()
            for i, p in enumerate(peers):
                remote(s_pack.at[pl.ds(pl.multiple_of(8 * p, 8), 8)], s_in.at[i], sa_s.at[0], sa_r.at[0], p).start()

        def small_second():
            remote(s_in, s_in, sa_s.at[0], sa_r.at[0], sib).wait()
            s_own[...] = s_pack[pl.ds(pl.multiple_of(8 * f, 8), 8)] + s_in[0] + s_in[1] + s_in[2]
            for k in range(1, NR):
                pltpu.make_async_remote_copy(
                    src_ref=s_own, dst_ref=s_rows.at[k - 1], send_sem=sb_s.at[0], recv_sem=sb_r.at[0],
                    device_id=((rw + k) % NR, f), device_id_type=MESH,
                ).start()

        def small_third():
            ref = s_rows.at[0 : NR - 1]
            remote(ref, ref, sb_s.at[0], sb_r.at[0], sib).wait()
            at = pl.ds(pl.multiple_of(8 * f, 8), 8)
            tot = s_own[...]
            for k in range(1, NR):
                tot = tot + s_rows[k - 1]
            s_all[at] = tot
            for p in peers:
                remote(s_all.at[at], s_all.at[at], sc_s.at[0], sc_r.at[0], p).start()

        def small_last():
            remote(s_in, s_in, sc_s.at[0], sc_r.at[0], sib).wait()

    def small_rows():
        hid = [hgrad[k : k + 1, q * C : (q + 1) * C] for k in range(3) for q in range(FF // C)]
        return jnp.concatenate([ggrad[...]] + hid + [jnp.zeros((4, C), F32)], axis=0)

    flat = lambda ref: ref[...].reshape(R * T, ref.shape[2])

    def put_n(first, value):
        n = value.shape[0]
        ngrad[first // 32 : (first + n) // 32] = value.astype(BF).reshape(n // 32, 2, 16, C)

    def put_b(first, value):
        bgrad[:, :, :, first : first + value.shape[1]] = value.astype(BF).reshape(C // 32, 2, 16, value.shape[1])

    zs[:, 0:C, :] = jnp.zeros((3, C, C), F32)

    def down_forward(r, carry):
        @pl.when(f > 0)
        def _():
            to_next(r3b.at[r, pl.ds(T - 16, 16)], r3b.at[r, pl.ds(T, 16)], r3_s.at[r], r3_r.at[r]).wait_recv()

        @pl.when(f < 3)
        def _():
            to_next(r3b.at[r, pl.ds(T - 16, 16)], r3b.at[r, pl.ds(T, 16)], r3_s.at[r], r3_r.at[r]).wait_send()

        @pl.when(f == 0)
        def _():
            r3b[r, T : T + 16, :] = jnp.zeros((16, C), BF)

        masks_strided(r)
        for hh in range(2):
            cols = slice(hh * 128, hh * 128 + 128)
            r3s[hh, 8 : 8 + T] = r3b[r, 0:T, cols].astype(F32)
            r3s[hh, 0:8] = r3b[r, T : T + 16, cols].astype(F32)[8:16]
        even = jnp.concatenate([r3s[hh, pl.ds(8, HT, stride=2), :] for hh in range(2)], axis=1).astype(BF)
        m_after = r3s[3, pl.ds(8, HT, stride=2), :]
        m_before = r3s[2, pl.ds(8, HT, stride=2), :]
        odd = jnp.concatenate([r3s[hh, pl.ds(9, HT, stride=2), :] * m_after for hh in range(2)], axis=1).astype(BF)
        before = jnp.concatenate([r3s[hh, pl.ds(7, HT, stride=2), :] * m_before for hh in range(2)], axis=1).astype(BF)
        gy = cot[r]
        out = gains[11:12, :]
        for j, blk in enumerate((before, even, odd)):
            out = out + dot(blk, wn(down + j * C, C))
            zs[j, 0:C, :] += dot_tn(blk, gy)
        fout[r] = out.astype(BF)
        return carry

    lax.fori_loop(0, R, down_forward, 0)
    for j in range(3):
        put_n(down + j * C, zs[j, 0:C, :])

    gf_all = flat(gf)
    for b in range(4):
        cols = slice(b * 256, b * 256 + 256)
        put_n(tw + TE + b * 256, dot_tn(shaped[:, :, cols].reshape(R * T, 256), gf_all))
        put_b(4 * INNER + b * 256, dot_tn(flat(nl2), ginner[:, :, cols].reshape(R * T, 256)))
    put_b(3 * INNER, dot_tn(flat(gm), flat(att)))
    hgrad[0:1, :] = colsum(hacc[0])
    hgrad[1:2, :] = colsum(hacc[1]) * alpha_beta
    hgrad[2:3, :] = colsum(hacc[2]) * (-inv_beta)
    if gather:
        red_core(1)

    def mean_tables(phase, norm_phase, gain_row):
        tot = total_stats(phase)
        iv = norm_scale(total_stats(norm_phase, wait=False))
        m1 = jnp.where(group_lanes, tot, 0.0)
        m2 = jnp.where(group_lanes, pltpu.roll(tot, 128 - G, 1), 0.0)
        tabs[:, 0:C], tabs[:, C : 2 * C], wide_iv = expand([m1 * iv, m2 * iv, iv])
        tabs[:, 2 * C : 3 * C] = wide_iv * gains[gain_row : gain_row + 1, :]

    def norm_back_start(r, gain_row):
        oh = ohrow[r].astype(BF)
        at = pl.ds(pl.multiple_of(8 * r, 8), 8)
        gain = gains[gain_row : gain_row + 1, :]
        first, second = segment_sums(oh, dn[r]), segment_sums(oh, zs[0, 0:T])
        ggrad[gain_row : gain_row + 1, :] += colsum(second)
        ggrad[gain_row + 1 : gain_row + 2, :] += colsum(first)
        sums[at], squares[at] = first * gain, second * gain

    def fold(x):
        return jnp.sum(x.reshape(x.shape[0] // 8, 8, x.shape[1]), axis=0)

    def phase_five(r, carry):
        cps = dkv_copies(r)
        cps[0].wait_recv()
        cps[2].wait_recv()
        for cp in cps:
            cp.wait_send()
        for i in range(2):
            tot = part[r, f, i].astype(F32) + rbuf[r, 0, i].astype(F32) + rbuf2[r, i].astype(F32)
            dqkv[r, :, (i + 1) * INNER : (i + 2) * INNER] = tot.T.astype(BF)
        zs[1, 0:T] = dot_nt(dqkv[r], broad[:, : 3 * INNER])
        acc_n = jnp.zeros((8, C), F32)
        acc = jnp.zeros((8, C), F32)
        for u in range(0, T, 64):
            rows = slice(u, u + 64)
            back = zs[1, rows]
            n, rs = layer_norm_parts(resid[r, rows])
            acc_n = acc_n + fold(back * n)
            acc = acc + fold(back)
            g_res = gr2[r, rows] + layer_norm_back(back, n, rs, gains[5:6, :])
            gr2[r, rows] = g_res
            d = g_res * der2[r, rows].astype(F32)
            dn[r, rows] = d
            zs[0, rows] = d * nrm2[r, rows]
        ggrad[5:6, :] += colsum(acc_n)
        ggrad[6:7, :] += colsum(acc)
        norm_back_start(r, 3)
        return carry

    lax.fori_loop(0, R, phase_five, 0)
    send_stats(2)
    send_edges(1, dn)
    if gather:
        red_cross(1)
    put_b(0, dot_tn(flat(ll1), flat(dqkv)))
    mean_tables(2, 1, 3)
    await_edges(2, nrm2)
    await_edges(1, dn)

    def norm_back_end(r, n, which, n_above, n_below):
        tab = row_table(r, 3 * C)

        def back(rows, d, norm):
            sp = dot(metab[r, rows], tab)[-d.shape[0] :] if rows.stop == OFF else dot(metab[r, rows], tab)[: d.shape[0]]
            return d * sp[:, 2 * C :] - sp[:, :C] - norm * sp[:, C : 2 * C]

        zero = jnp.zeros((8, C), F32)
        above = back(slice(OFF - 16, OFF), edge[which, 0, r], n_above)
        below = back(slice(OFF + T, OFF + T + 16), edge[which, 1, r], n_below)
        g2[r, OFF - 16 : OFF] = jnp.concatenate([zero, above], axis=0).astype(BF)
        g2[r, OFF + T : OFF + T + 16] = jnp.concatenate([below, zero], axis=0).astype(BF)
        for u in range(0, T, 128):
            rows = slice(OFF + u, OFF + u + 128)
            g2[r, rows] = back(rows, dn[r, u : u + 128], n[u : u + 128]).astype(BF)

    def build_g3(r):
        g = g2[r].astype(F32)
        zs[0] = g * metab[r, :, 24:25].astype(F32)
        zs[2] = g * metab[r, :, 25:26].astype(F32)
        g3[r, :, 0:C] = zs[0, OFF + 1 : OFF + T + 1].astype(BF)
        g3[r, :, C : 2 * C] = g2[r, OFF : OFF + T]
        g3[r, :, 2 * C : 3 * C] = zs[2, OFF - 1 : OFF + T - 1].astype(BF)

    def conv_back(r, first_row):
        out = jnp.zeros((T, C), F32)
        for j in range(3):
            out = out + dot_nt(g3[r, :, j * C : (j + 1) * C], wn(first_row + j * C, C))
        return out

    def kernel_grad(src, first_row):
        u = src[:, OFF : OFF + T, :].reshape(R * T, C)
        for j in range(3):
            put_n(first_row + j * C, dot_tn(u, g3[:, :, j * C : (j + 1) * C].reshape(R * T, C)))

    def phase_seven(r, carry):
        norm_back_end(r, nrm2[r], 1, edge[2, 0, r], edge[2, 1, r])
        build_g3(r)
        gh = conv_back(r, 3 * C)
        oh = ohrow[r].astype(BF)
        tgr = segment_sums(oh, gh)
        tg[pl.ds(pl.multiple_of(8 * r, 8), 8), :] = tgr
        ggrad[2:3, :] += colsum(tgr)
        for u in range(0, T, 64):
            d = gh[u : u + 64] * der1[r, OFF + u : OFF + u + 64].astype(F32)
            dn[r, u : u + 64] = d
            zs[0, u : u + 64] = d * nrm1[r, OFF + u : OFF + u + 64]
        norm_back_start(r, 0)
        return carry

    lax.fori_loop(0, R, phase_seven, 0)
    send_stats(3)
    send_edges(0, dn)
    if gather:
        terms_first()
        red_owner(1)
    kernel_grad(u2, 3 * C)
    if gather:
        red_core(2)
        terms_second()
    else:
        part_hi, part_lo = split2(tg[...])
        eb = emb[...].astype(BF)
        put_n(tw, dot_tn(eb, part_hi) + dot_tn(eb, part_lo))
    mean_tables(3, 0, 0)
    await_edges(0, dn)

    if gather:
        small_first()
        red_cross(2)
    else:
        small[...] = small_rows()

    def phase_g3(r, carry):
        norm_back_end(
            r, nrm1[r, OFF : OFF + T], 0, nrm1[r, OFF - 8 : OFF], nrm1[r, OFF + T : OFF + T + 8]
        )
        build_g3(r)
        return carry

    lax.fori_loop(0, R, phase_g3, 0)
    kernel_grad(uext, 0)
    if gather:
        red_core(3)
        small_second()
        red_owner(2)
        red_cross(3)
    for r in range(R):
        igrad[r] = gr2[r] + conv_back(r, 0)
        if gather and r == 1:
            red_owner(3)
    if gather:
        small_third()
        red_wait(1)
        red_wait(2)
        fin = red_finish_broad()
        red_wait(3)
        fin += red_finish_narrow()
        small_last()
        small[...] = s_all[...]
        for cp in fin:
            cp.wait()
        out_n[...] = gfull[...]
        out_b[...] = bfull[...]
        terms_third()

    @pl.when(f < 3)
    def _():
        feat_down.wait_send()

    @pl.when(f > 0)
    def _():
        feat_up.wait_send()
        cot_up.wait_send()


def run_main(fused, feat, ids, steps, cot, narrow, broad, gains, hidden):
    R, T, _ = feat.shape
    L = ids.shape[1]
    TX = T + 2 * OFF
    NR = fused
    vm = lambda shape, dt=F32: pltpu.VMEM(shape, dt)
    dma = lambda *shape: pltpu.SemaphoreType.DMA(shape)
    slots = max(NR, 1)
    if NR:
        wide = [vm((KC // 32, 2, 16, C), BF), vm((C, KR), BF)]
        red = [
            vm((KC // 32, 2, 16, C), BF), vm((C // 32, 2, 16, KR), BF), vm((KC // 32, 2, 16, 128), BF),
            vm((C // 32, 2, 16, KR // 2), BF), vm((KC // 32, 16, 128), BF), vm((C // 32, 16, KR // 2), BF),
            vm((NR, KC // NR // 32, 16, 128), BF), vm((NR, 16, KR // 2), BF),
            vm((KC // NR // 32, 2, 16, C), BF), vm((2, 16, KR), BF),
        ]
        outs = ((KC // NR // 32, 2, 16, C), (2, 16, KR))
    else:
        wide = [vm((16, 128), BF)] * 2
        red = [vm((16, 128), BF)] * 10
        outs = ((KC // 32, 2, 16, C), (C // 32, 2, 16, KR))
    scratch = wide + [
        vm((16, C)), vm((8, FF)), vm((slots, 16, 128), BF), vm((16, 128)), vm((8, FF)), vm((3, 8, FF)), vm((16, C)),
    ] + red + [
        vm((32, C)), vm((3, 8, C)), vm((8, C)), vm((slots, 8, C)), vm((32, C)),
        vm((slots * 8 * R, KC // slots if NR else 128), BF), vm((slots * 8 * R, C)), vm((slots, 8 * R, C)), vm((4, 8 * R, C)), vm((slots, 8 * R, C)),
        vm((R, TX, C), BF), vm((R, T // 2 + 16, C), BF), vm((R, TX, 128), BF),
        vm((R, 8, T)), vm((R, L, 128), BF), vm((24, L + 256)), vm((8 * R, 128)), vm((8 * R, TE)), vm((8 * R, C)),
        vm((8 * R, C)), vm((8 * R, C)), vm((8 * R, 3 * C)),
        vm((3, TX, C)), vm((R, TX, C)), vm((R, TX, C), BF), vm((R, TX, C), BF), vm((R, T, C)),
        vm((R, T, C), BF), vm((R, T, C)), vm((R, T, C), BF), vm((R, T, INNER), BF),
        vm((R, 2, L, INNER), BF),
        vm((4, 3, 8 * R, 128)), vm((4, 8 * R, 128)),
        vm((INNER, L), BF), vm((INNER, L), BF), vm((INNER, T), BF), vm((2, 2, T, C)), vm((2, L, T // 2)), vm((H, L, T), BF), vm((INNER, T)),
        vm((H, 8, T)), vm((T, INNER)), vm((INNER, T)),
        vm((R, T, C), BF), vm((R, T, C), BF),
        vm((R, T, FF), BF), vm((R, T, FF), BF), vm((4, T + 8, 128)), vm((R, T + 16, C), BF),
        vm((R, T, C), BF), vm((R, T, INNER), BF), vm((INNER, T)),
        vm((R, 4, 2, INNER, T), BF), vm((R, 2, 2, INNER, T), BF), vm((R, 2, INNER, T), BF), vm((R, 2, INNER, T), BF),
        vm((R, T, 3 * INNER), BF), vm((R, TX, C), BF), vm((8 * R, C)), vm((3, 2, R, 8, C)),
        dma(5), dma(5), dma(5), dma(5), dma(5, 2), dma(5, 2),
        dma(3, 3), dma(3, 3), dma(3, 3), dma(3, 3), dma(3, 2), dma(3, 2), dma(3), dma(3),
        dma(1), dma(1), dma(1), dma(1), dma(1), dma(1), dma(1), dma(1), dma(1), dma(1), dma(1), dma(1),
        dma(2), dma(2), dma(1), dma(1), dma(4), dma(4, 3), dma(3, R), dma(3, R),
        dma(3, R), dma(3, R), dma(3, 2), dma(3, 2), dma(R), dma(R),
    ]
    out_shape = (
        jax.ShapeDtypeStruct((R, T // 2, C), BF),
        jax.ShapeDtypeStruct((R, T, C), F32),
        jax.ShapeDtypeStruct((32, C), F32),
        jax.ShapeDtypeStruct(outs[0], BF),
        jax.ShapeDtypeStruct(outs[1], BF),
    )
    spec = pl.BlockSpec(memory_space=pltpu.VMEM)
    return pl.pallas_call(
        functools.partial(main_kernel, NR),
        out_shape=out_shape,
        in_specs=[spec] * 8,
        out_specs=tuple([spec] * 5),
        scratch_shapes=scratch,
        compiler_params=pltpu.CompilerParams(collective_id=0, has_side_effects=True, vmem_limit_bytes=63 * 2**20),
        cost_estimate=pl.CostEstimate(flops=2 * 10**10, bytes_accessed=2 * 10**7, transcendentals=10**7),
    )(feat, ids, steps, cot, narrow, broad, gains, hidden)


def adam_update(grad, master, first, second, rate):
    moment = BETA_ONE * first + (1.0 - BETA_ONE) * grad
    square = BETA_TWO * second + (1.0 - BETA_TWO) * grad * grad
    corrected = moment / (1.0 - BETA_ONE**STEP)
    scaled = jnp.sqrt(square / (1.0 - BETA_TWO**STEP)) + EPS_ADAM
    return (moment, square, master - rate * (corrected / scaled + DECAY_RATE * master))


def adam_kernel(
    NR,
    gfull, bfull, small, nm, nf, ns, bm, bf_, bs, gm, gf, gs, hm, hf, hs, fout_in, igrad_in,
    fout, igrad, nmo, nso, nuo, bmo, bso, buo, gmo, gso, guo, hmo, hso, huo, nco, bco,
):
    igrad[...] = igrad_in[...]
    fout[...] = fout_in[...]
    SH, SB = nm.shape[0], bm.shape[0]
    rw = lax.axis_index("rows")
    for lo in range(0, SH // 32):
        rows = slice(32 * lo, 32 * lo + 32)
        g = gfull[lo].reshape(32, C).astype(F32)
        m, sq, up = adam_update(g, nm[rows], nf[rows], ns[rows], RATE_SLABS)
        nmo[rows], nso[rows], nuo[rows], nco[rows] = m, sq, up, up.astype(BF)
    for q in range(KR // C):
        cols = slice(q * C, q * C + C)
        g = bfull[:, :, cols].reshape(SB, C).astype(F32)
        m, sq, up = adam_update(g, bm[:, cols], bf_[:, cols], bs[:, cols], RATE_SLABS)
        bmo[:, cols], bso[:, cols], buo[:, cols], bco[:, cols] = m, sq, up, up.astype(BF)
    tot = small[...]
    gains_g = pltpu.roll(tot[0:16], (NR - rw) * (C // NR), 1)[:12, : C // NR]
    q = rw * (FF // NR) // C
    off = rw * (FF // NR) % C
    pick = iota((4, C), 0) == q
    hid = jnp.concatenate(
        [jnp.sum(jnp.where(pick, tot[16 + 4 * k : 20 + 4 * k], 0.0), axis=0, keepdims=True) for k in range(3)]
        + [jnp.zeros((5, C), F32)],
        axis=0,
    )
    hidden_g = pltpu.roll(hid, C - off, 1)[:3, : FF // NR]
    gmo[...], gso[...], guo[...] = adam_update(gains_g, gm[...], gf[...], gs[...], RATE_GAINS)
    hmo[...], hso[...], huo[...] = adam_update(hidden_g, hm[...], hf[...], hs[...], RATE_GAINS)


def run_adam(NR, gfull, bfull, small, fout, igrad, *state):
    shape = lambda a, dt=F32: jax.ShapeDtypeStruct(a.shape, dt)
    nm, bm, gm, hm = state[0], state[3], state[6], state[9]
    out_shape = (shape(fout, BF), shape(igrad)) + tuple(shape(a) for a in (nm, bm, gm, hm) for _ in range(3))
    out_shape += (shape(nm, BF), shape(bm, BF))
    spec = pl.BlockSpec(memory_space=pltpu.VMEM)
    return pl.pallas_call(
        functools.partial(adam_kernel, NR),
        out_shape=out_shape,
        in_specs=[spec] * 17,
        out_specs=tuple([spec] * 16),
        compiler_params=pltpu.CompilerParams(vmem_limit_bytes=60 * 2**20),
    )(gfull, bfull, small, *state, fout, igrad)


def local(
    features, segment_ids, timesteps, cotangent, narrow_slab, broad_slab, model_gains, hidden_gains,
    narrow_first, narrow_second, broad_first, broad_second, gains_first, gains_second, hidden_first, hidden_second,
):
    steps = timesteps
    groups = lax.axis_size("rows")
    if groups == 8:
        fout, igrad, small, gfull, bfull = run_main(
            groups, features, segment_ids, steps, cotangent, narrow_slab, broad_slab, model_gains, hidden_gains
        )
        return tuple(
            run_adam(
                groups, gfull, bfull, small, fout, igrad,
                narrow_slab, narrow_first, narrow_second, broad_slab, broad_first, broad_second,
                model_gains, gains_first, gains_second, hidden_gains, hidden_first, hidden_second,
            )
        )
    narrow_w = lax.all_gather(narrow_slab.astype(BF), "rows", axis=0, tiled=True)
    broad_w = lax.all_gather(broad_slab.astype(BF), "rows", axis=0, tiled=True)
    gains_all = lax.all_gather(model_gains.astype(BF), "rows", axis=1, tiled=True).astype(F32)
    hidden_all = lax.all_gather(hidden_gains.astype(BF), "rows", axis=1, tiled=True).astype(F32)
    fout, igrad, small, ngrad, bgrad = run_main(
        0, features, segment_ids, steps, cotangent, narrow_w, broad_w, gains_all, hidden_all
    )
    scat = lambda v: lax.psum(lax.psum_scatter(v, "rows", scatter_dimension=0, tiled=True), "frames")
    narrow_g = scat(ngrad.astype(F32).reshape(KC, C))
    broad_g = scat(bgrad.astype(F32).reshape(C, KR))
    small = lax.psum(small, ("rows", "frames"))
    i = lax.axis_index("rows")
    own = lambda a, n: lax.dynamic_slice_in_dim(a, i * n, n, 1)
    gains_g = own(small[:12], model_gains.shape[1])
    hidden_g = own(small[16:28].reshape(3, FF), hidden_gains.shape[1])
    narrow_new = adam_update(narrow_g, narrow_slab, narrow_first, narrow_second, RATE_SLABS)
    broad_new = adam_update(broad_g, broad_slab, broad_first, broad_second, RATE_SLABS)
    gains_new = adam_update(gains_g, model_gains, gains_first, gains_second, RATE_GAINS)
    hidden_new = adam_update(hidden_g, hidden_gains, hidden_first, hidden_second, RATE_GAINS)
    return (
        fout, igrad, *narrow_new, *broad_new, *gains_new, *hidden_new,
        narrow_new[2].astype(BF), broad_new[2].astype(BF),
    )


def solution(mesh):
    rows = P("rows", None)
    cols = P(None, "rows")
    act = P("rows", "frames", None)
    return jax.shard_map(
        local,
        mesh=mesh,
        in_specs=(act, rows, rows, act, rows, rows, cols, cols, rows, rows, rows, rows, cols, cols, cols, cols),
        out_specs=(act, act, rows, rows, rows, rows, rows, rows, cols, cols, cols, cols, cols, cols, rows, rows),
        check_vma=False,
    )
```

```python
import functools
import math

import jax
import jax.numpy as jnp
from jax import lax
from jax.experimental import pallas as pl
from jax.experimental.pallas import tpu as pltpu
from jax.sharding import PartitionSpec as P

C = 256
TE = 1024
H = 2
HD = 64
FF = 1024
G = 8
NSEG = 8
STEP = 10
KC = 4352
KR = 1536
INNER = 128
EPS_NORM = 1e-05
EPS_ADAM = 1e-08
BETA_ONE = 0.9
BETA_TWO = 0.999
RATE_SLABS = 0.08
RATE_GAINS = 0.4
DECAY_RATE = 0.01
MASK_FILL = -1e30

F32 = jnp.float32
BF = jnp.bfloat16
MESH = pl.DeviceIdType.MESH
OFF = 32
GROUP = C // G


def dot(a, b):
    return jnp.dot(a, b, preferred_element_type=F32)


def dot_nt(a, b):
    return lax.dot_general(a, b, (((1,), (1,)), ((), ())), preferred_element_type=F32)


def dot_tn(a, b):
    return lax.dot_general(a, b, (((0,), (0,)), ((), ())), preferred_element_type=F32)


def recip(x):
    r = pltpu.reciprocal(x, approx=True)
    return r * (2.0 - x * r)


def split2(x):
    hi = x.astype(BF)
    lo = (x - hi.astype(F32)).astype(BF)
    return hi, lo


def split3(x):
    hi = x.astype(BF).astype(F32)
    mid = (x - hi).astype(BF).astype(F32)
    lo = (x - hi - mid).astype(BF).astype(F32)
    return hi, mid, lo


def mish_parts(y):
    e = jnp.exp(jnp.minimum(y, 30.0))
    n = e * (e + 2.0)
    rc = recip(n + 2.0)
    t = n * rc
    d = t + y * (2.0 * rc) * (1.0 + t) * (e * pltpu.reciprocal(1.0 + e, approx=True))
    return t, d


def reduced_angle(a):
    k = jnp.floor(a * (1.0 / math.pi) + 0.5)
    r = (a - k * 3.140625) - k * 9.67653589793e-4
    r2 = r * r
    s = r * (1.0 + r2 * (-1.0 / 6 + r2 * (1.0 / 120 + r2 * (-1.0 / 5040 + r2 * (1.0 / 362880)))))
    c = 1.0 + r2 * (
        -0.5 + r2 * (1.0 / 24 + r2 * (-1.0 / 720 + r2 * (1.0 / 40320 + r2 * (-1.0 / 3628800))))
    )
    return k, s, c


def sine_pair(x):
    t = x - jnp.floor(x + 0.5)
    t2 = t * t
    s = t * (3.141582022 + t2 * (-5.167142796 + t2 * (2.541899025 - t2 * 0.5546361918)))
    c = 1.9999999069 + t2 * (-9.869585718 + t2 * (8.116823828 + t2 * (-2.663760321 + t2 * 0.4393935944)))
    return s, c


def iota(shape, dim):
    return lax.broadcasted_iota(jnp.int32, shape, dim)


def group_sum_matrix(shift):
    return jnp.where(iota((C, 128), 0) // GROUP + shift == iota((C, 128), 1), 1.0, 0.0).astype(BF)


def group_spread_matrix():
    return jnp.where(iota((128, C), 0) == iota((128, C), 1) // GROUP, 1.0, 0.0).astype(BF)


def compact(sums, squares):
    n = sums.shape[0]
    a = jnp.concatenate(split3(sums), axis=0).astype(BF)
    b = jnp.concatenate(split3(squares), axis=0).astype(BF)
    both = dot(a, group_sum_matrix(0)) + dot(b, group_sum_matrix(G))
    return both[0:n] + both[n : 2 * n] + both[2 * n : 3 * n]


def expand(tables):
    n = tables[0].shape[0]
    stacked = jnp.concatenate([p for t in tables for p in split3(t)], axis=0).astype(BF)
    wide = dot(stacked, group_spread_matrix())
    part = lambda i: wide[n * i : n * i + n]
    return [part(3 * i) + part(3 * i + 1) + part(3 * i + 2) for i in range(len(tables))]


def table_of(columns):
    parts = split3(columns)
    zero = jnp.zeros((104, columns.shape[1]), F32)
    return jnp.concatenate(list(parts) + [zero], axis=0).astype(BF)


def segment_sums(onehot_rows, values):
    hi, lo = split2(values)
    return dot(onehot_rows, hi) + dot(onehot_rows, lo)


def layer_norm_parts(v):
    mu = jnp.mean(v, axis=-1, keepdims=True)
    cen = v - mu
    rs = lax.rsqrt(jnp.mean(cen * cen, axis=-1, keepdims=True) + EPS_NORM)
    return cen * rs, rs


def layer_norm_back(d, n, rs, gain):
    dg = d * gain
    return (dg - jnp.mean(dg, axis=-1, keepdims=True) - n * jnp.mean(dg * n, axis=-1, keepdims=True)) * rs


def colsum(x):
    return jnp.sum(x, axis=0, keepdims=True)


def main_kernel(
    NR,
    feat, ids, steps, cot, narrow_in, broad_in, gains_in, hidden_in,
    fout, igrad, small, out_n, out_b,
    narrow_s, broad_s, gains, hidden, smallw, packf, hgrad, hacc, ggrad,
    ngrad_s, bgrad_s, inh, inb, inq, inbq, got, bgot, gfull, bfull, s_pack, s_in, s_own, s_rows, s_all, embp, ttout, ttin, tgbuf, tgall,
    uext, gyext, metab, ohrow, keymask, idp, counts, emb, tterm, sums, squares, tabs,
    zs, nrm1, der1, u2, nrm2, der2, resid, ll1, qs, kvall,
    statin, statout,
    kt, vt, qt, ffbuf, sbuf, ebuf, otb, invl, dos, dost,
    gf, nl2, shaped, ginner, r3s, r3b, gm, att, dq,
    part, rbuf, rbuf2, sumbuf, dqkv, g2, tg, edge,
    ga_s, ga_r, gx_s, gx_r, gc_s, gc_r,
    rc_s, rc_r, rx_s, rx_r, rd_s, rd_r, rf_s, rf_r, sa_s, sa_r, sb_s, sb_r, sc_s, sc_r, tt_s, tt_r, tf_s, tf_r, to_s, to_r,
    halo_s, halo_r, cot_s, cot_r, stat_s, stat_r, kv_s, kv_r, dkv_s, dkv_r, eg_s, eg_r, r3_s, r3_r,
):
    R, T = feat.shape[0], feat.shape[1]
    gr2, dn, g3 = igrad, resid, shaped
    TX = T + 2 * OFF
    L = ids.shape[1]
    HT = T // 2
    f = lax.axis_index("frames")
    rw = lax.axis_index("rows")
    sib = f + 1 - 2 * (f % 2)
    cross = (f + 2) % 4
    diag = 3 - f
    peers = (sib, cross, diag)

    gather = NR > 0
    ngrad, bgrad = (ngrad_s, bgrad_s) if gather else (out_n, out_b)
    broad = broad_s if gather else broad_in
    if gather:
        SH, SB = narrow_in.shape[0], broad_in.shape[0]
        NB = SH // 32
        narrow_s[pl.ds(rw * NB, NB)] = narrow_in[...].astype(BF).reshape(NB, 2, 16, C)
        broad[pl.ds(pl.multiple_of(rw * SB, 16), SB), :] = broad_in[...].astype(BF)
        packf[...] = jnp.zeros(packf.shape, F32)
        packf[0:12, 0 : C // NR] = gains_in[...]
        packf[12:15, :] = hidden_in[...]
        step_f = steps[...].astype(F32)
        step_hi = jnp.floor(step_f * (1.0 / 32.0))
        for r in range(R):
            packf[15:16, NSEG * r : NSEG * r + NSEG] = step_hi[r : r + 1]
            packf[15:16, 64 + NSEG * r : 64 + NSEG * r + NSEG] = step_f[r : r + 1] - 32.0 * step_hi[r : r + 1]
        smallw[rw] = packf[...].astype(BF)
    else:
        gains[0:12, :] = gains_in[...]
        hidden[0:3, :] = hidden_in[...]

    def wn(first, n):
        if gather:
            return narrow_s[first // 32 : (first + n) // 32].reshape(n, C)
        return narrow_in[first : first + n, :]

    barrier = pltpu.get_barrier_semaphore()
    for p in peers:
        pl.semaphore_signal(barrier, inc=1, device_id=(rw, p), device_id_type=MESH)
    for k in range(1, NR):
        pl.semaphore_signal(barrier, inc=1, device_id=((rw + k) % NR, f), device_id_type=MESH)
    pl.semaphore_wait(barrier, 3 + max(NR - 1, 0))

    def remote(src, dst, ssem, rsem, target):
        return pltpu.make_async_remote_copy(
            src_ref=src, dst_ref=dst, send_sem=ssem, recv_sem=rsem,
            device_id=(rw, target), device_id_type=MESH,
        )

    if gather:
        gx, gc = f // 2, f % 2
        conv_blocks = 3 * C // 32
        own_blocks = {
            0: {0: (0, NB), 1: (NB, conv_blocks)},
            1: {1: (24, 34), 2: (34, 48)},
            4: {2: (48, 51), 3: (51, 68), 4: (68, 72), 6: (104, 119), 7: (119, 136)},
        }
        ranges = {0: ((0, 24),), 1: ((24, 48),), 4: ((48, 72), (104, 136))}
        t_lo, t_hi = 9 * C // 32, (9 * C + TE) // 32
        owners = [s for s in range(NR) if max(NB * s, t_lo) < min(NB * (s + 1), t_hi)]
        is_owner = functools.reduce(jnp.logical_or, [rw == o for o in owners])
        kinds = (0, 1, 2, 4)

        def narrow_piece(g, lo, hi):
            return narrow_s.at[lo:hi, g // 2, :, pl.ds(pl.multiple_of(g % 2 * 128, 128), 128)]

        def broad_piece(g, lo, hi):
            width = KR // 4
            return broad.at[lo:hi, pl.ds(pl.multiple_of(g * width, 128), width)]

        def to_row(ref, ssem, rsem, row):
            return pltpu.make_async_remote_copy(
                src_ref=ref, dst_ref=ref, send_sem=ssem, recv_sem=rsem, device_id=(row, f), device_id_type=MESH
            )

        def sized(kind, n):
            if kind == 2:
                return broad.at[0 : n * SB, 0 : KR // 4]
            if kind == 3:
                return smallw.at[0:n]
            return narrow_s.at[0:n, 0, :, 0:128]

        def waits(kind, n, sends, sem):
            ref = sized(kind, n)
            cp = remote(ref, ref, sem, sem, cross)
            (cp.wait_send if sends else cp.wait_recv)()

        def by_row(counts, act):
            for n in sorted(set(counts)):
                if n:
                    rows_of = [s for s in range(NR) if counts[s] == n]
                    cond = functools.reduce(jnp.logical_or, [rw == s for s in rows_of])

                    @pl.when(cond)
                    def _():
                        act(n)

        def spread_start(kind):
            if kind in own_blocks:
                for s, (lo, hi) in own_blocks[kind].items():

                    @pl.when(rw == s)
                    def _():
                        for k in range(1, NR):
                            to_row(narrow_piece(f, lo, hi), ga_s.at[kind], ga_r.at[kind], (s + k) % NR).start()

                return
            for k in range(1, NR):
                if kind == 2:
                    at = pl.ds(pl.multiple_of(rw * SB, 16), SB)
                    ref = broad.at[at, pl.ds(pl.multiple_of(f * (KR // 4), 128), KR // 4)]
                else:
                    ref = smallw.at[rw]
                to_row(ref, ga_s.at[kind], ga_r.at[kind], (rw + k) % NR).start()

        def held(kind):
            sizes = [0] * NR
            for s, (lo, hi) in own_blocks[kind].items():
                sizes[s] = hi - lo
            return sizes

        def spread_arrive(kind):
            if kind in own_blocks:
                sizes = held(kind)
                by_row([sum(sizes) - n for n in sizes], lambda n: waits(kind, n, False, ga_r.at[kind]))
            else:
                waits(kind, NR - 1, False, ga_r.at[kind])

        def spread_end(kind):
            if kind in own_blocks:
                by_row([(NR - 1) * n for n in held(kind)], lambda n: waits(kind, n, True, ga_s.at[kind]))
            else:
                waits(kind, NR - 1, True, ga_s.at[kind])

        def pieces(kind, g):
            if kind == 2:
                return [broad_piece(g, 0, C)]
            return [narrow_piece(g, lo, hi) for lo, hi in ranges[kind]]

        def units(kind):
            return NR if kind == 2 else sum(hi - lo for lo, hi in ranges[kind])

        def pass_on(kind):
            spread_arrive(kind)
            for ref in pieces(kind, f):
                remote(ref, ref, gx_s.at[kind], gx_r.at[kind], cross).start()
            for ref in pieces(kind, f):
                remote(ref, ref, gc_s.at[kind, 0], gc_r.at[kind, 0], sib).start()

        def pass_across(kind):
            waits(kind, units(kind), False, gx_r.at[kind])
            for ref in pieces(kind, cross):
                remote(ref, ref, gc_s.at[kind, 1], gc_r.at[kind, 1], sib).start()

        def arrive(kind):
            for i in range(2):
                waits(kind, units(kind), False, gc_r.at[kind, i])

        def gather_end():
            for kind in kinds:
                spread_end(kind)
                waits(kind, units(kind), True, gx_s.at[kind])
                for i in range(2):
                    waits(kind, units(kind), True, gc_s.at[kind, i])
            spread_end(3)

            @pl.when(is_owner)
            def _():
                ref = ttout.at[0 : (NR - 1) * 8 * R]
                remote(ref, ref, tt_s.at[0], tt_s.at[0], cross).wait_send()

        spread_start(3)
        spread_start(0)

    def to_next(src, dst, ssem, rsem):
        return remote(src, dst, ssem, rsem, (f + 1) % 4)

    def to_prev(src, dst, ssem, rsem):
        return remote(src, dst, ssem, rsem, (f + 3) % 4)

    feat_down = to_next(feat.at[:, pl.ds(T - 16, 16)], uext.at[:, pl.ds(OFF - 16, 16)], halo_s.at[0], halo_r.at[0])
    feat_up = to_prev(feat.at[:, pl.ds(0, 16)], uext.at[:, pl.ds(OFF + T, 16)], halo_s.at[1], halo_r.at[1])
    cot_up = to_prev(cot.at[:, pl.ds(0, 16)], gyext.at[:, pl.ds(HT, 16)], cot_s.at[0], cot_r.at[0])

    @pl.when(f < 3)
    def _():
        feat_down.start()

    @pl.when(f > 0)
    def _():
        feat_up.start()
        cot_up.start()

    uext[:, 0 : OFF - 16, :] = jnp.zeros((R, OFF - 16, C), BF)
    uext[:, OFF + T + 16 :, :] = jnp.zeros((R, TX - OFF - T - 16, C), BF)
    g2[:, 0 : OFF - 16, :] = jnp.zeros((R, OFF - 16, C), BF)
    g2[:, OFF + T + 16 :, :] = jnp.zeros((R, TX - OFF - T - 16, C), BF)

    @pl.when(f == 0)
    def _():
        edge[:, 0] = jnp.zeros((3, R, 8, C), F32)
        uext[:, OFF - 16 : OFF, :] = jnp.zeros((R, 16, C), BF)

    @pl.when(f == 3)
    def _():
        edge[:, 1] = jnp.zeros((3, R, 8, C), F32)
        uext[:, OFF + T : OFF + T + 16, :] = jnp.zeros((R, 16, C), BF)
        gyext[:, HT : HT + 16, :] = jnp.zeros((R, 16, C), BF)

    ggrad[...] = jnp.zeros(ggrad.shape, F32)
    hgrad[...] = jnp.zeros(hgrad.shape, F32)

    idp[...] = jnp.full(idp.shape, -1.0, F32)
    idp[0:R, 128 : 128 + L] = ids[...].astype(F32)
    idv = idp[0:8]
    width = idv.shape[1]
    prev_row = jnp.where(pltpu.roll(idv, 1, 1) == idv, 1.0, 0.0)
    next_row = jnp.where(pltpu.roll(idv, width - 1, 1) == idv, 1.0, 0.0)
    idp[8:16, :] = prev_row
    idp[16:24, :] = next_row
    base = pl.multiple_of(f * T, 128)
    WX = T + 256
    win = idp[:, pl.ds(base, WX)]
    win = pltpu.roll(win, WX - (128 - OFF), 1)[:, : T + 128]
    own = idp[:, pl.ds(pl.multiple_of(base + 128, 128), T)]
    for r in range(R):
        n_lane = T + 128
        row_id = jnp.broadcast_to(win[r : r + 1], (8, n_lane))
        lab = iota((8, n_lane), 0).astype(F32)
        oh = jnp.where(row_id == lab, 1.0, 0.0)
        pn = jnp.where(
            lab == 0.0,
            jnp.broadcast_to(win[8 + r : 9 + r], (8, n_lane)),
            jnp.where(lab == 1.0, jnp.broadcast_to(win[16 + r : 17 + r], (8, n_lane)), 0.0),
        )
        block = jnp.concatenate([oh, oh, oh, pn, jnp.zeros((96, n_lane), F32)], axis=0)
        turned = block.T
        metab[r] = turned[:TX].astype(BF)
        lab_own = iota((8, T), 0).astype(F32)
        ohrow[r] = jnp.where(jnp.broadcast_to(own[r : r + 1], (8, T)) == lab_own, 1.0, 0.0)
        full = jnp.broadcast_to(idv[r : r + 1, 128 : 128 + L], (8, L))
        lab_full = iota((8, L), 0).astype(F32)
        ohf = jnp.where(full == lab_full, 1.0, 0.0)
        counts[8 * r : 8 * r + 8] = jnp.broadcast_to(jnp.sum(ohf, axis=1, keepdims=True) * float(GROUP), (8, 128))
        km = jnp.concatenate([(1.0 - ohf) * MASK_FILL, jnp.zeros((120, L), F32)], axis=0)
        keymask[r] = km.T.astype(BF)

    uext[:, OFF : OFF + T, :] = feat[...]
    gyext[:, 0:HT, :] = cot[...]

    half = TE // 2
    if not gather:
        freq = jnp.exp(iota((8, half), 1).astype(F32) * (-math.log(10000.0) / half))
        for r in range(R):
            turn = jnp.broadcast_to(steps[r : r + 1, :].astype(F32), (8, NSEG))
            ang = jnp.sum(jnp.where(iota((8, NSEG), 0) == iota((8, NSEG), 1), turn, 0.0), axis=1, keepdims=True) * freq
            k, s, c = reduced_angle(ang)
            sign = 1.0 - 2.0 * (k - 2.0 * jnp.floor(k * 0.5))
            both = jnp.concatenate([s * sign, c * sign], axis=1)
            emb[8 * r : 8 * r + 8, :] = both * mish_parts(both)[0]
    tw = 9 * C

    if gather:
        spread_start(1)
        spread_start(2)
        pass_on(0)
        spread_start(4)
        spread_arrive(3)
        wide = smallw[...].astype(F32)
        gains[...] = jnp.concatenate([wide[s, :, 0 : C // NR] for s in range(NR)], axis=1)
        hidden[0:3, :] = jnp.concatenate([wide[s, 12:15, :] for s in range(NR)], axis=1)
        @pl.when(is_owner)
        def _():
            same = iota((8 * R, 8 * R), 0) == iota((8 * R, 8 * R), 1)
            column = []
            for g in range(NR):
                row = wide[g, 15:16, 0 : 8 * R] * 32.0 + wide[g, 15:16, 64 : 64 + 8 * R]
                spread = jnp.broadcast_to(row, (8 * R, 8 * R))
                column.append(jnp.sum(jnp.where(same, spread, 0.0), axis=1, keepdims=True))
            at = iota((1, SH), 1) + (NB * rw - t_lo) * 32
            low = at < half
            freq = jnp.exp(jnp.where(low, at, at - half).astype(F32) * (-math.log(10000.0) / half))
            k, si, co = reduced_angle(jnp.concatenate(column, axis=0) * freq)
            v = jnp.where(low, si, co) * (1.0 - 2.0 * (k - 2.0 * jnp.floor(k * 0.5)))
            v = jnp.where((at >= 0) & (at < TE), v * mish_parts(v)[0], 0.0)
            embp[...] = v.astype(BF)
            ttout[...] = dot(embp[...], narrow_s[pl.ds(rw * NB, NB)].reshape(SH, C))
            for k2 in range(1, NR):
                to = (rw + k2) % NR
                pltpu.make_async_remote_copy(
                    src_ref=ttout.at[pl.ds(pl.multiple_of(to * 8 * R, 8), 8 * R)], dst_ref=ttin.at[rw],
                    send_sem=tt_s.at[0], recv_sem=tt_r.at[0], device_id=(to, f), device_id_type=MESH,
                ).start()
            ttin[rw] = ttout[pl.ds(pl.multiple_of(rw * 8 * R, 8), 8 * R)]

        pass_across(0)
        arrive(0)

    def own_prev(r):
        return metab[r, OFF : OFF + T, 24:25].astype(F32)

    def own_next(r):
        return metab[r, OFF : OFF + T, 25:26].astype(F32)

    def edge_copies(which, src):
        return (
            to_next(src.at[:, pl.ds(T - 8, 8)], edge.at[which, 0], eg_s.at[which, 0], eg_r.at[which, 0]),
            to_prev(src.at[:, pl.ds(0, 8)], edge.at[which, 1], eg_s.at[which, 1], eg_r.at[which, 1]),
        )

    def send_edges(which, src):
        down_cp, up_cp = edge_copies(which, src)

        @pl.when(f < 3)
        def _():
            down_cp.start()

        @pl.when(f > 0)
        def _():
            up_cp.start()

    def await_edges(which, src):
        down_cp, up_cp = edge_copies(which, src)

        @pl.when(f < 3)
        def _():
            down_cp.wait_send()
            up_cp.wait_recv()

        @pl.when(f > 0)
        def _():
            up_cp.wait_send()
            down_cp.wait_recv()

    def stat_copies(phase):
        return [
            remote(statout.at[phase], statin.at[phase, i], stat_s.at[phase], stat_r.at[phase, i], peers[i])
            for i in range(3)
        ]

    def keep_sums(r, first, second):
        oh = ohrow[r].astype(BF)
        at = pl.ds(pl.multiple_of(8 * r, 8), 8)
        sums[at] = segment_sums(oh, first)
        squares[at] = segment_sums(oh, second)

    def send_stats(phase):
        statout[phase] = compact(sums[...], squares[...])
        for cp in stat_copies(phase):
            cp.start()

    def total_stats(phase, wait=True):
        if wait:
            for cp in stat_copies(phase):
                cp.wait_recv()
            remote(statin.at[phase], statin.at[phase], stat_s.at[phase], stat_s.at[phase], sib).wait_send()
        return (statout[phase] + statin[phase, 0] + statin[phase, 1] + statin[phase, 2]) / jnp.maximum(counts[...], 1.0)

    group_lanes = iota((8 * R, 128), 1) < G

    def norm_scale(tot):
        second = pltpu.roll(tot, 128 - G, 1)
        return jnp.where(group_lanes, lax.rsqrt(jnp.maximum(second - tot * tot, 0.0) + EPS_NORM), 0.0)

    def norm_tables(phase):
        tot = total_stats(phase)
        inv = norm_scale(tot)
        tabs[:, 0:C], tabs[:, C : 2 * C] = expand([tot * inv, inv])

    def row_table(r, width):
        return table_of(tabs[pl.ds(pl.multiple_of(8 * r, 8), 8), 0:width])

    def conv_into(r, src, first_row):
        for j in range(3):
            zs[j] = dot(src[r], wn(first_row + j * C, C))

    @pl.when(f > 0)
    def _():
        feat_down.wait_recv()

    @pl.when(f < 3)
    def _():
        feat_up.wait_recv()

    def phase_one(r):
        conv_into(r, uext, 0)
        lo, hi = OFF - 16, OFF + T + 16
        n = hi - lo
        v = (
            zs[0, lo - 1 : hi - 1] * metab[r, lo:hi, 24:25].astype(F32)
            + zs[1, lo:hi]
            + zs[2, lo + 1 : hi + 1] * metab[r, lo:hi, 25:26].astype(F32)
        )
        nrm1[r, lo:hi] = v
        nrm1[r, 0:lo] = jnp.zeros((lo, C), F32)
        nrm1[r, hi:] = jnp.zeros((TX - hi, C), F32)
        vo = v[OFF - lo : OFF - lo + T]
        keep_sums(r, vo, vo * vo)

    for r in range(R):
        phase_one(r)
        if r == R - 1:
            send_stats(0)
        if gather:
            if r == 0:
                pass_on(1)
            elif r == 1:
                pass_on(2)
                pass_across(1)

    if gather:
        arrive(1)
    if gather:

        def take_terms(n):
            remote(ttin.at[0:n], ttin.at[0:n], tt_r.at[0], tt_r.at[0], cross).wait_recv()

        by_row([len(owners) - (s in owners) for s in range(NR)], take_terms)
        total = gains[2:3, :]
        for o in owners:
            total = total + ttin[o]
        tterm[...] = total
    else:
        tterm[...] = dot(emb[...].astype(BF), wn(tw, TE)) + gains[2:3, :]

    CH = TX // 4
    tabs[:, 2 * C : 3 * C] = tterm[...]
    norm_tables(0)

    def phase_two(r, carry):
        tab = row_table(r, 3 * C)

        def chunk(i, c2):
            rows = pl.ds(pl.multiple_of(i * CH, 16), CH)
            sp = dot(metab[r, rows], tab)
            n = nrm1[r, rows] * sp[:, C : 2 * C] - sp[:, :C]
            y = n * gains[0:1, :] + gains[1:2, :]
            t, d = mish_parts(y)
            nrm1[r, rows] = n
            der1[r, rows] = d.astype(BF)
            u2[r, rows] = (y * t + sp[:, 2 * C :]).astype(BF)
            return c2

        lax.fori_loop(0, 4, chunk, 0, unroll=True)
        conv_into(r, u2, 3 * C)
        v = (
            zs[0, OFF - 1 : OFF + T - 1] * own_prev(r)
            + zs[1, OFF : OFF + T]
            + zs[2, OFF + 1 : OFF + T + 1] * own_next(r)
        )
        nrm2[r] = v
        keep_sums(r, v, v * v)
        return carry

    lax.fori_loop(0, R, phase_two, 0)
    send_stats(1)
    if gather:
        pass_across(2)
        pass_on(4)
        arrive(2)
    norm_tables(1)

    def kv_copies(r):
        slot = lambda g: kvall.at[r, :, pl.ds(pl.multiple_of(g * T, 128), T)]
        mine, other = slot(f), slot(cross)
        return (
            remote(mine, mine, kv_s.at[0, r], kv_r.at[0, r], sib),
            remote(mine, mine, kv_s.at[1, r], kv_r.at[1, r], cross),
            remote(other, other, kv_s.at[2, r], kv_r.at[2, r], sib),
        )

    NCH = 4
    CT = T // NCH

    def phase_three(r, carry):
        tab = row_table(r, 2 * C)

        def chunk(i, c2):
            rows = pl.ds(pl.multiple_of(i * CT, 16), CT)
            xrows = pl.ds(pl.multiple_of(OFF + i * CT, 16), CT)
            sp = dot(metab[r, xrows], tab)
            n = nrm2[r, rows] * sp[:, C : 2 * C] - sp[:, :C]
            y = n * gains[3:4, :] + gains[4:5, :]
            t, d = mish_parts(y)
            nrm2[r, rows] = n
            der2[r, rows] = d.astype(BF)
            res = y * t + feat[r, rows].astype(F32)
            resid[r, rows] = res
            m, rs = layer_norm_parts(res)
            low = (m * gains[5:6, :] + gains[6:7, :]).astype(BF)
            ll1[r, rows] = low
            qkv = dot(low, broad[:, : 3 * INNER])
            qs[r, rows] = (qkv[:, :INNER].astype(BF).astype(F32) * HD ** (-0.5)).astype(BF)
            krows = pl.ds(pl.multiple_of(f * T + i * CT, 16), CT)
            kvall[r, 0, krows] = qkv[:, INNER : 2 * INNER].astype(BF)
            kvall[r, 1, krows] = qkv[:, 2 * INNER :].astype(BF)
            return c2

        lax.fori_loop(0, NCH, chunk, 0, unroll=True)
        if gather:

            @pl.when(r == 0)
            def _():
                pass_across(4)

        cps = kv_copies(r)
        cps[1].start()
        cps[0].start()
        return carry

    lax.fori_loop(0, R, phase_three, 0)
    send_edges(2, nrm2)

    @pl.when(f < 3)
    def _():
        cot_up.wait_recv()

    down = 6 * C

    def phase_down_back(r, carry):
        gy = gyext[r, 0:HT]
        even = dot_nt(gy, wn(down + C, C))
        own_gy = dot_nt(gy, wn(down + 2 * C, C))
        nxt = dot_nt(gyext[r], wn(down, C))
        zs[0, 0 : HT + 16] = nxt
        for hh in range(2):
            cols = slice(hh * 128, hh * 128 + 128)
            pm = r3s[2, pl.ds(8 + 1, HT, stride=2), :]
            nm = r3s[3, pl.ds(8 + 1, HT, stride=2), :]
            r3s[hh, pl.ds(8, HT, stride=2), :] = even[:, cols]
            r3s[hh, pl.ds(9, HT, stride=2), :] = own_gy[:, cols] * pm + zs[0, 1 : HT + 1, cols] * nm
        return carry

    def masks_strided(r):
        r3s[2, 8 : 8 + T] = jnp.broadcast_to(own_prev(r), (T, 128))
        r3s[3, 8 : 8 + T] = jnp.broadcast_to(own_next(r), (T, 128))

    def down_back(r, carry):
        masks_strided(r)
        phase_down_back(r, carry)
        ggrad[11:12, :] += colsum(gyext[r, 0:HT].astype(F32))
        for hh in range(2):
            gf[r, :, hh * 128 : hh * 128 + 128] = r3s[hh, 8 : 8 + T].astype(BF)
        ggrad[10:11, :] += colsum(gf[r].astype(F32))
        return carry

    if gather:
        arrive(4)
    lax.fori_loop(0, R, down_back, 0)

    def relay(r):
        cps = kv_copies(r)
        cps[1].wait_recv()
        cps[2].start()

    relay(0)
    if gather:
        gather_end()

    alpha = jnp.exp(hidden[1:2, :])
    inv_beta = jnp.exp(-hidden[2:3, :])
    alpha_beta = alpha * inv_beta
    alpha_pi = alpha * (1.0 / math.pi)
    NK = L // 512
    CF = T
    hacc[...] = jnp.zeros(hacc.shape, F32)
    lane128 = iota((T, 128), 1)

    def dkv_copies(r):
        return (
            remote(part.at[r, sib], rbuf.at[r, 0], dkv_s.at[0, r], dkv_r.at[0, r], sib),
            remote(part.at[r, diag], rbuf.at[r, 1], dkv_s.at[1, r], dkv_r.at[1, r], sib),
            remote(sumbuf.at[r], rbuf2.at[r], dkv_s.at[2, r], dkv_r.at[2, r], cross),
        )

    def phase_sum(r):
        cps = dkv_copies(r)
        cps[1].wait_recv()
        sumbuf[r] = (part[r, cross].astype(F32) + rbuf[r, 1].astype(F32)).astype(BF)
        cps[2].start()

    def phase_four(r, carry):
        cps = kv_copies(r)
        cps[0].wait_recv()
        cps[2].wait_recv()
        for cp in cps:
            cp.wait_send()
        kt[...] = kvall[r, 0].T
        vt[...] = kvall[r, 1].T
        qv = qs[r]
        ohq = jnp.where(lane128 < 8, metab[r, OFF : OFF + T], jnp.zeros((T, 128), BF))
        zero_q = jnp.zeros((T, 128), BF)
        q_heads = [jnp.where(lane128 // HD == h, qv, zero_q) for h in range(H)]
        TQ = T // 2
        units = [(h, q) for h in range(H) for q in range(2)]

        def scores(n):
            h, q = units[n]
            qrows = slice(q * TQ, q * TQ + TQ)
            qa = jnp.concatenate([q_heads[h][qrows], ohq[qrows]], axis=1)
            m8 = jnp.full((8, TQ), -3e38, F32)
            for i in range(NK):
                keys = slice(i * 512, i * 512 + 512)
                ka = jnp.concatenate([kvall[r, 0, keys], keymask[r, keys]], axis=1)
                sc = dot_nt(ka, qa)
                sbuf[n % 2, keys] = sc
                m8 = jnp.maximum(m8, jnp.max(sc.reshape(64, 8, TQ), axis=0))
            return jnp.max(m8, axis=0, keepdims=True)

        top = scores(0)
        for n, (h, q) in enumerate(units):
            later = scores(n + 1) if n + 1 < len(units) else None
            qcols = slice(q * TQ, q * TQ + TQ)
            l8 = jnp.zeros((8, TQ), F32)
            for i in range(NK):
                keys = slice(i * 512, i * 512 + 512)
                e = jnp.exp(sbuf[n % 2, keys] - top)
                ebuf[h, keys, qcols] = e.astype(BF)
                l8 = l8 + jnp.sum(e.reshape(64, 8, TQ), axis=0)
            inv = 1.0 / jnp.sum(l8, axis=0, keepdims=True)
            invl[h, :, qcols] = jnp.broadcast_to(inv, (8, TQ))
            hrows = slice(h * HD, (h + 1) * HD)
            otb[hrows, qcols] = dot(vt[hrows, :], ebuf[h, :, qcols]) * inv
            top = later
        att[r] = otb[...].T.astype(BF)

        @pl.when(r + 1 < R)
        def _():
            relay(r + 1)

        def ff_chunk(i, c2):
            rows = pl.ds(pl.multiple_of(i * CF, 16), CF)
            res2 = resid[r, rows] + (dot_nt(att[r, rows], broad[:, 3 * INNER : 4 * INNER]) + gains[7:8, :])
            n, rs = layer_norm_parts(res2)
            low = (n * gains[8:9, :] + gains[9:10, :]).astype(BF)
            nl2[r, rows] = low
            gfr = gf[r, rows]
            def products(b):
                w_in = broad[:, 4 * INNER + b * 256 : 4 * INNER + b * 256 + 256]
                w_out = wn(tw + TE + b * 256, 256)
                ffbuf[b % 2, 0] = dot(low, w_in)
                ffbuf[b % 2, 1] = dot_nt(gfr, w_out)
                return w_in, w_out

            out, back = None, None
            weights = products(0)
            for b in range(4):
                following = products(b + 1) if b < 3 else None
                cols = slice(b * 256, b * 256 + 256)
                acc = [hacc[k, :, cols] for k in range(3)]
                shs, gis = [], []
                for u in range(0, CF, 32):
                    inner = ffbuf[b % 2, 0, u : u + 32] + hidden[0:1, cols]
                    gs = ffbuf[b % 2, 1, u : u + 32]
                    s, c = sine_pair(inner * alpha_pi[:, cols])
                    s2 = s * s
                    part_g = gs * (s * c)
                    shs.append((inner + s2 * inv_beta[:, cols]).astype(BF))
                    gi = gs + part_g * alpha_beta[:, cols]
                    gis.append(gi.astype(BF))
                    for k, v in enumerate((gi, part_g * inner, gs * s2)):
                        acc[k] = acc[k] + jnp.sum(v.reshape(4, 8, 256), axis=0)
                for k in range(3):
                    hacc[k, :, cols] = acc[k]
                sh_all, gi_all = jnp.concatenate(shs, axis=0), jnp.concatenate(gis, axis=0)
                shaped[r, rows, cols] = sh_all
                ginner[r, rows, cols] = gi_all
                more, more_back = dot(sh_all, weights[1]), dot_nt(gi_all, weights[0])
                out = more if out is None else out + more
                back = more_back if back is None else back + more_back
                weights = following
            r3 = (res2 + (out + gains[10:11, :])).astype(BF)
            r3b[r, rows] = r3
            g_in = gfr.astype(F32)
            ggrad[8:9, :] += colsum(back * n)
            ggrad[9:10, :] += colsum(back)
            g_res2 = g_in + layer_norm_back(back, n, rs, gains[8:9, :])
            gr2[r, rows] = g_res2
            low_g = g_res2.astype(BF)
            gm[r, rows] = low_g
            ggrad[7:8, :] += colsum(low_g.astype(F32))
            dos[rows] = dot(low_g, broad[:, 3 * INNER : 4 * INNER]).astype(BF).astype(F32)
            return c2

        lax.fori_loop(0, T // CF, ff_chunk, 0)

        @pl.when(f < 3)
        def _():
            to_next(r3b.at[r, pl.ds(T - 16, 16)], r3b.at[r, pl.ds(T, 16)], r3_s.at[r], r3_r.at[r]).start()

        dot_t = dos[...].T
        for h in range(H):
            hrows = slice(h * HD, (h + 1) * HD)
            dost[hrows, :] = dot_t[hrows] * invl[h, 0:1, :]
        zero_t = jnp.zeros((HD, T), BF)
        d_rows, d_cols, d_half = [], [], []
        per_block = 1
        for h in range(H):
            hrows = slice(h * HD, (h + 1) * HD)
            d_rows.append(colsum(otb[hrows, :] * dost[hrows, :]))
            dh = dost[hrows, :].astype(BF)
            d_half.append(dh)
            d_cols.append(jnp.concatenate([dh, zero_t] if h == 0 else [zero_t, dh], axis=0))
        qt[...] = qs[r].T
        cps = dkv_copies(r)
        for n, block in enumerate((diag, sib, cross, f)):
            for i in range(per_block):
                keys = pl.ds(pl.multiple_of(block * T, 256), T)
                within = slice(0, T)
                for h in range(H):
                    hrows = slice(h * HD, (h + 1) * HD)
                    eh = ebuf[h, keys]
                    dp = dot(kvall[r, 1, keys], d_cols[h])
                    ds = (eh.astype(F32) * (dp - d_rows[h])).astype(BF)
                    part[r, block, 0, hrows, within] = dot_nt(qt[hrows, :], ds).astype(BF)
                    part[r, block, 1, hrows, within] = dot_nt(d_half[h], eh).astype(BF)
                    if n == 0 and i == 0:
                        dq[hrows, :] = dot(kt[hrows, keys], ds)
                    else:
                        dq[hrows, :] += dot(kt[hrows, keys], ds)
            if n == 0:
                cps[1].start()
            elif n == 1:
                cps[0].start()
            elif n == 2:
                phase_sum(r)
        dqkv[r, :, 0:INNER] = (dq[...].T * HD ** (-0.5)).astype(BF)
        return carry

    lax.fori_loop(0, R, phase_four, 0)

    if gather:
        rx, rc = f // 2, f % 2
        shard_blocks = NB
        n_groups = {1: ((48, 72), (104, 136)), 2: ((24, 48),), 3: ((0, 24),)}
        b_groups = {1: (4 * INNER, 2 * C), 2: (0, C)}
        b_at = {1: C, 2: 0}

        def half_cols(core, first, n):
            return pl.ds(pl.multiple_of(first + core * n, 128), n)

        def core_copies(g):
            out = [
                remote(ngrad.at[lo:hi, :, :, half_cols(1 - rc, 0, 128)], inh.at[lo:hi], rc_s.at[g - 1, i], rc_r.at[g - 1, i], sib)
                for i, (lo, hi) in enumerate(n_groups[g])
            ]
            if g in b_groups:
                first, n = b_groups[g]
                out.append(
                    remote(
                        bgrad.at[:, :, :, half_cols(1 - rc, first, n)], inb.at[:, :, :, b_at[g] : b_at[g] + n],
                        rc_s.at[g - 1, 2], rc_r.at[g - 1, 2], sib,
                    )
                )
            return out

        def cross_copies(g):
            out = [
                remote(ngrad.at[lo:hi, 1 - rx, :, half_cols(rc, 0, 128)], inq.at[lo:hi], rx_s.at[g - 1, i], rx_r.at[g - 1, i], cross)
                for i, (lo, hi) in enumerate(n_groups[g])
            ]
            if g in b_groups:
                first, n = b_groups[g]
                out.append(
                    remote(
                        bgrad.at[:, 1 - rx, :, half_cols(rc, first, n)], inbq.at[:, :, b_at[g] : b_at[g] + n],
                        rx_s.at[g - 1, 2], rx_r.at[g - 1, 2], cross,
                    )
                )
            return out

        def owner_copies(g, s, source):
            out = []
            for i, (lo, hi) in enumerate(n_groups[g]):
                a, b = max(lo, shard_blocks * s), min(hi, shard_blocks * (s + 1))
                if a < b:
                    out.append(
                        pltpu.make_async_remote_copy(
                            src_ref=ngrad.at[a:b, rx, :, half_cols(rc, 0, 128)],
                            dst_ref=got.at[source, a - shard_blocks * s : b - shard_blocks * s],
                            send_sem=rd_s.at[g - 1, 0], recv_sem=rd_r.at[g - 1, 0],
                            device_id=(s, f), device_id_type=MESH,
                        )
                    )
            if g in b_groups:
                first, n = b_groups[g]
                out.append(
                    pltpu.make_async_remote_copy(
                        src_ref=bgrad.at[s, rx, :, half_cols(rc, first, n)],
                        dst_ref=bgot.at[source, :, b_at[g] : b_at[g] + n],
                        send_sem=rd_s.at[g - 1, 1], recv_sem=rd_r.at[g - 1, 1],
                        device_id=(s, f), device_id_type=MESH,
                    )
                )
            return out

        def red_core(g):
            for cp in core_copies(g):
                cp.start()

        def red_cross(g):
            for cp in core_copies(g):
                cp.wait()
            mine = half_cols(rc, 0, 128)
            for lo, hi in n_groups[g]:
                ngrad[lo:hi, :, :, mine] = (ngrad[lo:hi, :, :, mine].astype(F32) + inh[lo:hi].astype(F32)).astype(BF)
            if g in b_groups:
                first, n = b_groups[g]
                cols = half_cols(rc, first, n)
                other = inb[:, :, :, b_at[g] : b_at[g] + n]
                bgrad[:, :, :, cols] = (bgrad[:, :, :, cols].astype(F32) + other.astype(F32)).astype(BF)
            for cp in cross_copies(g):
                cp.start()

        def red_owner(g):
            for cp in cross_copies(g):
                cp.wait()
            mine = half_cols(rc, 0, 128)
            for lo, hi in n_groups[g]:
                ngrad[lo:hi, rx, :, mine] = (ngrad[lo:hi, rx, :, mine].astype(F32) + inq[lo:hi].astype(F32)).astype(BF)
            if g in b_groups:
                first, n = b_groups[g]
                cols = half_cols(rc, first, n)
                other = inbq[:, :, b_at[g] : b_at[g] + n]
                bgrad[:, rx, :, cols] = (bgrad[:, rx, :, cols].astype(F32) + other.astype(F32)).astype(BF)
            for s in range(NR):

                @pl.when(rw != s)
                def _():
                    for cp in owner_copies(g, s, rw):
                        cp.start()

        def red_wait(g):
            overlap = [
                sum(max(0, min(hi, NB * (s + 1)) - max(lo, NB * s)) for lo, hi in n_groups[g]) for s in range(NR)
            ]

            def take(n, sends, sem):
                cp = remote(inq.at[0:n], inq.at[0:n], sem, sem, cross)
                (cp.wait_send if sends else cp.wait_recv)()

            by_row([sum(overlap) - n for n in overlap], lambda n: take(n, True, rd_s.at[g - 1, 0]))
            by_row([(NR - 1) * n for n in overlap], lambda n: take(n, False, rd_r.at[g - 1, 0]))
            if g in b_groups:
                ref = bgot.at[0 : NR - 1, :, b_at[g] : b_at[g] + b_groups[g][1]]
                cp = remote(ref, ref, rd_s.at[g - 1, 1], rd_r.at[g - 1, 1], cross)
                cp.wait_send()
                cp.wait_recv()

        def send_final(j, blk, size):
            for p in peers:
                remote(blk, blk, rf_s.at[j], rf_r.at[j], p).start()
            return remote(size, size, rf_s.at[j], rf_r.at[j], cross)

        def red_finish_broad():
            out = []
            for j, g in enumerate((1, 2)):
                cols = half_cols(rc, *b_groups[g])
                here = slice(b_at[g], b_at[g] + b_groups[g][1])
                total = bgrad[rw, rx, :, cols].astype(F32)
                for k in range(1, NR):
                    total = total + bgot[(rw + k) % NR, :, here].astype(F32)
                bfull[rx, :, cols] = total.astype(BF)
                out.append(send_final(j, bfull.at[rx, :, cols], bgot.at[0:3, :, here]))
            return out

        def red_finish_narrow():
            mine = half_cols(rc, 0, 128)
            total = ngrad[pl.ds(shard_blocks * rw, shard_blocks), rx, :, mine].astype(F32)
            for k in range(1, NR):
                total = total + got[(rw + k) % NR].astype(F32)
            gfull[:, rx, :, mine] = total.astype(BF)
            return [send_final(2, gfull.at[:, rx, :, mine], inq.at[0 : 3 * NB])]

        def terms_first():
            tgbuf[f] = tg[...]
            for p in peers:
                remote(tgbuf.at[f], tgbuf.at[f], tf_s.at[0], tf_r.at[0], p).start()

        def terms_second():
            remote(tgbuf.at[0:3], tgbuf.at[0:3], tf_s.at[0], tf_r.at[0], cross).wait()
            tgall[rw] = tgbuf[0] + tgbuf[1] + tgbuf[2] + tgbuf[3]
            for o in owners:

                @pl.when(rw != o)
                def _():
                    pltpu.make_async_remote_copy(
                        src_ref=tgall.at[rw], dst_ref=tgall.at[rw], send_sem=to_s.at[0], recv_sem=to_r.at[0],
                        device_id=(o, f), device_id_type=MESH,
                    ).start()

        def terms_third():
            def sent(n):
                remote(tgall.at[0:n], tgall.at[0:n], to_s.at[0], to_s.at[0], cross).wait_send()

            by_row([len(owners) - (s in owners) for s in range(NR)], sent)

            @pl.when(is_owner)
            def _():
                ref = tgall.at[0 : NR - 1]
                remote(ref, ref, to_r.at[0], to_r.at[0], cross).wait_recv()
                hi, lo = split2(tgall[...].reshape(NR * 8 * R, C))
                grad = (dot_tn(embp[...], hi) + dot_tn(embp[...], lo)).astype(BF).reshape(NB, 2, 16, C)
                for o in owners:
                    a, b = max(NB * o, t_lo) - NB * o, min(NB * (o + 1), t_hi) - NB * o

                    @pl.when(rw == o)
                    def _():
                        out_n[a:b] = grad[a:b]

        def small_first():
            s_pack[...] = small_rows()
            for i, p in enumerate(peers):
                remote(s_pack.at[pl.ds(pl.multiple_of(8 * p, 8), 8)], s_in.at[i], sa_s.at[0], sa_r.at[0], p).start()

        def small_second():
            remote(s_in, s_in, sa_s.at[0], sa_r.at[0], sib).wait()
            s_own[...] = s_pack[pl.ds(pl.multiple_of(8 * f, 8), 8)] + s_in[0] + s_in[1] + s_in[2]
            for k in range(1, NR):
                pltpu.make_async_remote_copy(
                    src_ref=s_own, dst_ref=s_rows.at[k - 1], send_sem=sb_s.at[0], recv_sem=sb_r.at[0],
                    device_id=((rw + k) % NR, f), device_id_type=MESH,
                ).start()

        def small_third():
            ref = s_rows.at[0 : NR - 1]
            remote(ref, ref, sb_s.at[0], sb_r.at[0], sib).wait()
            at = pl.ds(pl.multiple_of(8 * f, 8), 8)
            tot = s_own[...]
            for k in range(1, NR):
                tot = tot + s_rows[k - 1]
            s_all[at] = tot
            for p in peers:
                remote(s_all.at[at], s_all.at[at], sc_s.at[0], sc_r.at[0], p).start()

        def small_last():
            remote(s_in, s_in, sc_s.at[0], sc_r.at[0], sib).wait()

    def small_rows():
        hid = [hgrad[k : k + 1, q * C : (q + 1) * C] for k in range(3) for q in range(FF // C)]
        return jnp.concatenate([ggrad[...]] + hid + [jnp.zeros((4, C), F32)], axis=0)

    flat = lambda ref: ref[...].reshape(R * T, ref.shape[2])

    def put_n(first, value):
        n = value.shape[0]
        ngrad[first // 32 : (first + n) // 32] = value.astype(BF).reshape(n // 32, 2, 16, C)

    def put_b(first, value):
        bgrad[:, :, :, first : first + value.shape[1]] = value.astype(BF).reshape(C // 32, 2, 16, value.shape[1])

    zs[:, 0:C, :] = jnp.zeros((3, C, C), F32)

    def down_forward(r, carry):
        @pl.when(f > 0)
        def _():
            to_next(r3b.at[r, pl.ds(T - 16, 16)], r3b.at[r, pl.ds(T, 16)], r3_s.at[r], r3_r.at[r]).wait_recv()

        @pl.when(f < 3)
        def _():
            to_next(r3b.at[r, pl.ds(T - 16, 16)], r3b.at[r, pl.ds(T, 16)], r3_s.at[r], r3_r.at[r]).wait_send()

        @pl.when(f == 0)
        def _():
            r3b[r, T : T + 16, :] = jnp.zeros((16, C), BF)

        masks_strided(r)
        for hh in range(2):
            cols = slice(hh * 128, hh * 128 + 128)
            r3s[hh, 8 : 8 + T] = r3b[r, 0:T, cols].astype(F32)
            r3s[hh, 0:8] = r3b[r, T : T + 16, cols].astype(F32)[8:16]
        even = jnp.concatenate([r3s[hh, pl.ds(8, HT, stride=2), :] for hh in range(2)], axis=1).astype(BF)
        m_after = r3s[3, pl.ds(8, HT, stride=2), :]
        m_before = r3s[2, pl.ds(8, HT, stride=2), :]
        odd = jnp.concatenate([r3s[hh, pl.ds(9, HT, stride=2), :] * m_after for hh in range(2)], axis=1).astype(BF)
        before = jnp.concatenate([r3s[hh, pl.ds(7, HT, stride=2), :] * m_before for hh in range(2)], axis=1).astype(BF)
        gy = cot[r]
        out = gains[11:12, :]
        for j, blk in enumerate((before, even, odd)):
            out = out + dot(blk, wn(down + j * C, C))
            zs[j, 0:C, :] += dot_tn(blk, gy)
        fout[r] = out.astype(BF)
        return carry

    lax.fori_loop(0, R, down_forward, 0)
    for j in range(3):
        put_n(down + j * C, zs[j, 0:C, :])

    gf_all = flat(gf)
    for b in range(4):
        cols = slice(b * 256, b * 256 + 256)
        put_n(tw + TE + b * 256, dot_tn(shaped[:, :, cols].reshape(R * T, 256), gf_all))
        put_b(4 * INNER + b * 256, dot_tn(flat(nl2), ginner[:, :, cols].reshape(R * T, 256)))
    put_b(3 * INNER, dot_tn(flat(gm), flat(att)))
    hgrad[0:1, :] = colsum(hacc[0])
    hgrad[1:2, :] = colsum(hacc[1]) * alpha_beta
    hgrad[2:3, :] = colsum(hacc[2]) * (-inv_beta)
    if gather:
        red_core(1)

    def mean_tables(phase, norm_phase, gain_row):
        tot = total_stats(phase)
        iv = norm_scale(total_stats(norm_phase, wait=False))
        m1 = jnp.where(group_lanes, tot, 0.0)
        m2 = jnp.where(group_lanes, pltpu.roll(tot, 128 - G, 1), 0.0)
        tabs[:, 0:C], tabs[:, C : 2 * C], wide_iv = expand([m1 * iv, m2 * iv, iv])
        tabs[:, 2 * C : 3 * C] = wide_iv * gains[gain_row : gain_row + 1, :]

    def norm_back_start(r, gain_row):
        oh = ohrow[r].astype(BF)
        at = pl.ds(pl.multiple_of(8 * r, 8), 8)
        gain = gains[gain_row : gain_row + 1, :]
        first, second = segment_sums(oh, dn[r]), segment_sums(oh, zs[0, 0:T])
        ggrad[gain_row : gain_row + 1, :] += colsum(second)
        ggrad[gain_row + 1 : gain_row + 2, :] += colsum(first)
        sums[at], squares[at] = first * gain, second * gain

    def fold(x):
        return jnp.sum(x.reshape(x.shape[0] // 8, 8, x.shape[1]), axis=0)

    def phase_five(r, carry):
        cps = dkv_copies(r)
        cps[0].wait_recv()
        cps[2].wait_recv()
        for cp in cps:
            cp.wait_send()
        for i in range(2):
            tot = part[r, f, i].astype(F32) + rbuf[r, 0, i].astype(F32) + rbuf2[r, i].astype(F32)
            dqkv[r, :, (i + 1) * INNER : (i + 2) * INNER] = tot.T.astype(BF)
        zs[1, 0:T] = dot_nt(dqkv[r], broad[:, : 3 * INNER])
        acc_n = jnp.zeros((8, C), F32)
        acc = jnp.zeros((8, C), F32)
        for u in range(0, T, 64):
            rows = slice(u, u + 64)
            back = zs[1, rows]
            n, rs = layer_norm_parts(resid[r, rows])
            acc_n = acc_n + fold(back * n)
            acc = acc + fold(back)
            g_res = gr2[r, rows] + layer_norm_back(back, n, rs, gains[5:6, :])
            gr2[r, rows] = g_res
            d = g_res * der2[r, rows].astype(F32)
            dn[r, rows] = d
            zs[0, rows] = d * nrm2[r, rows]
        ggrad[5:6, :] += colsum(acc_n)
        ggrad[6:7, :] += colsum(acc)
        norm_back_start(r, 3)
        return carry

    lax.fori_loop(0, R, phase_five, 0)
    send_stats(2)
    send_edges(1, dn)
    if gather:
        red_cross(1)
    put_b(0, dot_tn(flat(ll1), flat(dqkv)))
    mean_tables(2, 1, 3)
    await_edges(2, nrm2)
    await_edges(1, dn)

    def norm_back_end(r, n, which, n_above, n_below):
        tab = row_table(r, 3 * C)

        def back(rows, d, norm):
            sp = dot(metab[r, rows], tab)[-d.shape[0] :] if rows.stop == OFF else dot(metab[r, rows], tab)[: d.shape[0]]
            return d * sp[:, 2 * C :] - sp[:, :C] - norm * sp[:, C : 2 * C]

        zero = jnp.zeros((8, C), F32)
        above = back(slice(OFF - 16, OFF), edge[which, 0, r], n_above)
        below = back(slice(OFF + T, OFF + T + 16), edge[which, 1, r], n_below)
        g2[r, OFF - 16 : OFF] = jnp.concatenate([zero, above], axis=0).astype(BF)
        g2[r, OFF + T : OFF + T + 16] = jnp.concatenate([below, zero], axis=0).astype(BF)
        for u in range(0, T, 128):
            rows = slice(OFF + u, OFF + u + 128)
            g2[r, rows] = back(rows, dn[r, u : u + 128], n[u : u + 128]).astype(BF)

    def build_g3(r):
        g = g2[r].astype(F32)
        zs[0] = g * metab[r, :, 24:25].astype(F32)
        zs[2] = g * metab[r, :, 25:26].astype(F32)
        g3[r, :, 0:C] = zs[0, OFF + 1 : OFF + T + 1].astype(BF)
        g3[r, :, C : 2 * C] = g2[r, OFF : OFF + T]
        g3[r, :, 2 * C : 3 * C] = zs[2, OFF - 1 : OFF + T - 1].astype(BF)

    def conv_back(r, first_row):
        out = jnp.zeros((T, C), F32)
        for j in range(3):
            out = out + dot_nt(g3[r, :, j * C : (j + 1) * C], wn(first_row + j * C, C))
        return out

    def kernel_grad(src, first_row):
        u = src[:, OFF : OFF + T, :].reshape(R * T, C)
        for j in range(3):
            put_n(first_row + j * C, dot_tn(u, g3[:, :, j * C : (j + 1) * C].reshape(R * T, C)))

    def phase_seven(r, carry):
        norm_back_end(r, nrm2[r], 1, edge[2, 0, r], edge[2, 1, r])
        build_g3(r)
        gh = conv_back(r, 3 * C)
        oh = ohrow[r].astype(BF)
        tgr = segment_sums(oh, gh)
        tg[pl.ds(pl.multiple_of(8 * r, 8), 8), :] = tgr
        ggrad[2:3, :] += colsum(tgr)
        for u in range(0, T, 64):
            d = gh[u : u + 64] * der1[r, OFF + u : OFF + u + 64].astype(F32)
            dn[r, u : u + 64] = d
            zs[0, u : u + 64] = d * nrm1[r, OFF + u : OFF + u + 64]
        norm_back_start(r, 0)
        return carry

    lax.fori_loop(0, R, phase_seven, 0)
    send_stats(3)
    send_edges(0, dn)
    if gather:
        terms_first()
        red_owner(1)
    kernel_grad(u2, 3 * C)
    if gather:
        red_core(2)
        terms_second()
    else:
        part_hi, part_lo = split2(tg[...])
        eb = emb[...].astype(BF)
        put_n(tw, dot_tn(eb, part_hi) + dot_tn(eb, part_lo))
    mean_tables(3, 0, 0)
    await_edges(0, dn)

    if gather:
        small_first()
        red_cross(2)
    else:
        small[...] = small_rows()

    def phase_g3(r, carry):
        norm_back_end(
            r, nrm1[r, OFF : OFF + T], 0, nrm1[r, OFF - 8 : OFF], nrm1[r, OFF + T : OFF + T + 8]
        )
        build_g3(r)
        return carry

    lax.fori_loop(0, R, phase_g3, 0)
    kernel_grad(uext, 0)
    if gather:
        red_core(3)
        small_second()
        red_owner(2)
        red_cross(3)
    for r in range(R):
        igrad[r] = gr2[r] + conv_back(r, 0)
        if gather and r == 1:
            red_owner(3)
    if gather:
        small_third()
        red_wait(1)
        red_wait(2)
        fin = red_finish_broad()
        red_wait(3)
        fin += red_finish_narrow()
        small_last()
        small[...] = s_all[...]
        for cp in fin:
            cp.wait()
        out_n[...] = gfull[...]
        out_b[...] = bfull[...]
        terms_third()

    @pl.when(f < 3)
    def _():
        feat_down.wait_send()

    @pl.when(f > 0)
    def _():
        feat_up.wait_send()
        cot_up.wait_send()


def run_main(fused, feat, ids, steps, cot, narrow, broad, gains, hidden):
    R, T, _ = feat.shape
    L = ids.shape[1]
    TX = T + 2 * OFF
    NR = fused
    vm = lambda shape, dt=F32: pltpu.VMEM(shape, dt)
    dma = lambda *shape: pltpu.SemaphoreType.DMA(shape)
    slots = max(NR, 1)
    if NR:
        wide = [vm((KC // 32, 2, 16, C), BF), vm((C, KR), BF)]
        red = [
            vm((KC // 32, 2, 16, C), BF), vm((C // 32, 2, 16, KR), BF), vm((KC // 32, 2, 16, 128), BF),
            vm((C // 32, 2, 16, KR // 2), BF), vm((KC // 32, 16, 128), BF), vm((C // 32, 16, KR // 2), BF),
            vm((NR, KC // NR // 32, 16, 128), BF), vm((NR, 16, KR // 2), BF),
            vm((KC // NR // 32, 2, 16, C), BF), vm((2, 16, KR), BF),
        ]
        outs = ((KC // NR // 32, 2, 16, C), (2, 16, KR))
    else:
        wide = [vm((16, 128), BF)] * 2
        red = [vm((16, 128), BF)] * 10
        outs = ((KC // 32, 2, 16, C), (C // 32, 2, 16, KR))
    scratch = wide + [
        vm((16, C)), vm((8, FF)), vm((slots, 16, 128), BF), vm((16, 128)), vm((8, FF)), vm((3, 8, FF)), vm((16, C)),
    ] + red + [
        vm((32, C)), vm((3, 8, C)), vm((8, C)), vm((slots, 8, C)), vm((32, C)),
        vm((slots * 8 * R, KC // slots if NR else 128), BF), vm((slots * 8 * R, C)), vm((slots, 8 * R, C)), vm((4, 8 * R, C)), vm((slots, 8 * R, C)),
        vm((R, TX, C), BF), vm((R, T // 2 + 16, C), BF), vm((R, TX, 128), BF),
        vm((R, 8, T)), vm((R, L, 128), BF), vm((24, L + 256)), vm((8 * R, 128)), vm((8 * R, TE)), vm((8 * R, C)),
        vm((8 * R, C)), vm((8 * R, C)), vm((8 * R, 3 * C)),
        vm((3, TX, C)), vm((R, TX, C)), vm((R, TX, C), BF), vm((R, TX, C), BF), vm((R, T, C)),
        vm((R, T, C), BF), vm((R, T, C)), vm((R, T, C), BF), vm((R, T, INNER), BF),
        vm((R, 2, L, INNER), BF),
        vm((4, 3, 8 * R, 128)), vm((4, 8 * R, 128)),
        vm((INNER, L), BF), vm((INNER, L), BF), vm((INNER, T), BF), vm((2, 2, T, C)), vm((2, L, T // 2)), vm((H, L, T), BF), vm((INNER, T)),
        vm((H, 8, T)), vm((T, INNER)), vm((INNER, T)),
        vm((R, T, C), BF), vm((R, T, C), BF),
        vm((R, T, FF), BF), vm((R, T, FF), BF), vm((4, T + 8, 128)), vm((R, T + 16, C), BF),
        vm((R, T, C), BF), vm((R, T, INNER), BF), vm((INNER, T)),
        vm((R, 4, 2, INNER, T), BF), vm((R, 2, 2, INNER, T), BF), vm((R, 2, INNER, T), BF), vm((R, 2, INNER, T), BF),
        vm((R, T, 3 * INNER), BF), vm((R, TX, C), BF), vm((8 * R, C)), vm((3, 2, R, 8, C)),
        dma(5), dma(5), dma(5), dma(5), dma(5, 2), dma(5, 2),
        dma(3, 3), dma(3, 3), dma(3, 3), dma(3, 3), dma(3, 2), dma(3, 2), dma(3), dma(3),
        dma(1), dma(1), dma(1), dma(1), dma(1), dma(1), dma(1), dma(1), dma(1), dma(1), dma(1), dma(1),
        dma(2), dma(2), dma(1), dma(1), dma(4), dma(4, 3), dma(3, R), dma(3, R),
        dma(3, R), dma(3, R), dma(3, 2), dma(3, 2), dma(R), dma(R),
    ]
    out_shape = (
        jax.ShapeDtypeStruct((R, T // 2, C), BF),
        jax.ShapeDtypeStruct((R, T, C), F32),
        jax.ShapeDtypeStruct((32, C), F32),
        jax.ShapeDtypeStruct(outs[0], BF),
        jax.ShapeDtypeStruct(outs[1], BF),
    )
    spec = pl.BlockSpec(memory_space=pltpu.VMEM)
    return pl.pallas_call(
        functools.partial(main_kernel, NR),
        out_shape=out_shape,
        in_specs=[spec] * 8,
        out_specs=tuple([spec] * 5),
        scratch_shapes=scratch,
        compiler_params=pltpu.CompilerParams(collective_id=0, has_side_effects=True, vmem_limit_bytes=63 * 2**20),
        cost_estimate=pl.CostEstimate(flops=2 * 10**10, bytes_accessed=2 * 10**7, transcendentals=10**7),
    )(feat, ids, steps, cot, narrow, broad, gains, hidden)


def adam_update(grad, master, first, second, rate):
    moment = BETA_ONE * first + (1.0 - BETA_ONE) * grad
    square = BETA_TWO * second + (1.0 - BETA_TWO) * grad * grad
    corrected = moment / (1.0 - BETA_ONE**STEP)
    scaled = jnp.sqrt(square / (1.0 - BETA_TWO**STEP)) + EPS_ADAM
    return (moment, square, master - rate * (corrected / scaled + DECAY_RATE * master))


def adam_kernel(
    NR,
    gfull, bfull, small, nm, nf, ns, bm, bf_, bs, gm, gf, gs, hm, hf, hs, fout_in, igrad_in,
    fout, igrad, nmo, nso, nuo, bmo, bso, buo, gmo, gso, guo, hmo, hso, huo, nco, bco,
):
    igrad[...] = igrad_in[...]
    fout[...] = fout_in[...]
    SH, SB = nm.shape[0], bm.shape[0]
    rw = lax.axis_index("rows")
    for lo in range(0, SH // 32):
        rows = slice(32 * lo, 32 * lo + 32)
        g = gfull[lo].reshape(32, C).astype(F32)
        m, sq, up = adam_update(g, nm[rows], nf[rows], ns[rows], RATE_SLABS)
        nmo[rows], nso[rows], nuo[rows], nco[rows] = m, sq, up, up.astype(BF)
    for q in range(KR // C):
        cols = slice(q * C, q * C + C)
        g = bfull[:, :, cols].reshape(SB, C).astype(F32)
        m, sq, up = adam_update(g, bm[:, cols], bf_[:, cols], bs[:, cols], RATE_SLABS)
        bmo[:, cols], bso[:, cols], buo[:, cols], bco[:, cols] = m, sq, up, up.astype(BF)
    tot = small[...]
    gains_g = pltpu.roll(tot[0:16], (NR - rw) * (C // NR), 1)[:12, : C // NR]
    q = rw * (FF // NR) // C
    off = rw * (FF // NR) % C
    pick = iota((4, C), 0) == q
    hid = jnp.concatenate(
        [jnp.sum(jnp.where(pick, tot[16 + 4 * k : 20 + 4 * k], 0.0), axis=0, keepdims=True) for k in range(3)]
        + [jnp.zeros((5, C), F32)],
        axis=0,
    )
    hidden_g = pltpu.roll(hid, C - off, 1)[:3, : FF // NR]
    gmo[...], gso[...], guo[...] = adam_update(gains_g, gm[...], gf[...], gs[...], RATE_GAINS)
    hmo[...], hso[...], huo[...] = adam_update(hidden_g, hm[...], hf[...], hs[...], RATE_GAINS)


def run_adam(NR, gfull, bfull, small, fout, igrad, *state):
    shape = lambda a, dt=F32: jax.ShapeDtypeStruct(a.shape, dt)
    nm, bm, gm, hm = state[0], state[3], state[6], state[9]
    out_shape = (shape(fout, BF), shape(igrad)) + tuple(shape(a) for a in (nm, bm, gm, hm) for _ in range(3))
    out_shape += (shape(nm, BF), shape(bm, BF))
    spec = pl.BlockSpec(memory_space=pltpu.VMEM)
    return pl.pallas_call(
        functools.partial(adam_kernel, NR),
        out_shape=out_shape,
        in_specs=[spec] * 17,
        out_specs=tuple([spec] * 16),
        compiler_params=pltpu.CompilerParams(vmem_limit_bytes=60 * 2**20),
    )(gfull, bfull, small, *state, fout, igrad)


def local(
    features, segment_ids, timesteps, cotangent, narrow_slab, broad_slab, model_gains, hidden_gains,
    narrow_first, narrow_second, broad_first, broad_second, gains_first, gains_second, hidden_first, hidden_second,
):
    steps = timesteps
    groups = lax.axis_size("rows")
    if groups == 8:
        fout, igrad, small, gfull, bfull = run_main(
            groups, features, segment_ids, steps, cotangent, narrow_slab, broad_slab, model_gains, hidden_gains
        )
        return tuple(
            run_adam(
                groups, gfull, bfull, small, fout, igrad,
                narrow_slab, narrow_first, narrow_second, broad_slab, broad_first, broad_second,
                model_gains, gains_first, gains_second, hidden_gains, hidden_first, hidden_second,
            )
        )
    narrow_w = lax.all_gather(narrow_slab.astype(BF), "rows", axis=0, tiled=True)
    broad_w = lax.all_gather(broad_slab.astype(BF), "rows", axis=0, tiled=True)
    gains_all = lax.all_gather(model_gains.astype(BF), "rows", axis=1, tiled=True).astype(F32)
    hidden_all = lax.all_gather(hidden_gains.astype(BF), "rows", axis=1, tiled=True).astype(F32)
    fout, igrad, small, ngrad, bgrad = run_main(
        0, features, segment_ids, steps, cotangent, narrow_w, broad_w, gains_all, hidden_all
    )
    scat = lambda v: lax.psum(lax.psum_scatter(v, "rows", scatter_dimension=0, tiled=True), "frames")
    narrow_g = scat(ngrad.astype(F32).reshape(KC, C))
    broad_g = scat(bgrad.astype(F32).reshape(C, KR))
    small = lax.psum(small, ("rows", "frames"))
    i = lax.axis_index("rows")
    own = lambda a, n: lax.dynamic_slice_in_dim(a, i * n, n, 1)
    gains_g = own(small[:12], model_gains.shape[1])
    hidden_g = own(small[16:28].reshape(3, FF), hidden_gains.shape[1])
    narrow_new = adam_update(narrow_g, narrow_slab, narrow_first, narrow_second, RATE_SLABS)
    broad_new = adam_update(broad_g, broad_slab, broad_first, broad_second, RATE_SLABS)
    gains_new = adam_update(gains_g, model_gains, gains_first, gains_second, RATE_GAINS)
    hidden_new = adam_update(hidden_g, hidden_gains, hidden_first, hidden_second, RATE_GAINS)
    return (
        fout, igrad, *narrow_new, *broad_new, *gains_new, *hidden_new,
        narrow_new[2].astype(BF), broad_new[2].astype(BF),
    )


def solution(mesh):
    rows = P("rows", None)
    cols = P(None, "rows")
    act = P("rows", "frames", None)
    return jax.shard_map(
        local,
        mesh=mesh,
        in_specs=(act, rows, rows, act, rows, rows, cols, cols, rows, rows, rows, rows, cols, cols, cols, cols),
        out_specs=(act, act, rows, rows, rows, rows, rows, rows, cols, cols, cols, cols, cols, cols, rows, rows),
        check_vma=False,
    )
```
